32 devices in a mesh: groups: 2 (over x), gx: 8 (over z, y), gy: 2 (over core).
Axes of the slice: x: 2, y: 2, z: 4, core: 2. Of those that a mesh axis runs over, the one named last changes fastest.
Arguments:
- tokens: bfloat16 [512, 16384], P('groups', 'gx'), parts along dimension 0, may hold values from -4000 to 4000
- norm_gain: float32 [16384], P('gx'), may hold values from 0.1 to 1.9
- w_query: bfloat16 [16384, 8192], P('gx', 'gy'), may hold values from -0.046875 to 0.046875
- w_key: bfloat16 [16384, 512], P('gx', 'gy'), may hold values from -0.09375 to 0.09375
- w_value: bfloat16 [16384, 512], P('gx', 'gy'), may hold values from -0.046875 to 0.046875
- w_out: bfloat16 [8192, 16384], P('gy', 'gx'), may hold values from -0.1875 to 0.1875
- cache_keys: bfloat16 [128, 1024, 512], P(('groups', 'gx'), None, 'gy'), parts along dimension 0, may hold values from -400 to 400
- cache_values: bfloat16 [128, 1024, 512], P(('groups', 'gx'), None, 'gy'), parts along dimension 0, may hold values from -4 to 4
- cache_lengths: int32 [128], P(('groups', 'gx')), parts along dimension 0, may hold values from 128 to 1024, as said below
Outputs:
- attended: bfloat16 [512, 16384], P(('groups', 'gy'), 'gx'), parts along dimension 0
The draws below stay inside these ranges and needn't reach their ends.
There are 2 independent parts, one for each index of `groups`. The reference program is written for one: setup_inputs(seed, part) draws one part's arguments, and reference() takes and returns one part's arrays. A program takes and returns all parts, laid end to end along the dimension named above; an argument that names none is the same for every part. Nothing has to cross between parts.
Inputs may be any that keep to these rules, and one draw needn't show every extreme that they name: `cache_lengths`: one sequence has exactly 1024 live slots.
All inputs are finite; a program needn't handle non-finite values.
Results may differ from the reference program's by a relative error of at most 0.012.
The reference program's roundings to bfloat16 on the way count: a program that leaves them out, or rounds other values in their place, can miss the bound.
Values may be sent and summed in bfloat16 or wider, within the bound.
No kernel may reach another device: no remote copies, remote signals or barrier semaphores. Data moves between devices by JAX's collectives and lax.ppermute only.
A program may use at most 128 MiB of HBM per device.

```python
import math
import jax
import jax.numpy as jnp
from jax import lax

D = 16384
HQ = 64
KVH = 4
HD = 128
NEW = 4
CACHE = 1024
SEQS = 64
ROWS = 256
GROUP = 16


def draw_tokens(key, part):
    key = jax.random.fold_in(key, 11)
    base_key, row_key, col_key = jax.random.split(key, 3)
    rising = 3.0 ** (jnp.arange(D, dtype=jnp.float32) / D)
    row_scale = jnp.exp(jax.random.uniform(row_key, (ROWS, 1), minval=0.0, maxval=math.log(10.0)))
    col_scale = jnp.exp(jax.random.uniform(col_key, (1, D), minval=0.0, maxval=math.log(10.0))) * rising[None, :]
    values = jnp.clip(jax.random.normal(base_key, (ROWS, D)), -4.0, 4.0) * row_scale * col_scale
    return values.astype(jnp.bfloat16)


def draw_cache_keys(key, part):
    key = jax.random.fold_in(key, 23)
    base_key = jax.random.fold_in(key, 0)
    values = jnp.clip(jax.random.normal(base_key, (SEQS, CACHE, KVH, HD)), -4.0, 4.0) * 2.0
    return values.reshape(SEQS, CACHE, KVH * HD).astype(jnp.bfloat16)


def draw_cache_lengths(key, part):
    key = jax.random.fold_in(key, 37)
    length_key, full_key = jax.random.split(key)
    lengths = jax.random.randint(length_key, (SEQS,), CACHE // 8, CACHE + 1)
    full_seq = jax.random.randint(full_key, (), 0, SEQS)
    return jnp.where(jnp.arange(SEQS, dtype=jnp.int32) == full_seq, CACHE, lengths).astype(jnp.int32)


def block_levels(stream_key, dims, cuts, least, largest):
    gain, own = 1.0, jax.random.fold_in(stream_key, 6)
    for dim, parts in cuts:
        heights = jnp.exp(jax.random.uniform(jax.random.fold_in(own, dim), (parts,), jnp.float32, least / len(cuts), largest / len(cuts)))
        gain = gain * jnp.repeat(heights, dims[dim] // parts).reshape([-1 if axis == dim else 1 for axis in range(len(dims))])
    return gain


def bell_draw(key, dims, width, bound, cuts=(), kind=jnp.bfloat16):
    result = width * jax.random.normal(key, dims, jnp.float32)
    if cuts:
        result = result * block_levels(key, dims, cuts, -0.22, 0.18)
    return jnp.clip(result, -bound, bound).astype(kind)


def setup_inputs(seed: int = 0, part: int = 0) -> dict:
    arg_keys = jax.random.split(jax.random.key(seed), 10)
    part_splits = jax.random.split(jax.random.fold_in(arg_keys[9], part), 10)
    tokens = draw_tokens(jax.random.fold_in(jax.random.fold_in(arg_keys[9], part), 71), part)
    norm_gain = jnp.clip(1.0 + 0.18 * jax.random.normal(arg_keys[1], (D,), jnp.float32), 0.1, 1.9)
    w_query = bell_draw(arg_keys[2], (D, HQ * HD), D ** -0.5, 0.046875, ((0, 8), (1, 2)))
    w_key = bell_draw(arg_keys[3], (D, KVH * HD), (D // 4) ** -0.5, 0.09375, ((0, 8), (1, 2)))
    w_value = bell_draw(arg_keys[4], (D, KVH * HD), D ** -0.5, 0.046875, ((0, 8), (1, 2)))
    w_out = bell_draw(arg_keys[5], (HQ * HD, D), (HQ * HD // 8) ** -0.5, 0.1875, ((0, 2), (1, 8)))
    cache_keys = draw_cache_keys(jax.random.fold_in(jax.random.fold_in(arg_keys[9], part), 71), part)
    cache_values = bell_draw(part_splits[7], (SEQS, CACHE, KVH * HD), 1.0, 4.0, ((0, 8), (2, 2)))
    cache_lengths = draw_cache_lengths(jax.random.fold_in(jax.random.fold_in(arg_keys[9], part), 71), part)
    return dict(tokens=tokens, norm_gain=norm_gain, w_query=w_query, w_key=w_key, w_value=w_value, w_out=w_out, cache_keys=cache_keys, cache_values=cache_values, cache_lengths=cache_lengths)


EPS = 1e-05
THETA = 500000.0

def rotate(head_rows, position):
    half_size = head_rows.shape[-1] // 2
    freq_steps = jnp.arange(half_size, dtype=jnp.float32)
    inverse = THETA ** (-2.0 * freq_steps / head_rows.shape[-1])
    angles = position.astype(jnp.float32)[:, None] * inverse[None, :]
    cosine = jnp.cos(angles)[:, None, :]
    sine_part = jnp.sin(angles)[:, None, :]
    first_half = head_rows[..., :half_size]
    second_half = head_rows[..., half_size:]
    return jnp.concatenate([first_half * cosine - second_half * sine_part, second_half * cosine + first_half * sine_part], axis=-1)

def attend_one(seq_item):
    query, new_keys, new_values, old_keys, old_values, length = seq_item
    scale = HD ** (-0.5)
    query_wide = query.astype(jnp.float32)
    old_scores = jnp.einsum('jgqd,tgd->gjqt', query_wide, old_keys.astype(jnp.float32)) * scale
    new_scores = jnp.einsum('jgqd,kgd->gjqk', query_wide, new_keys.astype(jnp.float32)) * scale
    old_live = (jnp.arange(CACHE, dtype=jnp.int32) < length)[None, None, None, :]
    new_live = (jnp.arange(NEW, dtype=jnp.int32)[None, :] <= jnp.arange(NEW, dtype=jnp.int32)[:, None])[None, :, None, :]
    old_scores = jnp.where(old_live, old_scores, -1e+30)
    new_scores = jnp.where(new_live, new_scores, -1e+30)
    top_score = jnp.maximum(lax.optimization_barrier(jnp.max(old_scores, axis=-1, keepdims=True)), lax.optimization_barrier(jnp.max(new_scores, axis=-1, keepdims=True)))
    old_exp = jnp.where(old_live, jnp.exp(old_scores - top_score), 0.0)
    new_exp = jnp.where(new_live, jnp.exp(new_scores - top_score), 0.0)
    total = lax.optimization_barrier(jnp.sum(old_exp, axis=-1, keepdims=True)) + lax.optimization_barrier(jnp.sum(new_exp, axis=-1, keepdims=True))
    old_weights = (old_exp / total).astype(jnp.bfloat16)
    new_weights = (new_exp / total).astype(jnp.bfloat16)
    combined = jnp.einsum('gjqt,tgd->jgqd', old_weights.astype(jnp.float32), old_values.astype(jnp.float32))
    combined = combined + jnp.einsum('gjqk,kgd->jgqd', new_weights.astype(jnp.float32), new_values.astype(jnp.float32))
    return combined.astype(jnp.bfloat16)

def reference(tokens, norm_gain, w_query, w_key, w_value, w_out, cache_keys, cache_values, cache_lengths):
    widened = tokens.astype(jnp.float32)
    row_scale = lax.rsqrt(lax.optimization_barrier(jnp.mean(widened * widened, axis=1, keepdims=True)) + EPS)
    scaled = (widened * norm_gain[None, :]).astype(jnp.bfloat16)
    query_raw = jnp.dot(scaled, w_query, preferred_element_type=jnp.float32) * row_scale
    key_raw = jnp.dot(scaled, w_key, preferred_element_type=jnp.float32) * row_scale
    new_values = (jnp.dot(scaled, w_value, preferred_element_type=jnp.float32) * row_scale).astype(jnp.bfloat16)
    position = (cache_lengths[:, None] + jnp.arange(NEW, dtype=jnp.int32)[None, :]).reshape(-1)
    query = rotate(query_raw.reshape(ROWS, HQ, HD), position).astype(jnp.bfloat16)
    new_keys = rotate(key_raw.reshape(ROWS, KVH, HD), position).astype(jnp.bfloat16)
    seq_items = (query.reshape(SEQS, NEW, KVH, GROUP, HD), new_keys.reshape(SEQS, NEW, KVH, HD), new_values.reshape(SEQS, NEW, KVH, HD), cache_keys.reshape(SEQS, CACHE, KVH, HD), cache_values.reshape(SEQS, CACHE, KVH, HD), cache_lengths)
    attention = lax.map(attend_one, seq_items).reshape(ROWS, HQ * HD)
    return jnp.dot(attention, w_out, preferred_element_type=jnp.float32).astype(jnp.bfloat16)
```

```python
import functools

import jax
import jax.numpy as jnp
from jax import lax
from jax.experimental import pallas as pl
from jax.experimental.pallas import tpu as pltpu
from jax.sharding import PartitionSpec as P

D = 16384
HD = 128
NEW = 4
EPS = 1e-05
THETA = 500000.0

CHUNKS = 1
TILE = 512
MIB = 1 << 20


def bit_orders(n):
    levels = n.bit_length() - 1
    first = list(range(levels))
    second = list(first)
    if levels > 1:
        second[0], second[1] = second[1], second[0]
    return first, second


def slot_shift(slot, order):
    levels = len(order)
    shift = 0
    for stage in range(levels):
        shift |= ((slot >> (levels - 1 - stage)) & 1) << order[stage]
    return shift


def exchange(value, n, cores, stage):
    orders = bit_orders(n)
    pairs = []
    for gx in range(n):
        for gy in range(cores):
            other = gx ^ (1 << orders[gy % 2][stage])
            pairs.append((gx * cores + gy, other * cores + gy))
    return lax.ppermute(value, ("gx", "gy"), pairs)


def project_kernel(
    n, tile, chunk, blocks_ref, *refs
):
    first = chunk == 0
    if first:
        tokens_ref, gain_ref, wq_ref, wk_ref, wv_ref, send_ref, keep_ref, x_ref = refs[:8]
    else:
        x_ref, wq_ref, wk_ref, wv_ref, send_ref, keep_ref = refs[:6]
    wq_buf, wk_buf, wv_buf, sems = refs[-4:]
    rows, half = 2 * send_ref.shape[0], send_ref.shape[0]
    depth = wq_ref.shape[0]
    tiles = wq_buf.shape[0]
    kv = wk_buf.shape[1]
    cols = tiles * tile

    def q_copy(i):
        return pltpu.make_async_copy(
            wq_ref.at[:, pl.ds(pl.multiple_of(chunk * cols + i * tile, tile), tile)],
            wq_buf.at[i],
            sems.at[i],
        )

    k_copy = pltpu.make_async_copy(
        wk_ref.at[:, pl.ds(chunk * kv, kv)], wk_buf, sems.at[tiles]
    )
    v_copy = pltpu.make_async_copy(
        wv_ref.at[:, pl.ds(chunk * kv, kv)], wv_buf, sems.at[tiles + 1]
    )
    for i in range(tiles):
        q_copy(i).start()
    k_copy.start()
    v_copy.start()

    extra = cols + 2 * kv
    if first:
        block = rows // n
        me = blocks_ref[0]
        lanes = lax.broadcasted_iota(jnp.int32, (block, 128), 1)
        for slot in range(n):
            start = pl.multiple_of(blocks_ref[slot] * block, block)
            wide = tokens_ref[pl.ds(start, block), :].astype(jnp.float32)
            x_ref[slot * block : (slot + 1) * block, :] = (wide * gain_ref[...]).astype(jnp.bfloat16)
            square = jnp.sum(wide * wide, axis=1, keepdims=True)
            high = square.astype(jnp.bfloat16).astype(jnp.float32)
            rest = square - high
            middle = rest.astype(jnp.bfloat16).astype(jnp.float32)
            low = rest - middle
            packed = jnp.where(
                lanes == 3 * me,
                high,
                jnp.where(lanes == 3 * me + 1, middle, jnp.where(lanes == 3 * me + 2, low, 0.0)),
            )
            if slot < n // 2:
                keep_ref[slot * block : (slot + 1) * block, extra : extra + 128] = packed
            else:
                at = (slot - n // 2) * block
                send_ref[at : at + block, extra : extra + 128] = packed.astype(jnp.bfloat16)

    def emit(weights, start, width):
        product = jnp.dot(x_ref[...], weights, preferred_element_type=jnp.float32)
        keep_ref[:, pl.ds(start, width)] = product[:half]
        send_ref[:, pl.ds(start, width)] = product[half:].astype(jnp.bfloat16)

    @pl.loop(0, tiles)
    def _(i):
        q_copy(i).wait()
        emit(wq_buf[i], pl.multiple_of(i * tile, tile), tile)

    k_copy.wait()
    emit(wk_buf[...], cols, kv)
    v_copy.wait()
    emit(wv_buf[...], cols + kv, kv)


def project(n, chunk, blocks, x, gain, w_query, w_key, w_value):
    rows, depth = x.shape
    cols = w_query.shape[1] // CHUNKS
    kv = w_key.shape[1] // CHUNKS
    tile = min(TILE, cols)
    tiles = cols // tile
    first = chunk == 0
    width = cols + 2 * kv + (128 if first else 0)
    any_spec = pl.BlockSpec(memory_space=pl.ANY)
    vmem = pl.BlockSpec(memory_space=pltpu.VMEM)
    out_shape = [
        jax.ShapeDtypeStruct((rows // 2, width), jnp.bfloat16),
        jax.ShapeDtypeStruct((rows // 2, width), jnp.float32),
    ]
    args = [x]
    in_specs = [pl.BlockSpec(memory_space=pltpu.SMEM), vmem]
    if first:
        out_shape.append(jax.ShapeDtypeStruct((rows, depth), jnp.bfloat16))
        args.append(gain)
        in_specs.append(vmem)
    return pl.pallas_call(
        functools.partial(project_kernel, n, tile, chunk),
        out_shape=out_shape,
        in_specs=in_specs + [any_spec] * 3,
        out_specs=[vmem] * len(out_shape),
        scratch_shapes=[
            pltpu.VMEM((tiles, depth, tile), jnp.bfloat16),
            pltpu.VMEM((depth, kv), jnp.bfloat16),
            pltpu.VMEM((depth, kv), jnp.bfloat16),
            pltpu.SemaphoreType.DMA((tiles + 2,)),
        ],
        compiler_params=pltpu.CompilerParams(vmem_limit_bytes=40 * MIB),
        cost_estimate=pl.CostEstimate(
            flops=2 * rows * depth * (cols + 2 * kv),
            bytes_accessed=2 * depth * (cols + 2 * kv) + 8 * rows * depth,
            transcendentals=0,
        ),
        name="project",
    )(blocks, *args, w_query, w_key, w_value)


def attend_kernel(stages, groups, heads, seqs, length_ref, *refs):
    sums, squares = refs[: stages + 1], refs[stages + 1 : 2 * stages + 2]
    cos_ref, sin_ref, k_ref, v_ref, out_ref, q_scr, o_scr = refs[2 * stages + 2 :]
    rows = seqs * NEW
    cols = groups * heads * HD
    total_squares = squares[0][...]
    for part in squares[1:]:
        total_squares = total_squares + part[...].astype(jnp.float32)
    mean = jnp.sum(total_squares, axis=1, keepdims=True) / D
    row_scale = lax.rsqrt(mean + EPS)
    cosine, sine = cos_ref[...], sin_ref[...]

    def raw(start):
        value = sums[0][:, start : start + HD]
        for part in sums[1:]:
            value = value + part[:, start : start + HD].astype(jnp.float32)
        return value * row_scale

    def rotary(value):
        return value * cosine + pltpu.roll(value, HD // 2, 1) * sine

    step = pl.program_id(0)
    scale = HD**-0.5
    slots = k_ref.shape[1]
    many = heads * NEW
    slot_ids = lax.broadcasted_iota(jnp.int32, (many, slots), 1)
    new_cols = lax.broadcasted_iota(jnp.int32, (many, rows), 1)
    new_rows = lax.broadcasted_iota(jnp.int32, (many, rows), 0) % NEW
    for g in range(groups):
        for h in range(heads):
            turned = rotary(raw((g * heads + h) * HD))
            for s in range(seqs):
                q_scr[s, h * NEW : (h + 1) * NEW, :] = turned[s * NEW : (s + 1) * NEW]
        new_keys = rotary(raw(cols + g * HD)).astype(jnp.bfloat16)
        new_values = raw(cols + (groups + g) * HD).astype(jnp.bfloat16)
        for s in range(seqs):
            length = length_ref[step * seqs + s]
            query = q_scr[s].astype(jnp.bfloat16)
            keys = k_ref[s, :, g * HD : (g + 1) * HD]
            values = v_ref[s, :, g * HD : (g + 1) * HD]
            old = lax.dot_general(
                query, keys, (((1,), (1,)), ((), ())), preferred_element_type=jnp.float32
            )
            new = lax.dot_general(
                query, new_keys, (((1,), (1,)), ((), ())), preferred_element_type=jnp.float32
            )
            old = jnp.where(slot_ids < length, old * scale, -1e30)
            seen = (new_cols >= s * NEW) & (new_cols <= s * NEW + new_rows)
            new = jnp.where(seen, new * scale, -1e30)
            top = jnp.maximum(
                jnp.max(old, axis=1, keepdims=True), jnp.max(new, axis=1, keepdims=True)
            )
            old = jnp.exp(old - top)
            new = jnp.exp(new - top)
            total = jnp.sum(old, axis=1, keepdims=True) + jnp.sum(new, axis=1, keepdims=True)
            inverse = 1.0 / total
            mixed = jnp.dot(
                (old * inverse).astype(jnp.bfloat16), values, preferred_element_type=jnp.float32
            ) + jnp.dot(
                (new * inverse).astype(jnp.bfloat16), new_values, preferred_element_type=jnp.float32
            )
            for h in range(heads):
                at = (g * heads + h) * HD
                o_scr[s * NEW : (s + 1) * NEW, at : at + HD] = mixed[h * NEW : (h + 1) * NEW]
    out_ref[...] = o_scr[...].astype(jnp.bfloat16)


def attend(chunk, sums, squares, cosine, sine, cache_keys, cache_values, lengths, square_col):
    seq_count, slots, kv_all = cache_keys.shape
    kv = kv_all // CHUNKS
    groups = kv // HD
    width = sums[0].shape[1]
    cols = width - 2 * kv - (128 if chunk == 0 else 0)
    heads = cols // kv
    seqs = min(4, seq_count)
    rows = seqs * NEW
    stages = len(sums) - 1
    wide = pl.BlockSpec((rows, width), lambda i, _: (i, 0))
    square = pl.BlockSpec((rows, 128), lambda i, _: (i, square_col))
    turn = pl.BlockSpec((rows, HD), lambda i, _: (i, 0))
    cache = pl.BlockSpec((seqs, slots, kv), lambda i, _: (i, 0, chunk))
    flops = 4 * seq_count * groups * heads * NEW * slots * HD
    return pl.pallas_call(
        functools.partial(attend_kernel, stages, groups, heads, seqs),
        out_shape=jax.ShapeDtypeStruct((seq_count * NEW, cols), jnp.bfloat16),
        grid_spec=pltpu.PrefetchScalarGridSpec(
            num_scalar_prefetch=1,
            grid=(seq_count // seqs,),
            in_specs=[wide] * (stages + 1) + [square] * (stages + 1) + [turn] * 2 + [cache] * 2,
            out_specs=pl.BlockSpec((rows, cols), lambda i, _: (i, 0)),
            scratch_shapes=[
                pltpu.VMEM((seqs, heads * NEW, HD), jnp.float32),
                pltpu.VMEM((rows, cols), jnp.float32),
            ],
        ),
        compiler_params=pltpu.CompilerParams(vmem_limit_bytes=32 * MIB),
        cost_estimate=pl.CostEstimate(
            flops=flops,
            bytes_accessed=4 * seq_count * slots * kv,
            transcendentals=seq_count * groups * heads * NEW * slots,
        ),
        name="attend",
    )(lengths, *sums, *squares, cosine, sine, cache_keys, cache_values)


def combine_kernel(block, tile, chunk, places_ref, *refs):
    pieces = refs[: places_ref.shape[0]]
    refs = refs[len(pieces) :]
    if chunk:
        before_ref, refs = refs[0], refs[1:]
    w_ref, outs, (x_buf, w_buf, w_sems, x_sems) = refs[0], refs[1:-4], refs[-4:]
    depth, tiles = x_buf.shape[1], w_buf.shape[0]
    half = x_buf.shape[0] // 2

    def w_copy(i):
        return pltpu.make_async_copy(
            w_ref.at[pl.ds(chunk * depth, depth), pl.ds(pl.multiple_of(i * tile, tile), tile)],
            w_buf.at[i],
            w_sems.at[i],
        )

    x_copies = []
    for slot, piece in enumerate(pieces):
        ref, at = piece
        start = pl.multiple_of(places_ref[slot] * block, block)
        x_copies.append(
            pltpu.make_async_copy(
                ref.at[pl.ds(at, block), :], x_buf.at[pl.ds(start, block), :], x_sems.at[slot]
            )
        )
    for copy in x_copies:
        copy.start()
    for i in range(tiles):
        w_copy(i).start()
    for copy in x_copies:
        copy.wait()

    @pl.loop(0, tiles)
    def _(i):
        w_copy(i).wait()
        at = pl.ds(pl.multiple_of(i * tile, tile), tile)
        product = jnp.dot(x_buf[...], w_buf[i], preferred_element_type=jnp.float32)
        if chunk:
            product = product + before_ref[:, at]
        if len(outs) == 1:
            outs[0][:, at] = product
        else:
            outs[0][:, at] = product[:half].astype(jnp.bfloat16)
            outs[1][:, at] = product[half:]


def combine(chunk, places, pieces, before, w_out):
    block = pieces[0].shape[0]
    n = sum(piece.shape[0] for piece in pieces) // block
    rows, depth = n * block, pieces[0].shape[1]
    cols = w_out.shape[1]
    tile = min(TILE, cols)
    tiles = cols // tile
    last = chunk == CHUNKS - 1
    any_spec = pl.BlockSpec(memory_space=pl.ANY)
    vmem = pl.BlockSpec(memory_space=pltpu.VMEM)
    spans = [(p, at) for p, piece in enumerate(pieces) for at in range(0, piece.shape[0], block)]

    def body(places_ref, *refs):
        arrays, rest = refs[: len(pieces)], refs[len(pieces) :]
        slots = [(arrays[p], at) for p, at in spans]
        combine_kernel(block, tile, chunk, places_ref, *slots, *rest)

    if last:
        out_shape = [
            jax.ShapeDtypeStruct((rows // 2, cols), jnp.bfloat16),
            jax.ShapeDtypeStruct((rows // 2, cols), jnp.float32),
        ]
    else:
        out_shape = [jax.ShapeDtypeStruct((rows, cols), jnp.float32)]
    earlier = [] if chunk == 0 else [before]
    return pl.pallas_call(
        body,
        out_shape=out_shape,
        in_specs=[pl.BlockSpec(memory_space=pltpu.SMEM)]
        + [any_spec] * len(pieces)
        + [vmem] * len(earlier)
        + [any_spec],
        out_specs=[vmem] * len(out_shape),
        scratch_shapes=[
            pltpu.VMEM((rows, depth), jnp.bfloat16),
            pltpu.VMEM((tiles, depth, tile), jnp.bfloat16),
            pltpu.SemaphoreType.DMA((tiles,)),
            pltpu.SemaphoreType.DMA((n,)),
        ],
        compiler_params=pltpu.CompilerParams(vmem_limit_bytes=40 * MIB),
        cost_estimate=pl.CostEstimate(
            flops=2 * rows * depth * cols,
            bytes_accessed=2 * depth * cols + 2 * rows * depth + 4 * rows * cols,
            transcendentals=0,
        ),
        name="combine",
    )(places, *pieces, *earlier, w_out)


def shards(
    tokens, norm_gain, w_query, w_key, w_value, w_out, cache_keys, cache_values, cache_lengths
):
    n = lax.axis_size("gx")
    cores = lax.axis_size("gy")
    levels = n.bit_length() - 1
    gx, gy = lax.axis_index("gx"), lax.axis_index("gy")
    shifts = [
        jnp.array([slot_shift(slot, order) for slot in range(n)], jnp.int32)
        for order in bit_orders(n)
    ]
    blocks = gx.astype(jnp.int32) ^ jnp.where(gy == 0, shifts[0], shifts[1])
    places = blocks ^ jnp.where(gy == 0, n // 2, 0).astype(jnp.int32)

    position = (cache_lengths[:, None] + jnp.arange(NEW, dtype=jnp.int32)[None, :]).reshape(-1)
    inverse = THETA ** (-2.0 * jnp.arange(HD // 2, dtype=jnp.float32) / HD)
    angles = position.astype(jnp.float32)[:, None] * inverse[None, :]
    cosine, sine = jnp.cos(angles), jnp.sin(angles)
    cosine = jnp.concatenate([cosine, cosine], axis=1)
    sine = jnp.concatenate([-sine, sine], axis=1)

    x, gain = tokens, norm_gain[None, :]
    gathered = []
    squares = None
    for chunk in range(CHUNKS):
        out = project(n, chunk, blocks, x, gain, w_query, w_key, w_value)
        send, keep = out[:2]
        if chunk == 0:
            x = out[2]
        sums = [keep]
        rows = keep.shape[0]
        for stage in range(levels):
            sums.append(exchange(send, n, cores, stage))
            if stage < levels - 1:
                low = rows // 2
                value = sums[0][low:rows]
                for part in sums[1:]:
                    value = value + part[low:rows].astype(jnp.float32)
                send = value.astype(jnp.bfloat16)
                rows = low
        if chunk == 0:
            squares = sums
            square_col = keep.shape[1] // 128 - 1
        attention = attend(
            chunk, sums, squares, cosine, sine, cache_keys, cache_values, cache_lengths, square_col
        )
        pieces = [attention]
        for stage in reversed(range(levels)):
            send = pieces[0] if len(pieces) == 1 else jnp.concatenate(pieces, axis=0)
            pieces.append(exchange(send, n, cores, stage))
        gathered.append(pieces)
    result = None
    for chunk in range(CHUNKS):
        result = combine(chunk, places, gathered[chunk], result and result[0], w_out)
    send, keep = result
    other = lax.ppermute(send, "gy", [(0, 1), (1, 0)])
    return (keep + other.astype(jnp.float32)).astype(jnp.bfloat16)


def solution(mesh):
    return jax.shard_map(
        shards,
        mesh=mesh,
        in_specs=(
            P("groups", "gx"),
            P("gx"),
            P("gx", "gy"),
            P("gx", "gy"),
            P("gx", "gy"),
            P("gy", "gx"),
            P(("groups", "gx"), None, "gy"),
            P(("groups", "gx"), None, "gy"),
            P(("groups", "gx")),
        ),
        out_specs=P(("groups", "gy"), "gx"),
        check_vma=False,
    )
```

```python
import functools

import jax
import jax.numpy as jnp
from jax import lax
from jax.experimental import pallas as pl
from jax.experimental.pallas import tpu as pltpu
from jax.sharding import PartitionSpec as P

D = 16384
HD = 128
NEW = 4
EPS = 1e-05
THETA = 500000.0

CHUNKS = 2
TILE = 256
AHEAD = 4
MIB = 1 << 20


def bit_orders(n):
    levels = n.bit_length() - 1
    first = list(range(levels))
    second = list(first)
    if levels > 1:
        second[0], second[1] = second[1], second[0]
    return first, second


def slot_shift(slot, order):
    levels = len(order)
    shift = 0
    for stage in range(levels):
        shift |= ((slot >> (levels - 1 - stage)) & 1) << order[stage]
    return shift


def slot_owner(n, slot, gx, gy):
    first, second = (slot_shift(slot, order) for order in bit_orders(n))
    return gx ^ jnp.where(gy == 0, first, second)


def exchange(value, n, cores, stage):
    orders = bit_orders(n)
    pairs = []
    for gx in range(n):
        for gy in range(cores):
            other = gx ^ (1 << orders[gy % 2][stage])
            pairs.append((gx * cores + gy, other * cores + gy))
    return lax.ppermute(value, ("gx", "gy"), pairs)


def project_kernel(n, tile, chunk, *refs):
    first = chunk == 0
    if first:
        tokens_ref, gain_ref, wq_ref, wk_ref, wv_ref, send_ref, keep_ref, x_ref = refs[:8]
    else:
        x_ref, wq_ref, wk_ref, wv_ref, send_ref, keep_ref = refs[:6]
    wq_buf, wk_buf, wv_buf, sems = refs[-4:]
    rows, half = 2 * send_ref.shape[0], send_ref.shape[0]
    depth = wq_ref.shape[0]
    tiles = wq_buf.shape[0]
    kv = wk_buf.shape[1]
    cols = tiles * tile

    def q_copy(i):
        return pltpu.make_async_copy(
            wq_ref.at[:, pl.ds(pl.multiple_of(chunk * cols + i * tile, tile), tile)],
            wq_buf.at[i],
            sems.at[i],
        )

    k_copy = pltpu.make_async_copy(
        wk_ref.at[:, pl.ds(chunk * kv, kv)], wk_buf, sems.at[tiles]
    )
    v_copy = pltpu.make_async_copy(
        wv_ref.at[:, pl.ds(chunk * kv, kv)], wv_buf, sems.at[tiles + 1]
    )
    for i in range(min(AHEAD, tiles)):
        q_copy(i).start()

    extra = cols + 2 * kv
    if first:
        block = rows // n
        me = lax.axis_index("gx")
        gy = lax.axis_index("gy")
        lanes = lax.broadcasted_iota(jnp.int32, (block, 128), 1)
        for slot in range(n):
            start = pl.multiple_of(slot_owner(n, slot, me, gy) * block, block)
            wide = tokens_ref[pl.ds(start, block), :].astype(jnp.float32)
            x_ref[slot * block : (slot + 1) * block, :] = (wide * gain_ref[...]).astype(jnp.bfloat16)
            square = jnp.sum(wide * wide, axis=1, keepdims=True)
            high = square.astype(jnp.bfloat16).astype(jnp.float32)
            rest = square - high
            middle = rest.astype(jnp.bfloat16).astype(jnp.float32)
            low = rest - middle
            packed = jnp.where(
                lanes == 3 * me,
                high,
                jnp.where(lanes == 3 * me + 1, middle, jnp.where(lanes == 3 * me + 2, low, 0.0)),
            )
            if slot < n // 2:
                keep_ref[slot * block : (slot + 1) * block, extra : extra + 128] = packed
            else:
                at = (slot - n // 2) * block
                send_ref[at : at + block, extra : extra + 128] = packed.astype(jnp.bfloat16)

    def emit(weights, start, width):
        product = jnp.dot(x_ref[...], weights, preferred_element_type=jnp.float32)
        keep_ref[:, pl.ds(start, width)] = product[:half]
        send_ref[:, pl.ds(start, width)] = product[half:].astype(jnp.bfloat16)

    @pl.loop(0, tiles)
    def _(i):
        q_copy(i).wait()

        @pl.when(i + AHEAD < tiles)
        def _():
            q_copy(i + AHEAD).start()

        @pl.when(i + AHEAD == tiles)
        def _():
            k_copy.start()
            v_copy.start()

        emit(wq_buf[i], pl.multiple_of(i * tile, tile), tile)

    k_copy.wait()
    emit(wk_buf[...], cols, kv)
    v_copy.wait()
    emit(wv_buf[...], cols + kv, kv)


def project(n, chunk, x, gain, w_query, w_key, w_value):
    rows, depth = x.shape
    cols = w_query.shape[1] // CHUNKS
    kv = w_key.shape[1] // CHUNKS
    tile = min(TILE, cols)
    tiles = cols // tile
    assert tiles >= AHEAD
    first = chunk == 0
    width = cols + 2 * kv + (128 if first else 0)
    hbm = pl.BlockSpec(memory_space=pltpu.HBM)
    vmem = pl.BlockSpec(memory_space=pltpu.VMEM)
    out_shape = [
        jax.ShapeDtypeStruct((rows // 2, width), jnp.bfloat16),
        jax.ShapeDtypeStruct((rows // 2, width), jnp.float32),
    ]
    args = [x]
    in_specs = [vmem]
    if first:
        out_shape.append(jax.ShapeDtypeStruct((rows, depth), jnp.bfloat16))
        args.append(gain)
        in_specs.append(vmem)
    return pl.pallas_call(
        functools.partial(project_kernel, n, tile, chunk),
        out_shape=out_shape,
        in_specs=in_specs + [hbm] * 3,
        out_specs=[vmem] * len(out_shape),
        scratch_shapes=[
            pltpu.VMEM((tiles, depth, tile), jnp.bfloat16),
            pltpu.VMEM((depth, kv), jnp.bfloat16),
            pltpu.VMEM((depth, kv), jnp.bfloat16),
            pltpu.SemaphoreType.DMA((tiles + 2,)),
        ],
        compiler_params=pltpu.CompilerParams(vmem_limit_bytes=48 * MIB),
        cost_estimate=pl.CostEstimate(
            flops=2 * rows * depth * (cols + 2 * kv),
            bytes_accessed=2 * depth * (cols + 2 * kv) + 8 * rows * depth,
            transcendentals=0,
        ),
        name="project",
    )(*args, w_query, w_key, w_value)


def attend_kernel(chunk, stages, groups, heads, seqs, length_ref, *refs):
    sums, squares = refs[: stages + 1], refs[stages + 1 : 2 * stages + 2]
    cos_ref, sin_ref, k_ref, v_ref, out_ref, k_buf, v_buf, q_scr, o_scr, sems = refs[
        2 * stages + 2 :
    ]
    rows = seqs * NEW
    cols = groups * heads * HD
    kv = groups * HD
    seq_count = k_ref.shape[0]

    def copies(b):
        at = pl.ds(chunk * kv, kv)
        return (
            pltpu.make_async_copy(k_ref.at[b, :, at], k_buf.at[b], sems.at[0, b]),
            pltpu.make_async_copy(v_ref.at[b, :, at], v_buf.at[b], sems.at[1, b]),
        )

    for b in range(seq_count):
        for copy in copies(b):
            copy.start()

    scale = HD**-0.5
    slots = k_ref.shape[1]
    many = heads * NEW
    slot_ids = lax.broadcasted_iota(jnp.int32, (many, slots), 1)
    new_cols = lax.broadcasted_iota(jnp.int32, (many, rows), 1)
    new_rows = lax.broadcasted_iota(jnp.int32, (many, rows), 0) % NEW

    @pl.loop(0, seq_count // seqs)
    def _(step):
        mine = pl.ds(pl.multiple_of(step * rows, rows), rows)
        total_squares = squares[0][mine, :]
        for part in squares[1:]:
            total_squares = total_squares + part[mine, :].astype(jnp.float32)
        mean = jnp.sum(total_squares, axis=1, keepdims=True) / D
        row_scale = lax.rsqrt(mean + EPS)
        cosine, sine = cos_ref[mine, :], sin_ref[mine, :]

        def raw(start):
            value = sums[0][mine, start : start + HD]
            for part in sums[1:]:
                value = value + part[mine, start : start + HD].astype(jnp.float32)
            return value * row_scale

        def rotary(value):
            return value * cosine + pltpu.roll(value, HD // 2, 1) * sine

        for g in range(groups):
            for h in range(heads):
                turned = rotary(raw((g * heads + h) * HD))
                for s in range(seqs):
                    q_scr[s, h * NEW : (h + 1) * NEW, :] = turned[s * NEW : (s + 1) * NEW]
            new_keys = rotary(raw(cols + g * HD)).astype(jnp.bfloat16)
            new_values = raw(cols + (groups + g) * HD).astype(jnp.bfloat16)
            for s in range(seqs):
                b = step * seqs + s
                if g == 0:
                    for copy in copies(b):
                        copy.wait()
                length = length_ref[b]
                query = q_scr[s].astype(jnp.bfloat16)
                keys = k_buf[b, :, g * HD : (g + 1) * HD]
                values = v_buf[b, :, g * HD : (g + 1) * HD]
                old = lax.dot_general(
                    query, keys, (((1,), (1,)), ((), ())), preferred_element_type=jnp.float32
                )
                new = lax.dot_general(
                    query, new_keys, (((1,), (1,)), ((), ())), preferred_element_type=jnp.float32
                )
                old = jnp.where(slot_ids < length, old * scale, -1e30)
                seen = (new_cols >= s * NEW) & (new_cols <= s * NEW + new_rows)
                new = jnp.where(seen, new * scale, -1e30)
                top = jnp.maximum(
                    jnp.max(old, axis=1, keepdims=True), jnp.max(new, axis=1, keepdims=True)
                )
                old = jnp.exp(old - top)
                new = jnp.exp(new - top)
                total = jnp.sum(old, axis=1, keepdims=True) + jnp.sum(new, axis=1, keepdims=True)
                inverse = 1.0 / total
                mixed = jnp.dot(
                    (old * inverse).astype(jnp.bfloat16),
                    values,
                    preferred_element_type=jnp.float32,
                ) + jnp.dot(
                    (new * inverse).astype(jnp.bfloat16),
                    new_values,
                    preferred_element_type=jnp.float32,
                )
                for h in range(heads):
                    at = (g * heads + h) * HD
                    o_scr[s * NEW : (s + 1) * NEW, at : at + HD] = mixed[h * NEW : (h + 1) * NEW]
        out_ref[mine, :] = o_scr[...].astype(jnp.bfloat16)


def attend(chunk, sums, squares, cosine, sine, cache_keys, cache_values, lengths, square_col):
    seq_count, slots, kv_all = cache_keys.shape
    kv = kv_all // CHUNKS
    groups = kv // HD
    width = sums[0].shape[1]
    cols = width - 2 * kv - (128 if chunk == 0 else 0)
    heads = cols // kv
    seqs = min(4, seq_count)
    rows = seq_count * NEW
    stages = len(sums) - 1
    wide = pl.BlockSpec((rows, width), lambda i, _: (0, 0))
    square = pl.BlockSpec((rows, 128), lambda i, _: (0, square_col))
    turn = pl.BlockSpec((rows, HD), lambda i, _: (0, 0))
    cache = pl.BlockSpec(memory_space=pltpu.HBM)
    flops = 4 * seq_count * groups * heads * NEW * slots * HD
    return pl.pallas_call(
        functools.partial(attend_kernel, chunk, stages, groups, heads, seqs),
        out_shape=jax.ShapeDtypeStruct((rows, cols), jnp.bfloat16),
        grid_spec=pltpu.PrefetchScalarGridSpec(
            num_scalar_prefetch=1,
            grid=(1,),
            in_specs=[wide] * (stages + 1) + [square] * (stages + 1) + [turn] * 2 + [cache] * 2,
            out_specs=pl.BlockSpec((rows, cols), lambda i, _: (0, 0)),
            scratch_shapes=[
                pltpu.VMEM((seq_count, slots, kv), jnp.bfloat16),
                pltpu.VMEM((seq_count, slots, kv), jnp.bfloat16),
                pltpu.VMEM((seqs, heads * NEW, HD), jnp.float32),
                pltpu.VMEM((seqs * NEW, cols), jnp.float32),
                pltpu.SemaphoreType.DMA((2, seq_count)),
            ],
        ),
        compiler_params=pltpu.CompilerParams(vmem_limit_bytes=48 * MIB),
        cost_estimate=pl.CostEstimate(
            flops=flops,
            bytes_accessed=4 * seq_count * slots * kv,
            transcendentals=seq_count * groups * heads * NEW * slots,
        ),
        name="attend",
    )(lengths, *sums, *squares, cosine, sine, cache_keys, cache_values)


def combine_kernel(n, block, tile, chunk, *refs):
    pieces, refs = refs[:n], refs[n:]
    gx, gy = lax.axis_index("gx"), lax.axis_index("gy")
    moved = jnp.where(gy == 0, n // 2, 0)
    if chunk:
        before_ref, refs = refs[0], refs[1:]
    w_ref, outs, (x_buf, w_buf, w_sems, x_sems) = refs[0], refs[1:-4], refs[-4:]
    depth, tiles = x_buf.shape[1], w_buf.shape[0]
    half = x_buf.shape[0] // 2

    def w_copy(i):
        return pltpu.make_async_copy(
            w_ref.at[pl.ds(chunk * depth, depth), pl.ds(pl.multiple_of(i * tile, tile), tile)],
            w_buf.at[i],
            w_sems.at[i],
        )

    x_copies = []
    for slot, piece in enumerate(pieces):
        ref, at = piece
        start = pl.multiple_of((slot_owner(n, slot, gx, gy) ^ moved) * block, block)
        x_copies.append(
            pltpu.make_async_copy(
                ref.at[pl.ds(at, block), :], x_buf.at[pl.ds(start, block), :], x_sems.at[slot]
            )
        )
    for copy in x_copies:
        copy.start()
    for i in range(min(AHEAD, tiles)):
        w_copy(i).start()
    for copy in x_copies:
        copy.wait()

    @pl.loop(0, tiles)
    def _(i):
        w_copy(i).wait()

        @pl.when(i + AHEAD < tiles)
        def _():
            w_copy(i + AHEAD).start()

        at = pl.ds(pl.multiple_of(i * tile, tile), tile)
        product = jnp.dot(x_buf[...], w_buf[i], preferred_element_type=jnp.float32)
        if chunk:
            product = product + before_ref[:, at]
        if len(outs) == 1:
            outs[0][:, at] = product
        else:
            outs[0][:, at] = product[:half].astype(jnp.bfloat16)
            outs[1][:, at] = product[half:]


def combine(chunk, pieces, before, w_out):
    block = pieces[0].shape[0]
    n = sum(piece.shape[0] for piece in pieces) // block
    rows, depth = n * block, pieces[0].shape[1]
    cols = w_out.shape[1]
    tile = min(TILE, cols)
    tiles = cols // tile
    last = chunk == CHUNKS - 1
    hbm = pl.BlockSpec(memory_space=pltpu.HBM)
    vmem = pl.BlockSpec(memory_space=pltpu.VMEM)
    spans = [(p, at) for p, piece in enumerate(pieces) for at in range(0, piece.shape[0], block)]

    def body(*refs):
        arrays, rest = refs[: len(pieces)], refs[len(pieces) :]
        slots = [(arrays[p], at) for p, at in spans]
        combine_kernel(n, block, tile, chunk, *slots, *rest)

    if last:
        out_shape = [
            jax.ShapeDtypeStruct((rows // 2, cols), jnp.bfloat16),
            jax.ShapeDtypeStruct((rows // 2, cols), jnp.float32),
        ]
    else:
        out_shape = [jax.ShapeDtypeStruct((rows, cols), jnp.float32)]
    earlier = [] if chunk == 0 else [before]
    return pl.pallas_call(
        body,
        out_shape=out_shape,
        in_specs=[pl.BlockSpec(memory_space=pl.ANY)] * len(pieces)
        + [vmem] * len(earlier)
        + [hbm],
        out_specs=[vmem] * len(out_shape),
        scratch_shapes=[
            pltpu.VMEM((rows, depth), jnp.bfloat16),
            pltpu.VMEM((tiles, depth, tile), jnp.bfloat16),
            pltpu.SemaphoreType.DMA((tiles,)),
            pltpu.SemaphoreType.DMA((n,)),
        ],
        compiler_params=pltpu.CompilerParams(vmem_limit_bytes=48 * MIB),
        cost_estimate=pl.CostEstimate(
            flops=2 * rows * depth * cols,
            bytes_accessed=2 * depth * cols + 2 * rows * depth + 4 * rows * cols,
            transcendentals=0,
        ),
        name="combine",
    )(*pieces, *earlier, w_out)


def shards(
    tokens, norm_gain, w_query, w_key, w_value, w_out, cache_keys, cache_values, cache_lengths
):
    n = lax.axis_size("gx")
    cores = lax.axis_size("gy")
    levels = n.bit_length() - 1
    position = (cache_lengths[:, None] + jnp.arange(NEW, dtype=jnp.int32)[None, :]).reshape(-1)
    inverse = THETA ** (-2.0 * jnp.arange(HD // 2, dtype=jnp.float32) / HD)
    angles = position.astype(jnp.float32)[:, None] * inverse[None, :]
    cosine, sine = jnp.cos(angles), jnp.sin(angles)
    cosine = jnp.concatenate([cosine, cosine], axis=1)
    sine = jnp.concatenate([-sine, sine], axis=1)

    x, gain = tokens, norm_gain[None, :]
    gathered = []
    squares = None
    for chunk in range(CHUNKS):
        out = project(n, chunk, x, gain, w_query, w_key, w_value)
        send, keep = out[:2]
        if chunk == 0:
            x = out[2]
        sums = [keep]
        rows = keep.shape[0]
        for stage in range(levels):
            sums.append(exchange(send, n, cores, stage))
            if stage < levels - 1:
                low = rows // 2
                value = sums[0][low:rows]
                for part in sums[1:]:
                    value = value + part[low:rows].astype(jnp.float32)
                send = value.astype(jnp.bfloat16)
                rows = low
        if chunk == 0:
            squares = sums
            square_col = keep.shape[1] // 128 - 1
        attention = attend(
            chunk, sums, squares, cosine, sine, cache_keys, cache_values, cache_lengths, square_col
        )
        pieces = [attention]
        for stage in reversed(range(levels)):
            send = pieces[0] if len(pieces) == 1 else jnp.concatenate(pieces, axis=0)
            pieces.append(exchange(send, n, cores, stage))
        gathered.append(pieces)
    result = None
    for chunk in range(CHUNKS):
        result = combine(chunk, gathered[chunk], result and result[0], w_out)
    send, keep = result
    other = lax.ppermute(send, "gy", [(0, 1), (1, 0)])
    return (keep + other.astype(jnp.float32)).astype(jnp.bfloat16)


def solution(mesh):
    return jax.shard_map(
        shards,
        mesh=mesh,
        in_specs=(
            P("groups", "gx"),
            P("gx"),
            P("gx", "gy"),
            P("gx", "gy"),
            P("gx", "gy"),
            P("gy", "gx"),
            P(("groups", "gx"), None, "gy"),
            P(("groups", "gx"), None, "gy"),
            P(("groups", "gx")),
        ),
        out_specs=P(("groups", "gy"), "gx"),
        check_vma=False,
    )
```

```python
import functools
import math

import jax
import jax.numpy as jnp
from jax import lax
from jax.experimental import pallas as pl
from jax.experimental.pallas import tpu as pltpu
from jax.sharding import PartitionSpec as P

D = 16384
HD = 128
NEW = 4
EPS = 1e-05
THETA = 500000.0

CHUNKS = 2
PARTS = 2
MIB = 1 << 20


def bit_orders(n):
    levels = n.bit_length() - 1
    first = list(range(levels))
    second = list(first)
    if levels > 1:
        second[0], second[1] = second[1], second[0]
    return first, second


def slot_shift(slot, order):
    levels = len(order)
    shift = 0
    for stage in range(levels):
        shift |= ((slot >> (levels - 1 - stage)) & 1) << order[stage]
    return shift


def slot_owner(n, slot, gx, gy):
    first, second = (slot_shift(slot, order) for order in bit_orders(n))
    return gx ^ jnp.where(gy == 0, first, second)


def exchange(value, n, cores, stage):
    orders = bit_orders(n)
    pairs = []
    for gx in range(n):
        for gy in range(cores):
            other = gx ^ (1 << orders[gy % 2][stage])
            pairs.append((gx * cores + gy, other * cores + gy))
    return lax.ppermute(value, ("gx", "gy"), pairs)


def project_kernel(n, parts, chunk, *refs):
    first = chunk == 0
    if first:
        tokens_ref, gain_ref, wq_ref, wk_ref, wv_ref, send_ref, keep_ref, x_ref = refs[:8]
        t_buf, t_sems = refs[8:10]
    else:
        x_ref, wq_ref, wk_ref, wv_ref, send_ref, keep_ref = refs[:6]
    w_buf, sems = refs[-2:]
    half = send_ref.shape[0]
    rows = 2 * half
    kv = wk_ref.shape[1] // CHUNKS
    cols = wq_ref.shape[1] // CHUNKS
    part = cols // parts
    tile = part // 2

    def w_copy(ref, start, width, at, sem):
        return pltpu.make_async_copy(
            ref.at[:, start : start + width], w_buf.at[:, at : at + width], sems.at[sem]
        )

    copies = [
        [
            w_copy(wq_ref, chunk * cols + at, tile, at, at // tile)
            for at in range(p * part, (p + 1) * part, tile)
        ]
        for p in range(parts)
    ]
    copies[-1].append(w_copy(wk_ref, chunk * kv, kv, cols, 2 * parts))
    copies[-1].append(w_copy(wv_ref, chunk * kv, kv, cols + kv, 2 * parts + 1))

    if first:
        block = rows // n
        me, gy = lax.axis_index("gx"), lax.axis_index("gy")
        t_copies = []
        for slot in range(n):
            start = pl.multiple_of(slot_owner(n, slot, me, gy) * block, block)
            t_copies.append(
                pltpu.make_async_copy(
                    tokens_ref.at[pl.ds(start, block), :], t_buf.at[slot], t_sems.at[slot]
                )
            )
            t_copies[-1].start()
    for group in copies:
        for copy in group:
            copy.start()
    if first:
        extra = cols + 2 * kv
        lanes = lax.broadcasted_iota(jnp.int32, (block, 128), 1)
        for slot in range(n):
            t_copies[slot].wait()
            wide = t_buf[slot].astype(jnp.float32)
            x_ref[slot * block : (slot + 1) * block, :] = (wide * gain_ref[...]).astype(jnp.bfloat16)
            square = jnp.sum(wide * wide, axis=1, keepdims=True)
            high = square.astype(jnp.bfloat16).astype(jnp.float32)
            rest = square - high
            middle = rest.astype(jnp.bfloat16).astype(jnp.float32)
            low = rest - middle
            packed = jnp.where(
                lanes == 3 * me,
                high,
                jnp.where(lanes == 3 * me + 1, middle, jnp.where(lanes == 3 * me + 2, low, 0.0)),
            )
            if slot < n // 2:
                keep_ref[slot * block : (slot + 1) * block, extra : extra + 128] = packed
            else:
                at = (slot - n // 2) * block
                send_ref[at : at + block, extra : extra + 128] = packed.astype(jnp.bfloat16)

    for p in range(parts):
        for copy in copies[p]:
            copy.wait()
        start, end = p * part, (p + 1) * part if p < parts - 1 else cols + 2 * kv
        product = jnp.dot(x_ref[...], w_buf[:, start:end], preferred_element_type=jnp.float32)
        keep_ref[:, start:end] = product[:half]
        send_ref[:, start:end] = product[half:].astype(jnp.bfloat16)


def in_hbm(value):
    return pltpu.with_memory_space_constraint(value, pltpu.HBM)


def project(n, chunk, x, gain, w_query, w_key, w_value):
    rows, depth = x.shape
    cols = w_query.shape[1] // CHUNKS
    kv = w_key.shape[1] // CHUNKS
    first = chunk == 0
    width = cols + 2 * kv + (128 if first else 0)
    hbm = pl.BlockSpec(memory_space=pltpu.HBM)
    vmem = pl.BlockSpec(memory_space=pltpu.VMEM)
    out_shape = [
        jax.ShapeDtypeStruct((rows // 2, width), jnp.bfloat16),
        jax.ShapeDtypeStruct((rows // 2, width), jnp.float32),
    ]
    scratch = [
        pltpu.VMEM((depth, cols + 2 * kv), jnp.bfloat16),
        pltpu.SemaphoreType.DMA((2 * PARTS + 2,)),
    ]
    if first:
        out_shape.append(jax.ShapeDtypeStruct((rows, depth), jnp.bfloat16))
        args = [in_hbm(x), in_hbm(gain)]
        in_specs = [hbm, vmem]
        scratch = [
            pltpu.VMEM((n, rows // n, depth), jnp.bfloat16),
            pltpu.SemaphoreType.DMA((n,)),
        ] + scratch
    else:
        args, in_specs = [x], [vmem]
    return pl.pallas_call(
        functools.partial(project_kernel, n, PARTS, chunk),
        out_shape=out_shape,
        in_specs=in_specs + [hbm] * 3,
        out_specs=[vmem] * len(out_shape),
        scratch_shapes=scratch,
        compiler_params=pltpu.CompilerParams(vmem_limit_bytes=28 * MIB),
        cost_estimate=pl.CostEstimate(
            flops=2 * rows * depth * (cols + 2 * kv),
            bytes_accessed=2 * depth * (cols + 2 * kv) + 8 * rows * depth,
            transcendentals=0,
        ),
        name="project",
    )(*args, in_hbm(w_query), in_hbm(w_key), in_hbm(w_value))


def attend_kernel(chunk, stages, groups, heads, seqs, length_ref, *refs):
    sums, squares = refs[: stages + 1], refs[stages + 1 : 2 * stages + 2]
    cos_ref, sin_ref, k_ref, v_ref, out_ref, k_buf, v_buf, q_scr, o_scr, sems = refs[
        2 * stages + 2 :
    ]
    rows = seqs * NEW
    cols = groups * heads * HD
    kv = groups * HD
    seq_count = k_ref.shape[0]

    def cache_copy(kind, b):
        source, target = ((k_ref, k_buf), (v_ref, v_buf))[kind]
        return pltpu.make_async_copy(
            source.at[b, :, pl.ds(chunk * kv, kv)], target.at[b], sems.at[kind, b]
        )

    for start in range(0, seq_count, seqs):
        for kind in range(2):
            for b in range(start, start + seqs):
                cache_copy(kind, b).start()

    scale = HD**-0.5 * math.log2(math.e)
    slots = k_ref.shape[1]
    many = heads * NEW
    slot_ids = lax.broadcasted_iota(jnp.int32, (1, slots), 1)
    new_cols = lax.broadcasted_iota(jnp.int32, (many, rows), 1)
    new_rows = lax.broadcasted_iota(jnp.int32, (many, rows), 0) % NEW

    @pl.loop(0, seq_count // seqs)
    def _(step):
        mine = pl.ds(pl.multiple_of(step * rows, rows), rows)
        total_squares = squares[0][mine, :]
        for part in squares[1:]:
            total_squares = total_squares + part[mine, :].astype(jnp.float32)
        mean = jnp.sum(total_squares, axis=1, keepdims=True) / D
        row_scale = lax.rsqrt(mean + EPS)
        cosine, sine = cos_ref[mine, :], sin_ref[mine, :]

        def raw(start):
            value = sums[0][mine, start : start + HD]
            for part in sums[1:]:
                value = value + part[mine, start : start + HD].astype(jnp.float32)
            return value * row_scale

        def rotary(value):
            return value * cosine + pltpu.roll(value, HD // 2, 1) * sine

        for h in range(heads * groups):
            turned = rotary(raw(h * HD))
            for s in range(seqs):
                q_scr[s, h * NEW : (h + 1) * NEW, :] = turned[s * NEW : (s + 1) * NEW]
        for s in range(seqs):
            cache_copy(0, step * seqs + s).wait()
            cache_copy(1, step * seqs + s).wait()
        for g in range(groups):
            new_keys = rotary(raw(cols + g * HD)).astype(jnp.bfloat16)
            new_values = raw(cols + (groups + g) * HD).astype(jnp.bfloat16)
            lanes = slice(g * HD, (g + 1) * HD)
            olds, news, mixes = [], [], []
            for s in range(seqs):
                query = q_scr[s, g * many : (g + 1) * many, :].astype(jnp.bfloat16)
                keys = k_buf[step * seqs + s, :, lanes]
                olds.append(
                    lax.dot_general(
                        query, keys, (((1,), (1,)), ((), ())), preferred_element_type=jnp.float32
                    )
                )
                news.append(
                    lax.dot_general(
                        query, new_keys, (((1,), (1,)), ((), ())), preferred_element_type=jnp.float32
                    )
                )
            for s in range(seqs):
                live = slot_ids < length_ref[step * seqs + s]
                seen = (new_cols >= s * NEW) & (new_cols <= s * NEW + new_rows)
                old = jnp.where(live, olds[s] * scale, -1e30)
                new = jnp.where(seen, news[s] * scale, -1e30)
                top = jnp.maximum(
                    jnp.max(old, axis=1, keepdims=True), jnp.max(new, axis=1, keepdims=True)
                )
                old = jnp.exp2(old - top)
                new = jnp.exp2(new - top)
                total = jnp.sum(old, axis=1, keepdims=True) + jnp.sum(new, axis=1, keepdims=True)
                inverse = 1.0 / total
                olds[s] = (old * inverse).astype(jnp.bfloat16)
                news[s] = (new * inverse).astype(jnp.bfloat16)
            for s in range(seqs):
                values = v_buf[step * seqs + s, :, lanes]
                mixes.append(
                    jnp.dot(olds[s], values, preferred_element_type=jnp.float32)
                    + jnp.dot(news[s], new_values, preferred_element_type=jnp.float32)
                )
            for s in range(seqs):
                for h in range(heads):
                    at = (g * heads + h) * HD
                    o_scr[s * NEW : (s + 1) * NEW, at : at + HD] = mixes[s][
                        h * NEW : (h + 1) * NEW
                    ]
        out_ref[mine, :] = o_scr[...].astype(jnp.bfloat16)


def attend(chunk, sums, squares, cosine, sine, cache_keys, cache_values, lengths, square_col):
    seq_count, slots, kv_all = cache_keys.shape
    kv = kv_all // CHUNKS
    groups = kv // HD
    width = sums[0].shape[1]
    cols = width - 2 * kv - (128 if chunk == 0 else 0)
    heads = cols // kv
    seqs = min(4, seq_count)
    rows = seq_count * NEW
    stages = len(sums) - 1
    wide = pl.BlockSpec((rows, width), lambda i, _: (0, 0))
    square = pl.BlockSpec((rows, 128), lambda i, _: (0, square_col))
    turn = pl.BlockSpec((rows, HD), lambda i, _: (0, 0))
    cache = pl.BlockSpec(memory_space=pltpu.HBM)
    flops = 4 * seq_count * groups * heads * NEW * slots * HD
    return pl.pallas_call(
        functools.partial(attend_kernel, chunk, stages, groups, heads, seqs),
        out_shape=jax.ShapeDtypeStruct((rows, cols), jnp.bfloat16),
        grid_spec=pltpu.PrefetchScalarGridSpec(
            num_scalar_prefetch=1,
            grid=(1,),
            in_specs=[wide] * (stages + 1) + [square] * (stages + 1) + [turn] * 2 + [cache] * 2,
            out_specs=pl.BlockSpec((rows, cols), lambda i, _: (0, 0)),
            scratch_shapes=[
                pltpu.VMEM((seq_count, slots, kv), jnp.bfloat16),
                pltpu.VMEM((seq_count, slots, kv), jnp.bfloat16),
                pltpu.VMEM((seqs, groups * heads * NEW, HD), jnp.float32),
                pltpu.VMEM((seqs * NEW, cols), jnp.float32),
                pltpu.SemaphoreType.DMA((2, seq_count)),
            ],
        ),
        compiler_params=pltpu.CompilerParams(vmem_limit_bytes=24 * MIB),
        cost_estimate=pl.CostEstimate(
            flops=flops,
            bytes_accessed=4 * seq_count * slots * kv,
            transcendentals=seq_count * groups * heads * NEW * slots,
        ),
        name="attend",
    )(lengths, *sums, *squares, cosine, sine, in_hbm(cache_keys), in_hbm(cache_values))


def combine_kernel(n, block, chunk, *refs):
    pieces, refs = refs[:n], refs[n:]
    gx, gy = lax.axis_index("gx"), lax.axis_index("gy")
    moved = jnp.where(gy == 0, n // 2, 0)
    if chunk:
        before_ref, refs = refs[0], refs[1:]
    w_ref, outs, (x_buf, w_buf, w_sems, x_sems) = refs[0], refs[1:-4], refs[-4:]
    depth, cols = w_buf.shape
    half = x_buf.shape[0] // 2
    part = cols // PARTS
    tile = part // 2

    def w_copy(at):
        return pltpu.make_async_copy(
            w_ref.at[chunk * depth : (chunk + 1) * depth, at : at + tile],
            w_buf.at[:, at : at + tile],
            w_sems.at[at // tile],
        )

    x_copies = []
    for slot, piece in enumerate(pieces):
        ref, at = piece
        start = pl.multiple_of((slot_owner(n, slot, gx, gy) ^ moved) * block, block)
        x_copies.append(
            pltpu.make_async_copy(
                ref.at[pl.ds(at, block), :], x_buf.at[pl.ds(start, block), :], x_sems.at[slot]
            )
        )
    for copy in x_copies:
        copy.start()
    for at in range(0, cols, tile):
        w_copy(at).start()
    for copy in x_copies:
        copy.wait()

    for start in range(0, cols, part):
        for at in range(start, start + part, tile):
            w_copy(at).wait()
        at = slice(start, start + part)
        product = jnp.dot(x_buf[...], w_buf[:, at], preferred_element_type=jnp.float32)
        if chunk:
            product = product + before_ref[:, at]
        if len(outs) == 1:
            outs[0][:, at] = product
        else:
            outs[0][:, at] = product[:half].astype(jnp.bfloat16)
            outs[1][:, at] = product[half:]


def combine(chunk, pieces, before, w_out):
    block = pieces[0].shape[0]
    n = sum(piece.shape[0] for piece in pieces) // block
    rows, depth = n * block, pieces[0].shape[1]
    cols = w_out.shape[1]
    last = chunk == CHUNKS - 1
    hbm = pl.BlockSpec(memory_space=pltpu.HBM)
    vmem = pl.BlockSpec(memory_space=pltpu.VMEM)
    spans = [(p, at) for p, piece in enumerate(pieces) for at in range(0, piece.shape[0], block)]

    def body(*refs):
        arrays, rest = refs[: len(pieces)], refs[len(pieces) :]
        slots = [(arrays[p], at) for p, at in spans]
        combine_kernel(n, block, chunk, *slots, *rest)

    if last:
        out_shape = [
            jax.ShapeDtypeStruct((rows // 2, cols), jnp.bfloat16),
            jax.ShapeDtypeStruct((rows // 2, cols), jnp.float32),
        ]
    else:
        out_shape = [jax.ShapeDtypeStruct((rows, cols), jnp.float32)]
    earlier = [] if chunk == 0 else [before]
    return pl.pallas_call(
        body,
        out_shape=out_shape,
        in_specs=[pl.BlockSpec(memory_space=pl.ANY)] * len(pieces)
        + [vmem] * len(earlier)
        + [hbm],
        out_specs=[vmem] * len(out_shape),
        scratch_shapes=[
            pltpu.VMEM((rows, depth), jnp.bfloat16),
            pltpu.VMEM((depth, cols), jnp.bfloat16),
            pltpu.SemaphoreType.DMA((2 * PARTS,)),
            pltpu.SemaphoreType.DMA((n,)),
        ],
        compiler_params=pltpu.CompilerParams(vmem_limit_bytes=24 * MIB),
        cost_estimate=pl.CostEstimate(
            flops=2 * rows * depth * cols,
            bytes_accessed=2 * depth * cols + 2 * rows * depth + 4 * rows * cols,
            transcendentals=0,
        ),
        name="combine",
    )(*pieces, *earlier, in_hbm(w_out))


def shards(
    tokens, norm_gain, w_query, w_key, w_value, w_out, cache_keys, cache_values, cache_lengths
):
    n = lax.axis_size("gx")
    cores = lax.axis_size("gy")
    levels = n.bit_length() - 1
    position = (cache_lengths[:, None] + jnp.arange(NEW, dtype=jnp.int32)[None, :]).reshape(-1)
    inverse = THETA ** (-2.0 * jnp.arange(HD // 2, dtype=jnp.float32) / HD)
    angles = position.astype(jnp.float32)[:, None] * inverse[None, :]
    cosine, sine = jnp.cos(angles), jnp.sin(angles)
    cosine = jnp.concatenate([cosine, cosine], axis=1)
    sine = jnp.concatenate([-sine, sine], axis=1)

    x, gain = tokens, norm_gain[None, :]
    gathered = []
    squares = None
    for chunk in range(CHUNKS):
        out = project(n, chunk, x, gain, w_query, w_key, w_value)
        send, keep = out[:2]
        if chunk == 0:
            x = out[2]
        sums = [keep]
        rows = keep.shape[0]
        for stage in range(levels):
            sums.append(exchange(send, n, cores, stage))
            if stage < levels - 1:
                low = rows // 2
                value = sums[0][low:rows]
                for part in sums[1:]:
                    value = value + part[low:rows].astype(jnp.float32)
                send = value.astype(jnp.bfloat16)
                rows = low
        if chunk == 0:
            squares = sums
            square_col = keep.shape[1] // 128 - 1
        attention = attend(
            chunk, sums, squares, cosine, sine, cache_keys, cache_values, cache_lengths, square_col
        )
        pieces = [attention]
        for stage in reversed(range(levels)):
            send = pieces[0] if len(pieces) == 1 else jnp.concatenate(pieces, axis=0)
            pieces.append(exchange(send, n, cores, stage))
        gathered.append(pieces)
    result = None
    for chunk in range(CHUNKS):
        result = combine(chunk, gathered[chunk], result and result[0], w_out)
    send, keep = result
    other = lax.ppermute(send, "gy", [(0, 1), (1, 0)])
    return (keep + other.astype(jnp.float32)).astype(jnp.bfloat16)


def solution(mesh):
    return jax.shard_map(
        shards,
        mesh=mesh,
        in_specs=(
            P("groups", "gx"),
            P("gx"),
            P("gx", "gy"),
            P("gx", "gy"),
            P("gx", "gy"),
            P("gy", "gx"),
            P(("groups", "gx"), None, "gy"),
            P(("groups", "gx"), None, "gy"),
            P(("groups", "gx")),
        ),
        out_specs=P(("groups", "gy"), "gx"),
        check_vma=False,
    )
```

```python
import functools
import math

import jax
import jax.numpy as jnp
from jax import lax
from jax.experimental import pallas as pl
from jax.experimental.pallas import tpu as pltpu
from jax.sharding import PartitionSpec as P

D = 16384
HD = 128
NEW = 4
EPS = 1e-05
THETA = 500000.0

CHUNKS = 2
PARTS = 2
MIB = 1 << 20


def bit_orders(n):
    levels = n.bit_length() - 1
    first = list(range(levels))
    second = list(first)
    if levels > 1:
        second[0], second[1] = second[1], second[0]
    return first, second


def slot_shift(slot, order):
    levels = len(order)
    shift = 0
    for stage in range(levels):
        shift |= ((slot >> (levels - 1 - stage)) & 1) << order[stage]
    return shift


def slot_owner(n, slot, gx, gy):
    first, second = (slot_shift(slot, order) for order in bit_orders(n))
    return gx ^ jnp.where(gy == 0, first, second)


def exchange(value, n, cores, stage):
    orders = bit_orders(n)
    pairs = []
    for gx in range(n):
        for gy in range(cores):
            other = gx ^ (1 << orders[gy % 2][stage])
            pairs.append((gx * cores + gy, other * cores + gy))
    return lax.ppermute(value, ("gx", "gy"), pairs)


def project_kernel(n, q_start, kv_start, first, *refs):
    if first:
        tokens_ref, gain_ref, wq_ref, wk_ref, wv_ref, send_ref, keep_ref, x_ref = refs[:8]
        t_buf, t_sems = refs[8:10]
    else:
        x_ref, wq_ref, wk_ref, wv_ref, send_ref, keep_ref = refs[:6]
    w_buf, sems = refs[-2:]
    half = send_ref.shape[0]
    rows = 2 * half
    with_kv = kv_start is not None
    kv = wk_ref.shape[1] // CHUNKS if with_kv else 0
    width = w_buf.shape[1]
    cols = width - 2 * kv
    tile = cols // 2

    def w_copy(ref, start, size, at, sem):
        return pltpu.make_async_copy(
            ref.at[:, start : start + size], w_buf.at[:, at : at + size], sems.at[sem]
        )

    copies = [[w_copy(wq_ref, q_start + at, tile, at, at // tile)] for at in (0, tile)]
    if with_kv:
        copies[1].append(w_copy(wk_ref, kv_start, kv, cols, 2))
        copies[1].append(w_copy(wv_ref, kv_start, kv, cols + kv, 3))

    if first:
        block = rows // n
        me, gy = lax.axis_index("gx"), lax.axis_index("gy")
        t_copies = []
        for slot in range(n):
            start = pl.multiple_of(slot_owner(n, slot, me, gy) * block, block)
            t_copies.append(
                pltpu.make_async_copy(
                    tokens_ref.at[pl.ds(start, block), :], t_buf.at[slot], t_sems.at[slot]
                )
            )
            t_copies[-1].start()
    for group in copies:
        for copy in group:
            copy.start()
    if first:
        lanes = lax.broadcasted_iota(jnp.int32, (block, 128), 1)
        for slot in range(n):
            t_copies[slot].wait()
            wide = t_buf[slot].astype(jnp.float32)
            x_ref[slot * block : (slot + 1) * block, :] = (wide * gain_ref[...]).astype(jnp.bfloat16)
            square = jnp.sum(wide * wide, axis=1, keepdims=True)
            high = square.astype(jnp.bfloat16).astype(jnp.float32)
            rest = square - high
            middle = rest.astype(jnp.bfloat16).astype(jnp.float32)
            low = rest - middle
            packed = jnp.where(
                lanes == 3 * me,
                high,
                jnp.where(lanes == 3 * me + 1, middle, jnp.where(lanes == 3 * me + 2, low, 0.0)),
            )
            if slot < n // 2:
                keep_ref[slot * block : (slot + 1) * block, width : width + 128] = packed
            else:
                at = (slot - n // 2) * block
                send_ref[at : at + block, width : width + 128] = packed.astype(jnp.bfloat16)

    for p, (start, end) in enumerate(((0, tile), (tile, width))):
        for copy in copies[p]:
            copy.wait()
        product = jnp.dot(x_ref[...], w_buf[:, start:end], preferred_element_type=jnp.float32)
        keep_ref[:, start:end] = product[:half]
        send_ref[:, start:end] = product[half:].astype(jnp.bfloat16)


def in_hbm(value):
    return pltpu.with_memory_space_constraint(value, pltpu.HBM)


def project(n, q_start, q_cols, kv_start, first, x, gain, w_query, w_key, w_value):
    rows, depth = x.shape
    kv = w_key.shape[1] // CHUNKS if kv_start is not None else 0
    width = q_cols + 2 * kv
    full = width + (128 if first else 0)
    hbm = pl.BlockSpec(memory_space=pltpu.HBM)
    vmem = pl.BlockSpec(memory_space=pltpu.VMEM)
    out_shape = [
        pltpu.VMEM((rows // 2, full), jnp.bfloat16),
        pltpu.VMEM((rows // 2, full), jnp.float32),
    ]
    scratch = [pltpu.VMEM((depth, width), jnp.bfloat16), pltpu.SemaphoreType.DMA((4,))]
    if first:
        out_shape.append(pltpu.VMEM((rows, depth), jnp.bfloat16))
        args = [in_hbm(x), gain]
        in_specs = [hbm, vmem]
        scratch = [
            pltpu.VMEM((n, rows // n, depth), jnp.bfloat16),
            pltpu.SemaphoreType.DMA((n,)),
        ] + scratch
    else:
        args, in_specs = [x], [vmem]
    return pl.pallas_call(
        functools.partial(project_kernel, n, q_start, kv_start, first),
        out_shape=out_shape,
        in_specs=in_specs + [hbm] * 3,
        out_specs=[vmem] * len(out_shape),
        scratch_shapes=scratch,
        compiler_params=pltpu.CompilerParams(vmem_limit_bytes=16 * MIB),
        cost_estimate=pl.CostEstimate(
            flops=2 * rows * depth * width,
            bytes_accessed=2 * depth * width + 4 * rows * depth,
            transcendentals=0,
        ),
        name="project",
    )(*args, in_hbm(w_query), in_hbm(w_key), in_hbm(w_value))


def attend_kernel(chunk, parts, groups, heads, seqs, length_ref, *refs):
    sums, square_ref = refs[:parts], refs[parts]
    cos_ref, sin_ref, k_ref, v_ref, out_ref, k_buf, v_buf, q_scr, o_scr, sems = refs[parts + 1 :]
    rows = seqs * NEW
    cols = groups * heads * HD
    kv = groups * HD
    seq_count = k_ref.shape[0]
    share = cols // parts

    def cache_copy(kind, b):
        source, target = ((k_ref, k_buf), (v_ref, v_buf))[kind]
        return pltpu.make_async_copy(
            source.at[b, :, pl.ds(chunk * kv, kv)], target.at[b], sems.at[kind, b]
        )

    for start in range(0, seq_count, seqs):
        for kind in range(2):
            for b in range(start, start + seqs):
                cache_copy(kind, b).start()

    scale = HD**-0.5 * math.log2(math.e)
    slots = k_ref.shape[1]
    many = heads * NEW
    slot_ids = lax.broadcasted_iota(jnp.int32, (1, slots), 1)
    new_cols = lax.broadcasted_iota(jnp.int32, (many, rows), 1)
    new_rows = lax.broadcasted_iota(jnp.int32, (many, rows), 0) % NEW

    @pl.loop(0, seq_count // seqs)
    def _(step):
        mine = pl.ds(pl.multiple_of(step * rows, rows), rows)
        mean = jnp.sum(square_ref[mine, :], axis=1, keepdims=True) / D
        row_scale = lax.rsqrt(mean + EPS)
        cosine, sine = cos_ref[mine, :], sin_ref[mine, :]

        def raw(part, start):
            return sums[part][mine, start : start + HD] * row_scale

        def rotary(value):
            return value * cosine + pltpu.roll(value, HD // 2, 1) * sine

        for h in range(heads * groups):
            turned = rotary(raw(h * HD // share, h * HD % share))
            for s in range(seqs):
                q_scr[s, h * NEW : (h + 1) * NEW, :] = turned[s * NEW : (s + 1) * NEW]
        for s in range(seqs):
            cache_copy(0, step * seqs + s).wait()
            cache_copy(1, step * seqs + s).wait()
        for g in range(groups):
            new_keys = rotary(raw(parts - 1, share + g * HD)).astype(jnp.bfloat16)
            new_values = raw(parts - 1, share + (groups + g) * HD).astype(jnp.bfloat16)
            lanes = slice(g * HD, (g + 1) * HD)
            olds, news, mixes = [], [], []
            for s in range(seqs):
                query = q_scr[s, g * many : (g + 1) * many, :].astype(jnp.bfloat16)
                keys = k_buf[step * seqs + s, :, lanes]
                olds.append(
                    lax.dot_general(
                        query, keys, (((1,), (1,)), ((), ())), preferred_element_type=jnp.float32
                    )
                )
                news.append(
                    lax.dot_general(
                        query, new_keys, (((1,), (1,)), ((), ())), preferred_element_type=jnp.float32
                    )
                )
            for s in range(seqs):
                live = slot_ids < length_ref[step * seqs + s]
                seen = (new_cols >= s * NEW) & (new_cols <= s * NEW + new_rows)
                old = jnp.where(live, olds[s] * scale, -1e30)
                new = jnp.where(seen, news[s] * scale, -1e30)
                top = jnp.maximum(
                    jnp.max(old, axis=1, keepdims=True), jnp.max(new, axis=1, keepdims=True)
                )
                old = jnp.exp2(old - top)
                new = jnp.exp2(new - top)
                total = jnp.sum(old, axis=1, keepdims=True) + jnp.sum(new, axis=1, keepdims=True)
                inverse = 1.0 / total
                olds[s] = (old * inverse).astype(jnp.bfloat16)
                news[s] = (new * inverse).astype(jnp.bfloat16)
            for s in range(seqs):
                values = v_buf[step * seqs + s, :, lanes]
                mixes.append(
                    jnp.dot(olds[s], values, preferred_element_type=jnp.float32)
                    + jnp.dot(news[s], new_values, preferred_element_type=jnp.float32)
                )
            for s in range(seqs):
                for h in range(heads):
                    at = (g * heads + h) * HD
                    o_scr[s * NEW : (s + 1) * NEW, at : at + HD] = mixes[s][
                        h * NEW : (h + 1) * NEW
                    ]
        out_ref[mine, :] = o_scr[...].astype(jnp.bfloat16)


def attend(chunk, sums, squares, cosine, sine, cache_keys, cache_values, lengths):
    seq_count, slots, kv_all = cache_keys.shape
    kv = kv_all // CHUNKS
    groups = kv // HD
    parts = len(sums)
    cols = parts * (sums[-1].shape[1] - 2 * kv)
    heads = cols // kv
    seqs = min(4, seq_count)
    rows = seq_count * NEW
    vmem = pl.BlockSpec(memory_space=pltpu.VMEM)
    hbm = pl.BlockSpec(memory_space=pltpu.HBM)
    flops = 4 * seq_count * groups * heads * NEW * slots * HD
    return pl.pallas_call(
        functools.partial(attend_kernel, chunk, parts, groups, heads, seqs),
        out_shape=pltpu.VMEM((rows, cols), jnp.bfloat16),
        in_specs=[pl.BlockSpec(memory_space=pltpu.SMEM)] + [vmem] * (parts + 3) + [hbm] * 2,
        out_specs=vmem,
        scratch_shapes=[
            pltpu.VMEM((seq_count, slots, kv), jnp.bfloat16),
            pltpu.VMEM((seq_count, slots, kv), jnp.bfloat16),
            pltpu.VMEM((seqs, groups * heads * NEW, HD), jnp.float32),
            pltpu.VMEM((seqs * NEW, cols), jnp.float32),
            pltpu.SemaphoreType.DMA((2, seq_count)),
        ],
        compiler_params=pltpu.CompilerParams(vmem_limit_bytes=16 * MIB),
        cost_estimate=pl.CostEstimate(
            flops=flops,
            bytes_accessed=4 * seq_count * slots * kv,
            transcendentals=seq_count * groups * heads * NEW * slots,
        ),
        name="attend",
    )(lengths, *sums, squares, cosine, sine, in_hbm(cache_keys), in_hbm(cache_values))


def combine_kernel(n, block, chunk, *refs):
    pieces, refs = refs[:n], refs[n:]
    gx, gy = lax.axis_index("gx"), lax.axis_index("gy")
    moved = jnp.where(gy == 0, n // 2, 0)
    if chunk:
        before_ref, refs = refs[0], refs[1:]
    w_ref, outs, (x_buf, w_buf, w_sems, x_sems) = refs[0], refs[1:-4], refs[-4:]
    depth, cols = w_buf.shape
    half = x_buf.shape[0] // 2
    part = cols // PARTS
    tile = part // 2

    def w_copy(at):
        return pltpu.make_async_copy(
            w_ref.at[chunk * depth : (chunk + 1) * depth, at : at + tile],
            w_buf.at[:, at : at + tile],
            w_sems.at[at // tile],
        )

    x_copies = []
    for slot, piece in enumerate(pieces):
        start = pl.multiple_of((slot_owner(n, slot, gx, gy) ^ moved) * block, block)
        x_copies.append(
            pltpu.make_async_copy(piece, x_buf.at[pl.ds(start, block), :], x_sems.at[slot])
        )
    for copy in x_copies:
        copy.start()
    for at in range(0, cols, tile):
        w_copy(at).start()
    for copy in x_copies:
        copy.wait()

    for start in range(0, cols, part):
        for at in range(start, start + part, tile):
            w_copy(at).wait()
        at = slice(start, start + part)
        product = jnp.dot(x_buf[...], w_buf[:, at], preferred_element_type=jnp.float32)
        if chunk:
            product = product + before_ref[:, at]
        if len(outs) == 1:
            outs[0][:, at] = product
        else:
            outs[0][:, at] = product[:half].astype(jnp.bfloat16)
            outs[1][:, at] = product[half:]


def combine(chunk, pieces, before, w_out):
    n, (block, depth) = len(pieces), pieces[0].shape
    rows = n * block
    cols = w_out.shape[1]
    last = chunk == CHUNKS - 1
    hbm = pl.BlockSpec(memory_space=pltpu.HBM)
    vmem = pl.BlockSpec(memory_space=pltpu.VMEM)
    if last:
        out_shape = [
            pltpu.VMEM((rows // 2, cols), jnp.bfloat16),
            pltpu.VMEM((rows // 2, cols), jnp.float32),
        ]
    else:
        out_shape = [pltpu.VMEM((rows, cols), jnp.float32)]
    earlier = [] if chunk == 0 else [before]
    return pl.pallas_call(
        functools.partial(combine_kernel, n, block, chunk),
        out_shape=out_shape,
        in_specs=[pl.BlockSpec(memory_space=pl.ANY)] * len(pieces)
        + [vmem] * len(earlier)
        + [hbm],
        out_specs=[vmem] * len(out_shape),
        scratch_shapes=[
            pltpu.VMEM((rows, depth), jnp.bfloat16),
            pltpu.VMEM((depth, cols), jnp.bfloat16),
            pltpu.SemaphoreType.DMA((2 * PARTS,)),
            pltpu.SemaphoreType.DMA((n,)),
        ],
        compiler_params=pltpu.CompilerParams(vmem_limit_bytes=16 * MIB),
        cost_estimate=pl.CostEstimate(
            flops=2 * rows * depth * cols,
            bytes_accessed=2 * depth * cols + 2 * rows * depth + 4 * rows * cols,
            transcendentals=0,
        ),
        name="combine",
    )(*pieces, *earlier, in_hbm(w_out))


class Flow:
    def __init__(self, n, cores, levels, send, keep):
        self.n, self.cores, self.levels = n, cores, levels
        self.send, self.keep = send, keep
        self.rows = keep.shape[0]
        self.received = []
        self.value = None
        self.sends = []

    def start_exchange(self):
        stage = len(self.received)
        if stage < self.levels:
            self.sends.append(self.send)
            self.received.append(exchange(self.send, self.n, self.cores, stage))

    def add_received(self):
        if self.value is not None and len(self.received) == self.levels and self.rows == 0:
            return
        low = self.rows // 2 if len(self.received) < self.levels else 0
        value = self.keep[low : self.rows]
        for other in self.received:
            value = value + other[low : self.rows].astype(jnp.float32)
        self.value = value
        self.send = value.astype(jnp.bfloat16)
        self.rows = low


def shards(
    tokens, norm_gain, w_query, w_key, w_value, w_out, cache_keys, cache_values, cache_lengths
):
    n = lax.axis_size("gx")
    cores = lax.axis_size("gy")
    levels = n.bit_length() - 1
    position = (cache_lengths[:, None] + jnp.arange(NEW, dtype=jnp.int32)[None, :]).reshape(-1)
    inverse = THETA ** (-2.0 * jnp.arange(HD // 2, dtype=jnp.float32) / HD)
    angles = position.astype(jnp.float32)[:, None] * inverse[None, :]
    cosine, sine = jnp.cos(angles), jnp.sin(angles)
    cosine = jnp.concatenate([cosine, cosine], axis=1)
    sine = jnp.concatenate([-sine, sine], axis=1)

    x, gain = tokens, norm_gain[None, :]
    kv = w_key.shape[1] // CHUNKS
    q_cols = w_query.shape[1] // (CHUNKS * PARTS)
    count = CHUNKS * PARTS
    flows = []
    for part in range(count + levels):
        if part < count:
            kv_start = part // PARTS * kv if part % PARTS == PARTS - 1 else None
            out = project(
                n, part * q_cols, q_cols, kv_start, part == 0, x, gain, w_query, w_key, w_value
            )
            if part == 0:
                x = out[2]
            flows.append(Flow(n, cores, levels, out[0], out[1]))
        for flow in flows[max(0, part - levels) : part]:
            flow.add_received()
        if part + 1 < count:
            waiting = flows[max(0, part - levels) : part + 1]
            tied = lax.optimization_barrier((x, [flow.send for flow in waiting]))
            x = tied[0]
            for flow, send in zip(waiting, tied[1]):
                flow.send = send
        for flow in flows[max(0, part - levels) : part + 1]:
            flow.start_exchange()
    sums = [flow.value for flow in flows]
    squares = sums[0][:, q_cols:]

    gathered = []
    for chunk in range(CHUNKS):
        mine = sums[chunk * PARTS : (chunk + 1) * PARTS]
        if chunk < CHUNKS - 1 and levels > 1:
            mine, _ = lax.optimization_barrier((mine, flows[(chunk + 1) * PARTS].sends[1]))
        attention = attend(
            chunk,
            mine,
            squares,
            cosine,
            sine,
            cache_keys,
            cache_values,
            cache_lengths,
        )
        slots = [attention]
        for slot in range(1, n):
            top = slot.bit_length() - 1
            slots.append(exchange(slots[slot - (1 << top)], n, cores, levels - 1 - top))
        gathered.append(slots)
    result = None
    for chunk in range(CHUNKS):
        result = combine(chunk, gathered[chunk], result and result[0], w_out)
    send, keep = result
    other = lax.ppermute(send, "gy", [(0, 1), (1, 0)])
    return (keep + other.astype(jnp.float32)).astype(jnp.bfloat16)


def solution(mesh):
    return jax.shard_map(
        shards,
        mesh=mesh,
        in_specs=(
            P("groups", "gx"),
            P("gx"),
            P("gx", "gy"),
            P("gx", "gy"),
            P("gx", "gy"),
            P("gy", "gx"),
            P(("groups", "gx"), None, "gy"),
            P(("groups", "gx"), None, "gy"),
            P(("groups", "gx")),
        ),
        out_specs=P(("groups", "gy"), "gx"),
        check_vma=False,
    )
```

```python
import functools
import math

import jax
import jax.numpy as jnp
from jax import lax
from jax.experimental import pallas as pl
from jax.experimental.pallas import tpu as pltpu
from jax.sharding import PartitionSpec as P

D = 16384
HD = 128
NEW = 4
EPS = 1e-05
THETA = 500000.0

CHUNKS = 2
TILES = 4
MIB = 1 << 20


def bit_orders(n):
    levels = n.bit_length() - 1
    first = list(range(levels))
    second = list(first)
    if levels > 1:
        second[0], second[1] = second[1], second[0]
    return first, second


def slot_shift(slot, order):
    levels = len(order)
    shift = 0
    for stage in range(levels):
        shift |= ((slot >> (levels - 1 - stage)) & 1) << order[stage]
    return shift


def slot_owner(n, slot, gx, gy):
    first, second = (slot_shift(slot, order) for order in bit_orders(n))
    return gx ^ jnp.where(gy == 0, first, second)


def exchange(value, n, cores, stage):
    orders = bit_orders(n)
    pairs = []
    for gx in range(n):
        for gy in range(cores):
            other = gx ^ (1 << orders[gy % 2][stage])
            pairs.append((gx * cores + gy, other * cores + gy))
    return lax.ppermute(value, ("gx", "gy"), pairs)


def project_kernel(n, q_start, kv_start, first, *refs):
    if first:
        tokens_ref, gain_ref, wq_ref, wk_ref, wv_ref, send_ref, keep_ref, x_ref = refs[:8]
        t_buf, t_sems, g_buf, g_sem = refs[8:12]
    else:
        x_ref, wq_ref, wk_ref, wv_ref, send_ref, keep_ref = refs[:6]
    w_buf, sems = refs[-2:]
    half = send_ref.shape[0]
    rows = 2 * half
    with_kv = kv_start is not None
    kv = wk_ref.shape[1] // CHUNKS if with_kv else 0
    width = w_buf.shape[1]
    cols = width - 2 * kv
    tile = cols // 2

    def w_copy(ref, start, size, at, sem):
        return pltpu.make_async_copy(
            ref.at[:, start : start + size], w_buf.at[:, at : at + size], sems.at[sem]
        )

    copies = [[w_copy(wq_ref, q_start + at, tile, at, at // tile)] for at in (0, tile)]
    if with_kv:
        copies[1].append(w_copy(wk_ref, kv_start, kv, cols, 2))
        copies[1].append(w_copy(wv_ref, kv_start, kv, cols + kv, 3))

    if first:
        block = rows // n
        me, gy = lax.axis_index("gx"), lax.axis_index("gy")
        t_copies = []
        for slot in range(n):
            start = pl.multiple_of(slot_owner(n, slot, me, gy) * block, block)
            t_copies.append(
                pltpu.make_async_copy(
                    tokens_ref.at[pl.ds(start, block), :], t_buf.at[slot], t_sems.at[slot]
                )
            )
            t_copies[-1].start()
        g_copy = pltpu.make_async_copy(gain_ref, g_buf, g_sem)
        g_copy.start()
    for group in copies:
        for copy in group:
            copy.start()
    if first:
        lanes = lax.broadcasted_iota(jnp.int32, (block, 128), 1)
        g_copy.wait()
        for slot in range(n):
            t_copies[slot].wait()
            wide = t_buf[slot].astype(jnp.float32)
            x_ref[slot * block : (slot + 1) * block, :] = (wide * g_buf[...]).astype(jnp.bfloat16)
            square = jnp.sum(wide * wide, axis=1, keepdims=True)
            high = square.astype(jnp.bfloat16).astype(jnp.float32)
            rest = square - high
            middle = rest.astype(jnp.bfloat16).astype(jnp.float32)
            low = rest - middle
            packed = jnp.where(
                lanes == 3 * me,
                high,
                jnp.where(lanes == 3 * me + 1, middle, jnp.where(lanes == 3 * me + 2, low, 0.0)),
            )
            if slot < n // 2:
                keep_ref[slot * block : (slot + 1) * block, width : width + 128] = packed
            else:
                at = (slot - n // 2) * block
                send_ref[at : at + block, width : width + 128] = packed.astype(jnp.bfloat16)

    for p, (start, end) in enumerate(((0, tile), (tile, width))):
        for copy in copies[p]:
            copy.wait()
        product = jnp.dot(x_ref[...], w_buf[:, start:end], preferred_element_type=jnp.float32)
        keep_ref[:, start:end] = product[:half]
        send_ref[:, start:end] = product[half:].astype(jnp.bfloat16)


def in_vmem(value):
    return pltpu.with_memory_space_constraint(value, pltpu.VMEM)


def in_hbm(value):
    return pltpu.with_memory_space_constraint(value, pltpu.HBM)


def project(n, q_start, q_cols, kv_start, first, x, gain, w_query, w_key, w_value):
    rows, depth = x.shape
    kv = w_key.shape[1] // CHUNKS if kv_start is not None else 0
    width = q_cols + 2 * kv
    full = width + (128 if first else 0)
    hbm = pl.BlockSpec(memory_space=pltpu.HBM)
    vmem = pl.BlockSpec(memory_space=pltpu.VMEM)
    out_shape = [
        pltpu.VMEM((rows // 2, full), jnp.bfloat16),
        pltpu.VMEM((rows // 2, full), jnp.float32),
    ]
    scratch = [pltpu.VMEM((depth, width), jnp.bfloat16), pltpu.SemaphoreType.DMA((4,))]
    if first:
        out_shape.append(pltpu.VMEM((rows, depth), jnp.bfloat16))
        args = [in_hbm(x), in_hbm(gain)]
        in_specs = [hbm, hbm]
        scratch = [
            pltpu.VMEM((n, rows // n, depth), jnp.bfloat16),
            pltpu.SemaphoreType.DMA((n,)),
            pltpu.VMEM((1, depth), jnp.float32),
            pltpu.SemaphoreType.DMA,
        ] + scratch
    else:
        args, in_specs = [x], [vmem]
    return pl.pallas_call(
        functools.partial(project_kernel, n, q_start, kv_start, first),
        out_shape=out_shape,
        in_specs=in_specs + [hbm] * 3,
        out_specs=[vmem] * len(out_shape),
        scratch_shapes=scratch,
        compiler_params=pltpu.CompilerParams(vmem_limit_bytes=16 * MIB),
        cost_estimate=pl.CostEstimate(
            flops=2 * rows * depth * width,
            bytes_accessed=2 * depth * width + 4 * rows * depth,
            transcendentals=0,
        ),
        name="project",
    )(*args, in_hbm(w_query), in_hbm(w_key), in_hbm(w_value))


def attend_kernel(chunk, offsets, kv_offset, groups, heads, seqs, length_ref, *refs):
    sum_ref, square_ref = refs[:2]
    cos_ref, sin_ref, k_ref, v_ref, out_ref, q_scr, o_scr = refs[2:]
    rows = seqs * NEW
    cols = groups * heads * HD
    kv = groups * HD
    seq_count = k_ref.shape[0]

    scale = HD**-0.5 * math.log2(math.e)
    slots = k_ref.shape[1]
    many = heads * NEW
    slot_ids = lax.broadcasted_iota(jnp.int32, (1, slots), 1)
    new_cols = lax.broadcasted_iota(jnp.int32, (many, rows), 1)
    new_rows = lax.broadcasted_iota(jnp.int32, (many, rows), 0) % NEW

    @pl.loop(0, seq_count // seqs)
    def _(step):
        mine = pl.ds(pl.multiple_of(step * rows, rows), rows)
        mean = jnp.sum(square_ref[mine, :], axis=1, keepdims=True) / D
        row_scale = lax.rsqrt(mean + EPS)
        cosine, sine = cos_ref[mine, :], sin_ref[mine, :]

        def raw(start):
            return sum_ref[mine, start : start + HD] * row_scale

        def rotary(value):
            return value * cosine + pltpu.roll(value, HD // 2, 1) * sine

        for h in range(heads * groups):
            turned = rotary(raw(offsets[h]))
            for s in range(seqs):
                q_scr[s, h * NEW : (h + 1) * NEW, :] = turned[s * NEW : (s + 1) * NEW]
        for g in range(groups):
            new_keys = rotary(raw(kv_offset + g * HD)).astype(jnp.bfloat16)
            new_values = raw(kv_offset + (groups + g) * HD).astype(jnp.bfloat16)
            lanes = slice(chunk * kv + g * HD, chunk * kv + (g + 1) * HD)
            olds, news, mixes = [], [], []
            for s in range(seqs):
                query = q_scr[s, g * many : (g + 1) * many, :].astype(jnp.bfloat16)
                keys = k_ref[step * seqs + s, :, lanes]
                olds.append(
                    lax.dot_general(
                        query, keys, (((1,), (1,)), ((), ())), preferred_element_type=jnp.float32
                    )
                )
                news.append(
                    lax.dot_general(
                        query, new_keys, (((1,), (1,)), ((), ())), preferred_element_type=jnp.float32
                    )
                )
            for s in range(seqs):
                live = slot_ids < length_ref[step * seqs + s]
                seen = (new_cols >= s * NEW) & (new_cols <= s * NEW + new_rows)
                old = jnp.where(live, olds[s] * scale, -1e30)
                new = jnp.where(seen, news[s] * scale, -1e30)
                top = jnp.maximum(
                    jnp.max(old, axis=1, keepdims=True), jnp.max(new, axis=1, keepdims=True)
                )
                old = jnp.exp2(old - top)
                new = jnp.exp2(new - top)
                total = jnp.sum(old, axis=1, keepdims=True) + jnp.sum(new, axis=1, keepdims=True)
                inverse = 1.0 / total
                olds[s] = (old * inverse).astype(jnp.bfloat16)
                news[s] = (new * inverse).astype(jnp.bfloat16)
            for s in range(seqs):
                values = v_ref[step * seqs + s, :, lanes]
                mixes.append(
                    jnp.dot(olds[s], values, preferred_element_type=jnp.float32)
                    + jnp.dot(news[s], new_values, preferred_element_type=jnp.float32)
                )
            for s in range(seqs):
                for h in range(heads):
                    at = (g * heads + h) * HD
                    o_scr[s * NEW : (s + 1) * NEW, at : at + HD] = mixes[s][
                        h * NEW : (h + 1) * NEW
                    ]
        out_ref[mine, :] = o_scr[...].astype(jnp.bfloat16)


def attend(chunk, offsets, kv_offset, sums, squares, cosine, sine, cache_keys, cache_values, lengths):
    seq_count, slots, kv_all = cache_keys.shape
    kv = kv_all // CHUNKS
    groups = kv // HD
    heads = len(offsets) // groups
    cols = len(offsets) * HD
    seqs = min(4, seq_count)
    rows = seq_count * NEW
    vmem = pl.BlockSpec(memory_space=pltpu.VMEM)
    hbm = pl.BlockSpec(memory_space=pltpu.HBM)
    flops = 4 * seq_count * groups * heads * NEW * slots * HD
    return pl.pallas_call(
        functools.partial(attend_kernel, chunk, offsets, kv_offset, groups, heads, seqs),
        out_shape=pltpu.VMEM((rows, cols), jnp.bfloat16),
        in_specs=[pl.BlockSpec(memory_space=pltpu.SMEM)] + [vmem] * 6,
        out_specs=vmem,
        scratch_shapes=[
            pltpu.VMEM((seqs, groups * heads * NEW, HD), jnp.float32),
            pltpu.VMEM((seqs * NEW, cols), jnp.float32),
        ],
        compiler_params=pltpu.CompilerParams(vmem_limit_bytes=16 * MIB),
        cost_estimate=pl.CostEstimate(
            flops=flops,
            bytes_accessed=4 * seq_count * slots * kv,
            transcendentals=seq_count * groups * heads * NEW * slots,
        ),
        name="attend",
    )(lengths, sums, squares, cosine, sine, in_vmem(cache_keys), in_vmem(cache_values))


def combine_kernel(n, block, chunk, *refs):
    pieces, refs = refs[:n], refs[n:]
    gx, gy = lax.axis_index("gx"), lax.axis_index("gy")
    moved = jnp.where(gy == 0, n // 2, 0)
    if chunk:
        before_ref, refs = refs[0], refs[1:]
    w_ref, outs, (x_buf, x_sems) = refs[0], refs[1:-2], refs[-2:]
    depth, cols = x_buf.shape[1], w_ref.shape[1]
    half = x_buf.shape[0] // 2
    x_copies = []
    for slot, piece in enumerate(pieces):
        start = pl.multiple_of((slot_owner(n, slot, gx, gy) ^ moved) * block, block)
        x_copies.append(
            pltpu.make_async_copy(piece, x_buf.at[pl.ds(start, block), :], x_sems.at[slot])
        )
    for copy in x_copies:
        copy.start()
    for copy in x_copies:
        copy.wait()

    rows = slice(chunk * depth, (chunk + 1) * depth)
    tile = cols // TILES
    for start in range(0, cols, tile):
        at = slice(start, start + tile)
        product = jnp.dot(x_buf[...], w_ref[rows, at], preferred_element_type=jnp.float32)
        if chunk:
            product = product + before_ref[:, at]
        if len(outs) == 1:
            outs[0][:, at] = product
        else:
            outs[0][:, at] = product[:half].astype(jnp.bfloat16)
            outs[1][:, at] = product[half:]


def combine(chunk, pieces, before, w_out):
    n, (block, depth) = len(pieces), pieces[0].shape
    rows = n * block
    cols = w_out.shape[1]
    last = chunk == CHUNKS - 1
    hbm = pl.BlockSpec(memory_space=pltpu.HBM)
    vmem = pl.BlockSpec(memory_space=pltpu.VMEM)
    if last:
        out_shape = [
            pltpu.VMEM((rows // 2, cols), jnp.bfloat16),
            pltpu.VMEM((rows // 2, cols), jnp.float32),
        ]
    else:
        out_shape = [pltpu.VMEM((rows, cols), jnp.float32)]
    earlier = [] if chunk == 0 else [before]
    return pl.pallas_call(
        functools.partial(combine_kernel, n, block, chunk),
        out_shape=out_shape,
        in_specs=[pl.BlockSpec(memory_space=pl.ANY)] * len(pieces)
        + [vmem] * len(earlier)
        + [vmem],
        out_specs=[vmem] * len(out_shape),
        scratch_shapes=[
            pltpu.VMEM((rows, depth), jnp.bfloat16),
            pltpu.SemaphoreType.DMA((n,)),
        ],
        compiler_params=pltpu.CompilerParams(vmem_limit_bytes=16 * MIB),
        cost_estimate=pl.CostEstimate(
            flops=2 * rows * depth * cols,
            bytes_accessed=2 * depth * cols + 2 * rows * depth + 4 * rows * cols,
            transcendentals=0,
        ),
        name="combine",
    )(*pieces, *earlier, in_vmem(w_out))


def shards(
    tokens, norm_gain, w_query, w_key, w_value, w_out, cache_keys, cache_values, cache_lengths
):
    n = lax.axis_size("gx")
    cores = lax.axis_size("gy")
    levels = n.bit_length() - 1
    position = (cache_lengths[:, None] + jnp.arange(NEW, dtype=jnp.int32)[None, :]).reshape(-1)
    inverse = THETA ** (-2.0 * jnp.arange(HD // 2, dtype=jnp.float32) / HD)
    angles = position.astype(jnp.float32)[:, None] * inverse[None, :]
    cosine, sine = jnp.cos(angles), jnp.sin(angles)
    cosine = jnp.concatenate([cosine, cosine], axis=1)
    sine = jnp.concatenate([-sine, sine], axis=1)

    x, gain = tokens, norm_gain[None, :]
    kv = w_key.shape[1] // CHUNKS
    q_cols = w_query.shape[1] // CHUNKS

    def column_part(start, size, kv_start):
        return project(
            n, start, size, kv_start, start == 0, x, gain, w_query, w_key, w_value
        )

    def after(value, *earlier):
        return lax.optimization_barrier((value, earlier))[0]

    share = q_cols // 2
    send_a, keep_a, x = column_part(0, share, None)
    x = after(x, send_a)
    other_a = exchange(send_a, n, cores, 0)
    send_b, keep_b = column_part(share, share, 0)
    x = after(x, send_b)
    other_b = exchange(send_b, n, cores, 0)
    sum_a = keep_a + other_a.astype(jnp.float32)
    x = after(x, sum_a)
    later = []
    for chunk in range(1, CHUNKS):
        later.append(column_part(chunk * q_cols, q_cols, chunk * kv))
    other_b = after(other_b, *(send_c for send_c, _ in later))
    first = jnp.concatenate([sum_a, keep_b + other_b.astype(jnp.float32)], axis=1)
    half = first.shape[0] // 2
    send = first[half:].astype(jnp.bfloat16)
    flows = [[1, first[:half], send]]
    for send_c, keep_c in later:
        flows.append([0, keep_c, after(send_c, flows[-1][2])])

    def step(flow, *earlier):
        stage, keep, send = flow
        other = exchange(send, n, cores, stage)
        if earlier:
            other = after(other, *earlier)
        value = keep + other.astype(jnp.float32)
        low = value.shape[0] // 2 if stage < levels - 1 else 0
        flow[:] = stage + 1, value[:low] if low else value, value[low:].astype(jnp.bfloat16)

    lead, follow = flows
    while follow[0] < levels:
        if lead[0] < levels:
            step(lead)
        step(follow, *([lead[2]] if lead[0] < levels else []))
    sums = [flow[1] for flow in flows]
    squares = sums[0][:, share : share + 128]
    plain = [h * HD for h in range(q_cols // HD)]
    offsets = [[at if at < share else at + 128 for at in plain], plain]
    kv_offsets = [q_cols + 128, q_cols]

    gathered = []
    for chunk in range(CHUNKS):
        attention = attend(
            chunk,
            offsets[chunk],
            kv_offsets[chunk],
            sums[chunk],
            squares,
            cosine,
            sine,
            cache_keys,
            cache_values,
            cache_lengths,
        )
        slots = [attention]
        for slot in range(1, n):
            top = slot.bit_length() - 1
            slots.append(exchange(slots[slot - (1 << top)], n, cores, levels - 1 - top))
        gathered.append(slots)
    result = None
    for chunk in range(CHUNKS):
        result = combine(chunk, gathered[chunk], result and result[0], w_out)
    send, keep = result
    other = lax.ppermute(send, "gy", [(0, 1), (1, 0)])
    return (keep + other.astype(jnp.float32)).astype(jnp.bfloat16)


def solution(mesh):
    return jax.shard_map(
        shards,
        mesh=mesh,
        in_specs=(
            P("groups", "gx"),
            P("gx"),
            P("gx", "gy"),
            P("gx", "gy"),
            P("gx", "gy"),
            P("gy", "gx"),
            P(("groups", "gx"), None, "gy"),
            P(("groups", "gx"), None, "gy"),
            P(("groups", "gx")),
        ),
        out_specs=P(("groups", "gy"), "gx"),
        check_vma=False,
    )
```

```python
import functools
import math

import jax
import jax.numpy as jnp
from jax import lax
from jax.experimental import pallas as pl
from jax.experimental.pallas import tpu as pltpu
from jax.sharding import PartitionSpec as P

D = 16384
HD = 128
NEW = 4
EPS = 1e-05
THETA = 500000.0

CHUNKS = 2
TILES = 4
MIB = 1 << 20


def bit_orders(n):
    levels = n.bit_length() - 1
    first = list(range(levels))
    second = list(first)
    if levels > 1:
        second[0], second[1] = second[1], second[0]
    return first, second


def gather_orders(n, chunk):
    first, second = bit_orders(n)
    return (first, first) if chunk else (first, second)


def slot_shift(slot, order):
    levels = len(order)
    shift = 0
    for stage in range(levels):
        shift |= ((slot >> (levels - 1 - stage)) & 1) << order[stage]
    return shift


def slot_owner(n, slot, gx, gy, orders):
    first, second = (slot_shift(slot, order) for order in orders)
    return gx ^ jnp.where(gy == 0, first, second)


def exchange(value, n, cores, stage, orders):
    pairs = []
    for gx in range(n):
        for gy in range(cores):
            other = gx ^ (1 << orders[gy % 2][stage])
            pairs.append((gx * cores + gy, other * cores + gy))
    return lax.ppermute(value, ("gx", "gy"), pairs)


def project_kernel(n, q_start, kv_start, first, *refs):
    if first:
        tokens_ref, gain_ref, wq_ref, wk_ref, wv_ref, send_ref, keep_ref, x_ref = refs[:8]
        t_buf, t_sems, g_buf, g_sem = refs[8:12]
    else:
        x_ref, wq_ref, wk_ref, wv_ref, send_ref, keep_ref = refs[:6]
    w_buf, sems = refs[-2:]
    half = send_ref.shape[0]
    rows = 2 * half
    with_kv = kv_start is not None
    kv = wk_ref.shape[1] // CHUNKS if with_kv else 0
    width = w_buf.shape[1]
    cols = width - 2 * kv
    tile = cols // 2

    def w_copy(ref, start, size, at, sem):
        return pltpu.make_async_copy(
            ref.at[:, start : start + size], w_buf.at[:, at : at + size], sems.at[sem]
        )

    copies = [[w_copy(wq_ref, q_start + at, tile, at, at // tile)] for at in (0, tile)]
    if with_kv:
        copies[1].append(w_copy(wk_ref, kv_start, kv, cols, 2))
        copies[1].append(w_copy(wv_ref, kv_start, kv, cols + kv, 3))

    if first:
        block = rows // n
        me, gy = lax.axis_index("gx"), lax.axis_index("gy")
        t_copies = []
        for slot in range(n):
            start = pl.multiple_of(slot_owner(n, slot, me, gy, bit_orders(n)) * block, block)
            t_copies.append(
                pltpu.make_async_copy(
                    tokens_ref.at[pl.ds(start, block), :], t_buf.at[slot], t_sems.at[slot]
                )
            )
            t_copies[-1].start()
        g_copy = pltpu.make_async_copy(gain_ref, g_buf, g_sem)
        g_copy.start()
    for group in copies:
        for copy in group:
            copy.start()
    if first:
        lanes = lax.broadcasted_iota(jnp.int32, (block, 128), 1)
        g_copy.wait()
        for slot in range(n):
            t_copies[slot].wait()
            wide = t_buf[slot].astype(jnp.float32)
            x_ref[slot * block : (slot + 1) * block, :] = (wide * g_buf[...]).astype(jnp.bfloat16)
            square = jnp.sum(wide * wide, axis=1, keepdims=True)
            high = square.astype(jnp.bfloat16).astype(jnp.float32)
            rest = square - high
            middle = rest.astype(jnp.bfloat16).astype(jnp.float32)
            low = rest - middle
            packed = jnp.where(
                lanes == 3 * me,
                high,
                jnp.where(lanes == 3 * me + 1, middle, jnp.where(lanes == 3 * me + 2, low, 0.0)),
            )
            if slot < n // 2:
                keep_ref[slot * block : (slot + 1) * block, width : width + 128] = packed
            else:
                at = (slot - n // 2) * block
                send_ref[at : at + block, width : width + 128] = packed.astype(jnp.bfloat16)

    for p, (start, end) in enumerate(((0, tile), (tile, width))):
        for copy in copies[p]:
            copy.wait()
        product = jnp.dot(x_ref[...], w_buf[:, start:end], preferred_element_type=jnp.float32)
        keep_ref[:, start:end] = product[:half]
        send_ref[:, start:end] = product[half:].astype(jnp.bfloat16)


def in_hbm(value):
    return pltpu.with_memory_space_constraint(value, pltpu.HBM)


def project(n, q_start, q_cols, kv_start, first, x, gain, w_query, w_key, w_value):
    rows, depth = x.shape
    kv = w_key.shape[1] // CHUNKS if kv_start is not None else 0
    width = q_cols + 2 * kv
    full = width + (128 if first else 0)
    hbm = pl.BlockSpec(memory_space=pltpu.HBM)
    vmem = pl.BlockSpec(memory_space=pltpu.VMEM)
    out_shape = [
        pltpu.VMEM((rows // 2, full), jnp.bfloat16),
        pltpu.VMEM((rows // 2, full), jnp.float32),
    ]
    scratch = [pltpu.VMEM((depth, width), jnp.bfloat16), pltpu.SemaphoreType.DMA((4,))]
    if first:
        out_shape.append(pltpu.VMEM((rows, depth), jnp.bfloat16))
        args = [in_hbm(x), in_hbm(gain)]
        in_specs = [hbm, hbm]
        scratch = [
            pltpu.VMEM((n, rows // n, depth), jnp.bfloat16),
            pltpu.SemaphoreType.DMA((n,)),
            pltpu.VMEM((1, depth), jnp.float32),
            pltpu.SemaphoreType.DMA,
        ] + scratch
    else:
        args, in_specs = [x], [vmem]
    return pl.pallas_call(
        functools.partial(project_kernel, n, q_start, kv_start, first),
        out_shape=out_shape,
        in_specs=in_specs + [hbm] * 3,
        out_specs=[vmem] * len(out_shape),
        scratch_shapes=scratch,
        compiler_params=pltpu.CompilerParams(vmem_limit_bytes=16 * MIB),
        name="project",
    )(*args, in_hbm(w_query), in_hbm(w_key), in_hbm(w_value))


def attend_kernel(chunk, offsets, kv_offset, groups, heads, seqs, length_ref, *refs):
    sum_ref, square_ref = refs[:2]
    cos_ref, sin_ref, k_ref, v_ref, out_ref, q_scr, o_scr = refs[2:]
    rows = seqs * NEW
    cols = groups * heads * HD
    kv = groups * HD
    seq_count = k_ref.shape[0]

    scale = HD**-0.5 * math.log2(math.e)
    slots = k_ref.shape[1]
    many = heads * NEW
    slot_ids = lax.broadcasted_iota(jnp.int32, (1, slots), 1)
    new_cols = lax.broadcasted_iota(jnp.int32, (many, rows), 1)
    new_rows = lax.broadcasted_iota(jnp.int32, (many, rows), 0) % NEW

    @pl.loop(0, seq_count // seqs)
    def _(step):
        mine = pl.ds(pl.multiple_of(step * rows, rows), rows)
        mean = jnp.sum(square_ref[mine, :], axis=1, keepdims=True) / D
        row_scale = lax.rsqrt(mean + EPS)
        cosine, sine = cos_ref[mine, :], sin_ref[mine, :]

        def raw(start):
            return sum_ref[mine, start : start + HD] * row_scale

        def rotary(value):
            return value * cosine + pltpu.roll(value, HD // 2, 1) * sine

        for h in range(heads * groups):
            turned = rotary(raw(offsets[h]))
            for s in range(seqs):
                q_scr[s, h * NEW : (h + 1) * NEW, :] = turned[s * NEW : (s + 1) * NEW]
        for g in range(groups):
            new_keys = rotary(raw(kv_offset + g * HD)).astype(jnp.bfloat16)
            new_values = raw(kv_offset + (groups + g) * HD).astype(jnp.bfloat16)
            lanes = slice(chunk * kv + g * HD, chunk * kv + (g + 1) * HD)
            olds, news, mixes = [], [], []
            for s in range(seqs):
                query = q_scr[s, g * many : (g + 1) * many, :].astype(jnp.bfloat16)
                keys = k_ref[step * seqs + s, :, lanes]
                olds.append(
                    lax.dot_general(
                        query, keys, (((1,), (1,)), ((), ())), preferred_element_type=jnp.float32
                    )
                )
                news.append(
                    lax.dot_general(
                        query, new_keys, (((1,), (1,)), ((), ())), preferred_element_type=jnp.float32
                    )
                )
            for s in range(seqs):
                live = slot_ids < length_ref[step * seqs + s]
                seen = (new_cols >= s * NEW) & (new_cols <= s * NEW + new_rows)
                old = jnp.where(live, olds[s] * scale, -1e30)
                new = jnp.where(seen, news[s] * scale, -1e30)
                top = jnp.maximum(
                    jnp.max(old, axis=1, keepdims=True), jnp.max(new, axis=1, keepdims=True)
                )
                old = jnp.exp2(old - top)
                new = jnp.exp2(new - top)
                total = jnp.sum(old, axis=1, keepdims=True) + jnp.sum(new, axis=1, keepdims=True)
                inverse = 1.0 / total
                olds[s] = (old * inverse).astype(jnp.bfloat16)
                news[s] = (new * inverse).astype(jnp.bfloat16)
            for s in range(seqs):
                values = v_ref[step * seqs + s, :, lanes]
                mixes.append(
                    jnp.dot(olds[s], values, preferred_element_type=jnp.float32)
                    + jnp.dot(news[s], new_values, preferred_element_type=jnp.float32)
                )
            for s in range(seqs):
                for h in range(heads):
                    at = (g * heads + h) * HD
                    o_scr[s * NEW : (s + 1) * NEW, at : at + HD] = mixes[s][
                        h * NEW : (h + 1) * NEW
                    ]
        out_ref[mine, :] = o_scr[...].astype(jnp.bfloat16)


def attend(chunk, offsets, kv_offset, sums, squares, cosine, sine, cache_keys, cache_values, lengths):
    seq_count, slots, kv_all = cache_keys.shape
    kv = kv_all // CHUNKS
    groups = kv // HD
    heads = len(offsets) // groups
    cols = len(offsets) * HD
    seqs = min(4, seq_count)
    rows = seq_count * NEW
    vmem = pl.BlockSpec(memory_space=pltpu.VMEM)
    hbm = pl.BlockSpec(memory_space=pltpu.HBM)
    return pl.pallas_call(
        functools.partial(attend_kernel, chunk, offsets, kv_offset, groups, heads, seqs),
        out_shape=pltpu.VMEM((rows, cols), jnp.bfloat16),
        in_specs=[pl.BlockSpec(memory_space=pltpu.SMEM)] + [vmem] * 6,
        out_specs=vmem,
        scratch_shapes=[
            pltpu.VMEM((seqs, groups * heads * NEW, HD), jnp.float32),
            pltpu.VMEM((seqs * NEW, cols), jnp.float32),
        ],
        compiler_params=pltpu.CompilerParams(vmem_limit_bytes=16 * MIB),
        name="attend",
    )(lengths, sums, squares, cosine, sine, cache_keys, cache_values)


def fetch_kernel(count, pieces, *refs):
    sources, targets, sems = refs[:count], refs[count : 2 * count], refs[2 * count]
    copies = []
    for i, (source, target) in enumerate(zip(sources, targets)):
        size = target.shape[0] // pieces
        for p in range(pieces):
            at = slice(p * size, (p + 1) * size)
            copies.append(
                pltpu.make_async_copy(source.at[at], target.at[at], sems.at[i * pieces + p])
            )
    for copy in copies:
        copy.start()
    for copy in copies:
        copy.wait()


def fetch(*arrays):
    pieces = 4
    return pl.pallas_call(
        functools.partial(fetch_kernel, len(arrays), pieces),
        out_shape=[pltpu.VMEM(array.shape, array.dtype) for array in arrays],
        in_specs=[pl.BlockSpec(memory_space=pltpu.HBM)] * len(arrays),
        out_specs=[pl.BlockSpec(memory_space=pltpu.VMEM)] * len(arrays),
        scratch_shapes=[pltpu.SemaphoreType.DMA((pieces * len(arrays),))],
        compiler_params=pltpu.CompilerParams(vmem_limit_bytes=4 * MIB),
        name="fetch",
    )(*[in_hbm(array) for array in arrays])


def fetch_rows_kernel(start, pieces, source, target, sems):
    size = target.shape[0] // pieces
    copies = [
        pltpu.make_async_copy(
            source.at[start + p * size : start + (p + 1) * size],
            target.at[p * size : (p + 1) * size],
            sems.at[p],
        )
        for p in range(pieces)
    ]
    for copy in copies:
        copy.start()
    for copy in copies:
        copy.wait()


def fetch_rows(array, start, rows):
    pieces = 4
    return pl.pallas_call(
        functools.partial(fetch_rows_kernel, start, pieces),
        out_shape=pltpu.VMEM((rows, array.shape[1]), array.dtype),
        in_specs=[pl.BlockSpec(memory_space=pltpu.HBM)],
        out_specs=pl.BlockSpec(memory_space=pltpu.VMEM),
        scratch_shapes=[pltpu.SemaphoreType.DMA((pieces,))],
        compiler_params=pltpu.CompilerParams(vmem_limit_bytes=4 * MIB),
        name="fetch_rows",
    )(in_hbm(array))


def combine_kernel(n, block, chunk, *refs):
    pieces, refs = refs[:n], refs[n:]
    gx, gy = lax.axis_index("gx"), lax.axis_index("gy")
    moved = jnp.where(gy == 0, n // 2, 0)
    if chunk:
        before_ref, refs = refs[0], refs[1:]
    w_ref, outs, (x_buf, x_sems) = refs[0], refs[1:-2], refs[-2:]
    depth, cols = x_buf.shape[1], w_ref.shape[1]
    half = x_buf.shape[0] // 2
    x_copies = []
    for slot, piece in enumerate(pieces):
        start = pl.multiple_of((slot_owner(n, slot, gx, gy, gather_orders(n, chunk)) ^ moved) * block, block)
        x_copies.append(
            pltpu.make_async_copy(piece, x_buf.at[pl.ds(start, block), :], x_sems.at[slot])
        )
    for copy in x_copies:
        copy.start()
    for copy in x_copies:
        copy.wait()

    tile = cols // TILES
    for start in range(0, cols, tile):
        at = slice(start, start + tile)
        product = jnp.dot(x_buf[...], w_ref[:, at], preferred_element_type=jnp.float32)
        if chunk:
            product = product + before_ref[:, at]
        if len(outs) == 1:
            outs[0][:, at] = product
        else:
            outs[0][:, at] = product[:half].astype(jnp.bfloat16)
            outs[1][:, at] = product[half:]


def combine(chunk, pieces, before, w_out):
    n, (block, depth) = len(pieces), pieces[0].shape
    rows = n * block
    cols = w_out.shape[1]
    last = chunk == CHUNKS - 1
    hbm = pl.BlockSpec(memory_space=pltpu.HBM)
    vmem = pl.BlockSpec(memory_space=pltpu.VMEM)
    if last:
        out_shape = [
            pltpu.VMEM((rows // 2, cols), jnp.bfloat16),
            pltpu.VMEM((rows // 2, cols), jnp.float32),
        ]
    else:
        out_shape = [pltpu.VMEM((rows, cols), jnp.float32)]
    earlier = [] if chunk == 0 else [before]
    return pl.pallas_call(
        functools.partial(combine_kernel, n, block, chunk),
        out_shape=out_shape,
        in_specs=[pl.BlockSpec(memory_space=pl.ANY)] * len(pieces)
        + [vmem] * len(earlier)
        + [vmem],
        out_specs=[vmem] * len(out_shape),
        scratch_shapes=[
            pltpu.VMEM((rows, depth), jnp.bfloat16),
            pltpu.SemaphoreType.DMA((n,)),
        ],
        compiler_params=pltpu.CompilerParams(vmem_limit_bytes=16 * MIB),
        name="combine",
    )(*pieces, *earlier, w_out)


def shards(
    tokens, norm_gain, w_query, w_key, w_value, w_out, cache_keys, cache_values, cache_lengths
):
    n = lax.axis_size("gx")
    cores = lax.axis_size("gy")
    levels = n.bit_length() - 1
    position = (cache_lengths[:, None] + jnp.arange(NEW, dtype=jnp.int32)[None, :]).reshape(-1)
    inverse = THETA ** (-2.0 * jnp.arange(HD // 2, dtype=jnp.float32) / HD)
    angles = position.astype(jnp.float32)[:, None] * inverse[None, :]
    cosine, sine = jnp.cos(angles), jnp.sin(angles)
    cosine = jnp.concatenate([cosine, cosine], axis=1)
    sine = jnp.concatenate([-sine, sine], axis=1)

    x, gain = tokens, norm_gain[None, :]
    kv = w_key.shape[1] // CHUNKS
    q_cols = w_query.shape[1] // CHUNKS

    def column_part(start, size, kv_start):
        return project(
            n, start, size, kv_start, start == 0, x, gain, w_query, w_key, w_value
        )

    def after(value, *earlier):
        return lax.optimization_barrier((value, earlier))[0]

    share = q_cols // 2
    orders = bit_orders(n)
    send_a, keep_a, x = column_part(0, share, None)
    x = after(x, send_a)
    other_a = exchange(send_a, n, cores, 0, orders)
    send_b, keep_b = column_part(share, share, 0)
    x = after(x, send_b)
    other_b = exchange(send_b, n, cores, 0, orders)
    sum_a = keep_a + other_a.astype(jnp.float32)
    x = after(x, sum_a)
    later = []
    for chunk in range(1, CHUNKS):
        later.append(column_part(chunk * q_cols, q_cols, chunk * kv))
    other_b = after(other_b, *(send_c for send_c, _ in later))
    first = jnp.concatenate([sum_a, keep_b + other_b.astype(jnp.float32)], axis=1)
    half = first.shape[0] // 2
    send = first[half:].astype(jnp.bfloat16)
    flows = [[1, first[:half], send]]
    for send_c, keep_c in later:
        flows.append([0, keep_c, after(send_c, flows[-1][2])])

    def start(flow):
        return exchange(flow[2], n, cores, flow[0], orders)

    def finish(flow, other, *earlier):
        stage, keep, _ = flow
        if earlier:
            other = after(other, *earlier)
        value = keep + other.astype(jnp.float32)
        low = value.shape[0] // 2 if stage < levels - 1 else 0
        flow[:] = stage + 1, value[:low] if low else value, value[low:].astype(jnp.bfloat16)

    lead, follow = flows
    w_rows = w_out.shape[0] // CHUNKS
    source = after(w_out, lead[2], follow[2])
    weights = [fetch_rows(source, chunk * w_rows, w_rows) for chunk in range(CHUNKS)]
    stage = 0
    while follow[0] < levels:
        pending = [start(flow) for flow in flows if flow[0] < levels]
        if lead[0] == levels:
            finish(follow, pending[0])
        elif lead[0] == levels - 1:
            finish(lead, pending[0])
            finish(follow, pending[1], lead[1])
        else:
            finish(lead, pending[0], *weights)
            between = [lead[2]]
            if stage == 0:
                cache_keys, cache_values = fetch(*after((cache_keys, cache_values), lead[2]))
                between += [cache_keys, cache_values]
            finish(follow, pending[1], *between)
        stage += 1
    sums = [flow[1] for flow in flows]
    squares = sums[0][:, share : share + 128]
    plain = [h * HD for h in range(q_cols // HD)]
    offsets = [[at if at < share else at + 128 for at in plain], plain]
    kv_offsets = [q_cols + 128, q_cols]

    gathered = []
    for chunk in range(CHUNKS):
        attention = attend(
            chunk,
            offsets[chunk],
            kv_offsets[chunk],
            sums[chunk],
            squares,
            cosine,
            sine,
            cache_keys,
            cache_values,
            cache_lengths,
        )
        slots = [attention]
        for slot in range(1, n):
            top = slot.bit_length() - 1
            slots.append(exchange(
                    slots[slot - (1 << top)],
                    n,
                    cores,
                    levels - 1 - top,
                    gather_orders(n, chunk),
                ))
        gathered.append(slots)
    result = None
    for chunk in range(CHUNKS):
        result = combine(chunk, gathered[chunk], result and result[0], weights[chunk])
    send, keep = result
    other = lax.ppermute(send, "gy", [(0, 1), (1, 0)])
    return (keep + other.astype(jnp.float32)).astype(jnp.bfloat16)


def solution(mesh):
    return jax.shard_map(
        shards,
        mesh=mesh,
        in_specs=(
            P("groups", "gx"),
            P("gx"),
            P("gx", "gy"),
            P("gx", "gy"),
            P("gx", "gy"),
            P("gy", "gx"),
            P(("groups", "gx"), None, "gy"),
            P(("groups", "gx"), None, "gy"),
            P(("groups", "gx")),
        ),
        out_specs=P(("groups", "gy"), "gx"),
        check_vma=False,
    )
```

```python
import functools
import math

import jax
import jax.numpy as jnp
from jax import lax
from jax.experimental import pallas as pl
from jax.experimental.pallas import tpu as pltpu
from jax.sharding import PartitionSpec as P

D = 16384
HD = 128
NEW = 4
EPS = 1e-05
THETA = 500000.0

CHUNKS = 2
TILES = 4
MIB = 1 << 20


def bit_orders(n):
    levels = n.bit_length() - 1
    first = list(range(levels))
    second = list(first)
    if levels > 1:
        second[0], second[1] = second[1], second[0]
    return first, second


def sum_orders(n, chunk):
    first, second = bit_orders(n)
    return (second, first) if chunk else (first, second)


def gather_orders(n, chunk):
    first, second = bit_orders(n)
    return (first, second) if chunk else (first, first)


def slot_shift(slot, order):
    levels = len(order)
    shift = 0
    for stage in range(levels):
        shift |= ((slot >> (levels - 1 - stage)) & 1) << order[stage]
    return shift


def changed_slot(n, slot):
    first, second = bit_orders(n)
    return [slot_shift(other, first) for other in range(n)].index(slot_shift(slot, second))


def slot_owner(n, slot, gx, gy, orders):
    first, second = (slot_shift(slot, order) for order in orders)
    return gx ^ jnp.where(gy == 0, first, second)


def exchange(value, n, cores, stage, orders):
    pairs = []
    for gx in range(n):
        for gy in range(cores):
            other = gx ^ (1 << orders[gy % 2][stage])
            pairs.append((gx * cores + gy, other * cores + gy))
    return lax.ppermute(value, ("gx", "gy"), pairs)


def project_kernel(n, q_start, kv_start, first, chunk, *refs):
    if first:
        tokens_ref, gain_ref, wq_ref, wk_ref, wv_ref, send_ref, keep_ref, x_ref = refs[:8]
        t_buf, t_sems, g_buf, g_sem = refs[8:12]
    else:
        x_ref, wq_ref, wk_ref, wv_ref, send_ref, keep_ref = refs[:6]
    w_buf, sems = refs[-2:]
    half = send_ref.shape[0]
    rows = 2 * half
    with_kv = kv_start is not None
    kv = wk_ref.shape[1] // CHUNKS if with_kv else 0
    width = w_buf.shape[1]
    cols = width - 2 * kv
    tile = cols // 2

    def w_copy(ref, start, size, at, sem):
        return pltpu.make_async_copy(
            ref.at[:, start : start + size], w_buf.at[:, at : at + size], sems.at[sem]
        )

    copies = [[w_copy(wq_ref, q_start + at, tile, at, at // tile)] for at in (0, tile)]
    if with_kv:
        copies[1].append(w_copy(wk_ref, kv_start, kv, cols, 2))
        copies[1].append(w_copy(wv_ref, kv_start, kv, cols + kv, 3))

    if first:
        block = rows // n
        me, gy = lax.axis_index("gx"), lax.axis_index("gy")
        t_copies = []
        for slot in range(n):
            start = pl.multiple_of(slot_owner(n, slot, me, gy, sum_orders(n, 0)) * block, block)
            t_copies.append(
                pltpu.make_async_copy(
                    tokens_ref.at[pl.ds(start, block), :], t_buf.at[slot], t_sems.at[slot]
                )
            )
            t_copies[-1].start()
        g_copy = pltpu.make_async_copy(gain_ref, g_buf, g_sem)
        g_copy.start()
    for group in copies:
        for copy in group:
            copy.start()
    if first:
        lanes = lax.broadcasted_iota(jnp.int32, (block, 128), 1)
        g_copy.wait()
        for slot in range(n):
            t_copies[slot].wait()
            wide = t_buf[slot].astype(jnp.float32)
            x_ref[0, slot * block : (slot + 1) * block, :] = (wide * g_buf[...]).astype(jnp.bfloat16)
            square = jnp.sum(wide * wide, axis=1, keepdims=True)
            high = square.astype(jnp.bfloat16).astype(jnp.float32)
            rest = square - high
            middle = rest.astype(jnp.bfloat16).astype(jnp.float32)
            low = rest - middle
            packed = jnp.where(
                lanes == 3 * me,
                high,
                jnp.where(lanes == 3 * me + 1, middle, jnp.where(lanes == 3 * me + 2, low, 0.0)),
            )
            if slot < n // 2:
                keep_ref[slot * block : (slot + 1) * block, width : width + 128] = packed
            else:
                at = (slot - n // 2) * block
                send_ref[at : at + block, width : width + 128] = packed.astype(jnp.bfloat16)

        for slot in range(n):
            x_ref[1, slot * block : (slot + 1) * block, :] = x_ref[
                0, changed_slot(n, slot) * block : (changed_slot(n, slot) + 1) * block, :
            ]

    for p, (start, end) in enumerate(((0, tile), (tile, width))):
        for copy in copies[p]:
            copy.wait()
        product = jnp.dot(x_ref[chunk], w_buf[:, start:end], preferred_element_type=jnp.float32)
        keep_ref[:, start:end] = product[:half]
        send_ref[:, start:end] = product[half:].astype(jnp.bfloat16)


def in_hbm(value):
    return pltpu.with_memory_space_constraint(value, pltpu.HBM)


def project(n, q_start, q_cols, kv_start, first, x, gain, w_query, w_key, w_value):
    rows, depth = x.shape[-2:]
    chunk = q_start // (w_query.shape[1] // CHUNKS)
    kv = w_key.shape[1] // CHUNKS if kv_start is not None else 0
    width = q_cols + 2 * kv
    full = width + (128 if first else 0)
    hbm = pl.BlockSpec(memory_space=pltpu.HBM)
    vmem = pl.BlockSpec(memory_space=pltpu.VMEM)
    out_shape = [
        pltpu.VMEM((rows // 2, full), jnp.bfloat16),
        pltpu.VMEM((rows // 2, full), jnp.float32),
    ]
    scratch = [pltpu.VMEM((depth, width), jnp.bfloat16), pltpu.SemaphoreType.DMA((4,))]
    if first:
        out_shape.append(pltpu.VMEM((CHUNKS, rows, depth), jnp.bfloat16))
        args = [in_hbm(x), in_hbm(gain)]
        in_specs = [hbm, hbm]
        scratch = [
            pltpu.VMEM((n, rows // n, depth), jnp.bfloat16),
            pltpu.SemaphoreType.DMA((n,)),
            pltpu.VMEM((1, depth), jnp.float32),
            pltpu.SemaphoreType.DMA,
        ] + scratch
    else:
        args, in_specs = [x], [vmem]
    return pl.pallas_call(
        functools.partial(project_kernel, n, q_start, kv_start, first, chunk),
        out_shape=out_shape,
        in_specs=in_specs + [hbm] * 3,
        out_specs=[vmem] * len(out_shape),
        scratch_shapes=scratch,
        compiler_params=pltpu.CompilerParams(vmem_limit_bytes=16 * MIB),
        name="project",
    )(*args, in_hbm(w_query), in_hbm(w_key), in_hbm(w_value))


def attend_kernel(chunk, offsets, kv_offset, groups, heads, seqs, length_ref, *refs):
    sum_ref, square_ref = refs[:2]
    cos_ref, sin_ref, k_ref, v_ref, out_ref, q_scr, o_scr = refs[2:]
    rows = seqs * NEW
    cols = groups * heads * HD
    kv = groups * HD
    seq_count = k_ref.shape[0]

    scale = HD**-0.5 * math.log2(math.e)
    slots = k_ref.shape[1]
    many = heads * NEW
    slot_ids = lax.broadcasted_iota(jnp.int32, (1, slots), 1)
    new_cols = lax.broadcasted_iota(jnp.int32, (many, rows), 1)
    new_rows = lax.broadcasted_iota(jnp.int32, (many, rows), 0) % NEW

    @pl.loop(0, seq_count // seqs)
    def _(step):
        mine = pl.ds(pl.multiple_of(step * rows, rows), rows)
        mean = jnp.sum(square_ref[mine, :], axis=1, keepdims=True) / D
        row_scale = lax.rsqrt(mean + EPS)
        cosine, sine = cos_ref[mine, :], sin_ref[mine, :]

        def raw(start):
            return sum_ref[mine, start : start + HD] * row_scale

        def rotary(value):
            return value * cosine + pltpu.roll(value, HD // 2, 1) * sine

        for h in range(heads * groups):
            turned = rotary(raw(offsets[h]))
            for s in range(seqs):
                q_scr[s, h * NEW : (h + 1) * NEW, :] = turned[s * NEW : (s + 1) * NEW]
        for g in range(groups):
            new_keys = rotary(raw(kv_offset + g * HD)).astype(jnp.bfloat16)
            new_values = raw(kv_offset + (groups + g) * HD).astype(jnp.bfloat16)
            lanes = slice(chunk * kv + g * HD, chunk * kv + (g + 1) * HD)
            olds, news, mixes = [], [], []
            for s in range(seqs):
                query = q_scr[s, g * many : (g + 1) * many, :].astype(jnp.bfloat16)
                keys = k_ref[step * seqs + s, :, lanes]
                olds.append(
                    lax.dot_general(
                        query, keys, (((1,), (1,)), ((), ())), preferred_element_type=jnp.float32
                    )
                )
                news.append(
                    lax.dot_general(
                        query, new_keys, (((1,), (1,)), ((), ())), preferred_element_type=jnp.float32
                    )
                )
            for s in range(seqs):
                live = slot_ids < length_ref[step * seqs + s]
                seen = (new_cols >= s * NEW) & (new_cols <= s * NEW + new_rows)
                old = jnp.where(live, olds[s] * scale, -1e30)
                new = jnp.where(seen, news[s] * scale, -1e30)
                top = jnp.maximum(
                    jnp.max(old, axis=1, keepdims=True), jnp.max(new, axis=1, keepdims=True)
                )
                old = jnp.exp2(old - top)
                new = jnp.exp2(new - top)
                total = jnp.sum(old, axis=1, keepdims=True) + jnp.sum(new, axis=1, keepdims=True)
                inverse = 1.0 / total
                olds[s] = (old * inverse).astype(jnp.bfloat16)
                news[s] = (new * inverse).astype(jnp.bfloat16)
            for s in range(seqs):
                values = v_ref[step * seqs + s, :, lanes]
                mixes.append(
                    jnp.dot(olds[s], values, preferred_element_type=jnp.float32)
                    + jnp.dot(news[s], new_values, preferred_element_type=jnp.float32)
                )
            for s in range(seqs):
                for h in range(heads):
                    at = (g * heads + h) * HD
                    o_scr[s * NEW : (s + 1) * NEW, at : at + HD] = mixes[s][
                        h * NEW : (h + 1) * NEW
                    ]
        out_ref[mine, :] = o_scr[...].astype(jnp.bfloat16)


def attend(chunk, offsets, kv_offset, sums, squares, cosine, sine, cache_keys, cache_values, lengths):
    seq_count, slots, kv_all = cache_keys.shape
    kv = kv_all // CHUNKS
    groups = kv // HD
    heads = len(offsets) // groups
    cols = len(offsets) * HD
    seqs = min(4, seq_count)
    rows = seq_count * NEW
    vmem = pl.BlockSpec(memory_space=pltpu.VMEM)
    hbm = pl.BlockSpec(memory_space=pltpu.HBM)
    return pl.pallas_call(
        functools.partial(attend_kernel, chunk, offsets, kv_offset, groups, heads, seqs),
        out_shape=pltpu.VMEM((rows, cols), jnp.bfloat16),
        in_specs=[pl.BlockSpec(memory_space=pltpu.SMEM)] + [vmem] * 6,
        out_specs=vmem,
        scratch_shapes=[
            pltpu.VMEM((seqs, groups * heads * NEW, HD), jnp.float32),
            pltpu.VMEM((seqs * NEW, cols), jnp.float32),
        ],
        compiler_params=pltpu.CompilerParams(vmem_limit_bytes=16 * MIB),
        name="attend",
    )(lengths, sums, squares, cosine, sine, cache_keys, cache_values)


def fetch_kernel(count, pieces, *refs):
    sources, targets, sems = refs[:count], refs[count : 2 * count], refs[2 * count]
    copies = []
    for i, (source, target) in enumerate(zip(sources, targets)):
        size = target.shape[0] // pieces
        for p in range(pieces):
            at = slice(p * size, (p + 1) * size)
            copies.append(
                pltpu.make_async_copy(source.at[at], target.at[at], sems.at[i * pieces + p])
            )
    for copy in copies:
        copy.start()
    for copy in copies:
        copy.wait()


def fetch(*arrays):
    pieces = 4
    return pl.pallas_call(
        functools.partial(fetch_kernel, len(arrays), pieces),
        out_shape=[pltpu.VMEM(array.shape, array.dtype) for array in arrays],
        in_specs=[pl.BlockSpec(memory_space=pltpu.HBM)] * len(arrays),
        out_specs=[pl.BlockSpec(memory_space=pltpu.VMEM)] * len(arrays),
        scratch_shapes=[pltpu.SemaphoreType.DMA((pieces * len(arrays),))],
        compiler_params=pltpu.CompilerParams(vmem_limit_bytes=4 * MIB),
        name="fetch",
    )(*[in_hbm(array) for array in arrays])


def fetch_rows_kernel(start, pieces, source, target, sems):
    size = target.shape[0] // pieces
    copies = [
        pltpu.make_async_copy(
            source.at[start + p * size : start + (p + 1) * size],
            target.at[p * size : (p + 1) * size],
            sems.at[p],
        )
        for p in range(pieces)
    ]
    for copy in copies:
        copy.start()
    for copy in copies:
        copy.wait()


def fetch_rows(array, start, rows):
    pieces = 4
    return pl.pallas_call(
        functools.partial(fetch_rows_kernel, start, pieces),
        out_shape=pltpu.VMEM((rows, array.shape[1]), array.dtype),
        in_specs=[pl.BlockSpec(memory_space=pltpu.HBM)],
        out_specs=pl.BlockSpec(memory_space=pltpu.VMEM),
        scratch_shapes=[pltpu.SemaphoreType.DMA((pieces,))],
        compiler_params=pltpu.CompilerParams(vmem_limit_bytes=4 * MIB),
        name="fetch_rows",
    )(in_hbm(array))


def combine_kernel(n, block, chunk, slots, *refs):
    count = 1 + max(piece for piece, _ in slots)
    pieces, refs = refs[:count], refs[count:]
    gx, gy = lax.axis_index("gx"), lax.axis_index("gy")
    moved = jnp.where(gy == 0, n // 2, 0)
    if chunk:
        before_ref, refs = refs[0], refs[1:]
    w_ref, outs, (x_buf, x_sems) = refs[0], refs[1:-2], refs[-2:]
    depth, cols = x_buf.shape[1], w_ref.shape[1]
    half = x_buf.shape[0] // 2
    x_copies = []
    for slot, (piece, at) in enumerate(slots):
        start = pl.multiple_of((slot_owner(n, slot, gx, gy, gather_orders(n, chunk)) ^ moved) * block, block)
        x_copies.append(
            pltpu.make_async_copy(
                pieces[piece].at[at : at + block, :],
                x_buf.at[pl.ds(start, block), :],
                x_sems.at[slot],
            )
        )
    for copy in x_copies:
        copy.start()
    for copy in x_copies:
        copy.wait()

    tile = cols // TILES
    for start in range(0, cols, tile):
        at = slice(start, start + tile)
        product = jnp.dot(x_buf[...], w_ref[:, at], preferred_element_type=jnp.float32)
        if chunk:
            product = product + before_ref[:, at]
        if len(outs) == 1:
            outs[0][:, at] = product
        else:
            outs[0][:, at] = product[:half].astype(jnp.bfloat16)
            outs[1][:, at] = product[half:]


def combine(chunk, pieces, slots, before, w_out):
    n, (block, depth) = len(slots), pieces[0].shape
    rows = n * block
    cols = w_out.shape[1]
    last = chunk == CHUNKS - 1
    hbm = pl.BlockSpec(memory_space=pltpu.HBM)
    vmem = pl.BlockSpec(memory_space=pltpu.VMEM)
    if last:
        out_shape = [
            pltpu.VMEM((rows // 2, cols), jnp.bfloat16),
            pltpu.VMEM((rows // 2, cols), jnp.float32),
        ]
    else:
        out_shape = [pltpu.VMEM((rows, cols), jnp.float32)]
    earlier = [] if chunk == 0 else [before]
    return pl.pallas_call(
        functools.partial(combine_kernel, n, block, chunk, slots),
        out_shape=out_shape,
        in_specs=[pl.BlockSpec(memory_space=pl.ANY)] * len(pieces)
        + [vmem] * len(earlier)
        + [vmem],
        out_specs=[vmem] * len(out_shape),
        scratch_shapes=[
            pltpu.VMEM((rows, depth), jnp.bfloat16),
            pltpu.SemaphoreType.DMA((n,)),
        ],
        compiler_params=pltpu.CompilerParams(vmem_limit_bytes=16 * MIB),
        name="combine",
    )(*pieces, *earlier, w_out)


def shards(
    tokens, norm_gain, w_query, w_key, w_value, w_out, cache_keys, cache_values, cache_lengths
):
    n = lax.axis_size("gx")
    cores = lax.axis_size("gy")
    levels = n.bit_length() - 1
    position = (cache_lengths[:, None] + jnp.arange(NEW, dtype=jnp.int32)[None, :]).reshape(-1)
    inverse = THETA ** (-2.0 * jnp.arange(HD // 2, dtype=jnp.float32) / HD)
    angles = position.astype(jnp.float32)[:, None] * inverse[None, :]
    cosine, sine = jnp.cos(angles), jnp.sin(angles)
    cosine = jnp.concatenate([cosine, cosine], axis=1)
    sine = jnp.concatenate([-sine, sine], axis=1)

    x, gain = tokens, norm_gain[None, :]
    kv = w_key.shape[1] // CHUNKS
    q_cols = w_query.shape[1] // CHUNKS

    def column_part(start, size, kv_start):
        return project(
            n, start, size, kv_start, start == 0, x, gain, w_query, w_key, w_value
        )

    def after(value, *earlier):
        return lax.optimization_barrier((value, earlier))[0]

    share = q_cols // 2
    send_a, keep_a, x = column_part(0, share, None)
    x = after(x, send_a)
    other_a = exchange(send_a, n, cores, 0, sum_orders(n, 0))
    send_b, keep_b = column_part(share, share, 0)
    x = after(x, send_b)
    other_b = exchange(send_b, n, cores, 0, sum_orders(n, 0))
    sum_a = keep_a + other_a.astype(jnp.float32)
    x = after(x, sum_a)
    later = []
    for chunk in range(1, CHUNKS):
        later.append(column_part(chunk * q_cols, q_cols, chunk * kv))
    other_b = after(other_b, *(send_c for send_c, _ in later))
    first = jnp.concatenate([sum_a, keep_b + other_b.astype(jnp.float32)], axis=1)
    half = first.shape[0] // 2
    send = first[half:].astype(jnp.bfloat16)
    flows = [[1, first[:half], send]]
    for send_c, keep_c in later:
        flows.append([0, keep_c, after(send_c, flows[-1][2])])

    def start(flow):
        return exchange(flow[2], n, cores, flow[0], sum_orders(n, 0 if flow is flows[0] else 1))

    def finish(flow, other, *earlier):
        stage, keep, _ = flow
        if earlier:
            other = after(other, *earlier)
        value = keep + other.astype(jnp.float32)
        low = value.shape[0] // 2 if stage < levels - 1 else 0
        flow[:] = stage + 1, value[:low] if low else value, value[low:].astype(jnp.bfloat16)

    lead, follow = flows
    w_rows = w_out.shape[0] // CHUNKS
    weights = [fetch_rows(after(w_out, lead[2], follow[2]), 0, w_rows)]
    while follow[0] < levels:
        pending = [start(flow) for flow in flows if flow[0] < levels]
        if lead[0] == levels:
            finish(follow, pending[0])
        elif lead[0] == levels - 1:
            cache_keys, cache_values = fetch(*after((cache_keys, cache_values), follow[2]))
            finish(lead, pending[0], cache_keys, cache_values)
            weights.append(fetch_rows(after(w_out, cache_keys), w_rows, w_rows))
            finish(follow, pending[1], lead[1], weights[1])
        else:
            finish(lead, pending[0], *weights)
            finish(follow, pending[1], lead[2])
    sums = [flow[1] for flow in flows]
    squares = sums[0][:, share : share + 128]
    plain = [h * HD for h in range(q_cols // HD)]
    offsets = [[at if at < share else at + 128 for at in plain], plain]
    kv_offsets = [q_cols + 128, q_cols]

    attentions, own = [], []
    for chunk in range(CHUNKS):
        mine = sums[chunk]
        if chunk:
            mine = after(mine, *own[-1][:-1])
        attention = attend(
            chunk,
            offsets[chunk],
            kv_offsets[chunk],
            mine,
            squares,
            cosine,
            sine,
            cache_keys,
            cache_values,
            cache_lengths,
        )
        attentions.append(attention)
        own.append(
            [
                exchange(attention, n, cores, stage, gather_orders(n, chunk))
                for stage in range(levels)
            ]
        )
    gathered = []
    for chunk in range(CHUNKS):
        block = attentions[chunk].shape[0]
        pieces, slots = [attentions[chunk]], [(0, 0)]
        for top in range(levels):
            stage = levels - 1 - top
            received = [own[chunk][stage]]
            if top:
                others = pieces[1:]
                forward = jnp.concatenate(others, axis=0) if top > 1 else others[0]
                if top == 1:
                    forward = after(forward, *own[chunk][:-1], attentions[-1])
                if stage == 0:
                    forward = after(forward, *own[-1][:-1])
                received.append(exchange(forward, n, cores, stage, gather_orders(n, chunk)))
            for value in received:
                for at in range(0, value.shape[0], block):
                    slots.append((len(pieces), at))
                pieces.append(value)
        gathered.append((pieces, slots))
    result = None
    for chunk in range(CHUNKS):
        result = combine(chunk, *gathered[chunk], result and result[0], weights[chunk])
    send, keep = result
    other = lax.ppermute(send, "gy", [(0, 1), (1, 0)])
    return (keep + other.astype(jnp.float32)).astype(jnp.bfloat16)


def solution(mesh):
    return jax.shard_map(
        shards,
        mesh=mesh,
        in_specs=(
            P("groups", "gx"),
            P("gx"),
            P("gx", "gy"),
            P("gx", "gy"),
            P("gx", "gy"),
            P("gy", "gx"),
            P(("groups", "gx"), None, "gy"),
            P(("groups", "gx"), None, "gy"),
            P(("groups", "gx")),
        ),
        out_specs=P(("groups", "gy"), "gx"),
        check_vma=False,
    )
```

```python
import functools
import math

import jax
import jax.numpy as jnp
from jax import lax
from jax.experimental import pallas as pl
from jax.experimental.pallas import tpu as pltpu
from jax.sharding import PartitionSpec as P

D = 16384
HD = 128
NEW = 4
EPS = 1e-05
THETA = 500000.0

CHUNKS = 2
TILES = 4
MIB = 1 << 20


def bit_orders(n):
    levels = n.bit_length() - 1
    first = list(range(levels))
    second = list(first)
    if levels > 1:
        second[0], second[1] = second[1], second[0]
    return first, second


def gather_orders(n, chunk):
    first, second = bit_orders(n)
    return (first, second) if chunk else (first, first)


def slot_shift(slot, order):
    levels = len(order)
    shift = 0
    for stage in range(levels):
        shift |= ((slot >> (levels - 1 - stage)) & 1) << order[stage]
    return shift


def slot_owner(n, slot, gx, gy, orders):
    first, second = (slot_shift(slot, order) for order in orders)
    return gx ^ jnp.where(gy == 0, first, second)


def exchange(value, n, cores, stage, orders):
    pairs = []
    for gx in range(n):
        for gy in range(cores):
            other = gx ^ (1 << orders[gy % 2][stage])
            pairs.append((gx * cores + gy, other * cores + gy))
    return lax.ppermute(value, ("gx", "gy"), pairs)


def project_kernel(n, q_start, kv_start, first, *refs):
    if first:
        tokens_ref, gain_ref, wq_ref, wk_ref, wv_ref, send_ref, keep_ref, x_ref = refs[:8]
        t_buf, t_sems, g_buf, g_sem = refs[8:12]
    else:
        x_ref, wq_ref, wk_ref, wv_ref, send_ref, keep_ref = refs[:6]
    w_buf, sems = refs[-2:]
    half = send_ref.shape[0]
    rows = 2 * half
    with_kv = kv_start is not None
    kv = wk_ref.shape[1] // CHUNKS if with_kv else 0
    width = w_buf.shape[1]
    cols = width - 2 * kv
    tile = cols // 2

    def w_copy(ref, start, size, at, sem):
        return pltpu.make_async_copy(
            ref.at[:, start : start + size], w_buf.at[:, at : at + size], sems.at[sem]
        )

    copies = [[w_copy(wq_ref, q_start + at, tile, at, at // tile)] for at in (0, tile)]
    if with_kv:
        copies[1].append(w_copy(wk_ref, kv_start, kv, cols, 2))
        copies[1].append(w_copy(wv_ref, kv_start, kv, cols + kv, 3))

    if first:
        block = rows // n
        me, gy = lax.axis_index("gx"), lax.axis_index("gy")
        t_copies = []
        for slot in range(n):
            start = pl.multiple_of(slot_owner(n, slot, me, gy, bit_orders(n)) * block, block)
            t_copies.append(
                pltpu.make_async_copy(
                    tokens_ref.at[pl.ds(start, block), :], t_buf.at[slot], t_sems.at[slot]
                )
            )
            t_copies[-1].start()
        g_copy = pltpu.make_async_copy(gain_ref, g_buf, g_sem)
        g_copy.start()
    for group in copies:
        for copy in group:
            copy.start()
    if first:
        lanes = lax.broadcasted_iota(jnp.int32, (block, 128), 1)
        g_copy.wait()
        for slot in range(n):
            t_copies[slot].wait()
            wide = t_buf[slot].astype(jnp.float32)
            x_ref[slot * block : (slot + 1) * block, :] = (wide * g_buf[...]).astype(jnp.bfloat16)
            square = jnp.sum(wide * wide, axis=1, keepdims=True)
            high = square.astype(jnp.bfloat16).astype(jnp.float32)
            rest = square - high
            middle = rest.astype(jnp.bfloat16).astype(jnp.float32)
            low = rest - middle
            packed = jnp.where(
                lanes == 3 * me,
                high,
                jnp.where(lanes == 3 * me + 1, middle, jnp.where(lanes == 3 * me + 2, low, 0.0)),
            )
            if slot < n // 2:
                keep_ref[slot * block : (slot + 1) * block, width : width + 128] = packed
            else:
                at = (slot - n // 2) * block
                send_ref[at : at + block, width : width + 128] = packed.astype(jnp.bfloat16)

    for p, (start, end) in enumerate(((0, tile), (tile, width))):
        for copy in copies[p]:
            copy.wait()
        product = jnp.dot(x_ref[...], w_buf[:, start:end], preferred_element_type=jnp.float32)
        keep_ref[:, start:end] = product[:half]
        send_ref[:, start:end] = product[half:].astype(jnp.bfloat16)


def in_hbm(value):
    return pltpu.with_memory_space_constraint(value, pltpu.HBM)


def project(n, q_start, q_cols, kv_start, first, x, gain, w_query, w_key, w_value):
    rows, depth = x.shape
    kv = w_key.shape[1] // CHUNKS if kv_start is not None else 0
    width = q_cols + 2 * kv
    full = width + (128 if first else 0)
    hbm = pl.BlockSpec(memory_space=pltpu.HBM)
    vmem = pl.BlockSpec(memory_space=pltpu.VMEM)
    out_shape = [
        pltpu.VMEM((rows // 2, full), jnp.bfloat16),
        pltpu.VMEM((rows // 2, full), jnp.float32),
    ]
    scratch = [pltpu.VMEM((depth, width), jnp.bfloat16), pltpu.SemaphoreType.DMA((4,))]
    if first:
        out_shape.append(pltpu.VMEM((rows, depth), jnp.bfloat16))
        args = [in_hbm(x), in_hbm(gain)]
        in_specs = [hbm, hbm]
        scratch = [
            pltpu.VMEM((n, rows // n, depth), jnp.bfloat16),
            pltpu.SemaphoreType.DMA((n,)),
            pltpu.VMEM((1, depth), jnp.float32),
            pltpu.SemaphoreType.DMA,
        ] + scratch
    else:
        args, in_specs = [x], [vmem]
    return pl.pallas_call(
        functools.partial(project_kernel, n, q_start, kv_start, first),
        out_shape=out_shape,
        in_specs=in_specs + [hbm] * 3,
        out_specs=[vmem] * len(out_shape),
        scratch_shapes=scratch,
        compiler_params=pltpu.CompilerParams(vmem_limit_bytes=16 * MIB),
        name="project",
    )(*args, in_hbm(w_query), in_hbm(w_key), in_hbm(w_value))


def attend_kernel(chunk, offsets, kv_offset, groups, heads, seqs, length_ref, *refs):
    sum_ref, square_ref = refs[:2]
    cos_ref, sin_ref, k_ref, v_ref, out_ref, q_scr, o_scr = refs[2:]
    rows = seqs * NEW
    cols = groups * heads * HD
    kv = groups * HD
    seq_count = k_ref.shape[0]

    scale = HD**-0.5 * math.log2(math.e)
    slots = k_ref.shape[1]
    many = heads * NEW
    slot_ids = lax.broadcasted_iota(jnp.int32, (1, slots), 1)
    new_cols = lax.broadcasted_iota(jnp.int32, (many, rows), 1)
    new_rows = lax.broadcasted_iota(jnp.int32, (many, rows), 0) % NEW

    @pl.loop(0, seq_count // seqs)
    def _(step):
        mine = pl.ds(pl.multiple_of(step * rows, rows), rows)
        mean = jnp.sum(square_ref[mine, :], axis=1, keepdims=True) / D
        row_scale = lax.rsqrt(mean + EPS)
        cosine, sine = cos_ref[mine, :], sin_ref[mine, :]

        def raw(start):
            return sum_ref[mine, start : start + HD] * row_scale

        def rotary(value):
            return value * cosine + pltpu.roll(value, HD // 2, 1) * sine

        for h in range(heads * groups):
            turned = rotary(raw(offsets[h]))
            for s in range(seqs):
                q_scr[s, h * NEW : (h + 1) * NEW, :] = turned[s * NEW : (s + 1) * NEW]
        for g in range(groups):
            new_keys = rotary(raw(kv_offset + g * HD)).astype(jnp.bfloat16)
            new_values = raw(kv_offset + (groups + g) * HD).astype(jnp.bfloat16)
            lanes = slice(chunk * kv + g * HD, chunk * kv + (g + 1) * HD)
            olds, news, mixes = [], [], []
            for s in range(seqs):
                query = q_scr[s, g * many : (g + 1) * many, :].astype(jnp.bfloat16)
                keys = k_ref[step * seqs + s, :, lanes]
                olds.append(
                    lax.dot_general(
                        query, keys, (((1,), (1,)), ((), ())), preferred_element_type=jnp.float32
                    )
                )
                news.append(
                    lax.dot_general(
                        query, new_keys, (((1,), (1,)), ((), ())), preferred_element_type=jnp.float32
                    )
                )
            for s in range(seqs):
                live = slot_ids < length_ref[step * seqs + s]
                seen = (new_cols >= s * NEW) & (new_cols <= s * NEW + new_rows)
                old = jnp.where(live, olds[s] * scale, -1e30)
                new = jnp.where(seen, news[s] * scale, -1e30)
                top = jnp.maximum(
                    jnp.max(old, axis=1, keepdims=True), jnp.max(new, axis=1, keepdims=True)
                )
                old = jnp.exp2(old - top)
                new = jnp.exp2(new - top)
                total = jnp.sum(old, axis=1, keepdims=True) + jnp.sum(new, axis=1, keepdims=True)
                inverse = 1.0 / total
                olds[s] = (old * inverse).astype(jnp.bfloat16)
                news[s] = (new * inverse).astype(jnp.bfloat16)
            for s in range(seqs):
                values = v_ref[step * seqs + s, :, lanes]
                mixes.append(
                    jnp.dot(olds[s], values, preferred_element_type=jnp.float32)
                    + jnp.dot(news[s], new_values, preferred_element_type=jnp.float32)
                )
            for s in range(seqs):
                for h in range(heads):
                    at = (g * heads + h) * HD
                    o_scr[s * NEW : (s + 1) * NEW, at : at + HD] = mixes[s][
                        h * NEW : (h + 1) * NEW
                    ]
        out_ref[mine, :] = o_scr[...].astype(jnp.bfloat16)


def attend(chunk, offsets, kv_offset, sums, squares, cosine, sine, cache_keys, cache_values, lengths):
    seq_count, slots, kv_all = cache_keys.shape
    kv = kv_all // CHUNKS
    groups = kv // HD
    heads = len(offsets) // groups
    cols = len(offsets) * HD
    seqs = min(4, seq_count)
    rows = seq_count * NEW
    vmem = pl.BlockSpec(memory_space=pltpu.VMEM)
    hbm = pl.BlockSpec(memory_space=pltpu.HBM)
    return pl.pallas_call(
        functools.partial(attend_kernel, chunk, offsets, kv_offset, groups, heads, seqs),
        out_shape=pltpu.VMEM((rows, cols), jnp.bfloat16),
        in_specs=[pl.BlockSpec(memory_space=pltpu.SMEM)] + [vmem] * 6,
        out_specs=vmem,
        scratch_shapes=[
            pltpu.VMEM((seqs, groups * heads * NEW, HD), jnp.float32),
            pltpu.VMEM((seqs * NEW, cols), jnp.float32),
        ],
        compiler_params=pltpu.CompilerParams(vmem_limit_bytes=16 * MIB),
        name="attend",
    )(lengths, sums, squares, cosine, sine, cache_keys, cache_values)


def fetch_kernel(count, pieces, *refs):
    sources, targets, sems = refs[:count], refs[count : 2 * count], refs[2 * count]
    copies = []
    for i, (source, target) in enumerate(zip(sources, targets)):
        size = target.shape[0] // pieces
        for p in range(pieces):
            at = slice(p * size, (p + 1) * size)
            copies.append(
                pltpu.make_async_copy(source.at[at], target.at[at], sems.at[i * pieces + p])
            )
    for copy in copies:
        copy.start()
    for copy in copies:
        copy.wait()


def fetch(*arrays):
    pieces = 4
    return pl.pallas_call(
        functools.partial(fetch_kernel, len(arrays), pieces),
        out_shape=[pltpu.VMEM(array.shape, array.dtype) for array in arrays],
        in_specs=[pl.BlockSpec(memory_space=pltpu.HBM)] * len(arrays),
        out_specs=[pl.BlockSpec(memory_space=pltpu.VMEM)] * len(arrays),
        scratch_shapes=[pltpu.SemaphoreType.DMA((pieces * len(arrays),))],
        compiler_params=pltpu.CompilerParams(vmem_limit_bytes=4 * MIB),
        name="fetch",
    )(*[in_hbm(array) for array in arrays])


def fetch_rows_kernel(start, pieces, source, target, sems):
    size = target.shape[0] // pieces
    copies = [
        pltpu.make_async_copy(
            source.at[start + p * size : start + (p + 1) * size],
            target.at[p * size : (p + 1) * size],
            sems.at[p],
        )
        for p in range(pieces)
    ]
    for copy in copies:
        copy.start()
    for copy in copies:
        copy.wait()


def fetch_rows(array, start, rows):
    pieces = 4
    return pl.pallas_call(
        functools.partial(fetch_rows_kernel, start, pieces),
        out_shape=pltpu.VMEM((rows, array.shape[1]), array.dtype),
        in_specs=[pl.BlockSpec(memory_space=pltpu.HBM)],
        out_specs=pl.BlockSpec(memory_space=pltpu.VMEM),
        scratch_shapes=[pltpu.SemaphoreType.DMA((pieces,))],
        compiler_params=pltpu.CompilerParams(vmem_limit_bytes=4 * MIB),
        name="fetch_rows",
    )(in_hbm(array))


def combine_kernel(n, block, chunk, *refs):
    pieces, refs = refs[:n], refs[n:]
    gx, gy = lax.axis_index("gx"), lax.axis_index("gy")
    moved = jnp.where(gy == 0, n // 2, 0)
    if chunk:
        before_ref, refs = refs[0], refs[1:]
    w_ref, outs, (x_buf, x_sems) = refs[0], refs[1:-2], refs[-2:]
    depth, cols = x_buf.shape[1], w_ref.shape[1]
    half = x_buf.shape[0] // 2
    x_copies = []
    for slot, piece in enumerate(pieces):
        start = pl.multiple_of((slot_owner(n, slot, gx, gy, gather_orders(n, chunk)) ^ moved) * block, block)
        x_copies.append(
            pltpu.make_async_copy(piece, x_buf.at[pl.ds(start, block), :], x_sems.at[slot])
        )
    for copy in x_copies:
        copy.start()
    for copy in x_copies:
        copy.wait()

    tile = cols // TILES
    for start in range(0, cols, tile):
        at = slice(start, start + tile)
        product = jnp.dot(x_buf[...], w_ref[:, at], preferred_element_type=jnp.float32)
        if chunk:
            product = product + before_ref[:, at]
        if len(outs) == 1:
            outs[0][:, at] = product
        else:
            outs[0][:, at] = product[:half].astype(jnp.bfloat16)
            outs[1][:, at] = product[half:]


def combine(chunk, pieces, before, w_out):
    n, (block, depth) = len(pieces), pieces[0].shape
    rows = n * block
    cols = w_out.shape[1]
    last = chunk == CHUNKS - 1
    hbm = pl.BlockSpec(memory_space=pltpu.HBM)
    vmem = pl.BlockSpec(memory_space=pltpu.VMEM)
    if last:
        out_shape = [
            pltpu.VMEM((rows // 2, cols), jnp.bfloat16),
            pltpu.VMEM((rows // 2, cols), jnp.float32),
        ]
    else:
        out_shape = [pltpu.VMEM((rows, cols), jnp.float32)]
    earlier = [] if chunk == 0 else [before]
    return pl.pallas_call(
        functools.partial(combine_kernel, n, block, chunk),
        out_shape=out_shape,
        in_specs=[pl.BlockSpec(memory_space=pl.ANY)] * len(pieces)
        + [vmem] * len(earlier)
        + [vmem],
        out_specs=[vmem] * len(out_shape),
        scratch_shapes=[
            pltpu.VMEM((rows, depth), jnp.bfloat16),
            pltpu.SemaphoreType.DMA((n,)),
        ],
        compiler_params=pltpu.CompilerParams(vmem_limit_bytes=16 * MIB),
        name="combine",
    )(*pieces, *earlier, w_out)


def shards(
    tokens, norm_gain, w_query, w_key, w_value, w_out, cache_keys, cache_values, cache_lengths
):
    n = lax.axis_size("gx")
    cores = lax.axis_size("gy")
    levels = n.bit_length() - 1
    position = (cache_lengths[:, None] + jnp.arange(NEW, dtype=jnp.int32)[None, :]).reshape(-1)
    inverse = THETA ** (-2.0 * jnp.arange(HD // 2, dtype=jnp.float32) / HD)
    angles = position.astype(jnp.float32)[:, None] * inverse[None, :]
    cosine, sine = jnp.cos(angles), jnp.sin(angles)
    cosine = jnp.concatenate([cosine, cosine], axis=1)
    sine = jnp.concatenate([-sine, sine], axis=1)

    x, gain = tokens, norm_gain[None, :]
    kv = w_key.shape[1] // CHUNKS
    q_cols = w_query.shape[1] // CHUNKS

    def column_part(start, size, kv_start):
        return project(
            n, start, size, kv_start, start == 0, x, gain, w_query, w_key, w_value
        )

    def after(value, *earlier):
        return lax.optimization_barrier((value, earlier))[0]

    share = q_cols // 2
    orders = bit_orders(n)
    send_a, keep_a, x = column_part(0, share, None)
    x = after(x, send_a)
    other_a = exchange(send_a, n, cores, 0, orders)
    send_b, keep_b = column_part(share, share, 0)
    x = after(x, send_b)
    other_b = exchange(send_b, n, cores, 0, orders)
    sum_a = keep_a + other_a.astype(jnp.float32)
    x = after(x, sum_a)
    later = []
    for chunk in range(1, CHUNKS):
        later.append(column_part(chunk * q_cols, q_cols, chunk * kv))
    other_b = after(other_b, *(send_c for send_c, _ in later))
    first = jnp.concatenate([sum_a, keep_b + other_b.astype(jnp.float32)], axis=1)
    half = first.shape[0] // 2
    send = first[half:].astype(jnp.bfloat16)
    flows = [[1, first[:half], send]]
    for send_c, keep_c in later:
        flows.append([0, keep_c, after(send_c, flows[-1][2])])

    def start(flow):
        return exchange(flow[2], n, cores, flow[0], orders)

    def finish(flow, other, *earlier):
        stage, keep, _ = flow
        if earlier:
            other = after(other, *earlier)
        value = keep + other.astype(jnp.float32)
        low = value.shape[0] // 2 if stage < levels - 1 else 0
        flow[:] = stage + 1, value[:low] if low else value, value[low:].astype(jnp.bfloat16)

    lead, follow = flows
    w_rows = w_out.shape[0] // CHUNKS
    weights = [fetch_rows(after(w_out, lead[2], follow[2]), 0, w_rows)]
    while follow[0] < levels:
        pending = [start(flow) for flow in flows if flow[0] < levels]
        if lead[0] == levels:
            finish(follow, pending[0])
        elif lead[0] == levels - 1:
            cache_keys, cache_values = fetch(*after((cache_keys, cache_values), follow[2]))
            finish(lead, pending[0], cache_keys, cache_values)
            finish(follow, pending[1], lead[1])
        else:
            finish(lead, pending[0], *weights)
            finish(follow, pending[1], lead[2])
    sums = [flow[1] for flow in flows]
    squares = sums[0][:, share : share + 128]
    plain = [h * HD for h in range(q_cols // HD)]
    offsets = [[at if at < share else at + 128 for at in plain], plain]
    kv_offsets = [q_cols + 128, q_cols]

    attentions = []
    for chunk in range(CHUNKS):
        attentions.append(
            attend(
                chunk,
                offsets[chunk],
                kv_offsets[chunk],
                sums[chunk],
                squares,
                cosine,
                sine,
                cache_keys,
                cache_values,
                cache_lengths,
            )
        )
    weights.append(fetch_rows(after(w_out, attentions[1]), w_rows, w_rows))
    gathered = []
    for chunk in range(CHUNKS):
        slots = [attentions[chunk]]
        for slot in range(1, n):
            top = slot.bit_length() - 1
            source = slots[slot - (1 << top)]
            if slot == 1 and chunk == 0:
                source = after(source, sums[1])
            if slot == 3 and chunk == 1:
                source = after(source, weights[1])
            slots.append(
                exchange(source, n, cores, levels - 1 - top, gather_orders(n, chunk))
            )
        gathered.append(slots)
    result = None
    for chunk in range(CHUNKS):
        result = combine(chunk, gathered[chunk], result and result[0], weights[chunk])
    send, keep = result
    other = lax.ppermute(send, "gy", [(0, 1), (1, 0)])
    return (keep + other.astype(jnp.float32)).astype(jnp.bfloat16)


def solution(mesh):
    return jax.shard_map(
        shards,
        mesh=mesh,
        in_specs=(
            P("groups", "gx"),
            P("gx"),
            P("gx", "gy"),
            P("gx", "gy"),
            P("gx", "gy"),
            P("gy", "gx"),
            P(("groups", "gx"), None, "gy"),
            P(("groups", "gx"), None, "gy"),
            P(("groups", "gx")),
        ),
        out_specs=P(("groups", "gy"), "gx"),
        check_vma=False,
    )
```

```python
import functools
import math

import jax
import jax.numpy as jnp
from jax import lax
from jax.experimental import pallas as pl
from jax.experimental.pallas import tpu as pltpu
from jax.sharding import PartitionSpec as P

D = 16384
HD = 128
NEW = 4
EPS = 1e-05
THETA = 500000.0

CHUNKS = 2
TILES = 4
MIB = 1 << 20


def bit_orders(n):
    levels = n.bit_length() - 1
    first = list(range(levels))
    second = list(first)
    if levels > 1:
        second[0], second[1] = second[1], second[0]
    return first, second


def gather_orders(n, chunk):
    first, second = bit_orders(n)
    return (first, second) if chunk else (first, first)


def slot_shift(slot, order):
    levels = len(order)
    shift = 0
    for stage in range(levels):
        shift |= ((slot >> (levels - 1 - stage)) & 1) << order[stage]
    return shift


def slot_owner(n, slot, gx, gy, orders):
    first, second = (slot_shift(slot, order) for order in orders)
    return gx ^ jnp.where(gy == 0, first, second)


def exchange(value, n, cores, stage, orders):
    pairs = []
    for gx in range(n):
        for gy in range(cores):
            other = gx ^ (1 << orders[gy % 2][stage])
            pairs.append((gx * cores + gy, other * cores + gy))
    return lax.ppermute(value, ("gx", "gy"), pairs)


def project_kernel(n, q_start, kv_start, first, *refs):
    if first:
        tokens_ref, gain_ref, wq_ref, wk_ref, wv_ref, send_ref, keep_ref, x_ref = refs[:8]
        t_buf, t_sems, g_buf, g_sem = refs[8:12]
    else:
        x_ref, wq_ref, wk_ref, wv_ref, send_ref, keep_ref = refs[:6]
    w_buf, sems = refs[-2:]
    half = send_ref.shape[0]
    rows = 2 * half
    with_kv = kv_start is not None
    kv = wk_ref.shape[1] // CHUNKS if with_kv else 0
    width = w_buf.shape[1]
    cols = width - 2 * kv
    tile = cols // 2

    def w_copy(ref, start, size, at, sem):
        return pltpu.make_async_copy(
            ref.at[:, start : start + size], w_buf.at[:, at : at + size], sems.at[sem]
        )

    copies = [[w_copy(wq_ref, q_start + at, tile, at, at // tile)] for at in (0, tile)]
    if with_kv:
        copies[1].append(w_copy(wk_ref, kv_start, kv, cols, 2))
        copies[1].append(w_copy(wv_ref, kv_start, kv, cols + kv, 3))

    if first:
        block = rows // n
        me, gy = lax.axis_index("gx"), lax.axis_index("gy")
        t_copies = []
        for slot in range(n):
            start = pl.multiple_of(slot_owner(n, slot, me, gy, bit_orders(n)) * block, block)
            t_copies.append(
                pltpu.make_async_copy(
                    tokens_ref.at[pl.ds(start, block), :], t_buf.at[slot], t_sems.at[slot]
                )
            )
            t_copies[-1].start()
        g_copy = pltpu.make_async_copy(gain_ref, g_buf, g_sem)
        g_copy.start()
    for group in copies:
        for copy in group:
            copy.start()
    if first:
        lanes = lax.broadcasted_iota(jnp.int32, (block, 128), 1)
        g_copy.wait()
        for slot in range(n):
            t_copies[slot].wait()
            wide = t_buf[slot].astype(jnp.float32)
            x_ref[slot * block : (slot + 1) * block, :] = (wide * g_buf[...]).astype(jnp.bfloat16)
            square = jnp.sum(wide * wide, axis=1, keepdims=True)
            high = square.astype(jnp.bfloat16).astype(jnp.float32)
            rest = square - high
            middle = rest.astype(jnp.bfloat16).astype(jnp.float32)
            low = rest - middle
            packed = jnp.where(
                lanes == 3 * me,
                high,
                jnp.where(lanes == 3 * me + 1, middle, jnp.where(lanes == 3 * me + 2, low, 0.0)),
            )
            if slot < n // 2:
                keep_ref[slot * block : (slot + 1) * block, width : width + 128] = packed
            else:
                at = (slot - n // 2) * block
                send_ref[at : at + block, width : width + 128] = packed.astype(jnp.bfloat16)

    for p, (start, end) in enumerate(((0, tile), (tile, width))):
        for copy in copies[p]:
            copy.wait()
        product = jnp.dot(x_ref[...], w_buf[:, start:end], preferred_element_type=jnp.float32)
        keep_ref[:, start:end] = product[:half]
        send_ref[:, start:end] = product[half:].astype(jnp.bfloat16)


def in_hbm(value):
    return pltpu.with_memory_space_constraint(value, pltpu.HBM)


def project(n, q_start, q_cols, kv_start, first, x, gain, w_query, w_key, w_value):
    rows, depth = x.shape
    kv = w_key.shape[1] // CHUNKS if kv_start is not None else 0
    width = q_cols + 2 * kv
    full = width + (128 if first else 0)
    hbm = pl.BlockSpec(memory_space=pltpu.HBM)
    vmem = pl.BlockSpec(memory_space=pltpu.VMEM)
    out_shape = [
        pltpu.VMEM((rows // 2, full), jnp.bfloat16),
        pltpu.VMEM((rows // 2, full), jnp.float32),
    ]
    scratch = [pltpu.VMEM((depth, width), jnp.bfloat16), pltpu.SemaphoreType.DMA((4,))]
    if first:
        out_shape.append(pltpu.VMEM((rows, depth), jnp.bfloat16))
        args = [in_hbm(x), in_hbm(gain)]
        in_specs = [hbm, hbm]
        scratch = [
            pltpu.VMEM((n, rows // n, depth), jnp.bfloat16),
            pltpu.SemaphoreType.DMA((n,)),
            pltpu.VMEM((1, depth), jnp.float32),
            pltpu.SemaphoreType.DMA,
        ] + scratch
    else:
        args, in_specs = [x], [vmem]
    return pl.pallas_call(
        functools.partial(project_kernel, n, q_start, kv_start, first),
        out_shape=out_shape,
        in_specs=in_specs + [hbm] * 3,
        out_specs=[vmem] * len(out_shape),
        scratch_shapes=scratch,
        compiler_params=pltpu.CompilerParams(vmem_limit_bytes=16 * MIB),
        name="project",
    )(*args, in_hbm(w_query), in_hbm(w_key), in_hbm(w_value))


def attend_kernel(chunk, offsets, kv_offset, groups, heads, seqs, length_ref, *refs):
    sum_ref, square_ref = refs[:2]
    cos_ref, sin_ref, k_ref, v_ref, out_ref, q_scr, o_scr = refs[2:]
    rows = seqs * NEW
    cols = groups * heads * HD
    kv = groups * HD
    seq_count = k_ref.shape[0]

    scale = HD**-0.5 * math.log2(math.e)
    slots = k_ref.shape[1]
    many = heads * NEW
    slot_ids = lax.broadcasted_iota(jnp.int32, (1, slots), 1)
    new_cols = lax.broadcasted_iota(jnp.int32, (many, rows), 1)
    new_rows = lax.broadcasted_iota(jnp.int32, (many, rows), 0) % NEW

    @pl.loop(0, seq_count // seqs)
    def _(step):
        mine = pl.ds(pl.multiple_of(step * rows, rows), rows)
        mean = jnp.sum(square_ref[mine, :], axis=1, keepdims=True) / D
        row_scale = lax.rsqrt(mean + EPS)
        cosine, sine = cos_ref[mine, :], sin_ref[mine, :]

        def raw(start):
            return sum_ref[mine, start : start + HD] * row_scale

        def rotary(value):
            return value * cosine + pltpu.roll(value, HD // 2, 1) * sine

        for h in range(heads * groups):
            turned = rotary(raw(offsets[h]))
            for s in range(seqs):
                q_scr[s, h * NEW : (h + 1) * NEW, :] = turned[s * NEW : (s + 1) * NEW]
        for g in range(groups):
            new_keys = rotary(raw(kv_offset + g * HD)).astype(jnp.bfloat16)
            new_values = raw(kv_offset + (groups + g) * HD).astype(jnp.bfloat16)
            lanes = slice(chunk * kv + g * HD, chunk * kv + (g + 1) * HD)
            olds, news, mixes = [], [], []
            for s in range(seqs):
                query = q_scr[s, g * many : (g + 1) * many, :].astype(jnp.bfloat16)
                keys = k_ref[step * seqs + s, :, lanes]
                olds.append(
                    lax.dot_general(
                        query, keys, (((1,), (1,)), ((), ())), preferred_element_type=jnp.float32
                    )
                )
                news.append(
                    lax.dot_general(
                        query, new_keys, (((1,), (1,)), ((), ())), preferred_element_type=jnp.float32
                    )
                )
            for s in range(seqs):
                live = slot_ids < length_ref[step * seqs + s]
                seen = (new_cols >= s * NEW) & (new_cols <= s * NEW + new_rows)
                old = jnp.where(live, olds[s] * scale, -1e30)
                new = jnp.where(seen, news[s] * scale, -1e30)
                top = jnp.maximum(
                    jnp.max(old, axis=1, keepdims=True), jnp.max(new, axis=1, keepdims=True)
                )
                old = jnp.exp2(old - top)
                new = jnp.exp2(new - top)
                total = jnp.sum(old, axis=1, keepdims=True) + jnp.sum(new, axis=1, keepdims=True)
                inverse = 1.0 / total
                olds[s] = (old * inverse).astype(jnp.bfloat16)
                news[s] = (new * inverse).astype(jnp.bfloat16)
            for s in range(seqs):
                values = v_ref[step * seqs + s, :, lanes]
                mixes.append(
                    jnp.dot(olds[s], values, preferred_element_type=jnp.float32)
                    + jnp.dot(news[s], new_values, preferred_element_type=jnp.float32)
                )
            for s in range(seqs):
                for h in range(heads):
                    at = (g * heads + h) * HD
                    o_scr[s * NEW : (s + 1) * NEW, at : at + HD] = mixes[s][
                        h * NEW : (h + 1) * NEW
                    ]
        out_ref[mine, :] = o_scr[...].astype(jnp.bfloat16)


def attend(chunk, offsets, kv_offset, sums, squares, cosine, sine, cache_keys, cache_values, lengths):
    seq_count, slots, kv_all = cache_keys.shape
    kv = kv_all // CHUNKS
    groups = kv // HD
    heads = len(offsets) // groups
    cols = len(offsets) * HD
    seqs = min(4, seq_count)
    rows = seq_count * NEW
    vmem = pl.BlockSpec(memory_space=pltpu.VMEM)
    hbm = pl.BlockSpec(memory_space=pltpu.HBM)
    return pl.pallas_call(
        functools.partial(attend_kernel, chunk, offsets, kv_offset, groups, heads, seqs),
        out_shape=pltpu.VMEM((rows, cols), jnp.bfloat16),
        in_specs=[pl.BlockSpec(memory_space=pltpu.SMEM)] + [vmem] * 6,
        out_specs=vmem,
        scratch_shapes=[
            pltpu.VMEM((seqs, groups * heads * NEW, HD), jnp.float32),
            pltpu.VMEM((seqs * NEW, cols), jnp.float32),
        ],
        compiler_params=pltpu.CompilerParams(vmem_limit_bytes=16 * MIB),
        name="attend",
    )(lengths, sums, squares, cosine, sine, cache_keys, cache_values)


def fetch_kernel(count, pieces, *refs):
    sources, targets, sems = refs[:count], refs[count : 2 * count], refs[2 * count]
    copies = []
    for i, (source, target) in enumerate(zip(sources, targets)):
        size = target.shape[0] // pieces
        for p in range(pieces):
            at = slice(p * size, (p + 1) * size)
            copies.append(
                pltpu.make_async_copy(source.at[at], target.at[at], sems.at[i * pieces + p])
            )
    for copy in copies:
        copy.start()
    for copy in copies:
        copy.wait()


def fetch(*arrays):
    pieces = 4
    return pl.pallas_call(
        functools.partial(fetch_kernel, len(arrays), pieces),
        out_shape=[pltpu.VMEM(array.shape, array.dtype) for array in arrays],
        in_specs=[pl.BlockSpec(memory_space=pltpu.HBM)] * len(arrays),
        out_specs=[pl.BlockSpec(memory_space=pltpu.VMEM)] * len(arrays),
        scratch_shapes=[pltpu.SemaphoreType.DMA((pieces * len(arrays),))],
        compiler_params=pltpu.CompilerParams(vmem_limit_bytes=4 * MIB),
        name="fetch",
    )(*[in_hbm(array) for array in arrays])


def fetch_rows_kernel(start, pieces, source, target, sems):
    size = target.shape[0] // pieces
    copies = [
        pltpu.make_async_copy(
            source.at[start + p * size : start + (p + 1) * size],
            target.at[p * size : (p + 1) * size],
            sems.at[p],
        )
        for p in range(pieces)
    ]
    for copy in copies:
        copy.start()
    for copy in copies:
        copy.wait()


def fetch_rows(array, start, rows):
    pieces = 4
    return pl.pallas_call(
        functools.partial(fetch_rows_kernel, start, pieces),
        out_shape=pltpu.VMEM((rows, array.shape[1]), array.dtype),
        in_specs=[pl.BlockSpec(memory_space=pltpu.HBM)],
        out_specs=pl.BlockSpec(memory_space=pltpu.VMEM),
        scratch_shapes=[pltpu.SemaphoreType.DMA((pieces,))],
        compiler_params=pltpu.CompilerParams(vmem_limit_bytes=4 * MIB),
        name="fetch_rows",
    )(in_hbm(array))


def combine_kernel(n, block, chunk, *refs):
    pieces, refs = refs[:n], refs[n:]
    gx, gy = lax.axis_index("gx"), lax.axis_index("gy")
    moved = jnp.where(gy == 0, n // 2, 0)
    if chunk:
        before_ref, refs = refs[0], refs[1:]
    x_buf, x_sems, w_sems = refs[-3:]
    w_ref, outs = refs[0], refs[1:-3]
    w_copies = []
    if chunk == 0:
        more_ref, sums_ref, next_ref = outs
        outs = [sums_ref]
        size = next_ref.shape[0] // 4
        for p in range(4):
            w_copies.append(
                pltpu.make_async_copy(
                    more_ref.at[next_ref.shape[0] + p * size : next_ref.shape[0] + (p + 1) * size],
                    next_ref.at[p * size : (p + 1) * size],
                    w_sems.at[p],
                )
            )
    depth, cols = x_buf.shape[1], w_ref.shape[1]
    half = x_buf.shape[0] // 2
    x_copies = []
    for slot, piece in enumerate(pieces):
        start = pl.multiple_of((slot_owner(n, slot, gx, gy, gather_orders(n, chunk)) ^ moved) * block, block)
        x_copies.append(
            pltpu.make_async_copy(piece, x_buf.at[pl.ds(start, block), :], x_sems.at[slot])
        )
    for copy in x_copies + w_copies:
        copy.start()
    for copy in x_copies:
        copy.wait()

    tile = cols // TILES
    for start in range(0, cols, tile):
        at = slice(start, start + tile)
        product = jnp.dot(x_buf[...], w_ref[:, at], preferred_element_type=jnp.float32)
        if chunk:
            product = product + before_ref[:, at]
        if len(outs) == 1:
            outs[0][:, at] = product
        else:
            outs[0][:, at] = product[:half].astype(jnp.bfloat16)
            outs[1][:, at] = product[half:]
    for copy in w_copies:
        copy.wait()


def combine(chunk, pieces, before, w_rows, w_out):
    n, (block, depth) = len(pieces), pieces[0].shape
    rows = n * block
    cols = w_rows.shape[1]
    last = chunk == CHUNKS - 1
    hbm = pl.BlockSpec(memory_space=pltpu.HBM)
    vmem = pl.BlockSpec(memory_space=pltpu.VMEM)
    if last:
        out_shape = [
            pltpu.VMEM((rows // 2, cols), jnp.bfloat16),
            pltpu.VMEM((rows // 2, cols), jnp.float32),
        ]
    else:
        out_shape = [pltpu.VMEM((rows, cols), jnp.float32), pltpu.VMEM(w_rows.shape, w_rows.dtype)]
    earlier = [] if chunk == 0 else [before]
    later = [in_hbm(w_out)] if chunk == 0 else []
    return pl.pallas_call(
        functools.partial(combine_kernel, n, block, chunk),
        out_shape=out_shape,
        in_specs=[pl.BlockSpec(memory_space=pl.ANY)] * len(pieces)
        + [vmem] * len(earlier)
        + [vmem]
        + [pl.BlockSpec(memory_space=pltpu.HBM)] * len(later),
        out_specs=[vmem] * len(out_shape),
        scratch_shapes=[
            pltpu.VMEM((rows, depth), jnp.bfloat16),
            pltpu.SemaphoreType.DMA((n,)),
            pltpu.SemaphoreType.DMA((4,)),
        ],
        compiler_params=pltpu.CompilerParams(vmem_limit_bytes=16 * MIB),
        name="combine",
    )(*pieces, *earlier, w_rows, *later)


def shards(
    tokens, norm_gain, w_query, w_key, w_value, w_out, cache_keys, cache_values, cache_lengths
):
    n = lax.axis_size("gx")
    cores = lax.axis_size("gy")
    levels = n.bit_length() - 1
    position = (cache_lengths[:, None] + jnp.arange(NEW, dtype=jnp.int32)[None, :]).reshape(-1)
    inverse = THETA ** (-2.0 * jnp.arange(HD // 2, dtype=jnp.float32) / HD)
    angles = position.astype(jnp.float32)[:, None] * inverse[None, :]
    cosine, sine = jnp.cos(angles), jnp.sin(angles)
    cosine = jnp.concatenate([cosine, cosine], axis=1)
    sine = jnp.concatenate([-sine, sine], axis=1)

    x, gain = tokens, norm_gain[None, :]
    kv = w_key.shape[1] // CHUNKS
    q_cols = w_query.shape[1] // CHUNKS

    def column_part(start, size, kv_start):
        return project(
            n, start, size, kv_start, start == 0, x, gain, w_query, w_key, w_value
        )

    def after(value, *earlier):
        return lax.optimization_barrier((value, earlier))[0]

    share = q_cols // 2
    orders = bit_orders(n)

    def first_exchange(send):
        return exchange(send, n, cores, 0, orders)

    send_a, keep_a, x = column_part(0, share, None)
    x = after(x, send_a)
    other_a = first_exchange(send_a)
    send_b, keep_b = column_part(share, share, 0)
    x = after(x, send_b)
    other_b = first_exchange(send_b)
    sum_a = keep_a + other_a.astype(jnp.float32)
    x = after(x, sum_a)
    send_c, keep_c = column_part(q_cols, share, None)
    other_c = first_exchange(send_c)
    other_b = after(other_b, send_c)

    def joined(left, keep, other):
        value = jnp.concatenate([left, keep + other.astype(jnp.float32)], axis=1)
        half = value.shape[0] // 2
        return [1, value[:half], value[half:].astype(jnp.bfloat16)]

    lead = joined(sum_a, keep_b, other_b)
    x = after(x, lead[2], send_c)
    send_d, keep_d = column_part(q_cols + share, share, kv)
    other_d = first_exchange(send_d)

    def start(flow):
        return exchange(flow[2], n, cores, flow[0], orders)

    def finish(flow, other, *earlier):
        stage, keep, _ = flow
        if earlier:
            other = after(other, *earlier)
        value = keep + other.astype(jnp.float32)
        low = value.shape[0] // 2 if stage < levels - 1 else 0
        flow[:] = stage + 1, value[:low] if low else value, value[low:].astype(jnp.bfloat16)

    w_rows = w_out.shape[0] // CHUNKS
    w_first = fetch_rows(after(w_out, lead[2], send_d), 0, w_rows)
    finish(lead, start(lead), w_first)
    other_c, other_d = after((other_c, other_d), lead[2])
    follow = joined(keep_c + other_c.astype(jnp.float32), keep_d, other_d)
    flows = [lead, follow]
    cached = False
    while follow[0] < levels:
        pending = [start(flow) for flow in flows if flow[0] < levels]
        if not cached:
            cache_keys, cache_values = fetch(*after((cache_keys, cache_values), follow[2]))
            pending[0] = after(pending[0], cache_keys, cache_values)
            cached = True
        if lead[0] < levels:
            finish(lead, pending[0])
            finish(follow, pending[1], lead[1], lead[2])
        else:
            finish(follow, pending[0])
    sums = [flow[1] for flow in flows]
    squares = sums[0][:, share : share + 128]
    plain = [h * HD for h in range(q_cols // HD)]
    offsets = [[at if at < share else at + 128 for at in plain], plain]
    kv_offsets = [q_cols + 128, q_cols]

    attentions = []
    for chunk in range(CHUNKS):
        attentions.append(
            attend(
                chunk,
                offsets[chunk],
                kv_offsets[chunk],
                sums[chunk],
                squares,
                cosine,
                sine,
                cache_keys,
                cache_values,
                cache_lengths,
            )
        )
    gathered = []
    for chunk in range(CHUNKS):
        slots = [attentions[chunk]]
        for slot in range(1, n):
            top = slot.bit_length() - 1
            source = slots[slot - (1 << top)]
            if slot == 1 and chunk == 0:
                source = after(source, sums[1])
            if slot == 3 << (levels - 2):
                source = after(source, slots[1 << (levels - 1)])
            slots.append(
                exchange(source, n, cores, levels - 1 - top, gather_orders(n, chunk))
            )
        gathered.append(slots)
    before, w_second = combine(0, gathered[0], None, w_first, w_out)
    send, keep = combine(1, gathered[1], before, w_second, None)
    other = lax.ppermute(send, "gy", [(0, 1), (1, 0)])
    return (keep + other.astype(jnp.float32)).astype(jnp.bfloat16)


def solution(mesh):
    return jax.shard_map(
        shards,
        mesh=mesh,
        in_specs=(
            P("groups", "gx"),
            P("gx"),
            P("gx", "gy"),
            P("gx", "gy"),
            P("gx", "gy"),
            P("gy", "gx"),
            P(("groups", "gx"), None, "gy"),
            P(("groups", "gx"), None, "gy"),
            P(("groups", "gx")),
        ),
        out_specs=P(("groups", "gy"), "gx"),
        check_vma=False,
    )
```

```python
import functools
import math

import jax
import jax.numpy as jnp
from jax import lax
from jax.experimental import pallas as pl
from jax.experimental.pallas import tpu as pltpu
from jax.sharding import PartitionSpec as P

D = 16384
HD = 128
NEW = 4
EPS = 1e-05
THETA = 500000.0

CHUNKS = 2
TILES = 4
MIB = 1 << 20


def bit_orders(n):
    first = list(range(n.bit_length() - 1))
    second = list(first)
    if len(first) > 1:
        second[0], second[1] = second[1], second[0]
    if len(first) > 2:
        first[1], first[2] = first[2], first[1]
    return first, second


def gather_orders(n, chunk):
    second = bit_orders(n)[1]
    first = sorted(second)
    return (first, second) if chunk else (first, first)


def slot_shift(slot, order):
    levels = len(order)
    shift = 0
    for stage in range(levels):
        shift |= ((slot >> (levels - 1 - stage)) & 1) << order[stage]
    return shift


def slot_owner(n, slot, gx, gy, orders):
    first, second = (slot_shift(slot, order) for order in orders)
    return gx ^ jnp.where(gy == 0, first, second)


def exchange(value, n, cores, stage, orders):
    pairs = []
    for gx in range(n):
        for gy in range(cores):
            other = gx ^ (1 << orders[gy % 2][stage])
            pairs.append((gx * cores + gy, other * cores + gy))
    return lax.ppermute(value, ("gx", "gy"), pairs)


def project_kernel(n, q_start, kv_start, first, *refs):
    if first:
        tokens_ref, gain_ref, wq_ref, wk_ref, wv_ref, send_ref, keep_ref, x_ref = refs[:8]
        t_buf, t_sems, g_buf, g_sem = refs[8:12]
    else:
        x_ref, wq_ref, wk_ref, wv_ref, send_ref, keep_ref = refs[:6]
    w_buf, sems = refs[-2:]
    half = send_ref.shape[0]
    rows = 2 * half
    with_kv = kv_start is not None
    kv = wk_ref.shape[1] // CHUNKS if with_kv else 0
    width = w_buf.shape[1]
    cols = width - 2 * kv
    tile = cols // 2

    def w_copy(ref, start, size, at, sem):
        return pltpu.make_async_copy(
            ref.at[:, start : start + size], w_buf.at[:, at : at + size], sems.at[sem]
        )

    copies = [[w_copy(wq_ref, q_start + at, tile, at, at // tile)] for at in (0, tile)]
    if with_kv:
        copies[1].append(w_copy(wk_ref, kv_start, kv, cols, 2))
        copies[1].append(w_copy(wv_ref, kv_start, kv, cols + kv, 3))

    if first:
        block = rows // n
        me, gy = lax.axis_index("gx"), lax.axis_index("gy")
        t_copies = []
        for slot in range(n):
            start = pl.multiple_of(slot_owner(n, slot, me, gy, bit_orders(n)) * block, block)
            t_copies.append(
                pltpu.make_async_copy(
                    tokens_ref.at[pl.ds(start, block), :], t_buf.at[slot], t_sems.at[slot]
                )
            )
            t_copies[-1].start()
        g_copy = pltpu.make_async_copy(gain_ref, g_buf, g_sem)
        g_copy.start()
    for group in copies:
        for copy in group:
            copy.start()
    if first:
        lanes = lax.broadcasted_iota(jnp.int32, (block, 128), 1)
        g_copy.wait()
        for slot in range(n):
            t_copies[slot].wait()
            wide = t_buf[slot].astype(jnp.float32)
            x_ref[slot * block : (slot + 1) * block, :] = (wide * g_buf[...]).astype(jnp.bfloat16)
            square = jnp.sum(wide * wide, axis=1, keepdims=True)
            high = square.astype(jnp.bfloat16).astype(jnp.float32)
            rest = square - high
            middle = rest.astype(jnp.bfloat16).astype(jnp.float32)
            low = rest - middle
            packed = jnp.where(
                lanes == 3 * me,
                high,
                jnp.where(lanes == 3 * me + 1, middle, jnp.where(lanes == 3 * me + 2, low, 0.0)),
            )
            if slot < n // 2:
                keep_ref[slot * block : (slot + 1) * block, width : width + 128] = packed
            else:
                at = (slot - n // 2) * block
                send_ref[at : at + block, width : width + 128] = packed.astype(jnp.bfloat16)

    for p, (start, end) in enumerate(((0, tile), (tile, width))):
        for copy in copies[p]:
            copy.wait()
        product = jnp.dot(x_ref[...], w_buf[:, start:end], preferred_element_type=jnp.float32)
        keep_ref[:, start:end] = product[:half]
        send_ref[:, start:end] = product[half:].astype(jnp.bfloat16)


def in_hbm(value):
    return pltpu.with_memory_space_constraint(value, pltpu.HBM)


def project(n, q_start, q_cols, kv_start, first, x, gain, w_query, w_key, w_value):
    rows, depth = x.shape
    kv = w_key.shape[1] // CHUNKS if kv_start is not None else 0
    width = q_cols + 2 * kv
    full = width + (128 if first else 0)
    hbm = pl.BlockSpec(memory_space=pltpu.HBM)
    vmem = pl.BlockSpec(memory_space=pltpu.VMEM)
    out_shape = [
        pltpu.VMEM((rows // 2, full), jnp.bfloat16),
        pltpu.VMEM((rows // 2, full), jnp.float32),
    ]
    scratch = [pltpu.VMEM((depth, width), jnp.bfloat16), pltpu.SemaphoreType.DMA((4,))]
    if first:
        out_shape.append(pltpu.VMEM((rows, depth), jnp.bfloat16))
        args = [in_hbm(x), in_hbm(gain)]
        in_specs = [hbm, hbm]
        scratch = [
            pltpu.VMEM((n, rows // n, depth), jnp.bfloat16),
            pltpu.SemaphoreType.DMA((n,)),
            pltpu.VMEM((1, depth), jnp.float32),
            pltpu.SemaphoreType.DMA,
        ] + scratch
    else:
        args, in_specs = [x], [vmem]
    return pl.pallas_call(
        functools.partial(project_kernel, n, q_start, kv_start, first),
        out_shape=out_shape,
        in_specs=in_specs + [hbm] * 3,
        out_specs=[vmem] * len(out_shape),
        scratch_shapes=scratch,
        compiler_params=pltpu.CompilerParams(vmem_limit_bytes=16 * MIB),
        name="project",
    )(*args, in_hbm(w_query), in_hbm(w_key), in_hbm(w_value))


def attend_kernel(chunk, offsets, kv_offset, groups, heads, seqs, length_ref, *refs):
    sum_ref, square_ref = refs[:2]
    w_copies = []
    if chunk == 0:
        cos_ref, sin_ref, k_ref, v_ref, w_ref, out_ref, next_ref, q_scr, o_scr, w_sems = refs[2:]
        total = next_ref.shape[0]
        for p in range(4):
            at = slice(p * total // 4, (p + 1) * total // 4)
            w_copies.append(
                pltpu.make_async_copy(
                    w_ref.at[total + at.start : total + at.stop], next_ref.at[at], w_sems.at[p]
                )
            )
            w_copies[-1].start()
    else:
        cos_ref, sin_ref, k_ref, v_ref, out_ref, q_scr, o_scr = refs[2:]
    rows = seqs * NEW
    cols = groups * heads * HD
    kv = groups * HD
    seq_count = k_ref.shape[0]

    scale = HD**-0.5 * math.log2(math.e)
    slots = k_ref.shape[1]
    many = heads * NEW
    slot_ids = lax.broadcasted_iota(jnp.int32, (1, slots), 1)
    new_cols = lax.broadcasted_iota(jnp.int32, (many, rows), 1)
    new_rows = lax.broadcasted_iota(jnp.int32, (many, rows), 0) % NEW

    @pl.loop(0, seq_count // seqs)
    def _(step):
        mine = pl.ds(pl.multiple_of(step * rows, rows), rows)
        mean = jnp.sum(square_ref[mine, :], axis=1, keepdims=True) / D
        row_scale = lax.rsqrt(mean + EPS)
        cosine, sine = cos_ref[mine, :], sin_ref[mine, :]

        def raw(start):
            return sum_ref[mine, start : start + HD] * row_scale

        def rotary(value):
            return value * cosine + pltpu.roll(value, HD // 2, 1) * sine

        for h in range(heads * groups):
            turned = rotary(raw(offsets[h]))
            for s in range(seqs):
                q_scr[s, h * NEW : (h + 1) * NEW, :] = turned[s * NEW : (s + 1) * NEW]
        for g in range(groups):
            new_keys = rotary(raw(kv_offset + g * HD)).astype(jnp.bfloat16)
            new_values = raw(kv_offset + (groups + g) * HD).astype(jnp.bfloat16)
            lanes = slice(chunk * kv + g * HD, chunk * kv + (g + 1) * HD)
            olds, news, mixes = [], [], []
            for s in range(seqs):
                query = q_scr[s, g * many : (g + 1) * many, :].astype(jnp.bfloat16)
                keys = k_ref[step * seqs + s, :, lanes]
                olds.append(
                    lax.dot_general(
                        query, keys, (((1,), (1,)), ((), ())), preferred_element_type=jnp.float32
                    )
                )
                news.append(
                    lax.dot_general(
                        query, new_keys, (((1,), (1,)), ((), ())), preferred_element_type=jnp.float32
                    )
                )
            for s in range(seqs):
                live = slot_ids < length_ref[step * seqs + s]
                seen = (new_cols >= s * NEW) & (new_cols <= s * NEW + new_rows)
                old = jnp.where(live, olds[s] * scale, -1e30)
                new = jnp.where(seen, news[s] * scale, -1e30)
                top = jnp.maximum(
                    jnp.max(old, axis=1, keepdims=True), jnp.max(new, axis=1, keepdims=True)
                )
                old = jnp.exp2(old - top)
                new = jnp.exp2(new - top)
                total = jnp.sum(old, axis=1, keepdims=True) + jnp.sum(new, axis=1, keepdims=True)
                inverse = 1.0 / total
                olds[s] = (old * inverse).astype(jnp.bfloat16)
                news[s] = (new * inverse).astype(jnp.bfloat16)
            for s in range(seqs):
                values = v_ref[step * seqs + s, :, lanes]
                mixes.append(
                    jnp.dot(olds[s], values, preferred_element_type=jnp.float32)
                    + jnp.dot(news[s], new_values, preferred_element_type=jnp.float32)
                )
            for s in range(seqs):
                for h in range(heads):
                    at = (g * heads + h) * HD
                    o_scr[s * NEW : (s + 1) * NEW, at : at + HD] = mixes[s][
                        h * NEW : (h + 1) * NEW
                    ]
        out_ref[mine, :] = o_scr[...].astype(jnp.bfloat16)

    for copy in w_copies:
        copy.wait()


def attend(chunk, offsets, kv_offset, sums, squares, cosine, sine, cache_keys, cache_values, lengths, w_out):
    seq_count, slots, kv_all = cache_keys.shape
    kv = kv_all // CHUNKS
    groups = kv // HD
    heads = len(offsets) // groups
    cols = len(offsets) * HD
    seqs = min(4, seq_count)
    rows = seq_count * NEW
    source, copied = [], []
    if chunk == 0:
        source.append(in_hbm(w_out))
        copied.append(pltpu.VMEM((w_out.shape[0] // CHUNKS, w_out.shape[1]), w_out.dtype))
    vmem = pl.BlockSpec(memory_space=pltpu.VMEM)
    hbm = pl.BlockSpec(memory_space=pltpu.HBM)
    return pl.pallas_call(
        functools.partial(attend_kernel, chunk, offsets, kv_offset, groups, heads, seqs),
        out_shape=[pltpu.VMEM((rows, cols), jnp.bfloat16)] + copied,
        in_specs=[pl.BlockSpec(memory_space=pltpu.SMEM)] + [vmem] * 6 + [hbm] * len(source),
        out_specs=[vmem] * (1 + len(copied)),
        scratch_shapes=[
            pltpu.VMEM((seqs, groups * heads * NEW, HD), jnp.float32),
            pltpu.VMEM((seqs * NEW, cols), jnp.float32),
        ]
        + [pltpu.SemaphoreType.DMA((4,))] * len(copied),
        compiler_params=pltpu.CompilerParams(vmem_limit_bytes=16 * MIB),
        name="attend",
    )(lengths, sums, squares, cosine, sine, cache_keys, cache_values, *source)


def fetch_kernel(count, pieces, *refs):
    sources, targets, sems = refs[:count], refs[count : 2 * count], refs[2 * count]
    copies = []
    for i, (source, target) in enumerate(zip(sources, targets)):
        size = target.shape[0] // pieces
        for p in range(pieces):
            at = slice(p * size, (p + 1) * size)
            copies.append(
                pltpu.make_async_copy(source.at[at], target.at[at], sems.at[i * pieces + p])
            )
    for copy in copies:
        copy.start()
    for copy in copies:
        copy.wait()


def fetch(*arrays):
    pieces = 4
    return pl.pallas_call(
        functools.partial(fetch_kernel, len(arrays), pieces),
        out_shape=[pltpu.VMEM(array.shape, array.dtype) for array in arrays],
        in_specs=[pl.BlockSpec(memory_space=pltpu.HBM)] * len(arrays),
        out_specs=[pl.BlockSpec(memory_space=pltpu.VMEM)] * len(arrays),
        scratch_shapes=[pltpu.SemaphoreType.DMA((pieces * len(arrays),))],
        compiler_params=pltpu.CompilerParams(vmem_limit_bytes=4 * MIB),
        name="fetch",
    )(*[in_hbm(array) for array in arrays])


def fetch_rows_kernel(start, pieces, source, target, sems):
    size = target.shape[0] // pieces
    copies = [
        pltpu.make_async_copy(
            source.at[start + p * size : start + (p + 1) * size],
            target.at[p * size : (p + 1) * size],
            sems.at[p],
        )
        for p in range(pieces)
    ]
    for copy in copies:
        copy.start()
    for copy in copies:
        copy.wait()


def fetch_rows(array, start, rows):
    pieces = 4
    return pl.pallas_call(
        functools.partial(fetch_rows_kernel, start, pieces),
        out_shape=pltpu.VMEM((rows, array.shape[1]), array.dtype),
        in_specs=[pl.BlockSpec(memory_space=pltpu.HBM)],
        out_specs=pl.BlockSpec(memory_space=pltpu.VMEM),
        scratch_shapes=[pltpu.SemaphoreType.DMA((pieces,))],
        compiler_params=pltpu.CompilerParams(vmem_limit_bytes=4 * MIB),
        name="fetch_rows",
    )(in_hbm(array))


def combine_kernel(n, block, chunk, *refs):
    pieces, refs = refs[:n], refs[n:]
    gx, gy = lax.axis_index("gx"), lax.axis_index("gy")
    moved = jnp.where(gy == 0, n // 2, 0)
    if chunk:
        before_ref, refs = refs[0], refs[1:]
    w_ref, outs, (x_buf, x_sems) = refs[0], refs[1:-2], refs[-2:]
    depth, cols = x_buf.shape[1], w_ref.shape[1]
    half = x_buf.shape[0] // 2
    x_copies = []
    for slot, piece in enumerate(pieces):
        start = pl.multiple_of((slot_owner(n, slot, gx, gy, gather_orders(n, chunk)) ^ moved) * block, block)
        x_copies.append(
            pltpu.make_async_copy(piece, x_buf.at[pl.ds(start, block), :], x_sems.at[slot])
        )
    for copy in x_copies:
        copy.start()
    for copy in x_copies:
        copy.wait()

    tile = cols // TILES
    for start in range(0, cols, tile):
        at = slice(start, start + tile)
        product = jnp.dot(x_buf[...], w_ref[:, at], preferred_element_type=jnp.float32)
        if chunk:
            product = product + before_ref[:, at]
        if len(outs) == 1:
            outs[0][:, at] = product
        else:
            outs[0][:, at] = product[:half].astype(jnp.bfloat16)
            outs[1][:, at] = product[half:]


def combine(chunk, pieces, before, w_out):
    n, (block, depth) = len(pieces), pieces[0].shape
    rows = n * block
    cols = w_out.shape[1]
    last = chunk == CHUNKS - 1
    hbm = pl.BlockSpec(memory_space=pltpu.HBM)
    vmem = pl.BlockSpec(memory_space=pltpu.VMEM)
    if last:
        out_shape = [
            pltpu.VMEM((rows // 2, cols), jnp.bfloat16),
            pltpu.VMEM((rows // 2, cols), jnp.float32),
        ]
    else:
        out_shape = [pltpu.VMEM((rows, cols), jnp.float32)]
    earlier = [] if chunk == 0 else [before]
    return pl.pallas_call(
        functools.partial(combine_kernel, n, block, chunk),
        out_shape=out_shape,
        in_specs=[pl.BlockSpec(memory_space=pl.ANY)] * len(pieces)
        + [vmem] * len(earlier)
        + [vmem],
        out_specs=[vmem] * len(out_shape),
        scratch_shapes=[
            pltpu.VMEM((rows, depth), jnp.bfloat16),
            pltpu.SemaphoreType.DMA((n,)),
        ],
        compiler_params=pltpu.CompilerParams(vmem_limit_bytes=16 * MIB),
        name="combine",
    )(*pieces, *earlier, w_out)


def shards(
    tokens, norm_gain, w_query, w_key, w_value, w_out, cache_keys, cache_values, cache_lengths
):
    n = lax.axis_size("gx")
    cores = lax.axis_size("gy")
    levels = n.bit_length() - 1
    position = (cache_lengths[:, None] + jnp.arange(NEW, dtype=jnp.int32)[None, :]).reshape(-1)
    inverse = THETA ** (-2.0 * jnp.arange(HD // 2, dtype=jnp.float32) / HD)
    angles = position.astype(jnp.float32)[:, None] * inverse[None, :]
    cosine, sine = jnp.cos(angles), jnp.sin(angles)
    cosine = jnp.concatenate([cosine, cosine], axis=1)
    sine = jnp.concatenate([-sine, sine], axis=1)

    x, gain = tokens, norm_gain[None, :]
    kv = w_key.shape[1] // CHUNKS
    q_cols = w_query.shape[1] // CHUNKS

    def column_part(start, size, kv_start):
        return project(
            n, start, size, kv_start, start == 0, x, gain, w_query, w_key, w_value
        )

    def after(value, *earlier):
        return lax.optimization_barrier((value, earlier))[0]

    share = q_cols // 2
    orders = bit_orders(n)
    send_a, keep_a, x = column_part(0, share, None)
    x = after(x, send_a)
    other_a = exchange(send_a, n, cores, 0, orders)
    send_b, keep_b = column_part(share, share, 0)
    x = after(x, send_b)
    other_b = exchange(send_b, n, cores, 0, orders)
    sum_a = keep_a + other_a.astype(jnp.float32)
    x = after(x, sum_a)
    later = []
    for chunk in range(1, CHUNKS):
        later.append(column_part(chunk * q_cols, q_cols, chunk * kv))
    other_b = after(other_b, *(send_c for send_c, _ in later))
    first = jnp.concatenate([sum_a, keep_b + other_b.astype(jnp.float32)], axis=1)
    half = first.shape[0] // 2
    send = first[half:].astype(jnp.bfloat16)
    flows = [[1, first[:half], send]]
    for send_c, keep_c in later:
        flows.append([0, keep_c, after(send_c, flows[-1][2])])

    def start(flow):
        return exchange(flow[2], n, cores, flow[0], orders)

    def finish(flow, other, *earlier):
        stage, keep, _ = flow
        if earlier:
            other = after(other, *earlier)
        value = keep + other.astype(jnp.float32)
        low = value.shape[0] // 2 if stage < levels - 1 else 0
        flow[:] = stage + 1, value[:low] if low else value, value[low:].astype(jnp.bfloat16)

    lead, follow = flows
    w_rows = w_out.shape[0] // CHUNKS
    weights = [fetch_rows(after(w_out, lead[2], follow[2]), 0, w_rows)]
    while follow[0] < levels:
        pending = [start(flow) for flow in flows if flow[0] < levels]
        if lead[0] == levels:
            finish(follow, pending[0])
        elif lead[0] == levels - 1:
            cache_keys, cache_values = fetch(*after((cache_keys, cache_values), follow[2]))
            finish(lead, pending[0], cache_keys, cache_values)
            finish(follow, pending[1], lead[1])
        else:
            finish(lead, pending[0], *weights)
            finish(follow, pending[1], lead[2])
    sums = [flow[1] for flow in flows]
    squares = sums[0][:, share : share + 128]
    plain = [h * HD for h in range(q_cols // HD)]
    offsets = [[at if at < share else at + 128 for at in plain], plain]
    kv_offsets = [q_cols + 128, q_cols]

    attentions = []
    for chunk in range(CHUNKS):
        out = attend(
            chunk,
            offsets[chunk],
            kv_offsets[chunk],
            sums[chunk],
            squares,
            cosine,
            sine,
            cache_keys,
            cache_values,
            cache_lengths,
            w_out,
        )
        attentions.append(out[0])
        weights += out[1:]
    gathered = []
    for chunk in range(CHUNKS):
        slots = [attentions[chunk]]
        for slot in range(1, n):
            top = slot.bit_length() - 1
            source = slots[slot - (1 << top)]
            if slot == 1 and chunk == 0:
                source = after(source, sums[1])
            if chunk == 1 and slot == 3 << (levels - 2):
                source = after(source, slots[1 << (levels - 1)])
            slots.append(
                exchange(source, n, cores, levels - 1 - top, gather_orders(n, chunk))
            )
        gathered.append(slots)
    result = None
    for chunk in range(CHUNKS):
        result = combine(chunk, gathered[chunk], result and result[0], weights[chunk])
    send, keep = result
    other = lax.ppermute(send, "gy", [(0, 1), (1, 0)])
    return (keep + other.astype(jnp.float32)).astype(jnp.bfloat16)


def solution(mesh):
    return jax.shard_map(
        shards,
        mesh=mesh,
        in_specs=(
            P("groups", "gx"),
            P("gx"),
            P("gx", "gy"),
            P("gx", "gy"),
            P("gx", "gy"),
            P("gy", "gx"),
            P(("groups", "gx"), None, "gy"),
            P(("groups", "gx"), None, "gy"),
            P(("groups", "gx")),
        ),
        out_specs=P(("groups", "gy"), "gx"),
        check_vma=False,
    )
```

```python
import functools
import math

import jax
import jax.numpy as jnp
from jax import lax
from jax.experimental import pallas as pl
from jax.experimental.pallas import tpu as pltpu
from jax.sharding import PartitionSpec as P

D = 16384
HD = 128
NEW = 4
EPS = 1e-05
THETA = 500000.0

CHUNKS = 2
TILES = 4
MIB = 1 << 20


def bit_orders(n):
    levels = n.bit_length() - 1
    first = list(range(levels))
    second = list(first)
    if levels > 1:
        second[0], second[1] = second[1], second[0]
    return first, second


def gather_orders(n, chunk):
    first, second = bit_orders(n)
    return (first, second) if chunk else (first, first)


def slot_shift(slot, order):
    levels = len(order)
    shift = 0
    for stage in range(levels):
        shift |= ((slot >> (levels - 1 - stage)) & 1) << order[stage]
    return shift


def slot_owner(n, slot, gx, gy, orders):
    first, second = (slot_shift(slot, order) for order in orders)
    return gx ^ jnp.where(gy == 0, first, second)


def exchange(value, n, cores, stage, orders):
    pairs = []
    for gx in range(n):
        for gy in range(cores):
            other = gx ^ (1 << orders[gy % 2][stage])
            pairs.append((gx * cores + gy, other * cores + gy))
    return lax.ppermute(value, ("gx", "gy"), pairs)


def project_kernel(n, q_start, kv_start, first, *refs):
    if first:
        tokens_ref, gain_ref, wq_ref, wk_ref, wv_ref, send_ref, keep_ref, x_ref = refs[:8]
        t_buf, t_sems, g_buf, g_sem = refs[8:12]
    else:
        x_ref, wq_ref, wk_ref, wv_ref, send_ref, keep_ref = refs[:6]
    w_buf, sems = refs[-2:]
    half = send_ref.shape[0]
    rows = 2 * half
    with_kv = kv_start is not None
    kv = wk_ref.shape[1] // CHUNKS if with_kv else 0
    width = w_buf.shape[1]
    cols = width - 2 * kv
    tile = cols // 2

    def w_copy(ref, start, size, at, sem):
        return pltpu.make_async_copy(
            ref.at[:, start : start + size], w_buf.at[:, at : at + size], sems.at[sem]
        )

    copies = [[w_copy(wq_ref, q_start + at, tile, at, at // tile)] for at in (0, tile)]
    if with_kv:
        copies[1].append(w_copy(wk_ref, kv_start, kv, cols, 2))
        copies[1].append(w_copy(wv_ref, kv_start, kv, cols + kv, 3))

    if first:
        block = rows // n
        me, gy = lax.axis_index("gx"), lax.axis_index("gy")
        t_copies = []
        for slot in range(n):
            start = pl.multiple_of(slot_owner(n, slot, me, gy, bit_orders(n)) * block, block)
            t_copies.append(
                pltpu.make_async_copy(
                    tokens_ref.at[pl.ds(start, block), :], t_buf.at[slot], t_sems.at[slot]
                )
            )
            t_copies[-1].start()
        g_copy = pltpu.make_async_copy(gain_ref, g_buf, g_sem)
        g_copy.start()
    for group in copies:
        for copy in group:
            copy.start()
    if first:
        lanes = lax.broadcasted_iota(jnp.int32, (block, 128), 1)
        g_copy.wait()
        for slot in range(n):
            t_copies[slot].wait()
            wide = t_buf[slot].astype(jnp.float32)
            x_ref[slot * block : (slot + 1) * block, :] = (wide * g_buf[...]).astype(jnp.bfloat16)
            square = jnp.sum(wide * wide, axis=1, keepdims=True)
            high = square.astype(jnp.bfloat16).astype(jnp.float32)
            rest = square - high
            middle = rest.astype(jnp.bfloat16).astype(jnp.float32)
            low = rest - middle
            packed = jnp.where(
                lanes == 3 * me,
                high,
                jnp.where(lanes == 3 * me + 1, middle, jnp.where(lanes == 3 * me + 2, low, 0.0)),
            )
            if slot < n // 2:
                keep_ref[slot * block : (slot + 1) * block, width : width + 128] = packed
            else:
                at = (slot - n // 2) * block
                send_ref[at : at + block, width : width + 128] = packed.astype(jnp.bfloat16)

    for p, (start, end) in enumerate(((0, tile), (tile, width))):
        for copy in copies[p]:
            copy.wait()
        product = jnp.dot(x_ref[...], w_buf[:, start:end], preferred_element_type=jnp.float32)
        keep_ref[:, start:end] = product[:half]
        send_ref[:, start:end] = product[half:].astype(jnp.bfloat16)


def in_hbm(value):
    return pltpu.with_memory_space_constraint(value, pltpu.HBM)


def project(n, q_start, q_cols, kv_start, first, x, gain, w_query, w_key, w_value):
    rows, depth = x.shape
    kv = w_key.shape[1] // CHUNKS if kv_start is not None else 0
    width = q_cols + 2 * kv
    full = width + (128 if first else 0)
    hbm = pl.BlockSpec(memory_space=pltpu.HBM)
    vmem = pl.BlockSpec(memory_space=pltpu.VMEM)
    out_shape = [
        pltpu.VMEM((rows // 2, full), jnp.bfloat16),
        pltpu.VMEM((rows // 2, full), jnp.float32),
    ]
    scratch = [pltpu.VMEM((depth, width), jnp.bfloat16), pltpu.SemaphoreType.DMA((4,))]
    if first:
        out_shape.append(pltpu.VMEM((rows, depth), jnp.bfloat16))
        args = [in_hbm(x), in_hbm(gain)]
        in_specs = [hbm, hbm]
        scratch = [
            pltpu.VMEM((n, rows // n, depth), jnp.bfloat16),
            pltpu.SemaphoreType.DMA((n,)),
            pltpu.VMEM((1, depth), jnp.float32),
            pltpu.SemaphoreType.DMA,
        ] + scratch
    else:
        args, in_specs = [x], [vmem]
    return pl.pallas_call(
        functools.partial(project_kernel, n, q_start, kv_start, first),
        out_shape=out_shape,
        in_specs=in_specs + [hbm] * 3,
        out_specs=[vmem] * len(out_shape),
        scratch_shapes=scratch,
        compiler_params=pltpu.CompilerParams(vmem_limit_bytes=16 * MIB),
        name="project",
    )(*args, in_hbm(w_query), in_hbm(w_key), in_hbm(w_value))


def attend_kernel(chunk, offsets, kv_offset, groups, heads, seqs, length_ref, *refs):
    sum_ref, square_ref = refs[:2]
    cos_ref, sin_ref, k_ref, v_ref, out_ref, q_scr, o_scr = refs[2:]
    rows = seqs * NEW
    cols = groups * heads * HD
    kv = groups * HD
    seq_count = k_ref.shape[0]

    scale = HD**-0.5 * math.log2(math.e)
    slots = k_ref.shape[1]
    many = heads * NEW
    slot_ids = lax.broadcasted_iota(jnp.int32, (1, slots), 1)
    new_cols = lax.broadcasted_iota(jnp.int32, (many, rows), 1)
    new_rows = lax.broadcasted_iota(jnp.int32, (many, rows), 0) % NEW

    @pl.loop(0, seq_count // seqs)
    def _(step):
        mine = pl.ds(pl.multiple_of(step * rows, rows), rows)
        mean = jnp.sum(square_ref[mine, :], axis=1, keepdims=True) / D
        row_scale = lax.rsqrt(mean + EPS)
        cosine, sine = cos_ref[mine, :], sin_ref[mine, :]

        def raw(start):
            return sum_ref[mine, start : start + HD] * row_scale

        def rotary(value):
            return value * cosine + pltpu.roll(value, HD // 2, 1) * sine

        for h in range(heads * groups):
            turned = rotary(raw(offsets[h]))
            for s in range(seqs):
                q_scr[s, h * NEW : (h + 1) * NEW, :] = turned[s * NEW : (s + 1) * NEW]
        for g in range(groups):
            new_keys = rotary(raw(kv_offset + g * HD)).astype(jnp.bfloat16)
            new_values = raw(kv_offset + (groups + g) * HD).astype(jnp.bfloat16)
            lanes = slice(chunk * kv + g * HD, chunk * kv + (g + 1) * HD)
            olds, news, mixes = [], [], []
            for s in range(seqs):
                query = q_scr[s, g * many : (g + 1) * many, :].astype(jnp.bfloat16)
                keys = k_ref[step * seqs + s, :, lanes]
                olds.append(
                    lax.dot_general(
                        query, keys, (((1,), (1,)), ((), ())), preferred_element_type=jnp.float32
                    )
                )
                news.append(
                    lax.dot_general(
                        query, new_keys, (((1,), (1,)), ((), ())), preferred_element_type=jnp.float32
                    )
                )
            for s in range(seqs):
                live = slot_ids < length_ref[step * seqs + s]
                seen = (new_cols >= s * NEW) & (new_cols <= s * NEW + new_rows)
                old = jnp.where(live, olds[s] * scale, -1e30)
                new = jnp.where(seen, news[s] * scale, -1e30)
                top = jnp.maximum(
                    jnp.max(old, axis=1, keepdims=True), jnp.max(new, axis=1, keepdims=True)
                )
                old = jnp.exp2(old - top)
                new = jnp.exp2(new - top)
                total = jnp.sum(old, axis=1, keepdims=True) + jnp.sum(new, axis=1, keepdims=True)
                inverse = 1.0 / total
                olds[s] = (old * inverse).astype(jnp.bfloat16)
                news[s] = (new * inverse).astype(jnp.bfloat16)
            for s in range(seqs):
                values = v_ref[step * seqs + s, :, lanes]
                mixes.append(
                    jnp.dot(olds[s], values, preferred_element_type=jnp.float32)
                    + jnp.dot(news[s], new_values, preferred_element_type=jnp.float32)
                )
            for s in range(seqs):
                for h in range(heads):
                    at = (g * heads + h) * HD
                    o_scr[s * NEW : (s + 1) * NEW, at : at + HD] = mixes[s][
                        h * NEW : (h + 1) * NEW
                    ]
        out_ref[mine, :] = o_scr[...].astype(jnp.bfloat16)


def attend(chunk, offsets, kv_offset, sums, squares, cosine, sine, cache_keys, cache_values, lengths):
    seq_count, slots, kv_all = cache_keys.shape
    kv = kv_all // CHUNKS
    groups = kv // HD
    heads = len(offsets) // groups
    cols = len(offsets) * HD
    seqs = min(4, seq_count)
    rows = seq_count * NEW
    vmem = pl.BlockSpec(memory_space=pltpu.VMEM)
    hbm = pl.BlockSpec(memory_space=pltpu.HBM)
    return pl.pallas_call(
        functools.partial(attend_kernel, chunk, offsets, kv_offset, groups, heads, seqs),
        out_shape=pltpu.VMEM((rows, cols), jnp.bfloat16),
        in_specs=[pl.BlockSpec(memory_space=pltpu.SMEM)] + [vmem] * 6,
        out_specs=vmem,
        scratch_shapes=[
            pltpu.VMEM((seqs, groups * heads * NEW, HD), jnp.float32),
            pltpu.VMEM((seqs * NEW, cols), jnp.float32),
        ],
        compiler_params=pltpu.CompilerParams(vmem_limit_bytes=16 * MIB),
        name="attend",
    )(lengths, sums, squares, cosine, sine, cache_keys, cache_values)


def fetch_kernel(count, pieces, *refs):
    sources, targets, sems = refs[:count], refs[count : 2 * count], refs[2 * count]
    copies = []
    for i, (source, target) in enumerate(zip(sources, targets)):
        size = target.shape[0] // pieces
        for p in range(pieces):
            at = slice(p * size, (p + 1) * size)
            copies.append(
                pltpu.make_async_copy(source.at[at], target.at[at], sems.at[i * pieces + p])
            )
    for copy in copies:
        copy.start()
    for copy in copies:
        copy.wait()


def fetch(*arrays):
    pieces = 4
    return pl.pallas_call(
        functools.partial(fetch_kernel, len(arrays), pieces),
        out_shape=[pltpu.VMEM(array.shape, array.dtype) for array in arrays],
        in_specs=[pl.BlockSpec(memory_space=pltpu.HBM)] * len(arrays),
        out_specs=[pl.BlockSpec(memory_space=pltpu.VMEM)] * len(arrays),
        scratch_shapes=[pltpu.SemaphoreType.DMA((pieces * len(arrays),))],
        compiler_params=pltpu.CompilerParams(vmem_limit_bytes=4 * MIB),
        name="fetch",
    )(*[in_hbm(array) for array in arrays])


def fetch_rows_kernel(start, pieces, source, target, sems):
    size = target.shape[0] // pieces
    copies = [
        pltpu.make_async_copy(
            source.at[start + p * size : start + (p + 1) * size],
            target.at[p * size : (p + 1) * size],
            sems.at[p],
        )
        for p in range(pieces)
    ]
    for copy in copies:
        copy.start()
    for copy in copies:
        copy.wait()


def fetch_rows(array, start, rows):
    pieces = 4
    return pl.pallas_call(
        functools.partial(fetch_rows_kernel, start, pieces),
        out_shape=pltpu.VMEM((rows, array.shape[1]), array.dtype),
        in_specs=[pl.BlockSpec(memory_space=pltpu.HBM)],
        out_specs=pl.BlockSpec(memory_space=pltpu.VMEM),
        scratch_shapes=[pltpu.SemaphoreType.DMA((pieces,))],
        compiler_params=pltpu.CompilerParams(vmem_limit_bytes=4 * MIB),
        name="fetch_rows",
    )(in_hbm(array))


def combine_kernel(n, block, chunk, *refs):
    pieces, refs = refs[:n], refs[n:]
    gx, gy = lax.axis_index("gx"), lax.axis_index("gy")
    moved = jnp.where(gy == 0, n // 2, 0)
    if chunk:
        before_ref, refs = refs[0], refs[1:]
    w_ref, outs, (x_buf, x_sems) = refs[0], refs[1:-2], refs[-2:]
    depth, cols = x_buf.shape[1], w_ref.shape[1]
    half = x_buf.shape[0] // 2
    x_copies = []
    for slot, piece in enumerate(pieces):
        start = pl.multiple_of((slot_owner(n, slot, gx, gy, gather_orders(n, chunk)) ^ moved) * block, block)
        x_copies.append(
            pltpu.make_async_copy(piece, x_buf.at[pl.ds(start, block), :], x_sems.at[slot])
        )
    for copy in x_copies:
        copy.start()
    for copy in x_copies:
        copy.wait()

    tile = cols // TILES
    for start in range(0, cols, tile):
        at = slice(start, start + tile)
        product = jnp.dot(x_buf[...], w_ref[:, at], preferred_element_type=jnp.float32)
        if chunk:
            product = product + before_ref[:, at]
        if len(outs) == 1:
            outs[0][:, at] = product
        else:
            outs[0][:, at] = product[:half].astype(jnp.bfloat16)
            outs[1][:, at] = product[half:]


def combine(chunk, pieces, before, w_out):
    n, (block, depth) = len(pieces), pieces[0].shape
    rows = n * block
    cols = w_out.shape[1]
    last = chunk == CHUNKS - 1
    hbm = pl.BlockSpec(memory_space=pltpu.HBM)
    vmem = pl.BlockSpec(memory_space=pltpu.VMEM)
    if last:
        out_shape = [
            pltpu.VMEM((rows // 2, cols), jnp.bfloat16),
            pltpu.VMEM((rows // 2, cols), jnp.float32),
        ]
    else:
        out_shape = [pltpu.VMEM((rows, cols), jnp.float32)]
    earlier = [] if chunk == 0 else [before]
    return pl.pallas_call(
        functools.partial(combine_kernel, n, block, chunk),
        out_shape=out_shape,
        in_specs=[pl.BlockSpec(memory_space=pl.ANY)] * len(pieces)
        + [vmem] * len(earlier)
        + [vmem],
        out_specs=[vmem] * len(out_shape),
        scratch_shapes=[
            pltpu.VMEM((rows, depth), jnp.bfloat16),
            pltpu.SemaphoreType.DMA((n,)),
        ],
        compiler_params=pltpu.CompilerParams(vmem_limit_bytes=16 * MIB),
        name="combine",
    )(*pieces, *earlier, w_out)


def shards(
    tokens, norm_gain, w_query, w_key, w_value, w_out, cache_keys, cache_values, cache_lengths
):
    n = lax.axis_size("gx")
    cores = lax.axis_size("gy")
    levels = n.bit_length() - 1
    position = (cache_lengths[:, None] + jnp.arange(NEW, dtype=jnp.int32)[None, :]).reshape(-1)
    inverse = THETA ** (-2.0 * jnp.arange(HD // 2, dtype=jnp.float32) / HD)
    angles = position.astype(jnp.float32)[:, None] * inverse[None, :]
    cosine, sine = jnp.cos(angles), jnp.sin(angles)
    cosine = jnp.concatenate([cosine, cosine], axis=1)
    sine = jnp.concatenate([-sine, sine], axis=1)

    x, gain = tokens, norm_gain[None, :]
    kv = w_key.shape[1] // CHUNKS
    q_cols = w_query.shape[1] // CHUNKS

    def column_part(start, size, kv_start):
        return project(
            n, start, size, kv_start, start == 0, x, gain, w_query, w_key, w_value
        )

    def after(value, *earlier):
        return lax.optimization_barrier((value, earlier))[0]

    share = q_cols // 2
    orders = bit_orders(n)

    def start(stage, send):
        return exchange(send, n, cores, stage, orders)

    def added(stage, keep, other):
        value = keep + other.astype(jnp.float32)
        low = value.shape[0] // 2 if stage < levels - 1 else 0
        return value[low:].astype(jnp.bfloat16), value[:low] if low else value

    send_a, keep_a, x = column_part(0, share, None)
    x = after(x, send_a)
    other_a = start(0, send_a)
    send_b, keep_b = column_part(share, share, 0)
    x = after(x, send_b)
    other_b = start(0, send_b)
    sum_a = keep_a + other_a.astype(jnp.float32)
    x = after(x, sum_a)
    send_c, keep_c = column_part(q_cols, share, None)
    other_b = after(other_b, send_c)
    first = jnp.concatenate([sum_a, keep_b + other_b.astype(jnp.float32)], axis=1)
    half = first.shape[0] // 2
    send, keep = first[half:].astype(jnp.bfloat16), first[:half]
    x = after(x, send, send_c)
    send_d, keep_d = column_part(q_cols + share, share, kv)

    other = after(start(1, send), send_d)
    send, keep = added(1, keep, other)
    send_1 = after(jnp.concatenate([send_c, send_d], axis=1), send)
    keep_1 = jnp.concatenate([keep_c, keep_d], axis=1)
    other_1 = start(0, send_1)
    w_rows = w_out.shape[0] // CHUNKS
    w_first = fetch_rows(after(w_out, send_1), 0, w_rows)
    cache_keys, cache_values = fetch(*after((cache_keys, cache_values), w_first))
    for stage in range(2, levels):
        other = start(stage, send)
        if stage == 2:
            other = after(other, cache_keys, cache_values)
        send, keep = added(stage, keep, other)
    sum_0 = keep
    other_1 = after(other_1, sum_0)
    send_1, keep_1 = added(0, keep_1, other_1)
    sum_0 = after(sum_0, send_1)
    squares = sum_0[:, share : share + 128]
    plain = [h * HD for h in range(q_cols // HD)]
    offsets = [[at if at < share else at + 128 for at in plain], plain]
    kv_offsets = [q_cols + 128, q_cols]

    def attended(chunk, total):
        return attend(
            chunk,
            offsets[chunk],
            kv_offsets[chunk],
            total,
            squares,
            cosine,
            sine,
            cache_keys,
            cache_values,
            cache_lengths,
        )

    attentions = [attended(0, sum_0)]
    other_1 = after(start(1, send_1), attentions[0])
    send_1, keep_1 = added(1, keep_1, other_1)
    w_second = fetch_rows(after(w_out, send_1), w_rows, w_rows)
    for stage in range(2, levels):
        other_1 = start(stage, send_1)
        if stage == 2:
            other_1 = after(other_1, w_second)
        send_1, keep_1 = added(stage, keep_1, other_1)
    sums = [sum_0, keep_1]
    weights = [w_first, w_second]
    attentions.append(attended(1, sums[1]))
    gathered = []
    for chunk in range(CHUNKS):
        slots = [attentions[chunk]]
        for slot in range(1, n):
            top = slot.bit_length() - 1
            source = slots[slot - (1 << top)]
            if slot == 1 and chunk == 0:
                source = after(source, sums[1])
            slots.append(
                exchange(source, n, cores, levels - 1 - top, gather_orders(n, chunk))
            )
        gathered.append(slots)
    result = None
    for chunk in range(CHUNKS):
        result = combine(chunk, gathered[chunk], result and result[0], weights[chunk])
    send, keep = result
    other = lax.ppermute(send, "gy", [(0, 1), (1, 0)])
    return (keep + other.astype(jnp.float32)).astype(jnp.bfloat16)


def solution(mesh):
    return jax.shard_map(
        shards,
        mesh=mesh,
        in_specs=(
            P("groups", "gx"),
            P("gx"),
            P("gx", "gy"),
            P("gx", "gy"),
            P("gx", "gy"),
            P("gy", "gx"),
            P(("groups", "gx"), None, "gy"),
            P(("groups", "gx"), None, "gy"),
            P(("groups", "gx")),
        ),
        out_specs=P(("groups", "gy"), "gx"),
        check_vma=False,
    )
```

```python
import functools
import math

import jax
import jax.numpy as jnp
from jax import lax
from jax.experimental import pallas as pl
from jax.experimental.pallas import tpu as pltpu
from jax.sharding import PartitionSpec as P

D = 16384
HD = 128
NEW = 4
EPS = 1e-05
THETA = 500000.0

CHUNKS = 2
TILES = 4
MIB = 1 << 20


def bit_orders(n):
    levels = n.bit_length() - 1
    first = list(range(levels))
    second = list(first)
    if levels > 1:
        second[0], second[1] = second[1], second[0]
    return first, second


def gather_orders(n, chunk):
    first, second = bit_orders(n)
    return (first, second) if chunk else (first, first)


def slot_shift(slot, order):
    levels = len(order)
    shift = 0
    for stage in range(levels):
        shift |= ((slot >> (levels - 1 - stage)) & 1) << order[stage]
    return shift


def slot_owner(n, slot, gx, gy, orders):
    first, second = (slot_shift(slot, order) for order in orders)
    return gx ^ jnp.where(gy == 0, first, second)


def exchange(value, n, cores, stage, orders):
    pairs = []
    for gx in range(n):
        for gy in range(cores):
            other = gx ^ (1 << orders[gy % 2][stage])
            pairs.append((gx * cores + gy, other * cores + gy))
    return lax.ppermute(value, ("gx", "gy"), pairs)


def project_kernel(n, q_start, kv_start, first, *refs):
    if first:
        tokens_ref, gain_ref, wq_ref, wk_ref, wv_ref, send_ref, keep_ref, x_ref = refs[:8]
        t_buf, t_sems, g_buf, g_sem = refs[8:12]
    else:
        x_ref, wq_ref, wk_ref, wv_ref, send_ref, keep_ref = refs[:6]
    w_buf, sems = refs[-2:]
    half = send_ref.shape[0]
    rows = 2 * half
    with_kv = kv_start is not None
    kv = wk_ref.shape[1] // CHUNKS if with_kv else 0
    width = w_buf.shape[1]
    cols = width - 2 * kv
    tile = cols // 2

    def w_copy(ref, start, size, at, sem):
        return pltpu.make_async_copy(
            ref.at[:, start : start + size], w_buf.at[:, at : at + size], sems.at[sem]
        )

    copies = [[w_copy(wq_ref, q_start + at, tile, at, at // tile)] for at in (0, tile)]
    if with_kv:
        copies[1].append(w_copy(wk_ref, kv_start, kv, cols, 2))
        copies[1].append(w_copy(wv_ref, kv_start, kv, cols + kv, 3))

    if first:
        block = rows // n
        me, gy = lax.axis_index("gx"), lax.axis_index("gy")
        t_copies = []
        for slot in range(n):
            start = pl.multiple_of(slot_owner(n, slot, me, gy, bit_orders(n)) * block, block)
            t_copies.append(
                pltpu.make_async_copy(
                    tokens_ref.at[pl.ds(start, block), :], t_buf.at[slot], t_sems.at[slot]
                )
            )
            t_copies[-1].start()
        g_copy = pltpu.make_async_copy(gain_ref, g_buf, g_sem)
        g_copy.start()
    for group in copies:
        for copy in group:
            copy.start()
    if first:
        lanes = lax.broadcasted_iota(jnp.int32, (block, 128), 1)
        g_copy.wait()
        for slot in range(n):
            t_copies[slot].wait()
            wide = t_buf[slot].astype(jnp.float32)
            x_ref[slot * block : (slot + 1) * block, :] = (wide * g_buf[...]).astype(jnp.bfloat16)
            square = jnp.sum(wide * wide, axis=1, keepdims=True)
            high = square.astype(jnp.bfloat16).astype(jnp.float32)
            rest = square - high
            middle = rest.astype(jnp.bfloat16).astype(jnp.float32)
            low = rest - middle
            packed = jnp.where(
                lanes == 3 * me,
                high,
                jnp.where(lanes == 3 * me + 1, middle, jnp.where(lanes == 3 * me + 2, low, 0.0)),
            )
            if slot < n // 2:
                keep_ref[slot * block : (slot + 1) * block, width : width + 128] = packed
            else:
                at = (slot - n // 2) * block
                send_ref[at : at + block, width : width + 128] = packed.astype(jnp.bfloat16)

    for p, (start, end) in enumerate(((0, tile), (tile, width))):
        for copy in copies[p]:
            copy.wait()
        product = jnp.dot(x_ref[...], w_buf[:, start:end], preferred_element_type=jnp.float32)
        keep_ref[:, start:end] = product[:half]
        send_ref[:, start:end] = product[half:].astype(jnp.bfloat16)


def in_hbm(value):
    return pltpu.with_memory_space_constraint(value, pltpu.HBM)


def project(n, q_start, q_cols, kv_start, first, x, gain, w_query, w_key, w_value):
    rows, depth = x.shape
    kv = w_key.shape[1] // CHUNKS if kv_start is not None else 0
    width = q_cols + 2 * kv
    full = width + (128 if first else 0)
    hbm = pl.BlockSpec(memory_space=pltpu.HBM)
    vmem = pl.BlockSpec(memory_space=pltpu.VMEM)
    out_shape = [
        pltpu.VMEM((rows // 2, full), jnp.bfloat16),
        pltpu.VMEM((rows // 2, full), jnp.float32),
    ]
    scratch = [pltpu.VMEM((depth, width), jnp.bfloat16), pltpu.SemaphoreType.DMA((4,))]
    if first:
        out_shape.append(pltpu.VMEM((rows, depth), jnp.bfloat16))
        args = [in_hbm(x), in_hbm(gain)]
        in_specs = [hbm, hbm]
        scratch = [
            pltpu.VMEM((n, rows // n, depth), jnp.bfloat16),
            pltpu.SemaphoreType.DMA((n,)),
            pltpu.VMEM((1, depth), jnp.float32),
            pltpu.SemaphoreType.DMA,
        ] + scratch
    else:
        args, in_specs = [x], [vmem]
    return pl.pallas_call(
        functools.partial(project_kernel, n, q_start, kv_start, first),
        out_shape=out_shape,
        in_specs=in_specs + [hbm] * 3,
        out_specs=[vmem] * len(out_shape),
        scratch_shapes=scratch,
        compiler_params=pltpu.CompilerParams(vmem_limit_bytes=16 * MIB),
        name="project",
    )(*args, in_hbm(w_query), in_hbm(w_key), in_hbm(w_value))


def attend_kernel(chunk, offsets, kv_offset, groups, heads, seqs, length_ref, *refs):
    sum_ref, square_ref = refs[:2]
    w_copies = []
    if chunk == 0:
        cos_ref, sin_ref, k_ref, v_ref, w_ref, out_ref, next_ref, q_scr, o_scr, w_sems = refs[2:]
        total = next_ref.shape[0]
        for p in range(4):
            at = slice(p * total // 4, (p + 1) * total // 4)
            w_copies.append(
                pltpu.make_async_copy(
                    w_ref.at[total + at.start : total + at.stop], next_ref.at[at], w_sems.at[p]
                )
            )
            w_copies[-1].start()
    else:
        cos_ref, sin_ref, k_ref, v_ref, out_ref, q_scr, o_scr = refs[2:]
    rows = seqs * NEW
    cols = groups * heads * HD
    kv = groups * HD
    seq_count = k_ref.shape[0]

    scale = HD**-0.5 * math.log2(math.e)
    slots = k_ref.shape[1]
    many = heads * NEW
    slot_ids = lax.broadcasted_iota(jnp.int32, (1, slots), 1)
    new_cols = lax.broadcasted_iota(jnp.int32, (many, rows), 1)
    new_rows = lax.broadcasted_iota(jnp.int32, (many, rows), 0) % NEW

    @pl.loop(0, seq_count // seqs)
    def _(step):
        mine = pl.ds(pl.multiple_of(step * rows, rows), rows)
        mean = jnp.sum(square_ref[mine, :], axis=1, keepdims=True) / D
        row_scale = lax.rsqrt(mean + EPS)
        cosine, sine = cos_ref[mine, :], sin_ref[mine, :]

        def raw(start):
            return sum_ref[mine, start : start + HD] * row_scale

        def rotary(value):
            return value * cosine + pltpu.roll(value, HD // 2, 1) * sine

        for h in range(heads * groups):
            turned = rotary(raw(offsets[h]))
            for s in range(seqs):
                q_scr[s, h * NEW : (h + 1) * NEW, :] = turned[s * NEW : (s + 1) * NEW]
        for g in range(groups):
            new_keys = rotary(raw(kv_offset + g * HD)).astype(jnp.bfloat16)
            new_values = raw(kv_offset + (groups + g) * HD).astype(jnp.bfloat16)
            lanes = slice(chunk * kv + g * HD, chunk * kv + (g + 1) * HD)
            olds, news, mixes = [], [], []
            for s in range(seqs):
                query = q_scr[s, g * many : (g + 1) * many, :].astype(jnp.bfloat16)
                keys = k_ref[step * seqs + s, :, lanes]
                olds.append(
                    lax.dot_general(
                        query, keys, (((1,), (1,)), ((), ())), preferred_element_type=jnp.float32
                    )
                )
                news.append(
                    lax.dot_general(
                        query, new_keys, (((1,), (1,)), ((), ())), preferred_element_type=jnp.float32
                    )
                )
            for s in range(seqs):
                live = slot_ids < length_ref[step * seqs + s]
                seen = (new_cols >= s * NEW) & (new_cols <= s * NEW + new_rows)
                old = jnp.where(live, olds[s] * scale, -1e30)
                new = jnp.where(seen, news[s] * scale, -1e30)
                top = jnp.maximum(
                    jnp.max(old, axis=1, keepdims=True), jnp.max(new, axis=1, keepdims=True)
                )
                old = jnp.exp2(old - top)
                new = jnp.exp2(new - top)
                total = jnp.sum(old, axis=1, keepdims=True) + jnp.sum(new, axis=1, keepdims=True)
                inverse = 1.0 / total
                olds[s] = (old * inverse).astype(jnp.bfloat16)
                news[s] = (new * inverse).astype(jnp.bfloat16)
            for s in range(seqs):
                values = v_ref[step * seqs + s, :, lanes]
                mixes.append(
                    jnp.dot(olds[s], values, preferred_element_type=jnp.float32)
                    + jnp.dot(news[s], new_values, preferred_element_type=jnp.float32)
                )
            for s in range(seqs):
                for h in range(heads):
                    at = (g * heads + h) * HD
                    o_scr[s * NEW : (s + 1) * NEW, at : at + HD] = mixes[s][
                        h * NEW : (h + 1) * NEW
                    ]
        out_ref[mine, :] = o_scr[...].astype(jnp.bfloat16)

    for copy in w_copies:
        copy.wait()


def attend(chunk, offsets, kv_offset, sums, squares, cosine, sine, cache_keys, cache_values, lengths, w_out):
    seq_count, slots, kv_all = cache_keys.shape
    kv = kv_all // CHUNKS
    groups = kv // HD
    heads = len(offsets) // groups
    cols = len(offsets) * HD
    seqs = min(4, seq_count)
    rows = seq_count * NEW
    source, copied = [], []
    if chunk == 0:
        source.append(in_hbm(w_out))
        copied.append(pltpu.VMEM((w_out.shape[0] // CHUNKS, w_out.shape[1]), w_out.dtype))
    vmem = pl.BlockSpec(memory_space=pltpu.VMEM)
    hbm = pl.BlockSpec(memory_space=pltpu.HBM)
    return pl.pallas_call(
        functools.partial(attend_kernel, chunk, offsets, kv_offset, groups, heads, seqs),
        out_shape=[pltpu.VMEM((rows, cols), jnp.bfloat16)] + copied,
        in_specs=[pl.BlockSpec(memory_space=pltpu.SMEM)] + [vmem] * 6 + [hbm] * len(source),
        out_specs=[vmem] * (1 + len(copied)),
        scratch_shapes=[
            pltpu.VMEM((seqs, groups * heads * NEW, HD), jnp.float32),
            pltpu.VMEM((seqs * NEW, cols), jnp.float32),
        ]
        + [pltpu.SemaphoreType.DMA((4,))] * len(copied),
        compiler_params=pltpu.CompilerParams(vmem_limit_bytes=16 * MIB),
        name="attend",
    )(lengths, sums, squares, cosine, sine, cache_keys, cache_values, *source)


def fetch_kernel(count, pieces, *refs):
    sources, targets, sems = refs[:count], refs[count : 2 * count], refs[2 * count]
    copies = []
    for i, (source, target) in enumerate(zip(sources, targets)):
        size = target.shape[0] // pieces
        for p in range(pieces):
            at = slice(p * size, (p + 1) * size)
            copies.append(
                pltpu.make_async_copy(source.at[at], target.at[at], sems.at[i * pieces + p])
            )
    for copy in copies:
        copy.start()
    for copy in copies:
        copy.wait()


def fetch(*arrays):
    pieces = 4
    return pl.pallas_call(
        functools.partial(fetch_kernel, len(arrays), pieces),
        out_shape=[pltpu.VMEM(array.shape, array.dtype) for array in arrays],
        in_specs=[pl.BlockSpec(memory_space=pltpu.HBM)] * len(arrays),
        out_specs=[pl.BlockSpec(memory_space=pltpu.VMEM)] * len(arrays),
        scratch_shapes=[pltpu.SemaphoreType.DMA((pieces * len(arrays),))],
        compiler_params=pltpu.CompilerParams(vmem_limit_bytes=4 * MIB),
        name="fetch",
    )(*[in_hbm(array) for array in arrays])


def fetch_rows_kernel(start, pieces, source, target, sems):
    size = target.shape[0] // pieces
    copies = [
        pltpu.make_async_copy(
            source.at[start + p * size : start + (p + 1) * size],
            target.at[p * size : (p + 1) * size],
            sems.at[p],
        )
        for p in range(pieces)
    ]
    for copy in copies:
        copy.start()
    for copy in copies:
        copy.wait()


def fetch_rows(array, start, rows):
    pieces = 4
    return pl.pallas_call(
        functools.partial(fetch_rows_kernel, start, pieces),
        out_shape=pltpu.VMEM((rows, array.shape[1]), array.dtype),
        in_specs=[pl.BlockSpec(memory_space=pltpu.HBM)],
        out_specs=pl.BlockSpec(memory_space=pltpu.VMEM),
        scratch_shapes=[pltpu.SemaphoreType.DMA((pieces,))],
        compiler_params=pltpu.CompilerParams(vmem_limit_bytes=4 * MIB),
        name="fetch_rows",
    )(in_hbm(array))


def combine_kernel(n, block, chunk, *refs):
    pieces, refs = refs[:n], refs[n:]
    gx, gy = lax.axis_index("gx"), lax.axis_index("gy")
    moved = jnp.where(gy == 0, n // 2, 0)
    if chunk:
        before_ref, refs = refs[0], refs[1:]
    w_ref, outs, (x_buf, x_sems) = refs[0], refs[1:-2], refs[-2:]
    depth, cols = x_buf.shape[1], w_ref.shape[1]
    half = x_buf.shape[0] // 2
    x_copies = []
    for slot, piece in enumerate(pieces):
        start = pl.multiple_of((slot_owner(n, slot, gx, gy, gather_orders(n, chunk)) ^ moved) * block, block)
        x_copies.append(
            pltpu.make_async_copy(piece, x_buf.at[pl.ds(start, block), :], x_sems.at[slot])
        )
    for copy in x_copies:
        copy.start()
    for copy in x_copies:
        copy.wait()

    tile = cols // TILES
    for start in range(0, cols, tile):
        at = slice(start, start + tile)
        product = jnp.dot(x_buf[...], w_ref[:, at], preferred_element_type=jnp.float32)
        if chunk:
            product = product + before_ref[:, at]
        if len(outs) == 1:
            outs[0][:, at] = product
        else:
            outs[0][:, at] = product[:half].astype(jnp.bfloat16)
            outs[1][:, at] = product[half:]


def combine(chunk, pieces, before, w_out):
    n, (block, depth) = len(pieces), pieces[0].shape
    rows = n * block
    cols = w_out.shape[1]
    last = chunk == CHUNKS - 1
    hbm = pl.BlockSpec(memory_space=pltpu.HBM)
    vmem = pl.BlockSpec(memory_space=pltpu.VMEM)
    if last:
        out_shape = [
            pltpu.VMEM((rows // 2, cols), jnp.bfloat16),
            pltpu.VMEM((rows // 2, cols), jnp.float32),
        ]
    else:
        out_shape = [pltpu.VMEM((rows, cols), jnp.float32)]
    earlier = [] if chunk == 0 else [before]
    return pl.pallas_call(
        functools.partial(combine_kernel, n, block, chunk),
        out_shape=out_shape,
        in_specs=[pl.BlockSpec(memory_space=pl.ANY)] * len(pieces)
        + [vmem] * len(earlier)
        + [vmem],
        out_specs=[vmem] * len(out_shape),
        scratch_shapes=[
            pltpu.VMEM((rows, depth), jnp.bfloat16),
            pltpu.SemaphoreType.DMA((n,)),
        ],
        compiler_params=pltpu.CompilerParams(vmem_limit_bytes=16 * MIB),
        name="combine",
    )(*pieces, *earlier, w_out)


def shards(
    tokens, norm_gain, w_query, w_key, w_value, w_out, cache_keys, cache_values, cache_lengths
):
    n = lax.axis_size("gx")
    cores = lax.axis_size("gy")
    levels = n.bit_length() - 1
    position = (cache_lengths[:, None] + jnp.arange(NEW, dtype=jnp.int32)[None, :]).reshape(-1)
    inverse = THETA ** (-2.0 * jnp.arange(HD // 2, dtype=jnp.float32) / HD)
    angles = position.astype(jnp.float32)[:, None] * inverse[None, :]
    cosine, sine = jnp.cos(angles), jnp.sin(angles)
    cosine = jnp.concatenate([cosine, cosine], axis=1)
    sine = jnp.concatenate([-sine, sine], axis=1)

    x, gain = tokens, norm_gain[None, :]
    kv = w_key.shape[1] // CHUNKS
    q_cols = w_query.shape[1] // CHUNKS

    def column_part(start, size, kv_start):
        return project(
            n, start, size, kv_start, start == 0, x, gain, w_query, w_key, w_value
        )

    def after(value, *earlier):
        return lax.optimization_barrier((value, earlier))[0]

    share = q_cols // 2
    orders = bit_orders(n)
    send_a, keep_a, x = column_part(0, share, None)
    x = after(x, send_a)
    other_a = exchange(send_a, n, cores, 0, orders)
    send_b, keep_b = column_part(share, share, 0)
    x = after(x, send_b)
    other_b = exchange(send_b, n, cores, 0, orders)
    sum_a = keep_a + other_a.astype(jnp.float32)
    x = after(x, sum_a)
    later = []
    for chunk in range(1, CHUNKS):
        later.append(column_part(chunk * q_cols, q_cols, chunk * kv))
    other_b = after(other_b, *(send_c for send_c, _ in later))
    first = jnp.concatenate([sum_a, keep_b + other_b.astype(jnp.float32)], axis=1)
    half = first.shape[0] // 2
    send = first[half:].astype(jnp.bfloat16)
    flows = [[1, first[:half], send]]
    for send_c, keep_c in later:
        flows.append([0, keep_c, after(send_c, flows[-1][2])])

    def start(flow):
        return exchange(flow[2], n, cores, flow[0], orders)

    def finish(flow, other, *earlier):
        stage, keep, _ = flow
        if earlier:
            other = after(other, *earlier)
        value = keep + other.astype(jnp.float32)
        low = value.shape[0] // 2 if stage < levels - 1 else 0
        flow[:] = stage + 1, value[:low] if low else value, value[low:].astype(jnp.bfloat16)

    lead, follow = flows
    w_rows = w_out.shape[0] // CHUNKS
    weights = [fetch_rows(after(w_out, lead[2], follow[2]), 0, w_rows)]
    while follow[0] < levels:
        pending = [start(flow) for flow in flows if flow[0] < levels]
        if lead[0] == levels:
            finish(follow, pending[0])
        elif lead[0] == levels - 1:
            cache_keys, cache_values = fetch(*after((cache_keys, cache_values), follow[2]))
            finish(lead, pending[0], cache_keys, cache_values)
            finish(follow, pending[1], lead[1])
        else:
            finish(lead, pending[0], *weights)
            finish(follow, pending[1], lead[2])
    sums = [flow[1] for flow in flows]
    squares = sums[0][:, share : share + 128]
    plain = [h * HD for h in range(q_cols // HD)]
    offsets = [[at if at < share else at + 128 for at in plain], plain]
    kv_offsets = [q_cols + 128, q_cols]

    attentions = []
    for chunk in range(CHUNKS):
        out = attend(
            chunk,
            offsets[chunk],
            kv_offsets[chunk],
            sums[chunk],
            squares,
            cosine,
            sine,
            cache_keys,
            cache_values,
            cache_lengths,
            w_out,
        )
        attentions.append(out[0])
        weights += out[1:]
    gathered = []
    for chunk in range(CHUNKS):
        slots = [attentions[chunk]]
        for slot in range(1, n):
            top = slot.bit_length() - 1
            source = slots[slot - (1 << top)]
            slots.append(
                exchange(source, n, cores, levels - 1 - top, gather_orders(n, chunk))
            )
        gathered.append(slots)
    result = None
    for chunk in range(CHUNKS):
        result = combine(chunk, gathered[chunk], result and result[0], weights[chunk])
    send, keep = result
    other = lax.ppermute(send, "gy", [(0, 1), (1, 0)])
    return (keep + other.astype(jnp.float32)).astype(jnp.bfloat16)


def solution(mesh):
    return jax.shard_map(
        shards,
        mesh=mesh,
        in_specs=(
            P("groups", "gx"),
            P("gx"),
            P("gx", "gy"),
            P("gx", "gy"),
            P("gx", "gy"),
            P("gy", "gx"),
            P(("groups", "gx"), None, "gy"),
            P(("groups", "gx"), None, "gy"),
            P(("groups", "gx")),
        ),
        out_specs=P(("groups", "gy"), "gx"),
        check_vma=False,
    )
```

```python
import functools
import math

import jax
import jax.numpy as jnp
from jax import lax
from jax.experimental import pallas as pl
from jax.experimental.pallas import tpu as pltpu
from jax.sharding import PartitionSpec as P

D = 16384
HD = 128
NEW = 4
EPS = 1e-05
THETA = 500000.0

CHUNKS = 2
TILES = 4
MIB = 1 << 20


def bit_orders(n):
    levels = n.bit_length() - 1
    first = list(range(levels))
    second = list(first)
    if levels > 1:
        second[0], second[1] = second[1], second[0]
    return first, second


def gather_orders(n, chunk):
    first, second = bit_orders(n)
    return (first, first) if chunk else (first, second)


def slot_shift(slot, order):
    levels = len(order)
    shift = 0
    for stage in range(levels):
        shift |= ((slot >> (levels - 1 - stage)) & 1) << order[stage]
    return shift


def slot_owner(n, slot, gx, gy, orders):
    first, second = (slot_shift(slot, order) for order in orders)
    return gx ^ jnp.where(gy == 0, first, second)


def exchange(value, n, cores, stage, orders):
    pairs = []
    for gx in range(n):
        for gy in range(cores):
            other = gx ^ (1 << orders[gy % 2][stage])
            pairs.append((gx * cores + gy, other * cores + gy))
    return lax.ppermute(value, ("gx", "gy"), pairs)


def project_kernel(n, q_start, kv_start, first, *refs):
    if first:
        tokens_ref, gain_ref, wq_ref, wk_ref, wv_ref, send_ref, keep_ref, x_ref = refs[:8]
        t_buf, t_sems, g_buf, g_sem = refs[8:12]
    else:
        x_ref, wq_ref, wk_ref, wv_ref, send_ref, keep_ref = refs[:6]
    w_buf, sems = refs[-2:]
    half = send_ref.shape[0]
    rows = 2 * half
    with_kv = kv_start is not None
    kv = wk_ref.shape[1] if with_kv else 0
    width = w_buf.shape[1]
    cols = width - 2 * kv
    tile = cols // 2

    def w_copy(ref, start, size, at, sem):
        return pltpu.make_async_copy(
            ref.at[:, start : start + size], w_buf.at[:, at : at + size], sems.at[sem]
        )

    copies = [[w_copy(wq_ref, q_start + at, tile, at, at // tile)] for at in (0, tile)]
    if with_kv:
        copies[1].append(w_copy(wk_ref, kv_start, kv, cols, 2))
        copies[1].append(w_copy(wv_ref, kv_start, kv, cols + kv, 3))

    if first:
        block = rows // n
        me, gy = lax.axis_index("gx"), lax.axis_index("gy")
        t_copies = []
        for slot in range(n):
            start = pl.multiple_of(slot_owner(n, slot, me, gy, bit_orders(n)) * block, block)
            t_copies.append(
                pltpu.make_async_copy(
                    tokens_ref.at[pl.ds(start, block), :], t_buf.at[slot], t_sems.at[slot]
                )
            )
            t_copies[-1].start()
        g_copy = pltpu.make_async_copy(gain_ref, g_buf, g_sem)
        g_copy.start()
    for group in copies:
        for copy in group:
            copy.start()
    if first:
        lanes = lax.broadcasted_iota(jnp.int32, (block, 128), 1)
        g_copy.wait()
        for slot in range(n):
            t_copies[slot].wait()
            wide = t_buf[slot].astype(jnp.float32)
            x_ref[slot * block : (slot + 1) * block, :] = (wide * g_buf[...]).astype(jnp.bfloat16)
            square = jnp.sum(wide * wide, axis=1, keepdims=True)
            high = square.astype(jnp.bfloat16).astype(jnp.float32)
            rest = square - high
            middle = rest.astype(jnp.bfloat16).astype(jnp.float32)
            low = rest - middle
            packed = jnp.where(
                lanes == 3 * me,
                high,
                jnp.where(lanes == 3 * me + 1, middle, jnp.where(lanes == 3 * me + 2, low, 0.0)),
            )
            if slot < n // 2:
                keep_ref[slot * block : (slot + 1) * block, width : width + 128] = packed
            else:
                at = (slot - n // 2) * block
                send_ref[at : at + block, width : width + 128] = packed.astype(jnp.bfloat16)

    for p, (start, end) in enumerate(((0, tile), (tile, width))):
        for copy in copies[p]:
            copy.wait()
        product = jnp.dot(x_ref[...], w_buf[:, start:end], preferred_element_type=jnp.float32)
        keep_ref[:, start:end] = product[:half]
        send_ref[:, start:end] = product[half:].astype(jnp.bfloat16)


def in_hbm(value):
    return pltpu.with_memory_space_constraint(value, pltpu.HBM)


def project(n, q_start, q_cols, kv_start, first, x, gain, w_query, w_key, w_value):
    rows, depth = x.shape
    kv = w_key.shape[1] if kv_start is not None else 0
    width = q_cols + 2 * kv
    full = width + (128 if first else 0)
    hbm = pl.BlockSpec(memory_space=pltpu.HBM)
    vmem = pl.BlockSpec(memory_space=pltpu.VMEM)
    out_shape = [
        pltpu.VMEM((rows // 2, full), jnp.bfloat16),
        pltpu.VMEM((rows // 2, full), jnp.float32),
    ]
    scratch = [pltpu.VMEM((depth, width), jnp.bfloat16), pltpu.SemaphoreType.DMA((4,))]
    if first:
        out_shape.append(pltpu.VMEM((rows, depth), jnp.bfloat16))
        args = [in_hbm(x), in_hbm(gain)]
        in_specs = [hbm, hbm]
        scratch = [
            pltpu.VMEM((n, rows // n, depth), jnp.bfloat16),
            pltpu.SemaphoreType.DMA((n,)),
            pltpu.VMEM((1, depth), jnp.float32),
            pltpu.SemaphoreType.DMA,
        ] + scratch
    else:
        args, in_specs = [x], [vmem]
    return pl.pallas_call(
        functools.partial(project_kernel, n, q_start, kv_start, first),
        out_shape=out_shape,
        in_specs=in_specs + [hbm] * 3,
        out_specs=[vmem] * len(out_shape),
        scratch_shapes=scratch,
        compiler_params=pltpu.CompilerParams(vmem_limit_bytes=16 * MIB),
        name="project",
    )(*args, in_hbm(w_query), in_hbm(w_key), in_hbm(w_value))


def attend_kernel(layout, kv_offset, square_offset, seqs, length_ref, *refs):
    sum_ref, shared_ref, cos_ref, sin_ref, k_ref, v_ref, out_ref, q_scr, o_scr = refs
    rows = seqs * NEW
    kv = k_ref.shape[2]
    seq_count, slots = k_ref.shape[:2]
    scale = HD**-0.5 * math.log2(math.e)
    slot_ids = lax.broadcasted_iota(jnp.int32, (1, slots), 1)

    @pl.loop(0, seq_count // seqs)
    def _(step):
        mine = pl.ds(pl.multiple_of(step * rows, rows), rows)
        squares = shared_ref[mine, square_offset : square_offset + 128]
        mean = jnp.sum(squares, axis=1, keepdims=True) / D
        row_scale = lax.rsqrt(mean + EPS)
        cosine, sine = cos_ref[mine, :], sin_ref[mine, :]

        def raw(ref, start):
            return ref[mine, start : start + HD] * row_scale

        def rotary(value):
            return value * cosine + pltpu.roll(value, HD // 2, 1) * sine

        done = 0
        for g, offsets in layout:
            heads = len(offsets)
            many = heads * NEW
            for h, offset in enumerate(offsets):
                turned = rotary(raw(sum_ref, offset))
                at = (done + h) * NEW
                for s in range(seqs):
                    q_scr[s, at : at + NEW, :] = turned[s * NEW : (s + 1) * NEW]
            new_cols = lax.broadcasted_iota(jnp.int32, (many, rows), 1)
            new_rows = lax.broadcasted_iota(jnp.int32, (many, rows), 0) % NEW
            new_keys = rotary(raw(shared_ref, kv_offset + g * HD)).astype(jnp.bfloat16)
            new_values = raw(shared_ref, kv_offset + kv + g * HD).astype(jnp.bfloat16)
            lanes = slice(g * HD, (g + 1) * HD)
            olds, news, mixes = [], [], []
            for s in range(seqs):
                query = q_scr[s, done * NEW : (done + heads) * NEW, :].astype(jnp.bfloat16)
                keys = k_ref[step * seqs + s, :, lanes]
                olds.append(
                    lax.dot_general(
                        query, keys, (((1,), (1,)), ((), ())), preferred_element_type=jnp.float32
                    )
                )
                news.append(
                    lax.dot_general(
                        query, new_keys, (((1,), (1,)), ((), ())), preferred_element_type=jnp.float32
                    )
                )
            for s in range(seqs):
                live = slot_ids < length_ref[step * seqs + s]
                seen = (new_cols >= s * NEW) & (new_cols <= s * NEW + new_rows)
                old = jnp.where(live, olds[s] * scale, -1e30)
                new = jnp.where(seen, news[s] * scale, -1e30)
                top = jnp.maximum(
                    jnp.max(old, axis=1, keepdims=True), jnp.max(new, axis=1, keepdims=True)
                )
                old = jnp.exp2(old - top)
                new = jnp.exp2(new - top)
                total = jnp.sum(old, axis=1, keepdims=True) + jnp.sum(new, axis=1, keepdims=True)
                inverse = 1.0 / total
                olds[s] = (old * inverse).astype(jnp.bfloat16)
                news[s] = (new * inverse).astype(jnp.bfloat16)
            for s in range(seqs):
                values = v_ref[step * seqs + s, :, lanes]
                mixes.append(
                    jnp.dot(olds[s], values, preferred_element_type=jnp.float32)
                    + jnp.dot(news[s], new_values, preferred_element_type=jnp.float32)
                )
            for s in range(seqs):
                for h in range(heads):
                    at = (done + h) * HD
                    o_scr[s * NEW : (s + 1) * NEW, at : at + HD] = mixes[s][
                        h * NEW : (h + 1) * NEW
                    ]
            done += heads
        out_ref[mine, :] = o_scr[...].astype(jnp.bfloat16)


def attend(layout, kv_offset, square_offset, sums, shared, cosine, sine, keys, values, lengths):
    seq_count = keys.shape[0]
    heads = sum(len(offsets) for _, offsets in layout)
    seqs = min(4, seq_count)
    vmem = pl.BlockSpec(memory_space=pltpu.VMEM)
    return pl.pallas_call(
        functools.partial(attend_kernel, layout, kv_offset, square_offset, seqs),
        out_shape=pltpu.VMEM((seq_count * NEW, heads * HD), jnp.bfloat16),
        in_specs=[pl.BlockSpec(memory_space=pltpu.SMEM)] + [vmem] * 6,
        out_specs=vmem,
        scratch_shapes=[
            pltpu.VMEM((seqs, heads * NEW, HD), jnp.float32),
            pltpu.VMEM((seqs * NEW, heads * HD), jnp.float32),
        ],
        compiler_params=pltpu.CompilerParams(vmem_limit_bytes=16 * MIB),
        name="attend",
    )(lengths, sums, shared, cosine, sine, keys, values)


def fetch_kernel(count, pieces, *refs):
    sources, targets, sems = refs[:count], refs[count : 2 * count], refs[2 * count]
    copies = []
    for i, (source, target) in enumerate(zip(sources, targets)):
        size = target.shape[0] // pieces
        for p in range(pieces):
            at = slice(p * size, (p + 1) * size)
            copies.append(
                pltpu.make_async_copy(source.at[at], target.at[at], sems.at[i * pieces + p])
            )
    for copy in copies:
        copy.start()
    for copy in copies:
        copy.wait()


def fetch(*arrays):
    pieces = 4
    return pl.pallas_call(
        functools.partial(fetch_kernel, len(arrays), pieces),
        out_shape=[pltpu.VMEM(array.shape, array.dtype) for array in arrays],
        in_specs=[pl.BlockSpec(memory_space=pltpu.HBM)] * len(arrays),
        out_specs=[pl.BlockSpec(memory_space=pltpu.VMEM)] * len(arrays),
        scratch_shapes=[pltpu.SemaphoreType.DMA((pieces * len(arrays),))],
        compiler_params=pltpu.CompilerParams(vmem_limit_bytes=4 * MIB),
        name="fetch",
    )(*[in_hbm(array) for array in arrays])


def fetch_rows_kernel(start, pieces, source, target, sems):
    size = target.shape[0] // pieces
    copies = [
        pltpu.make_async_copy(
            source.at[start + p * size : start + (p + 1) * size],
            target.at[p * size : (p + 1) * size],
            sems.at[p],
        )
        for p in range(pieces)
    ]
    for copy in copies:
        copy.start()
    for copy in copies:
        copy.wait()


def fetch_rows(array, start, rows):
    pieces = 4
    return pl.pallas_call(
        functools.partial(fetch_rows_kernel, start, pieces),
        out_shape=pltpu.VMEM((rows, array.shape[1]), array.dtype),
        in_specs=[pl.BlockSpec(memory_space=pltpu.HBM)],
        out_specs=pl.BlockSpec(memory_space=pltpu.VMEM),
        scratch_shapes=[pltpu.SemaphoreType.DMA((pieces,))],
        compiler_params=pltpu.CompilerParams(vmem_limit_bytes=4 * MIB),
        name="fetch_rows",
    )(in_hbm(array))


def combine_kernel(n, block, chunk, *refs):
    pieces, refs = refs[:n], refs[n:]
    gx, gy = lax.axis_index("gx"), lax.axis_index("gy")
    moved = jnp.where(gy == 0, n // 2, 0)
    if chunk:
        before_ref, refs = refs[0], refs[1:]
    w_ref, outs, (x_buf, x_sems) = refs[0], refs[1:-2], refs[-2:]
    depth, cols = x_buf.shape[1], w_ref.shape[1]
    half = x_buf.shape[0] // 2
    x_copies = []
    for slot, piece in enumerate(pieces):
        start = pl.multiple_of((slot_owner(n, slot, gx, gy, gather_orders(n, chunk)) ^ moved) * block, block)
        x_copies.append(
            pltpu.make_async_copy(piece, x_buf.at[pl.ds(start, block), :], x_sems.at[slot])
        )
    for copy in x_copies:
        copy.start()
    for copy in x_copies:
        copy.wait()

    tile = cols // TILES
    for start in range(0, cols, tile):
        at = slice(start, start + tile)
        product = jnp.dot(x_buf[...], w_ref[:, at], preferred_element_type=jnp.float32)
        if chunk:
            product = product + before_ref[:, at]
        if len(outs) == 1:
            outs[0][:, at] = product
        else:
            outs[0][:, at] = product[:half].astype(jnp.bfloat16)
            outs[1][:, at] = product[half:]


def combine(chunk, pieces, before, w_out):
    n, (block, depth) = len(pieces), pieces[0].shape
    rows = n * block
    cols = w_out.shape[1]
    last = chunk == CHUNKS - 1
    hbm = pl.BlockSpec(memory_space=pltpu.HBM)
    vmem = pl.BlockSpec(memory_space=pltpu.VMEM)
    if last:
        out_shape = [
            pltpu.VMEM((rows // 2, cols), jnp.bfloat16),
            pltpu.VMEM((rows // 2, cols), jnp.float32),
        ]
    else:
        out_shape = [pltpu.VMEM((rows, cols), jnp.float32)]
    earlier = [] if chunk == 0 else [before]
    return pl.pallas_call(
        functools.partial(combine_kernel, n, block, chunk),
        out_shape=out_shape,
        in_specs=[pl.BlockSpec(memory_space=pl.ANY)] * len(pieces)
        + [vmem] * len(earlier)
        + [vmem],
        out_specs=[vmem] * len(out_shape),
        scratch_shapes=[
            pltpu.VMEM((rows, depth), jnp.bfloat16),
            pltpu.SemaphoreType.DMA((n,)),
        ],
        compiler_params=pltpu.CompilerParams(vmem_limit_bytes=16 * MIB),
        name="combine",
    )(*pieces, *earlier, w_out)


def shards(
    tokens, norm_gain, w_query, w_key, w_value, w_out, cache_keys, cache_values, cache_lengths
):
    n = lax.axis_size("gx")
    cores = lax.axis_size("gy")
    levels = n.bit_length() - 1
    position = (cache_lengths[:, None] + jnp.arange(NEW, dtype=jnp.int32)[None, :]).reshape(-1)
    inverse = THETA ** (-2.0 * jnp.arange(HD // 2, dtype=jnp.float32) / HD)
    angles = position.astype(jnp.float32)[:, None] * inverse[None, :]
    cosine, sine = jnp.cos(angles), jnp.sin(angles)
    cosine = jnp.concatenate([cosine, cosine], axis=1)
    sine = jnp.concatenate([-sine, sine], axis=1)

    x, gain = tokens, norm_gain[None, :]
    q_cols = w_query.shape[1]
    share = q_cols // 4
    orders = bit_orders(n)

    def column_part(part, with_kv):
        kv_start = 0 if with_kv else None
        return project(
            n, part * share, share, kv_start, part == 0, x, gain, w_query, w_key, w_value
        )

    def after(value, *earlier):
        return lax.optimization_barrier((value, earlier))[0]

    def start(stage, send):
        return exchange(send, n, cores, stage, orders)

    def added(stage, keep, other):
        value = keep + other.astype(jnp.float32)
        low = value.shape[0] // 2 if stage < levels - 1 else 0
        return value[low:].astype(jnp.bfloat16), value[:low] if low else value

    send_a, keep_a, x = column_part(0, False)
    x = after(x, send_a)
    other_a = start(0, send_a)
    send_b, keep_b = column_part(1, False)
    x = after(x, send_b)
    other_b = start(0, send_b)
    sum_a = keep_a + other_a.astype(jnp.float32)
    x = after(x, sum_a)
    send_c, keep_c = column_part(2, True)
    x = after(x, send_c)
    other_c = start(0, send_c)
    sum_b = keep_b + other_b.astype(jnp.float32)
    x = after(x, sum_b)
    send_1, keep_1 = column_part(3, False)
    other_c = after(other_c, send_1)
    first = jnp.concatenate([sum_a, sum_b, keep_c + other_c.astype(jnp.float32)], axis=1)
    half = first.shape[0] // 2
    send, keep = first[half:].astype(jnp.bfloat16), first[:half]

    w_rows = 3 * w_out.shape[0] // 4
    w_first = fetch_rows(after(w_out, send), 0, w_rows)
    send_1 = after(send_1, send)
    other = after(start(1, send), w_first)
    other_1 = start(0, send_1)
    send, keep = added(1, keep, other)
    send_1, keep_1 = added(0, keep_1, after(other_1, send))
    cache_keys, cache_values = fetch(*after((cache_keys, cache_values), send, send_1))
    w_second = fetch_rows(after(w_out, cache_keys), w_rows, w_out.shape[0] - w_rows)
    for stage in range(2, levels):
        other = start(stage, send)
        other_1 = start(stage - 1, send_1)
        if stage == 2:
            other = after(other, cache_keys, cache_values, w_second)
        send, keep = added(stage, keep, other)
        send_1, keep_1 = added(stage - 1, keep_1, after(other_1, keep))
    sum_0 = keep
    send_1 = after(send_1, sum_0)
    _, sum_1 = added(levels - 1, keep_1, start(levels - 1, send_1))

    plain = [h * HD for h in range(q_cols // HD)]
    group_heads = q_cols // w_key.shape[1]
    lead = 3 * share // HD
    columns = [at if at < share else at + 128 for at in plain[:lead]] + plain[: share // HD]
    layouts = [{}, {}]
    for h, column in enumerate(columns):
        layouts[h >= lead].setdefault(h // group_heads, []).append(column)
    attentions = [
        attend(
            list(layouts[chunk].items()),
            3 * share + 128,
            share,
            total,
            sum_0,
            cosine,
            sine,
            cache_keys,
            cache_values,
            cache_lengths,
        )
        for chunk, total in enumerate((sum_0, sum_1))
    ]
    weights = [w_first, w_second]
    gathered = []
    for chunk in range(CHUNKS):
        slots = [attentions[chunk]]
        for slot in range(1, n):
            top = slot.bit_length() - 1
            source = slots[slot - (1 << top)]
            if chunk == 0 and slot == 1:
                source = after(source, sum_1)
            if chunk == 0 and slot & (slot - 1):
                source = after(source, attentions[1])
            if chunk == 0 and slot == 3 << (levels - 2):
                source = after(source, slots[1 << (levels - 1)])
            slots.append(
                exchange(source, n, cores, levels - 1 - top, gather_orders(n, chunk))
            )
        gathered.append(slots)
    result = None
    for chunk in range(CHUNKS):
        result = combine(chunk, gathered[chunk], result and result[0], weights[chunk])
    send, keep = result
    other = lax.ppermute(send, "gy", [(0, 1), (1, 0)])
    return (keep + other.astype(jnp.float32)).astype(jnp.bfloat16)


def solution(mesh):
    return jax.shard_map(
        shards,
        mesh=mesh,
        in_specs=(
            P("groups", "gx"),
            P("gx"),
            P("gx", "gy"),
            P("gx", "gy"),
            P("gx", "gy"),
            P("gy", "gx"),
            P(("groups", "gx"), None, "gy"),
            P(("groups", "gx"), None, "gy"),
            P(("groups", "gx")),
        ),
        out_specs=P(("groups", "gy"), "gx"),
        check_vma=False,
    )
```

```python
import functools
import math

import jax
import jax.numpy as jnp
from jax import lax
from jax.experimental import pallas as pl
from jax.experimental.pallas import tpu as pltpu
from jax.sharding import PartitionSpec as P

D = 16384
HD = 128
NEW = 4
EPS = 1e-05
THETA = 500000.0

CHUNKS = 2
TILES = 4
MIB = 1 << 20


def bit_orders(n):
    levels = n.bit_length() - 1
    first = list(range(levels))
    second = list(first)
    if levels > 1:
        second[0], second[1] = second[1], second[0]
    return first, second


def gather_orders(n, chunk):
    first, second = bit_orders(n)
    return (first, second) if chunk else (first, first)


def slot_shift(slot, order):
    levels = len(order)
    shift = 0
    for stage in range(levels):
        shift |= ((slot >> (levels - 1 - stage)) & 1) << order[stage]
    return shift


def slot_owner(n, slot, gx, gy, orders):
    first, second = (slot_shift(slot, order) for order in orders)
    return gx ^ jnp.where(gy == 0, first, second)


def exchange(value, n, cores, stage, orders):
    pairs = []
    for gx in range(n):
        for gy in range(cores):
            other = gx ^ (1 << orders[gy % 2][stage])
            pairs.append((gx * cores + gy, other * cores + gy))
    return lax.ppermute(value, ("gx", "gy"), pairs)


def project_kernel(n, q_start, kv_start, first, *refs):
    if first:
        tokens_ref, gain_ref, wq_ref, wk_ref, wv_ref, send_ref, keep_ref, x_ref = refs[:8]
        t_buf, t_sems, g_buf, g_sem = refs[8:12]
    else:
        x_ref, wq_ref, wk_ref, wv_ref, send_ref, keep_ref = refs[:6]
    w_buf, sems = refs[-2:]
    half = send_ref.shape[0]
    rows = 2 * half
    with_kv = kv_start is not None
    kv = wk_ref.shape[1] // CHUNKS if with_kv else 0
    width = w_buf.shape[1]
    cols = width - 2 * kv
    tile = cols // 2

    def w_copy(ref, start, size, at, sem):
        return pltpu.make_async_copy(
            ref.at[:, start : start + size], w_buf.at[:, at : at + size], sems.at[sem]
        )

    copies = [[w_copy(wq_ref, q_start + at, tile, at, at // tile)] for at in (0, tile)]
    if with_kv:
        copies[1].append(w_copy(wk_ref, kv_start, kv, cols, 2))
        copies[1].append(w_copy(wv_ref, kv_start, kv, cols + kv, 3))

    if first:
        block = rows // n
        me, gy = lax.axis_index("gx"), lax.axis_index("gy")
        t_copies = []
        for slot in range(n):
            start = pl.multiple_of(slot_owner(n, slot, me, gy, bit_orders(n)) * block, block)
            t_copies.append(
                pltpu.make_async_copy(
                    tokens_ref.at[pl.ds(start, block), :], t_buf.at[slot], t_sems.at[slot]
                )
            )
            t_copies[-1].start()
        g_copy = pltpu.make_async_copy(gain_ref, g_buf, g_sem)
        g_copy.start()
    for group in copies:
        for copy in group:
            copy.start()
    if first:
        lanes = lax.broadcasted_iota(jnp.int32, (block, 128), 1)
        g_copy.wait()
        for slot in range(n):
            t_copies[slot].wait()
            wide = t_buf[slot].astype(jnp.float32)
            x_ref[slot * block : (slot + 1) * block, :] = (wide * g_buf[...]).astype(jnp.bfloat16)
            square = jnp.sum(wide * wide, axis=1, keepdims=True)
            high = square.astype(jnp.bfloat16).astype(jnp.float32)
            rest = square - high
            middle = rest.astype(jnp.bfloat16).astype(jnp.float32)
            low = rest - middle
            packed = jnp.where(
                lanes == 3 * me,
                high,
                jnp.where(lanes == 3 * me + 1, middle, jnp.where(lanes == 3 * me + 2, low, 0.0)),
            )
            if slot < n // 2:
                keep_ref[slot * block : (slot + 1) * block, width : width + 128] = packed
            else:
                at = (slot - n // 2) * block
                send_ref[at : at + block, width : width + 128] = packed.astype(jnp.bfloat16)

    for p, (start, end) in enumerate(((0, tile), (tile, width))):
        for copy in copies[p]:
            copy.wait()
        product = jnp.dot(x_ref[...], w_buf[:, start:end], preferred_element_type=jnp.float32)
        keep_ref[:, start:end] = product[:half]
        send_ref[:, start:end] = product[half:].astype(jnp.bfloat16)


def in_hbm(value):
    return pltpu.with_memory_space_constraint(value, pltpu.HBM)


def project(n, q_start, q_cols, kv_start, first, x, gain, w_query, w_key, w_value):
    rows, depth = x.shape
    kv = w_key.shape[1] // CHUNKS if kv_start is not None else 0
    width = q_cols + 2 * kv
    full = width + (128 if first else 0)
    hbm = pl.BlockSpec(memory_space=pltpu.HBM)
    vmem = pl.BlockSpec(memory_space=pltpu.VMEM)
    out_shape = [
        pltpu.VMEM((rows // 2, full), jnp.bfloat16),
        pltpu.VMEM((rows // 2, full), jnp.float32),
    ]
    scratch = [pltpu.VMEM((depth, width), jnp.bfloat16), pltpu.SemaphoreType.DMA((4,))]
    if first:
        out_shape.append(pltpu.VMEM((rows, depth), jnp.bfloat16))
        args = [in_hbm(x), in_hbm(gain)]
        in_specs = [hbm, hbm]
        scratch = [
            pltpu.VMEM((n, rows // n, depth), jnp.bfloat16),
            pltpu.SemaphoreType.DMA((n,)),
            pltpu.VMEM((1, depth), jnp.float32),
            pltpu.SemaphoreType.DMA,
        ] + scratch
    else:
        args, in_specs = [x], [vmem]
    return pl.pallas_call(
        functools.partial(project_kernel, n, q_start, kv_start, first),
        out_shape=out_shape,
        in_specs=in_specs + [hbm] * 3,
        out_specs=[vmem] * len(out_shape),
        scratch_shapes=scratch,
        compiler_params=pltpu.CompilerParams(vmem_limit_bytes=16 * MIB),
        name="project",
    )(*args, in_hbm(w_query), in_hbm(w_key), in_hbm(w_value))


def attend_kernel(chunk, offsets, kv_offset, groups, heads, seqs, length_ref, *refs):
    sum_ref, square_ref = refs[:2]
    w_copies = []
    if chunk == 0:
        cos_ref, sin_ref, k_ref, v_ref, w_ref, out_ref, next_ref, q_scr, o_scr, w_sems = refs[2:]
        total = next_ref.shape[0]
        for p in range(4):
            at = slice(p * total // 4, (p + 1) * total // 4)
            w_copies.append(
                pltpu.make_async_copy(
                    w_ref.at[total + at.start : total + at.stop], next_ref.at[at], w_sems.at[p]
                )
            )
            w_copies[-1].start()
    else:
        cos_ref, sin_ref, k_ref, v_ref, out_ref, q_scr, o_scr = refs[2:]
    rows = seqs * NEW
    cols = groups * heads * HD
    kv = groups * HD
    seq_count = k_ref.shape[0]

    scale = HD**-0.5 * math.log2(math.e)
    slots = k_ref.shape[1]
    many = heads * NEW
    slot_ids = lax.broadcasted_iota(jnp.int32, (1, slots), 1)
    new_cols = lax.broadcasted_iota(jnp.int32, (many, rows), 1)
    new_rows = lax.broadcasted_iota(jnp.int32, (many, rows), 0) % NEW

    @pl.loop(0, seq_count // seqs)
    def _(step):
        mine = pl.ds(pl.multiple_of(step * rows, rows), rows)
        mean = jnp.sum(square_ref[mine, :], axis=1, keepdims=True) / D
        row_scale = lax.rsqrt(mean + EPS)
        cosine, sine = cos_ref[mine, :], sin_ref[mine, :]

        def raw(start):
            return sum_ref[mine, start : start + HD] * row_scale

        def rotary(value):
            return value * cosine + pltpu.roll(value, HD // 2, 1) * sine

        for h in range(heads * groups):
            turned = rotary(raw(offsets[h]))
            for s in range(seqs):
                q_scr[s, h * NEW : (h + 1) * NEW, :] = turned[s * NEW : (s + 1) * NEW]
        for g in range(groups):
            new_keys = rotary(raw(kv_offset + g * HD)).astype(jnp.bfloat16)
            new_values = raw(kv_offset + (groups + g) * HD).astype(jnp.bfloat16)
            lanes = slice(chunk * kv + g * HD, chunk * kv + (g + 1) * HD)
            olds, news, mixes = [], [], []
            for s in range(seqs):
                query = q_scr[s, g * many : (g + 1) * many, :].astype(jnp.bfloat16)
                keys = k_ref[step * seqs + s, :, lanes]
                olds.append(
                    lax.dot_general(
                        query, keys, (((1,), (1,)), ((), ())), preferred_element_type=jnp.float32
                    )
                )
                news.append(
                    lax.dot_general(
                        query, new_keys, (((1,), (1,)), ((), ())), preferred_element_type=jnp.float32
                    )
                )
            for s in range(seqs):
                live = slot_ids < length_ref[step * seqs + s]
                seen = (new_cols >= s * NEW) & (new_cols <= s * NEW + new_rows)
                old = jnp.where(live, olds[s] * scale, -1e30)
                new = jnp.where(seen, news[s] * scale, -1e30)
                top = jnp.maximum(
                    jnp.max(old, axis=1, keepdims=True), jnp.max(new, axis=1, keepdims=True)
                )
                old = jnp.exp2(old - top)
                new = jnp.exp2(new - top)
                total = jnp.sum(old, axis=1, keepdims=True) + jnp.sum(new, axis=1, keepdims=True)
                inverse = 1.0 / total
                olds[s] = (old * inverse).astype(jnp.bfloat16)
                news[s] = (new * inverse).astype(jnp.bfloat16)
            for s in range(seqs):
                values = v_ref[step * seqs + s, :, lanes]
                mixes.append(
                    jnp.dot(olds[s], values, preferred_element_type=jnp.float32)
                    + jnp.dot(news[s], new_values, preferred_element_type=jnp.float32)
                )
            for s in range(seqs):
                for h in range(heads):
                    at = (g * heads + h) * HD
                    o_scr[s * NEW : (s + 1) * NEW, at : at + HD] = mixes[s][
                        h * NEW : (h + 1) * NEW
                    ]
        out_ref[mine, :] = o_scr[...].astype(jnp.bfloat16)

    for copy in w_copies:
        copy.wait()


def attend(chunk, offsets, kv_offset, sums, squares, cosine, sine, cache_keys, cache_values, lengths, w_out):
    seq_count, slots, kv_all = cache_keys.shape
    kv = kv_all // CHUNKS
    groups = kv // HD
    heads = len(offsets) // groups
    cols = len(offsets) * HD
    seqs = min(4, seq_count)
    rows = seq_count * NEW
    source, copied = [], []
    if chunk == 0:
        source.append(in_hbm(w_out))
        copied.append(pltpu.VMEM((w_out.shape[0] // CHUNKS, w_out.shape[1]), w_out.dtype))
    vmem = pl.BlockSpec(memory_space=pltpu.VMEM)
    hbm = pl.BlockSpec(memory_space=pltpu.HBM)
    return pl.pallas_call(
        functools.partial(attend_kernel, chunk, offsets, kv_offset, groups, heads, seqs),
        out_shape=[pltpu.VMEM((rows, cols), jnp.bfloat16)] + copied,
        in_specs=[pl.BlockSpec(memory_space=pltpu.SMEM)] + [vmem] * 6 + [hbm] * len(source),
        out_specs=[vmem] * (1 + len(copied)),
        scratch_shapes=[
            pltpu.VMEM((seqs, groups * heads * NEW, HD), jnp.float32),
            pltpu.VMEM((seqs * NEW, cols), jnp.float32),
        ]
        + [pltpu.SemaphoreType.DMA((4,))] * len(copied),
        compiler_params=pltpu.CompilerParams(vmem_limit_bytes=16 * MIB),
        name="attend",
    )(lengths, sums, squares, cosine, sine, cache_keys, cache_values, *source)


def fetch_kernel(count, pieces, *refs):
    sources, targets, sems = refs[:count], refs[count : 2 * count], refs[2 * count]
    copies = []
    for i, (source, target) in enumerate(zip(sources, targets)):
        size = target.shape[0] // pieces
        for p in range(pieces):
            at = slice(p * size, (p + 1) * size)
            copies.append(
                pltpu.make_async_copy(source.at[at], target.at[at], sems.at[i * pieces + p])
            )
    for copy in copies:
        copy.start()
    for copy in copies:
        copy.wait()


def fetch(*arrays):
    pieces = 4
    return pl.pallas_call(
        functools.partial(fetch_kernel, len(arrays), pieces),
        out_shape=[pltpu.VMEM(array.shape, array.dtype) for array in arrays],
        in_specs=[pl.BlockSpec(memory_space=pltpu.HBM)] * len(arrays),
        out_specs=[pl.BlockSpec(memory_space=pltpu.VMEM)] * len(arrays),
        scratch_shapes=[pltpu.SemaphoreType.DMA((pieces * len(arrays),))],
        compiler_params=pltpu.CompilerParams(vmem_limit_bytes=4 * MIB),
        name="fetch",
    )(*[in_hbm(array) for array in arrays])


def fetch_rows_kernel(start, pieces, source, target, sems):
    size = target.shape[0] // pieces
    copies = [
        pltpu.make_async_copy(
            source.at[start + p * size : start + (p + 1) * size],
            target.at[p * size : (p + 1) * size],
            sems.at[p],
        )
        for p in range(pieces)
    ]
    for copy in copies:
        copy.start()
    for copy in copies:
        copy.wait()


def fetch_rows(array, start, rows):
    pieces = 4
    return pl.pallas_call(
        functools.partial(fetch_rows_kernel, start, pieces),
        out_shape=pltpu.VMEM((rows, array.shape[1]), array.dtype),
        in_specs=[pl.BlockSpec(memory_space=pltpu.HBM)],
        out_specs=pl.BlockSpec(memory_space=pltpu.VMEM),
        scratch_shapes=[pltpu.SemaphoreType.DMA((pieces,))],
        compiler_params=pltpu.CompilerParams(vmem_limit_bytes=4 * MIB),
        name="fetch_rows",
    )(in_hbm(array))


def combine_kernel(n, block, chunk, *refs):
    pieces, refs = refs[:n], refs[n:]
    gx, gy = lax.axis_index("gx"), lax.axis_index("gy")
    moved = jnp.where(gy == 0, n // 2, 0)
    if chunk:
        before_ref, refs = refs[0], refs[1:]
    w_ref, outs, (x_buf, x_sems) = refs[0], refs[1:-2], refs[-2:]
    depth, cols = x_buf.shape[1], w_ref.shape[1]
    half = x_buf.shape[0] // 2
    x_copies = []
    for slot, piece in enumerate(pieces):
        start = pl.multiple_of((slot_owner(n, slot, gx, gy, gather_orders(n, chunk)) ^ moved) * block, block)
        x_copies.append(
            pltpu.make_async_copy(piece, x_buf.at[pl.ds(start, block), :], x_sems.at[slot])
        )
    for copy in x_copies:
        copy.start()
    for copy in x_copies:
        copy.wait()

    tile = cols // TILES
    for start in range(0, cols, tile):
        at = slice(start, start + tile)
        product = jnp.dot(x_buf[...], w_ref[:, at], preferred_element_type=jnp.float32)
        if chunk:
            product = product + before_ref[:, at]
        if len(outs) == 1:
            outs[0][:, at] = product
        else:
            outs[0][:, at] = product[:half].astype(jnp.bfloat16)
            outs[1][:, at] = product[half:]


def combine(chunk, pieces, before, w_out):
    n, (block, depth) = len(pieces), pieces[0].shape
    rows = n * block
    cols = w_out.shape[1]
    last = chunk == CHUNKS - 1
    hbm = pl.BlockSpec(memory_space=pltpu.HBM)
    vmem = pl.BlockSpec(memory_space=pltpu.VMEM)
    if last:
        out_shape = [
            pltpu.VMEM((rows // 2, cols), jnp.bfloat16),
            pltpu.VMEM((rows // 2, cols), jnp.float32),
        ]
    else:
        out_shape = [pltpu.VMEM((rows, cols), jnp.float32)]
    earlier = [] if chunk == 0 else [before]
    return pl.pallas_call(
        functools.partial(combine_kernel, n, block, chunk),
        out_shape=out_shape,
        in_specs=[pl.BlockSpec(memory_space=pl.ANY)] * len(pieces)
        + [vmem] * len(earlier)
        + [vmem],
        out_specs=[vmem] * len(out_shape),
        scratch_shapes=[
            pltpu.VMEM((rows, depth), jnp.bfloat16),
            pltpu.SemaphoreType.DMA((n,)),
        ],
        compiler_params=pltpu.CompilerParams(vmem_limit_bytes=16 * MIB),
        name="combine",
    )(*pieces, *earlier, w_out)


def shards(
    tokens, norm_gain, w_query, w_key, w_value, w_out, cache_keys, cache_values, cache_lengths
):
    n = lax.axis_size("gx")
    cores = lax.axis_size("gy")
    levels = n.bit_length() - 1
    position = (cache_lengths[:, None] + jnp.arange(NEW, dtype=jnp.int32)[None, :]).reshape(-1)
    inverse = THETA ** (-2.0 * jnp.arange(HD // 2, dtype=jnp.float32) / HD)
    angles = position.astype(jnp.float32)[:, None] * inverse[None, :]
    cosine, sine = jnp.cos(angles), jnp.sin(angles)
    cosine = jnp.concatenate([cosine, cosine], axis=1)
    sine = jnp.concatenate([-sine, sine], axis=1)

    x, gain = tokens, norm_gain[None, :]
    kv = w_key.shape[1] // CHUNKS
    q_cols = w_query.shape[1] // CHUNKS

    def column_part(start, size, kv_start):
        return project(
            n, start, size, kv_start, start == 0, x, gain, w_query, w_key, w_value
        )

    def after(value, *earlier):
        return lax.optimization_barrier((value, earlier))[0]

    share = q_cols // 2
    orders = bit_orders(n)
    send_a, keep_a, x = column_part(0, share, None)
    x = after(x, send_a)
    other_a = exchange(send_a, n, cores, 0, orders)
    send_b, keep_b = column_part(share, share, 0)
    x = after(x, send_b)
    other_b = exchange(send_b, n, cores, 0, orders)
    sum_a = keep_a + other_a.astype(jnp.float32)
    x = after(x, sum_a)
    later = []
    for chunk in range(1, CHUNKS):
        later.append(column_part(chunk * q_cols, q_cols, chunk * kv))
    other_b = after(other_b, *(send_c for send_c, _ in later))
    first = jnp.concatenate([sum_a, keep_b + other_b.astype(jnp.float32)], axis=1)
    half = first.shape[0] // 2
    send = first[half:].astype(jnp.bfloat16)
    flows = [[1, first[:half], send]]
    for send_c, keep_c in later:
        flows.append([0, keep_c, after(send_c, flows[-1][2])])

    def start(flow):
        return exchange(flow[2], n, cores, flow[0], orders)

    def finish(flow, other, *earlier):
        stage, keep, _ = flow
        if earlier:
            other = after(other, *earlier)
        value = keep + other.astype(jnp.float32)
        low = value.shape[0] // 2 if stage < levels - 1 else 0
        flow[:] = stage + 1, value[:low] if low else value, value[low:].astype(jnp.bfloat16)

    lead, follow = flows
    w_rows = w_out.shape[0] // CHUNKS
    weights = [fetch_rows(after(w_out, lead[2], follow[2]), 0, w_rows)]
    while follow[0] < levels:
        pending = [start(flow) for flow in flows if flow[0] < levels]
        if lead[0] == levels:
            finish(follow, pending[0])
        elif lead[0] == levels - 1:
            cache_keys, cache_values = fetch(*after((cache_keys, cache_values), follow[2]))
            finish(lead, pending[0], cache_keys, cache_values)
            finish(follow, pending[1], lead[1])
        else:
            finish(lead, pending[0], *weights)
            finish(follow, pending[1], lead[2])
    sums = [flow[1] for flow in flows]
    squares = sums[0][:, share : share + 128]
    plain = [h * HD for h in range(q_cols // HD)]
    offsets = [[at if at < share else at + 128 for at in plain], plain]
    kv_offsets = [q_cols + 128, q_cols]

    attentions = []
    for chunk in range(CHUNKS):
        out = attend(
            chunk,
            offsets[chunk],
            kv_offsets[chunk],
            sums[chunk],
            squares,
            cosine,
            sine,
            cache_keys,
            cache_values,
            cache_lengths,
            w_out,
        )
        attentions.append(out[0])
        weights += out[1:]
    gathered = []
    for chunk in range(CHUNKS):
        slots = [attentions[chunk]]
        for slot in range(1, n):
            top = slot.bit_length() - 1
            source = slots[slot - (1 << top)]
            if slot == 1 and chunk == 0:
                source = after(source, sums[1])
            if slot == 3 << (levels - 2):
                source = after(source, slots[1 << (levels - 1)])
            slots.append(
                exchange(source, n, cores, levels - 1 - top, gather_orders(n, chunk))
            )
        gathered.append(slots)
    result = None
    for chunk in range(CHUNKS):
        result = combine(chunk, gathered[chunk], result and result[0], weights[chunk])
    send, keep = result
    other = lax.ppermute(send, "gy", [(0, 1), (1, 0)])
    return (keep + other.astype(jnp.float32)).astype(jnp.bfloat16)


def solution(mesh):
    return jax.shard_map(
        shards,
        mesh=mesh,
        in_specs=(
            P("groups", "gx"),
            P("gx"),
            P("gx", "gy"),
            P("gx", "gy"),
            P("gx", "gy"),
            P("gy", "gx"),
            P(("groups", "gx"), None, "gy"),
            P(("groups", "gx"), None, "gy"),
            P(("groups", "gx")),
        ),
        out_specs=P(("groups", "gy"), "gx"),
        check_vma=False,
    )
```

```python
import functools
import math

import jax
import jax.numpy as jnp
from jax import lax
from jax.experimental import pallas as pl
from jax.experimental.pallas import tpu as pltpu
from jax.sharding import PartitionSpec as P

D = 16384
HD = 128
NEW = 4
EPS = 1e-05
THETA = 500000.0

CHUNKS = 2
TILES = 2
MIB = 1 << 20


def bit_orders(n):
    levels = n.bit_length() - 1
    first = list(range(levels))
    second = list(first)
    if levels > 1:
        second[0], second[1] = second[1], second[0]
    return first, second


def gather_orders(n, chunk):
    first, second = bit_orders(n)
    return (first, second) if chunk else (first, first)


def slot_shift(slot, order):
    levels = len(order)
    shift = 0
    for stage in range(levels):
        shift |= ((slot >> (levels - 1 - stage)) & 1) << order[stage]
    return shift


def slot_owner(n, slot, gx, gy, orders):
    first, second = (slot_shift(slot, order) for order in orders)
    return gx ^ jnp.where(gy == 0, first, second)


def exchange(value, n, cores, stage, orders):
    pairs = []
    for gx in range(n):
        for gy in range(cores):
            other = gx ^ (1 << orders[gy % 2][stage])
            pairs.append((gx * cores + gy, other * cores + gy))
    return lax.ppermute(value, ("gx", "gy"), pairs)


def project_kernel(n, q_start, kv_start, first, *refs):
    if first:
        tokens_ref, gain_ref, wq_ref, wk_ref, wv_ref, send_ref, keep_ref, x_ref = refs[:8]
        t_buf, t_sems, g_buf, g_sem = refs[8:12]
    else:
        x_ref, wq_ref, wk_ref, wv_ref, send_ref, keep_ref = refs[:6]
    w_buf, sems = refs[-2:]
    half = send_ref.shape[0]
    rows = 2 * half
    with_kv = kv_start is not None
    kv = wk_ref.shape[1] // CHUNKS if with_kv else 0
    width = w_buf.shape[1]
    cols = width - 2 * kv
    tile = cols // 2

    def w_copy(ref, start, size, at, sem):
        return pltpu.make_async_copy(
            ref.at[:, start : start + size], w_buf.at[:, at : at + size], sems.at[sem]
        )

    copies = [[w_copy(wq_ref, q_start + at, tile, at, at // tile)] for at in (0, tile)]
    if with_kv:
        copies[1].append(w_copy(wk_ref, kv_start, kv, cols, 2))
        copies[1].append(w_copy(wv_ref, kv_start, kv, cols + kv, 3))

    if first:
        block = rows // n
        me, gy = lax.axis_index("gx"), lax.axis_index("gy")
        t_copies = []
        for slot in range(n):
            start = pl.multiple_of(slot_owner(n, slot, me, gy, bit_orders(n)) * block, block)
            t_copies.append(
                pltpu.make_async_copy(
                    tokens_ref.at[pl.ds(start, block), :], t_buf.at[slot], t_sems.at[slot]
                )
            )
            t_copies[-1].start()
        g_copy = pltpu.make_async_copy(gain_ref, g_buf, g_sem)
        g_copy.start()
    for group in copies:
        for copy in group:
            copy.start()
    if first:
        lanes = lax.broadcasted_iota(jnp.int32, (block, 128), 1)
        g_copy.wait()
        for slot in range(n):
            t_copies[slot].wait()
            wide = t_buf[slot].astype(jnp.float32)
            x_ref[slot * block : (slot + 1) * block, :] = (wide * g_buf[...]).astype(jnp.bfloat16)
            square = jnp.sum(wide * wide, axis=1, keepdims=True)
            high = square.astype(jnp.bfloat16).astype(jnp.float32)
            rest = square - high
            middle = rest.astype(jnp.bfloat16).astype(jnp.float32)
            low = rest - middle
            packed = jnp.where(
                lanes == 3 * me,
                high,
                jnp.where(lanes == 3 * me + 1, middle, jnp.where(lanes == 3 * me + 2, low, 0.0)),
            )
            if slot < n // 2:
                keep_ref[slot * block : (slot + 1) * block, width : width + 128] = packed
            else:
                at = (slot - n // 2) * block
                send_ref[at : at + block, width : width + 128] = packed.astype(jnp.bfloat16)

    for p, (start, end) in enumerate(((0, tile), (tile, width))):
        for copy in copies[p]:
            copy.wait()
        product = jnp.dot(x_ref[...], w_buf[:, start:end], preferred_element_type=jnp.float32)
        keep_ref[:, start:end] = product[:half]
        send_ref[:, start:end] = product[half:].astype(jnp.bfloat16)


def in_hbm(value):
    return pltpu.with_memory_space_constraint(value, pltpu.HBM)


def project(n, q_start, q_cols, kv_start, first, x, gain, w_query, w_key, w_value):
    rows, depth = x.shape
    kv = w_key.shape[1] // CHUNKS if kv_start is not None else 0
    width = q_cols + 2 * kv
    full = width + (128 if first else 0)
    hbm = pl.BlockSpec(memory_space=pltpu.HBM)
    vmem = pl.BlockSpec(memory_space=pltpu.VMEM)
    out_shape = [
        pltpu.VMEM((rows // 2, full), jnp.bfloat16),
        pltpu.VMEM((rows // 2, full), jnp.float32),
    ]
    scratch = [pltpu.VMEM((depth, width), jnp.bfloat16), pltpu.SemaphoreType.DMA((4,))]
    if first:
        out_shape.append(pltpu.VMEM((rows, depth), jnp.bfloat16))
        args = [in_hbm(x), in_hbm(gain)]
        in_specs = [hbm, hbm]
        scratch = [
            pltpu.VMEM((n, rows // n, depth), jnp.bfloat16),
            pltpu.SemaphoreType.DMA((n,)),
            pltpu.VMEM((1, depth), jnp.float32),
            pltpu.SemaphoreType.DMA,
        ] + scratch
    else:
        args, in_specs = [x], [vmem]
    return pl.pallas_call(
        functools.partial(project_kernel, n, q_start, kv_start, first),
        out_shape=out_shape,
        in_specs=in_specs + [hbm] * 3,
        out_specs=[vmem] * len(out_shape),
        scratch_shapes=scratch,
        compiler_params=pltpu.CompilerParams(vmem_limit_bytes=16 * MIB),
        name="project",
    )(*args, in_hbm(w_query), in_hbm(w_key), in_hbm(w_value))


def attend_kernel(chunk, offsets, kv_offset, groups, heads, seqs, length_ref, *refs):
    sum_ref, square_ref = refs[:2]
    w_copies = []
    if chunk == 0:
        cos_ref, sin_ref, k_ref, v_ref, w_ref, out_ref, next_ref, q_scr, o_scr, w_sems = refs[2:]
        total = next_ref.shape[0]
        for p in range(4):
            at = slice(p * total // 4, (p + 1) * total // 4)
            w_copies.append(
                pltpu.make_async_copy(
                    w_ref.at[total + at.start : total + at.stop], next_ref.at[at], w_sems.at[p]
                )
            )
            w_copies[-1].start()
    else:
        cos_ref, sin_ref, k_ref, v_ref, out_ref, q_scr, o_scr = refs[2:]
    rows = seqs * NEW
    cols = groups * heads * HD
    kv = groups * HD
    seq_count = k_ref.shape[0]

    scale = HD**-0.5 * math.log2(math.e)
    slots = k_ref.shape[1]
    many = heads * NEW
    slot_ids = lax.broadcasted_iota(jnp.int32, (1, slots), 1)
    new_cols = lax.broadcasted_iota(jnp.int32, (many, rows), 1)
    new_rows = lax.broadcasted_iota(jnp.int32, (many, rows), 0) % NEW

    @pl.loop(0, seq_count // seqs)
    def _(step):
        mine = pl.ds(pl.multiple_of(step * rows, rows), rows)
        mean = jnp.sum(square_ref[mine, :], axis=1, keepdims=True) / D
        row_scale = lax.rsqrt(mean + EPS)
        cosine, sine = cos_ref[mine, :], sin_ref[mine, :]

        def raw(start):
            return sum_ref[mine, start : start + HD] * row_scale

        def rotary(value):
            return value * cosine + pltpu.roll(value, HD // 2, 1) * sine

        for h in range(heads * groups):
            turned = rotary(raw(offsets[h]))
            for s in range(seqs):
                q_scr[s, h * NEW : (h + 1) * NEW, :] = turned[s * NEW : (s + 1) * NEW]
        for g in range(groups):
            new_keys = rotary(raw(kv_offset + g * HD)).astype(jnp.bfloat16)
            new_values = raw(kv_offset + (groups + g) * HD).astype(jnp.bfloat16)
            lanes = slice(chunk * kv + g * HD, chunk * kv + (g + 1) * HD)
            olds, news, mixes = [], [], []
            for s in range(seqs):
                query = q_scr[s, g * many : (g + 1) * many, :].astype(jnp.bfloat16)
                keys = k_ref[step * seqs + s, :, lanes]
                olds.append(
                    lax.dot_general(
                        query, keys, (((1,), (1,)), ((), ())), preferred_element_type=jnp.float32
                    )
                )
                news.append(
                    lax.dot_general(
                        query, new_keys, (((1,), (1,)), ((), ())), preferred_element_type=jnp.float32
                    )
                )
            for s in range(seqs):
                live = slot_ids < length_ref[step * seqs + s]
                seen = (new_cols >= s * NEW) & (new_cols <= s * NEW + new_rows)
                old = jnp.where(live, olds[s] * scale, -1e30)
                new = jnp.where(seen, news[s] * scale, -1e30)
                top = jnp.maximum(
                    jnp.max(old, axis=1, keepdims=True), jnp.max(new, axis=1, keepdims=True)
                )
                old = jnp.exp2(old - top)
                new = jnp.exp2(new - top)
                total = jnp.sum(old, axis=1, keepdims=True) + jnp.sum(new, axis=1, keepdims=True)
                inverse = 1.0 / total
                olds[s] = (old * inverse).astype(jnp.bfloat16)
                news[s] = (new * inverse).astype(jnp.bfloat16)
            for s in range(seqs):
                values = v_ref[step * seqs + s, :, lanes]
                mixes.append(
                    jnp.dot(olds[s], values, preferred_element_type=jnp.float32)
                    + jnp.dot(news[s], new_values, preferred_element_type=jnp.float32)
                )
            for s in range(seqs):
                for h in range(heads):
                    at = (g * heads + h) * HD
                    o_scr[s * NEW : (s + 1) * NEW, at : at + HD] = mixes[s][
                        h * NEW : (h + 1) * NEW
                    ]
        out_ref[mine, :] = o_scr[...].astype(jnp.bfloat16)

    for copy in w_copies:
        copy.wait()


def attend(chunk, offsets, kv_offset, sums, squares, cosine, sine, cache_keys, cache_values, lengths, w_out):
    seq_count, slots, kv_all = cache_keys.shape
    kv = kv_all // CHUNKS
    groups = kv // HD
    heads = len(offsets) // groups
    cols = len(offsets) * HD
    seqs = min(4, seq_count)
    rows = seq_count * NEW
    source, copied = [], []
    if chunk == 0:
        source.append(in_hbm(w_out))
        copied.append(pltpu.VMEM((w_out.shape[0] // CHUNKS, w_out.shape[1]), w_out.dtype))
    vmem = pl.BlockSpec(memory_space=pltpu.VMEM)
    hbm = pl.BlockSpec(memory_space=pltpu.HBM)
    return pl.pallas_call(
        functools.partial(attend_kernel, chunk, offsets, kv_offset, groups, heads, seqs),
        out_shape=[pltpu.VMEM((rows, cols), jnp.bfloat16)] + copied,
        in_specs=[pl.BlockSpec(memory_space=pltpu.SMEM)] + [vmem] * 6 + [hbm] * len(source),
        out_specs=[vmem] * (1 + len(copied)),
        scratch_shapes=[
            pltpu.VMEM((seqs, groups * heads * NEW, HD), jnp.float32),
            pltpu.VMEM((seqs * NEW, cols), jnp.float32),
        ]
        + [pltpu.SemaphoreType.DMA((4,))] * len(copied),
        compiler_params=pltpu.CompilerParams(vmem_limit_bytes=16 * MIB),
        name="attend",
    )(lengths, sums, squares, cosine, sine, cache_keys, cache_values, *source)


def fetch_kernel(count, pieces, *refs):
    sources, targets, sems = refs[:count], refs[count : 2 * count], refs[2 * count]
    copies = []
    for i, (source, target) in enumerate(zip(sources, targets)):
        size = target.shape[0] // pieces
        for p in range(pieces):
            at = slice(p * size, (p + 1) * size)
            copies.append(
                pltpu.make_async_copy(source.at[at], target.at[at], sems.at[i * pieces + p])
            )
    for copy in copies:
        copy.start()
    for copy in copies:
        copy.wait()


def fetch(*arrays):
    pieces = 4
    return pl.pallas_call(
        functools.partial(fetch_kernel, len(arrays), pieces),
        out_shape=[pltpu.VMEM(array.shape, array.dtype) for array in arrays],
        in_specs=[pl.BlockSpec(memory_space=pltpu.HBM)] * len(arrays),
        out_specs=[pl.BlockSpec(memory_space=pltpu.VMEM)] * len(arrays),
        scratch_shapes=[pltpu.SemaphoreType.DMA((pieces * len(arrays),))],
        compiler_params=pltpu.CompilerParams(vmem_limit_bytes=4 * MIB),
        name="fetch",
    )(*[in_hbm(array) for array in arrays])


def fetch_rows_kernel(start, pieces, source, target, sems):
    size = target.shape[0] // pieces
    copies = [
        pltpu.make_async_copy(
            source.at[start + p * size : start + (p + 1) * size],
            target.at[p * size : (p + 1) * size],
            sems.at[p],
        )
        for p in range(pieces)
    ]
    for copy in copies:
        copy.start()
    for copy in copies:
        copy.wait()


def fetch_rows(array, start, rows):
    pieces = 4
    return pl.pallas_call(
        functools.partial(fetch_rows_kernel, start, pieces),
        out_shape=pltpu.VMEM((rows, array.shape[1]), array.dtype),
        in_specs=[pl.BlockSpec(memory_space=pltpu.HBM)],
        out_specs=pl.BlockSpec(memory_space=pltpu.VMEM),
        scratch_shapes=[pltpu.SemaphoreType.DMA((pieces,))],
        compiler_params=pltpu.CompilerParams(vmem_limit_bytes=4 * MIB),
        name="fetch_rows",
    )(in_hbm(array))


def combine_kernel(n, block, chunk, *refs):
    pieces, refs = refs[:n], refs[n:]
    gx, gy = lax.axis_index("gx"), lax.axis_index("gy")
    moved = jnp.where(gy == 0, n // 2, 0)
    if chunk:
        before_ref, refs = refs[0], refs[1:]
    w_ref, outs, x_buf = refs[0], refs[1:-1], refs[-1]
    depth, cols = x_buf.shape[1], w_ref.shape[1]
    half = x_buf.shape[0] // 2
    for slot, piece in enumerate(pieces):
        start = pl.multiple_of((slot_owner(n, slot, gx, gy, gather_orders(n, chunk)) ^ moved) * block, block)
        x_buf[pl.ds(start, block), :] = piece[...]

    tile = cols // TILES
    for start in range(0, cols, tile):
        at = slice(start, start + tile)
        product = jnp.dot(x_buf[...], w_ref[:, at], preferred_element_type=jnp.float32)
        if chunk:
            product = product + before_ref[:, at]
        if len(outs) == 1:
            outs[0][:, at] = product
        else:
            outs[0][:, at] = product[:half].astype(jnp.bfloat16)
            outs[1][:, at] = product[half:]


def combine(chunk, pieces, before, w_out):
    n, (block, depth) = len(pieces), pieces[0].shape
    rows = n * block
    cols = w_out.shape[1]
    last = chunk == CHUNKS - 1
    hbm = pl.BlockSpec(memory_space=pltpu.HBM)
    vmem = pl.BlockSpec(memory_space=pltpu.VMEM)
    if last:
        out_shape = [
            pltpu.VMEM((rows // 2, cols), jnp.bfloat16),
            pltpu.VMEM((rows // 2, cols), jnp.float32),
        ]
    else:
        out_shape = [pltpu.VMEM((rows, cols), jnp.float32)]
    earlier = [] if chunk == 0 else [before]
    return pl.pallas_call(
        functools.partial(combine_kernel, n, block, chunk),
        out_shape=out_shape,
        in_specs=[vmem] * (len(pieces) + len(earlier) + 1),
        out_specs=[vmem] * len(out_shape),
        scratch_shapes=[
            pltpu.VMEM((rows, depth), jnp.bfloat16),
        ],
        compiler_params=pltpu.CompilerParams(vmem_limit_bytes=16 * MIB),
        name="combine",
    )(*pieces, *earlier, w_out)


def shards(
    tokens, norm_gain, w_query, w_key, w_value, w_out, cache_keys, cache_values, cache_lengths
):
    n = lax.axis_size("gx")
    cores = lax.axis_size("gy")
    levels = n.bit_length() - 1
    position = (cache_lengths[:, None] + jnp.arange(NEW, dtype=jnp.int32)[None, :]).reshape(-1)
    inverse = THETA ** (-2.0 * jnp.arange(HD // 2, dtype=jnp.float32) / HD)
    angles = position.astype(jnp.float32)[:, None] * inverse[None, :]
    cosine, sine = jnp.cos(angles), jnp.sin(angles)
    cosine = jnp.concatenate([cosine, cosine], axis=1)
    sine = jnp.concatenate([-sine, sine], axis=1)

    x, gain = tokens, norm_gain[None, :]
    kv = w_key.shape[1] // CHUNKS
    q_cols = w_query.shape[1] // CHUNKS

    def column_part(start, size, kv_start):
        return project(
            n, start, size, kv_start, start == 0, x, gain, w_query, w_key, w_value
        )

    def after(value, *earlier):
        return lax.optimization_barrier((value, earlier))[0]

    share = q_cols // 2
    orders = bit_orders(n)
    send_a, keep_a, x = column_part(0, share, None)
    x = after(x, send_a)
    other_a = exchange(send_a, n, cores, 0, orders)
    send_b, keep_b = column_part(share, share, 0)
    x = after(x, send_b)
    other_b = exchange(send_b, n, cores, 0, orders)
    sum_a = keep_a + other_a.astype(jnp.float32)
    x = after(x, sum_a)
    later = []
    for chunk in range(1, CHUNKS):
        later.append(column_part(chunk * q_cols, q_cols, chunk * kv))
    other_b = after(other_b, *(send_c for send_c, _ in later))
    first = jnp.concatenate([sum_a, keep_b + other_b.astype(jnp.float32)], axis=1)
    half = first.shape[0] // 2
    send = first[half:].astype(jnp.bfloat16)
    flows = [[1, first[:half], send]]
    for send_c, keep_c in later:
        flows.append([0, keep_c, after(send_c, flows[-1][2])])

    def start(flow):
        return exchange(flow[2], n, cores, flow[0], orders)

    def finish(flow, other, *earlier):
        stage, keep, _ = flow
        if earlier:
            other = after(other, *earlier)
        value = keep + other.astype(jnp.float32)
        low = value.shape[0] // 2 if stage < levels - 1 else 0
        flow[:] = stage + 1, value[:low] if low else value, value[low:].astype(jnp.bfloat16)

    lead, follow = flows
    w_rows = w_out.shape[0] // CHUNKS
    weights = [fetch_rows(after(w_out, lead[2], follow[2]), 0, w_rows)]
    while follow[0] < levels:
        pending = [start(flow) for flow in flows if flow[0] < levels]
        if lead[0] == levels:
            finish(follow, pending[0])
        elif lead[0] == levels - 1:
            cache_keys, cache_values = fetch(*after((cache_keys, cache_values), follow[2]))
            finish(lead, pending[0], cache_keys, cache_values)
            finish(follow, pending[1], lead[1])
        else:
            finish(lead, pending[0], *weights)
            finish(follow, pending[1], lead[2])
    sums = [flow[1] for flow in flows]
    squares = sums[0][:, share : share + 128]
    plain = [h * HD for h in range(q_cols // HD)]
    offsets = [[at if at < share else at + 128 for at in plain], plain]
    kv_offsets = [q_cols + 128, q_cols]

    attentions, early = [], {}
    for chunk in range(CHUNKS):
        total = sums[chunk]
        if chunk == 1:
            total = after(total, *early.values())
        out = attend(
            chunk,
            offsets[chunk],
            kv_offsets[chunk],
            total,
            squares,
            cosine,
            sine,
            cache_keys,
            cache_values,
            cache_lengths,
            w_out,
        )
        attentions.append(out[0])
        weights += out[1:]
        if chunk == 0:
            for stage in [0]:
                early[1 << (levels - 1 - stage)] = exchange(
                    out[0], n, cores, stage, gather_orders(n, 0)
                )
    gathered = []
    for chunk in range(CHUNKS):
        slots = [attentions[chunk]]
        for slot in range(1, n):
            top = slot.bit_length() - 1
            source = slots[slot - (1 << top)]
            if slot == 1 and chunk == 0:
                source = after(source, sums[1])
            if slot == 3 << (levels - 2):
                source = after(source, slots[1 << (levels - 1)])
            if chunk == 1 and slot > n // 2:
                source = after(source, gathered[0][slot])
            if chunk == 0 and slot in early:
                slots.append(early[slot])
                continue
            slots.append(
                exchange(source, n, cores, levels - 1 - top, gather_orders(n, chunk))
            )
        gathered.append(slots)
    result = None
    for chunk in range(CHUNKS):
        result = combine(chunk, gathered[chunk], result and result[0], weights[chunk])
    send, keep = result
    other = lax.ppermute(send, "gy", [(0, 1), (1, 0)])
    return (keep + other.astype(jnp.float32)).astype(jnp.bfloat16)


def solution(mesh):
    return jax.shard_map(
        shards,
        mesh=mesh,
        in_specs=(
            P("groups", "gx"),
            P("gx"),
            P("gx", "gy"),
            P("gx", "gy"),
            P("gx", "gy"),
            P("gy", "gx"),
            P(("groups", "gx"), None, "gy"),
            P(("groups", "gx"), None, "gy"),
            P(("groups", "gx")),
        ),
        out_specs=P(("groups", "gy"), "gx"),
        check_vma=False,
    )
```

```python
import functools
import math

import jax
import jax.numpy as jnp
from jax import lax
from jax.experimental import pallas as pl
from jax.experimental.pallas import tpu as pltpu
from jax.sharding import PartitionSpec as P

D = 16384
HD = 128
NEW = 4
EPS = 1e-05
THETA = 500000.0

CHUNKS = 2
TILES = 2
MIB = 1 << 20


def bit_orders(n):
    levels = n.bit_length() - 1
    first = list(range(levels))
    second = list(first)
    if levels > 1:
        second[0], second[1] = second[1], second[0]
    return first, second


def gather_orders(n, chunk):
    first, second = bit_orders(n)
    return (first, second) if chunk else (first, first)


def slot_shift(slot, order):
    levels = len(order)
    shift = 0
    for stage in range(levels):
        shift |= ((slot >> (levels - 1 - stage)) & 1) << order[stage]
    return shift


def slot_owner(n, slot, gx, gy, orders):
    first, second = (slot_shift(slot, order) for order in orders)
    return gx ^ jnp.where(gy == 0, first, second)


def exchange(value, n, cores, stage, orders):
    pairs = []
    for gx in range(n):
        for gy in range(cores):
            other = gx ^ (1 << orders[gy % 2][stage])
            pairs.append((gx * cores + gy, other * cores + gy))
    return lax.ppermute(value, ("gx", "gy"), pairs)


def project_kernel(n, q_start, kv_start, first, *refs):
    if first:
        tokens_ref, gain_ref, wq_ref, wk_ref, wv_ref, send_ref, keep_ref, x_ref = refs[:8]
        t_buf, t_sems, g_buf, g_sem = refs[8:12]
    else:
        x_ref, wq_ref, wk_ref, wv_ref, send_ref, keep_ref = refs[:6]
    w_buf, sems = refs[-2:]
    half = send_ref.shape[0]
    rows = 2 * half
    with_kv = kv_start is not None
    kv = wk_ref.shape[1] // CHUNKS if with_kv else 0
    width = w_buf.shape[1]
    cols = width - 2 * kv
    pieces = 4 if cols > 1024 else 2
    tile = cols // pieces

    def w_copy(ref, start, size, at, sem):
        return pltpu.make_async_copy(
            ref.at[:, start : start + size], w_buf.at[:, at : at + size], sems.at[sem]
        )

    copies = [[w_copy(wq_ref, q_start + p * tile, tile, p * tile, p)] for p in range(pieces)]
    if with_kv:
        copies[-1].append(w_copy(wk_ref, kv_start, kv, cols, pieces))
        copies[-1].append(w_copy(wv_ref, kv_start, kv, cols + kv, pieces + 1))

    if first:
        block = rows // n
        me, gy = lax.axis_index("gx"), lax.axis_index("gy")
        t_copies = []
        for slot in range(n):
            start = pl.multiple_of(slot_owner(n, slot, me, gy, bit_orders(n)) * block, block)
            t_copies.append(
                pltpu.make_async_copy(
                    tokens_ref.at[pl.ds(start, block), :], t_buf.at[slot], t_sems.at[slot]
                )
            )
            t_copies[-1].start()
        g_copy = pltpu.make_async_copy(gain_ref, g_buf, g_sem)
        g_copy.start()
    for group in copies:
        for copy in group:
            copy.start()
    if first:
        lanes = lax.broadcasted_iota(jnp.int32, (block, 128), 1)
        g_copy.wait()
        for slot in range(n):
            t_copies[slot].wait()
            wide = t_buf[slot].astype(jnp.float32)
            x_ref[slot * block : (slot + 1) * block, :] = (wide * g_buf[...]).astype(jnp.bfloat16)
            square = jnp.sum(wide * wide, axis=1, keepdims=True)
            high = square.astype(jnp.bfloat16).astype(jnp.float32)
            rest = square - high
            middle = rest.astype(jnp.bfloat16).astype(jnp.float32)
            low = rest - middle
            packed = jnp.where(
                lanes == 3 * me,
                high,
                jnp.where(lanes == 3 * me + 1, middle, jnp.where(lanes == 3 * me + 2, low, 0.0)),
            )
            if slot < n // 2:
                keep_ref[slot * block : (slot + 1) * block, width : width + 128] = packed
            else:
                at = (slot - n // 2) * block
                send_ref[at : at + block, width : width + 128] = packed.astype(jnp.bfloat16)

    for p in range(pieces):
        start, end = p * tile, (p + 1) * tile if p < pieces - 1 else width
        for copy in copies[p]:
            copy.wait()
        product = jnp.dot(x_ref[...], w_buf[:, start:end], preferred_element_type=jnp.float32)
        keep_ref[:, start:end] = product[:half]
        send_ref[:, start:end] = product[half:].astype(jnp.bfloat16)


def in_hbm(value):
    return pltpu.with_memory_space_constraint(value, pltpu.HBM)


def project(n, q_start, q_cols, kv_start, first, x, gain, w_query, w_key, w_value):
    rows, depth = x.shape
    kv = w_key.shape[1] // CHUNKS if kv_start is not None else 0
    width = q_cols + 2 * kv
    full = width + (128 if first else 0)
    hbm = pl.BlockSpec(memory_space=pltpu.HBM)
    vmem = pl.BlockSpec(memory_space=pltpu.VMEM)
    out_shape = [
        pltpu.VMEM((rows // 2, full), jnp.bfloat16),
        pltpu.VMEM((rows // 2, full), jnp.float32),
    ]
    scratch = [pltpu.VMEM((depth, width), jnp.bfloat16), pltpu.SemaphoreType.DMA((6,))]
    if first:
        out_shape.append(pltpu.VMEM((rows, depth), jnp.bfloat16))
        args = [in_hbm(x), in_hbm(gain)]
        in_specs = [hbm, hbm]
        scratch = [
            pltpu.VMEM((n, rows // n, depth), jnp.bfloat16),
            pltpu.SemaphoreType.DMA((n,)),
            pltpu.VMEM((1, depth), jnp.float32),
            pltpu.SemaphoreType.DMA,
        ] + scratch
    else:
        args, in_specs = [x], [vmem]
    return pl.pallas_call(
        functools.partial(project_kernel, n, q_start, kv_start, first),
        out_shape=out_shape,
        in_specs=in_specs + [hbm] * 3,
        out_specs=[vmem] * len(out_shape),
        scratch_shapes=scratch,
        compiler_params=pltpu.CompilerParams(vmem_limit_bytes=16 * MIB),
        name="project",
    )(*args, in_hbm(w_query), in_hbm(w_key), in_hbm(w_value))


def attend_kernel(chunk, offsets, kv_offset, groups, heads, seqs, length_ref, *refs):
    sum_ref, square_ref = refs[:2]
    w_copies = []
    if chunk == 0:
        cos_ref, sin_ref, k_ref, v_ref, w_ref, out_ref, next_ref, q_scr, o_scr, w_sems = refs[2:]
        total = next_ref.shape[0]
        for p in range(4):
            at = slice(p * total // 4, (p + 1) * total // 4)
            w_copies.append(
                pltpu.make_async_copy(
                    w_ref.at[total + at.start : total + at.stop], next_ref.at[at], w_sems.at[p]
                )
            )
            w_copies[-1].start()
    else:
        cos_ref, sin_ref, k_ref, v_ref, out_ref, q_scr, o_scr = refs[2:]
    rows = seqs * NEW
    cols = groups * heads * HD
    kv = groups * HD
    seq_count = k_ref.shape[0]

    scale = HD**-0.5 * math.log2(math.e)
    slots = k_ref.shape[1]
    many = heads * NEW
    slot_ids = lax.broadcasted_iota(jnp.int32, (1, slots), 1)
    new_cols = lax.broadcasted_iota(jnp.int32, (many, rows), 1)
    new_rows = lax.broadcasted_iota(jnp.int32, (many, rows), 0) % NEW

    @pl.loop(0, seq_count // seqs)
    def _(step):
        mine = pl.ds(pl.multiple_of(step * rows, rows), rows)
        mean = jnp.sum(square_ref[mine, :], axis=1, keepdims=True) / D
        row_scale = lax.rsqrt(mean + EPS)
        cosine, sine = cos_ref[mine, :], sin_ref[mine, :]

        def raw(start):
            return sum_ref[mine, start : start + HD] * row_scale

        def rotary(value):
            return value * cosine + pltpu.roll(value, HD // 2, 1) * sine

        for h in range(heads * groups):
            turned = rotary(raw(offsets[h]))
            for s in range(seqs):
                q_scr[s, h * NEW : (h + 1) * NEW, :] = turned[s * NEW : (s + 1) * NEW]
        for g in range(groups):
            new_keys = rotary(raw(kv_offset + g * HD)).astype(jnp.bfloat16)
            new_values = raw(kv_offset + (groups + g) * HD).astype(jnp.bfloat16)
            lanes = slice(chunk * kv + g * HD, chunk * kv + (g + 1) * HD)
            olds, news, mixes = [], [], []
            for s in range(seqs):
                query = q_scr[s, g * many : (g + 1) * many, :].astype(jnp.bfloat16)
                keys = k_ref[step * seqs + s, :, lanes]
                olds.append(
                    lax.dot_general(
                        query, keys, (((1,), (1,)), ((), ())), preferred_element_type=jnp.float32
                    )
                )
                news.append(
                    lax.dot_general(
                        query, new_keys, (((1,), (1,)), ((), ())), preferred_element_type=jnp.float32
                    )
                )
            for s in range(seqs):
                live = slot_ids < length_ref[step * seqs + s]
                seen = (new_cols >= s * NEW) & (new_cols <= s * NEW + new_rows)
                old = jnp.where(live, olds[s] * scale, -1e30)
                new = jnp.where(seen, news[s] * scale, -1e30)
                top = jnp.maximum(
                    jnp.max(old, axis=1, keepdims=True), jnp.max(new, axis=1, keepdims=True)
                )
                old = jnp.exp2(old - top)
                new = jnp.exp2(new - top)
                total = jnp.sum(old, axis=1, keepdims=True) + jnp.sum(new, axis=1, keepdims=True)
                inverse = 1.0 / total
                olds[s] = (old * inverse).astype(jnp.bfloat16)
                news[s] = (new * inverse).astype(jnp.bfloat16)
            for s in range(seqs):
                values = v_ref[step * seqs + s, :, lanes]
                mixes.append(
                    jnp.dot(olds[s], values, preferred_element_type=jnp.float32)
                    + jnp.dot(news[s], new_values, preferred_element_type=jnp.float32)
                )
            for s in range(seqs):
                for h in range(heads):
                    at = (g * heads + h) * HD
                    o_scr[s * NEW : (s + 1) * NEW, at : at + HD] = mixes[s][
                        h * NEW : (h + 1) * NEW
                    ]
        out_ref[mine, :] = o_scr[...].astype(jnp.bfloat16)

    for copy in w_copies:
        copy.wait()


def attend(chunk, offsets, kv_offset, sums, squares, cosine, sine, cache_keys, cache_values, lengths, w_out):
    seq_count, slots, kv_all = cache_keys.shape
    kv = kv_all // CHUNKS
    groups = kv // HD
    heads = len(offsets) // groups
    cols = len(offsets) * HD
    seqs = min(4, seq_count)
    rows = seq_count * NEW
    source, copied = [], []
    if chunk == 0:
        source.append(in_hbm(w_out))
        copied.append(pltpu.VMEM((w_out.shape[0] // CHUNKS, w_out.shape[1]), w_out.dtype))
    vmem = pl.BlockSpec(memory_space=pltpu.VMEM)
    hbm = pl.BlockSpec(memory_space=pltpu.HBM)
    return pl.pallas_call(
        functools.partial(attend_kernel, chunk, offsets, kv_offset, groups, heads, seqs),
        out_shape=[pltpu.VMEM((rows, cols), jnp.bfloat16)] + copied,
        in_specs=[pl.BlockSpec(memory_space=pltpu.SMEM)] + [vmem] * 6 + [hbm] * len(source),
        out_specs=[vmem] * (1 + len(copied)),
        scratch_shapes=[
            pltpu.VMEM((seqs, groups * heads * NEW, HD), jnp.float32),
            pltpu.VMEM((seqs * NEW, cols), jnp.float32),
        ]
        + [pltpu.SemaphoreType.DMA((4,))] * len(copied),
        compiler_params=pltpu.CompilerParams(vmem_limit_bytes=16 * MIB),
        name="attend",
    )(lengths, sums, squares, cosine, sine, cache_keys, cache_values, *source)


def fetch_kernel(count, pieces, *refs):
    sources, targets, sems = refs[:count], refs[count : 2 * count], refs[2 * count]
    copies = []
    for i, (source, target) in enumerate(zip(sources, targets)):
        size = target.shape[0] // pieces
        for p in range(pieces):
            at = slice(p * size, (p + 1) * size)
            copies.append(
                pltpu.make_async_copy(source.at[at], target.at[at], sems.at[i * pieces + p])
            )
    for copy in copies:
        copy.start()
    for copy in copies:
        copy.wait()


def fetch(*arrays):
    pieces = 4
    return pl.pallas_call(
        functools.partial(fetch_kernel, len(arrays), pieces),
        out_shape=[pltpu.VMEM(array.shape, array.dtype) for array in arrays],
        in_specs=[pl.BlockSpec(memory_space=pltpu.HBM)] * len(arrays),
        out_specs=[pl.BlockSpec(memory_space=pltpu.VMEM)] * len(arrays),
        scratch_shapes=[pltpu.SemaphoreType.DMA((pieces * len(arrays),))],
        compiler_params=pltpu.CompilerParams(vmem_limit_bytes=4 * MIB),
        name="fetch",
    )(*[in_hbm(array) for array in arrays])


def fetch_rows_kernel(start, pieces, source, target, sems):
    size = target.shape[0] // pieces
    copies = [
        pltpu.make_async_copy(
            source.at[start + p * size : start + (p + 1) * size],
            target.at[p * size : (p + 1) * size],
            sems.at[p],
        )
        for p in range(pieces)
    ]
    for copy in copies:
        copy.start()
    for copy in copies:
        copy.wait()


def fetch_rows(array, start, rows):
    pieces = 4
    return pl.pallas_call(
        functools.partial(fetch_rows_kernel, start, pieces),
        out_shape=pltpu.VMEM((rows, array.shape[1]), array.dtype),
        in_specs=[pl.BlockSpec(memory_space=pltpu.HBM)],
        out_specs=pl.BlockSpec(memory_space=pltpu.VMEM),
        scratch_shapes=[pltpu.SemaphoreType.DMA((pieces,))],
        compiler_params=pltpu.CompilerParams(vmem_limit_bytes=4 * MIB),
        name="fetch_rows",
    )(in_hbm(array))


def combine_kernel(n, block, chunk, *refs):
    pieces, refs = refs[:n], refs[n:]
    gx, gy = lax.axis_index("gx"), lax.axis_index("gy")
    moved = jnp.where(gy == 0, n // 2, 0)
    if chunk:
        before_ref, refs = refs[0], refs[1:]
    w_ref, outs, x_buf = refs[0], refs[1:-1], refs[-1]
    depth, cols = x_buf.shape[1], w_ref.shape[1]
    half = x_buf.shape[0] // 2
    for slot, piece in enumerate(pieces):
        start = pl.multiple_of((slot_owner(n, slot, gx, gy, gather_orders(n, chunk)) ^ moved) * block, block)
        x_buf[pl.ds(start, block), :] = piece[...]

    tile = cols // TILES
    for start in range(0, cols, tile):
        at = slice(start, start + tile)
        product = jnp.dot(x_buf[...], w_ref[:, at], preferred_element_type=jnp.float32)
        if chunk:
            product = product + before_ref[:, at]
        if len(outs) == 1:
            outs[0][:, at] = product
        else:
            outs[0][:, at] = product[:half].astype(jnp.bfloat16)
            outs[1][:, at] = product[half:]


def combine(chunk, pieces, before, w_out):
    n, (block, depth) = len(pieces), pieces[0].shape
    rows = n * block
    cols = w_out.shape[1]
    last = chunk == CHUNKS - 1
    hbm = pl.BlockSpec(memory_space=pltpu.HBM)
    vmem = pl.BlockSpec(memory_space=pltpu.VMEM)
    if last:
        out_shape = [
            pltpu.VMEM((rows // 2, cols), jnp.bfloat16),
            pltpu.VMEM((rows // 2, cols), jnp.float32),
        ]
    else:
        out_shape = [pltpu.VMEM((rows, cols), jnp.float32)]
    earlier = [] if chunk == 0 else [before]
    return pl.pallas_call(
        functools.partial(combine_kernel, n, block, chunk),
        out_shape=out_shape,
        in_specs=[vmem] * (len(pieces) + len(earlier) + 1),
        out_specs=[vmem] * len(out_shape),
        scratch_shapes=[
            pltpu.VMEM((rows, depth), jnp.bfloat16),
        ],
        compiler_params=pltpu.CompilerParams(vmem_limit_bytes=16 * MIB),
        name="combine",
    )(*pieces, *earlier, w_out)


def shards(
    tokens, norm_gain, w_query, w_key, w_value, w_out, cache_keys, cache_values, cache_lengths
):
    n = lax.axis_size("gx")
    cores = lax.axis_size("gy")
    levels = n.bit_length() - 1
    position = (cache_lengths[:, None] + jnp.arange(NEW, dtype=jnp.int32)[None, :]).reshape(-1)
    inverse = THETA ** (-2.0 * jnp.arange(HD // 2, dtype=jnp.float32) / HD)
    angles = position.astype(jnp.float32)[:, None] * inverse[None, :]
    cosine, sine = jnp.cos(angles), jnp.sin(angles)
    cosine = jnp.concatenate([cosine, cosine], axis=1)
    sine = jnp.concatenate([-sine, sine], axis=1)

    x, gain = tokens, norm_gain[None, :]
    kv = w_key.shape[1] // CHUNKS
    q_cols = w_query.shape[1] // CHUNKS

    def column_part(start, size, kv_start):
        return project(
            n, start, size, kv_start, start == 0, x, gain, w_query, w_key, w_value
        )

    def after(value, *earlier):
        return lax.optimization_barrier((value, earlier))[0]

    share = q_cols // 2
    orders = bit_orders(n)
    send_a, keep_a, x = column_part(0, share, None)
    x = after(x, send_a)
    other_a = exchange(send_a, n, cores, 0, orders)
    send_b, keep_b = column_part(share, share, 0)
    x = after(x, send_b)
    other_b = exchange(send_b, n, cores, 0, orders)
    sum_a = keep_a + other_a.astype(jnp.float32)
    x = after(x, sum_a)
    later = []
    for chunk in range(1, CHUNKS):
        later.append(column_part(chunk * q_cols, q_cols, chunk * kv))
    other_b = after(other_b, *(send_c for send_c, _ in later))
    first = jnp.concatenate([sum_a, keep_b + other_b.astype(jnp.float32)], axis=1)
    half = first.shape[0] // 2
    send = first[half:].astype(jnp.bfloat16)
    flows = [[1, first[:half], send]]
    for send_c, keep_c in later:
        flows.append([0, keep_c, after(send_c, flows[-1][2])])

    def start(flow):
        return exchange(flow[2], n, cores, flow[0], orders)

    def finish(flow, other, *earlier):
        stage, keep, _ = flow
        if earlier:
            other = after(other, *earlier)
        value = keep + other.astype(jnp.float32)
        low = value.shape[0] // 2 if stage < levels - 1 else 0
        flow[:] = stage + 1, value[:low] if low else value, value[low:].astype(jnp.bfloat16)

    lead, follow = flows
    w_rows = w_out.shape[0] // CHUNKS
    weights = [fetch_rows(after(w_out, lead[2], follow[2]), 0, w_rows)]
    while follow[0] < levels:
        pending = [start(flow) for flow in flows if flow[0] < levels]
        if lead[0] == levels:
            finish(follow, pending[0])
        elif lead[0] == levels - 1:
            cache_keys, cache_values = fetch(*after((cache_keys, cache_values), follow[2]))
            finish(lead, pending[0], cache_keys, cache_values)
            finish(follow, pending[1], lead[1])
        else:
            finish(lead, pending[0], *weights)
            finish(follow, pending[1], lead[2])
    sums = [flow[1] for flow in flows]
    squares = sums[0][:, share : share + 128]
    plain = [h * HD for h in range(q_cols // HD)]
    offsets = [[at if at < share else at + 128 for at in plain], plain]
    kv_offsets = [q_cols + 128, q_cols]

    attentions = []
    for chunk in range(CHUNKS):
        out = attend(
            chunk,
            offsets[chunk],
            kv_offsets[chunk],
            sums[chunk],
            squares,
            cosine,
            sine,
            cache_keys,
            cache_values,
            cache_lengths,
            w_out,
        )
        attentions.append(out[0])
        weights += out[1:]
    gathered = []
    for chunk in range(CHUNKS):
        slots = [attentions[chunk]]
        for slot in range(1, n):
            top = slot.bit_length() - 1
            source = slots[slot - (1 << top)]
            if slot == 1 and chunk == 0:
                source = after(source, sums[1])
            if slot == 3 << (levels - 2):
                source = after(source, slots[1 << (levels - 1)])
            slots.append(
                exchange(source, n, cores, levels - 1 - top, gather_orders(n, chunk))
            )
        gathered.append(slots)
    result = None
    for chunk in range(CHUNKS):
        result = combine(chunk, gathered[chunk], result and result[0], weights[chunk])
    send, keep = result
    other = lax.ppermute(send, "gy", [(0, 1), (1, 0)])
    return (keep + other.astype(jnp.float32)).astype(jnp.bfloat16)


def solution(mesh):
    return jax.shard_map(
        shards,
        mesh=mesh,
        in_specs=(
            P("groups", "gx"),
            P("gx"),
            P("gx", "gy"),
            P("gx", "gy"),
            P("gx", "gy"),
            P("gy", "gx"),
            P(("groups", "gx"), None, "gy"),
            P(("groups", "gx"), None, "gy"),
            P(("groups", "gx")),
        ),
        out_specs=P(("groups", "gy"), "gx"),
        check_vma=False,
    )
```

```python
import functools
import math

import jax
import jax.numpy as jnp
from jax import lax
from jax.experimental import pallas as pl
from jax.experimental.pallas import tpu as pltpu
from jax.sharding import PartitionSpec as P

D = 16384
HD = 128
NEW = 4
EPS = 1e-05
THETA = 500000.0

CHUNKS = 2
TILES = 2
MIB = 1 << 20


def bit_orders(n):
    levels = n.bit_length() - 1
    first = list(range(levels))
    second = list(first)
    if levels > 1:
        second[0], second[1] = second[1], second[0]
    return first, second


def gather_orders(n, chunk):
    first, second = bit_orders(n)
    return (first, second) if chunk else (first, first)


def slot_shift(slot, order):
    levels = len(order)
    shift = 0
    for stage in range(levels):
        shift |= ((slot >> (levels - 1 - stage)) & 1) << order[stage]
    return shift


def slot_owner(n, slot, gx, gy, orders):
    first, second = (slot_shift(slot, order) for order in orders)
    return gx ^ jnp.where(gy == 0, first, second)


def exchange(value, n, cores, stage, orders):
    pairs = []
    for gx in range(n):
        for gy in range(cores):
            other = gx ^ (1 << orders[gy % 2][stage])
            pairs.append((gx * cores + gy, other * cores + gy))
    return lax.ppermute(value, ("gx", "gy"), pairs)


def project_kernel(n, q_start, kv_start, first, *refs):
    if first:
        tokens_ref, gain_ref, wq_ref, wk_ref, wv_ref, send_ref, keep_ref, x_ref = refs[:8]
        t_buf, t_sems, g_buf, g_sem = refs[8:12]
    else:
        x_ref, wq_ref, wk_ref, wv_ref, send_ref, keep_ref = refs[:6]
    w_buf, sems = refs[-2:]
    half = send_ref.shape[0]
    rows = 2 * half
    with_kv = kv_start is not None
    kv = wk_ref.shape[1] // CHUNKS if with_kv else 0
    width = w_buf.shape[1]
    cols = width - 2 * kv
    pieces = 4 if cols > 1024 else 2
    tile = cols // pieces

    def w_copy(ref, start, size, at, sem):
        return pltpu.make_async_copy(
            ref.at[:, start : start + size], w_buf.at[:, at : at + size], sems.at[sem]
        )

    copies = [[w_copy(wq_ref, q_start + p * tile, tile, p * tile, p)] for p in range(pieces)]
    if with_kv:
        copies[-1].append(w_copy(wk_ref, kv_start, kv, cols, pieces))
        copies[-1].append(w_copy(wv_ref, kv_start, kv, cols + kv, pieces + 1))

    if first:
        block = rows // n
        me, gy = lax.axis_index("gx"), lax.axis_index("gy")
        t_copies = []
        for slot in range(n):
            start = pl.multiple_of(slot_owner(n, slot, me, gy, bit_orders(n)) * block, block)
            t_copies.append(
                pltpu.make_async_copy(
                    tokens_ref.at[pl.ds(start, block), :], t_buf.at[slot], t_sems.at[slot]
                )
            )
            t_copies[-1].start()
        g_copy = pltpu.make_async_copy(gain_ref, g_buf, g_sem)
        g_copy.start()
    for group in copies:
        for copy in group:
            copy.start()
    if first:
        lanes = lax.broadcasted_iota(jnp.int32, (block, 128), 1)
        g_copy.wait()
        for slot in range(n):
            t_copies[slot].wait()
            wide = t_buf[slot].astype(jnp.float32)
            x_ref[slot * block : (slot + 1) * block, :] = (wide * g_buf[...]).astype(jnp.bfloat16)
            square = jnp.sum(wide * wide, axis=1, keepdims=True)
            high = square.astype(jnp.bfloat16).astype(jnp.float32)
            rest = square - high
            middle = rest.astype(jnp.bfloat16).astype(jnp.float32)
            low = rest - middle
            packed = jnp.where(
                lanes == 3 * me,
                high,
                jnp.where(lanes == 3 * me + 1, middle, jnp.where(lanes == 3 * me + 2, low, 0.0)),
            )
            if slot < n // 2:
                keep_ref[slot * block : (slot + 1) * block, width : width + 128] = packed
            else:
                at = (slot - n // 2) * block
                send_ref[at : at + block, width : width + 128] = packed.astype(jnp.bfloat16)

    for p in range(pieces):
        start, end = p * tile, (p + 1) * tile if p < pieces - 1 else width
        for copy in copies[p]:
            copy.wait()
        product = jnp.dot(x_ref[...], w_buf[:, start:end], preferred_element_type=jnp.float32)
        keep_ref[:, start:end] = product[:half]
        send_ref[:, start:end] = product[half:].astype(jnp.bfloat16)


def in_hbm(value):
    return pltpu.with_memory_space_constraint(value, pltpu.HBM)


def project(n, q_start, q_cols, kv_start, first, x, gain, w_query, w_key, w_value):
    rows, depth = x.shape
    kv = w_key.shape[1] // CHUNKS if kv_start is not None else 0
    width = q_cols + 2 * kv
    full = width + (128 if first else 0)
    hbm = pl.BlockSpec(memory_space=pltpu.HBM)
    vmem = pl.BlockSpec(memory_space=pltpu.VMEM)
    out_shape = [
        pltpu.VMEM((rows // 2, full), jnp.bfloat16),
        pltpu.VMEM((rows // 2, full), jnp.float32),
    ]
    scratch = [pltpu.VMEM((depth, width), jnp.bfloat16), pltpu.SemaphoreType.DMA((6,))]
    if first:
        out_shape.append(pltpu.VMEM((rows, depth), jnp.bfloat16))
        args = [in_hbm(x), in_hbm(gain)]
        in_specs = [hbm, hbm]
        scratch = [
            pltpu.VMEM((n, rows // n, depth), jnp.bfloat16),
            pltpu.SemaphoreType.DMA((n,)),
            pltpu.VMEM((1, depth), jnp.float32),
            pltpu.SemaphoreType.DMA,
        ] + scratch
    else:
        args, in_specs = [x], [vmem]
    return pl.pallas_call(
        functools.partial(project_kernel, n, q_start, kv_start, first),
        out_shape=out_shape,
        in_specs=in_specs + [hbm] * 3,
        out_specs=[vmem] * len(out_shape),
        scratch_shapes=scratch,
        compiler_params=pltpu.CompilerParams(vmem_limit_bytes=16 * MIB),
        name="project",
    )(*args, in_hbm(w_query), in_hbm(w_key), in_hbm(w_value))


def attend_kernel(chunk, offsets, kv_offset, groups, heads, seqs, length_ref, *refs):
    sum_ref, square_ref = refs[:2]
    w_copies = []
    if chunk == 0:
        cos_ref, sin_ref, k_ref, v_ref, w_ref, out_ref, next_ref, q_scr, o_scr, w_sems = refs[2:]
        total = next_ref.shape[0]
        for p in range(4):
            at = slice(p * total // 4, (p + 1) * total // 4)
            w_copies.append(
                pltpu.make_async_copy(
                    w_ref.at[total + at.start : total + at.stop], next_ref.at[at], w_sems.at[p]
                )
            )
            w_copies[-1].start()
    else:
        cos_ref, sin_ref, k_ref, v_ref, out_ref, q_scr, o_scr = refs[2:]
    rows = seqs * NEW
    cols = groups * heads * HD
    kv = groups * HD
    seq_count = k_ref.shape[0]

    scale = HD**-0.5 * math.log2(math.e)
    slots = k_ref.shape[1]
    many = heads * NEW
    slot_ids = lax.broadcasted_iota(jnp.int32, (1, slots), 1)
    new_cols = lax.broadcasted_iota(jnp.int32, (many, rows), 1)
    new_rows = lax.broadcasted_iota(jnp.int32, (many, rows), 0) % NEW

    @pl.loop(0, seq_count // seqs)
    def _(step):
        mine = pl.ds(pl.multiple_of(step * rows, rows), rows)
        mean = jnp.sum(square_ref[mine, :], axis=1, keepdims=True) / D
        row_scale = lax.rsqrt(mean + EPS)
        cosine, sine = cos_ref[mine, :], sin_ref[mine, :]

        def raw(start):
            return sum_ref[mine, start : start + HD] * row_scale

        def rotary(value):
            return value * cosine + pltpu.roll(value, HD // 2, 1) * sine

        for h in range(heads * groups):
            turned = rotary(raw(offsets[h]))
            for s in range(seqs):
                q_scr[s, h * NEW : (h + 1) * NEW, :] = turned[s * NEW : (s + 1) * NEW]
        for g in range(groups):
            new_keys = rotary(raw(kv_offset + g * HD)).astype(jnp.bfloat16)
            new_values = raw(kv_offset + (groups + g) * HD).astype(jnp.bfloat16)
            lanes = slice(chunk * kv + g * HD, chunk * kv + (g + 1) * HD)
            olds, news, mixes = [], [], []
            for s in range(seqs):
                query = q_scr[s, g * many : (g + 1) * many, :].astype(jnp.bfloat16)
                keys = k_ref[step * seqs + s, :, lanes]
                olds.append(
                    lax.dot_general(
                        query, keys, (((1,), (1,)), ((), ())), preferred_element_type=jnp.float32
                    )
                )
                news.append(
                    lax.dot_general(
                        query, new_keys, (((1,), (1,)), ((), ())), preferred_element_type=jnp.float32
                    )
                )
            for s in range(seqs):
                live = slot_ids < length_ref[step * seqs + s]
                seen = (new_cols >= s * NEW) & (new_cols <= s * NEW + new_rows)
                old = jnp.where(live, olds[s] * scale, -1e30)
                new = jnp.where(seen, news[s] * scale, -1e30)
                top = jnp.maximum(
                    jnp.max(old, axis=1, keepdims=True), jnp.max(new, axis=1, keepdims=True)
                )
                old = jnp.exp2(old - top)
                new = jnp.exp2(new - top)
                total = jnp.sum(old, axis=1, keepdims=True) + jnp.sum(new, axis=1, keepdims=True)
                inverse = 1.0 / total
                olds[s] = (old * inverse).astype(jnp.bfloat16)
                news[s] = (new * inverse).astype(jnp.bfloat16)
            for s in range(seqs):
                values = v_ref[step * seqs + s, :, lanes]
                mixes.append(
                    jnp.dot(olds[s], values, preferred_element_type=jnp.float32)
                    + jnp.dot(news[s], new_values, preferred_element_type=jnp.float32)
                )
            for s in range(seqs):
                for h in range(heads):
                    at = (g * heads + h) * HD
                    o_scr[s * NEW : (s + 1) * NEW, at : at + HD] = mixes[s][
                        h * NEW : (h + 1) * NEW
                    ]
        out_ref[mine, :] = o_scr[...].astype(jnp.bfloat16)

    for copy in w_copies:
        copy.wait()


def attend(chunk, offsets, kv_offset, sums, squares, cosine, sine, cache_keys, cache_values, lengths, w_out):
    seq_count, slots, kv_all = cache_keys.shape
    kv = kv_all // CHUNKS
    groups = kv // HD
    heads = len(offsets) // groups
    cols = len(offsets) * HD
    seqs = min(4, seq_count)
    rows = seq_count * NEW
    source, copied = [], []
    if chunk == 0:
        source.append(in_hbm(w_out))
        copied.append(pltpu.VMEM((w_out.shape[0] // CHUNKS, w_out.shape[1]), w_out.dtype))
    vmem = pl.BlockSpec(memory_space=pltpu.VMEM)
    hbm = pl.BlockSpec(memory_space=pltpu.HBM)
    return pl.pallas_call(
        functools.partial(attend_kernel, chunk, offsets, kv_offset, groups, heads, seqs),
        out_shape=[pltpu.VMEM((rows, cols), jnp.bfloat16)] + copied,
        in_specs=[pl.BlockSpec(memory_space=pltpu.SMEM)] + [vmem] * 6 + [hbm] * len(source),
        out_specs=[vmem] * (1 + len(copied)),
        scratch_shapes=[
            pltpu.VMEM((seqs, groups * heads * NEW, HD), jnp.float32),
            pltpu.VMEM((seqs * NEW, cols), jnp.float32),
        ]
        + [pltpu.SemaphoreType.DMA((4,))] * len(copied),
        compiler_params=pltpu.CompilerParams(vmem_limit_bytes=16 * MIB),
        name="attend",
    )(lengths, sums, squares, cosine, sine, cache_keys, cache_values, *source)


def fetch_kernel(count, pieces, *refs):
    sources, targets, sems = refs[:count], refs[count : 2 * count], refs[2 * count]
    copies = []
    for i, (source, target) in enumerate(zip(sources, targets)):
        size = target.shape[0] // pieces
        for p in range(pieces):
            at = slice(p * size, (p + 1) * size)
            copies.append(
                pltpu.make_async_copy(source.at[at], target.at[at], sems.at[i * pieces + p])
            )
    for copy in copies:
        copy.start()
    for copy in copies:
        copy.wait()


def fetch(*arrays):
    pieces = 4
    return pl.pallas_call(
        functools.partial(fetch_kernel, len(arrays), pieces),
        out_shape=[pltpu.VMEM(array.shape, array.dtype) for array in arrays],
        in_specs=[pl.BlockSpec(memory_space=pltpu.HBM)] * len(arrays),
        out_specs=[pl.BlockSpec(memory_space=pltpu.VMEM)] * len(arrays),
        scratch_shapes=[pltpu.SemaphoreType.DMA((pieces * len(arrays),))],
        compiler_params=pltpu.CompilerParams(vmem_limit_bytes=4 * MIB),
        name="fetch",
    )(*[in_hbm(array) for array in arrays])


def fetch_rows_kernel(start, pieces, source, target, sems):
    size = target.shape[0] // pieces
    copies = [
        pltpu.make_async_copy(
            source.at[start + p * size : start + (p + 1) * size],
            target.at[p * size : (p + 1) * size],
            sems.at[p],
        )
        for p in range(pieces)
    ]
    for copy in copies:
        copy.start()
    for copy in copies:
        copy.wait()


def fetch_rows(array, start, rows):
    pieces = 4
    return pl.pallas_call(
        functools.partial(fetch_rows_kernel, start, pieces),
        out_shape=pltpu.VMEM((rows, array.shape[1]), array.dtype),
        in_specs=[pl.BlockSpec(memory_space=pltpu.HBM)],
        out_specs=pl.BlockSpec(memory_space=pltpu.VMEM),
        scratch_shapes=[pltpu.SemaphoreType.DMA((pieces,))],
        compiler_params=pltpu.CompilerParams(vmem_limit_bytes=4 * MIB),
        name="fetch_rows",
    )(in_hbm(array))


def combine_kernel(n, block, chunk, *refs):
    pieces, refs = refs[:n], refs[n:]
    gx, gy = lax.axis_index("gx"), lax.axis_index("gy")
    moved = jnp.where(gy == 0, n // 2, 0)
    if chunk:
        before_ref, refs = refs[0], refs[1:]
    w_ref, outs, x_buf = refs[0], refs[1:-1], refs[-1]
    depth, cols = x_buf.shape[1], w_ref.shape[1]
    half = x_buf.shape[0] // 2
    for slot, piece in enumerate(pieces):
        start = pl.multiple_of((slot_owner(n, slot, gx, gy, gather_orders(n, chunk)) ^ moved) * block, block)
        x_buf[pl.ds(start, block), :] = piece[...]

    tile = cols // TILES
    for start in range(0, cols, tile):
        at = slice(start, start + tile)
        product = jnp.dot(x_buf[...], w_ref[:, at], preferred_element_type=jnp.float32)
        if chunk:
            product = product + before_ref[:, at]
        if len(outs) == 1:
            outs[0][:, at] = product
        else:
            outs[0][:, at] = product[:half].astype(jnp.bfloat16)
            outs[1][:, at] = product[half:]


def combine(chunk, pieces, before, w_out):
    n, (block, depth) = len(pieces), pieces[0].shape
    rows = n * block
    cols = w_out.shape[1]
    last = chunk == CHUNKS - 1
    hbm = pl.BlockSpec(memory_space=pltpu.HBM)
    vmem = pl.BlockSpec(memory_space=pltpu.VMEM)
    if last:
        out_shape = [
            pltpu.VMEM((rows // 2, cols), jnp.bfloat16),
            pltpu.VMEM((rows // 2, cols), jnp.float32),
        ]
    else:
        out_shape = [pltpu.VMEM((rows, cols), jnp.float32)]
    earlier = [] if chunk == 0 else [before]
    return pl.pallas_call(
        functools.partial(combine_kernel, n, block, chunk),
        out_shape=out_shape,
        in_specs=[vmem] * (len(pieces) + len(earlier) + 1),
        out_specs=[vmem] * len(out_shape),
        scratch_shapes=[
            pltpu.VMEM((rows, depth), jnp.bfloat16),
        ],
        compiler_params=pltpu.CompilerParams(vmem_limit_bytes=16 * MIB),
        name="combine",
    )(*pieces, *earlier, w_out)


def shards(
    tokens, norm_gain, w_query, w_key, w_value, w_out, cache_keys, cache_values, cache_lengths
):
    n = lax.axis_size("gx")
    cores = lax.axis_size("gy")
    levels = n.bit_length() - 1
    position = (cache_lengths[:, None] + jnp.arange(NEW, dtype=jnp.int32)[None, :]).reshape(-1)
    inverse = THETA ** (-2.0 * jnp.arange(HD // 2, dtype=jnp.float32) / HD)
    angles = position.astype(jnp.float32)[:, None] * inverse[None, :]
    cosine, sine = jnp.cos(angles), jnp.sin(angles)
    cosine = jnp.concatenate([cosine, cosine], axis=1)
    sine = jnp.concatenate([-sine, sine], axis=1)

    x, gain = tokens, norm_gain[None, :]
    kv = w_key.shape[1] // CHUNKS
    q_cols = w_query.shape[1] // CHUNKS

    def column_part(start, size, kv_start):
        return project(
            n, start, size, kv_start, start == 0, x, gain, w_query, w_key, w_value
        )

    def after(value, *earlier):
        return lax.optimization_barrier((value, earlier))[0]

    share = q_cols // 2
    orders = bit_orders(n)
    send_a, keep_a, x = column_part(0, share, None)
    x = after(x, send_a)
    other_a = exchange(send_a, n, cores, 0, orders)
    send_b, keep_b = column_part(share, share, 0)
    x = after(x, send_b)
    other_b = exchange(send_b, n, cores, 0, orders)
    sum_a = keep_a + other_a.astype(jnp.float32)
    x = after(x, sum_a)
    later = []
    for chunk in range(1, CHUNKS):
        later.append(column_part(chunk * q_cols, q_cols, chunk * kv))
    other_b = after(other_b, *(send_c for send_c, _ in later))
    first = jnp.concatenate([sum_a, keep_b + other_b.astype(jnp.float32)], axis=1)
    half = first.shape[0] // 2
    send = first[half:].astype(jnp.bfloat16)
    flows = [[1, first[:half], send]]
    for send_c, keep_c in later:
        flows.append([0, keep_c, after(send_c, flows[-1][2])])

    def start(flow):
        return exchange(flow[2], n, cores, flow[0], orders)

    def finish(flow, other, *earlier):
        stage, keep, _ = flow
        if earlier:
            other = after(other, *earlier)
        value = keep + other.astype(jnp.float32)
        low = value.shape[0] // 2 if stage < levels - 1 else 0
        flow[:] = stage + 1, value[:low] if low else value, value[low:].astype(jnp.bfloat16)

    lead, follow = flows
    w_rows = w_out.shape[0] // CHUNKS
    weights = [fetch_rows(after(w_out, lead[2], follow[2]), 0, w_rows)]
    follow[2] = after(follow[2], weights[0])
    while follow[0] < levels:
        pending = [start(flow) for flow in flows if flow[0] < levels]
        if lead[0] == levels:
            finish(follow, pending[0])
        elif lead[0] == levels - 1:
            cache_keys, cache_values = fetch(*after((cache_keys, cache_values), follow[2]))
            finish(lead, pending[0], cache_keys, cache_values)
            finish(follow, pending[1], lead[1])
        else:
            finish(lead, pending[0], *weights)
            finish(follow, pending[1], lead[2])
    sums = [flow[1] for flow in flows]
    squares = sums[0][:, share : share + 128]
    plain = [h * HD for h in range(q_cols // HD)]
    offsets = [[at if at < share else at + 128 for at in plain], plain]
    kv_offsets = [q_cols + 128, q_cols]

    attentions = []
    for chunk in range(CHUNKS):
        out = attend(
            chunk,
            offsets[chunk],
            kv_offsets[chunk],
            sums[chunk],
            squares,
            cosine,
            sine,
            cache_keys,
            cache_values,
            cache_lengths,
            w_out,
        )
        attentions.append(out[0])
        weights += out[1:]
    gathered = []
    for chunk in range(CHUNKS):
        slots = [attentions[chunk]]
        for slot in range(1, n):
            top = slot.bit_length() - 1
            source = slots[slot - (1 << top)]
            if slot == 1 and chunk == 0:
                source = after(source, sums[1])
            if slot == 3 << (levels - 2):
                source = after(source, slots[1 << (levels - 1)])
            slots.append(
                exchange(source, n, cores, levels - 1 - top, gather_orders(n, chunk))
            )
        gathered.append(slots)
    result = None
    for chunk in range(CHUNKS):
        result = combine(chunk, gathered[chunk], result and result[0], weights[chunk])
    send, keep = result
    other = lax.ppermute(send, "gy", [(0, 1), (1, 0)])
    return (keep + other.astype(jnp.float32)).astype(jnp.bfloat16)


def solution(mesh):
    return jax.shard_map(
        shards,
        mesh=mesh,
        in_specs=(
            P("groups", "gx"),
            P("gx"),
            P("gx", "gy"),
            P("gx", "gy"),
            P("gx", "gy"),
            P("gy", "gx"),
            P(("groups", "gx"), None, "gy"),
            P(("groups", "gx"), None, "gy"),
            P(("groups", "gx")),
        ),
        out_specs=P(("groups", "gy"), "gx"),
        check_vma=False,
    )
```

```python
import functools
import math

import jax
import jax.numpy as jnp
from jax import lax
from jax.experimental import pallas as pl
from jax.experimental.pallas import tpu as pltpu
from jax.sharding import PartitionSpec as P

D = 16384
HD = 128
NEW = 4
EPS = 1e-05
THETA = 500000.0

CHUNKS = 2
TILES = 2
MIB = 1 << 20


def bit_orders(n):
    levels = n.bit_length() - 1
    first = list(range(levels))
    second = list(first)
    if levels > 1:
        second[0], second[1] = second[1], second[0]
    return first, second


def gather_orders(n, chunk):
    first, second = bit_orders(n)
    return (second, first) if chunk else (first, first)


def slot_shift(slot, order):
    levels = len(order)
    shift = 0
    for stage in range(levels):
        shift |= ((slot >> (levels - 1 - stage)) & 1) << order[stage]
    return shift


def slot_owner(n, slot, gx, gy, orders):
    first, second = (slot_shift(slot, order) for order in orders)
    return gx ^ jnp.where(gy == 0, first, second)


def exchange(value, n, cores, stage, orders):
    pairs = []
    for gx in range(n):
        for gy in range(cores):
            other = gx ^ (1 << orders[gy % 2][stage])
            pairs.append((gx * cores + gy, other * cores + gy))
    return lax.ppermute(value, ("gx", "gy"), pairs)


def project_kernel(n, q_start, kv_start, first, *refs):
    if first:
        tokens_ref, gain_ref, wq_ref, wk_ref, wv_ref, send_ref, keep_ref, x_ref = refs[:8]
        t_buf, t_sems, g_buf, g_sem = refs[8:12]
    else:
        x_ref, wq_ref, wk_ref, wv_ref, send_ref, keep_ref = refs[:6]
    w_buf, sems = refs[-2:]
    half = send_ref.shape[0]
    rows = 2 * half
    with_kv = kv_start is not None
    kv = wk_ref.shape[1] // CHUNKS if with_kv else 0
    width = w_buf.shape[1]
    cols = width - 2 * kv
    pieces = 4 if cols > 1024 else 2
    tile = cols // pieces

    def w_copy(ref, start, size, at, sem):
        return pltpu.make_async_copy(
            ref.at[:, start : start + size], w_buf.at[:, at : at + size], sems.at[sem]
        )

    copies = [[w_copy(wq_ref, q_start + p * tile, tile, p * tile, p)] for p in range(pieces)]
    if with_kv:
        copies[-1].append(w_copy(wk_ref, kv_start, kv, cols, pieces))
        copies[-1].append(w_copy(wv_ref, kv_start, kv, cols + kv, pieces + 1))

    if first:
        block = rows // n
        me, gy = lax.axis_index("gx"), lax.axis_index("gy")
        t_copies = []
        for slot in range(n):
            start = pl.multiple_of(slot_owner(n, slot, me, gy, bit_orders(n)) * block, block)
            t_copies.append(
                pltpu.make_async_copy(
                    tokens_ref.at[pl.ds(start, block), :], t_buf.at[slot], t_sems.at[slot]
                )
            )
            t_copies[-1].start()
        g_copy = pltpu.make_async_copy(gain_ref, g_buf, g_sem)
        g_copy.start()
    for group in copies:
        for copy in group:
            copy.start()
    if first:
        lanes = lax.broadcasted_iota(jnp.int32, (block, 128), 1)
        g_copy.wait()
        for slot in range(n):
            t_copies[slot].wait()
            wide = t_buf[slot].astype(jnp.float32)
            x_ref[slot * block : (slot + 1) * block, :] = (wide * g_buf[...]).astype(jnp.bfloat16)
            square = jnp.sum(wide * wide, axis=1, keepdims=True)
            high = square.astype(jnp.bfloat16).astype(jnp.float32)
            rest = square - high
            middle = rest.astype(jnp.bfloat16).astype(jnp.float32)
            low = rest - middle
            packed = jnp.where(
                lanes == 3 * me,
                high,
                jnp.where(lanes == 3 * me + 1, middle, jnp.where(lanes == 3 * me + 2, low, 0.0)),
            )
            if slot < n // 2:
                keep_ref[slot * block : (slot + 1) * block, width : width + 128] = packed
            else:
                at = (slot - n // 2) * block
                send_ref[at : at + block, width : width + 128] = packed.astype(jnp.bfloat16)

    for p in range(pieces):
        start, end = p * tile, (p + 1) * tile if p < pieces - 1 else width
        for copy in copies[p]:
            copy.wait()
        product = jnp.dot(x_ref[...], w_buf[:, start:end], preferred_element_type=jnp.float32)
        keep_ref[:, start:end] = product[:half]
        send_ref[:, start:end] = product[half:].astype(jnp.bfloat16)


def in_hbm(value):
    return pltpu.with_memory_space_constraint(value, pltpu.HBM)


def project(n, q_start, q_cols, kv_start, first, x, gain, w_query, w_key, w_value):
    rows, depth = x.shape
    kv = w_key.shape[1] // CHUNKS if kv_start is not None else 0
    width = q_cols + 2 * kv
    full = width + (128 if first else 0)
    hbm = pl.BlockSpec(memory_space=pltpu.HBM)
    vmem = pl.BlockSpec(memory_space=pltpu.VMEM)
    out_shape = [
        pltpu.VMEM((rows // 2, full), jnp.bfloat16),
        pltpu.VMEM((rows // 2, full), jnp.float32),
    ]
    scratch = [pltpu.VMEM((depth, width), jnp.bfloat16), pltpu.SemaphoreType.DMA((6,))]
    if first:
        out_shape.append(pltpu.VMEM((rows, depth), jnp.bfloat16))
        args = [in_hbm(x), in_hbm(gain)]
        in_specs = [hbm, hbm]
        scratch = [
            pltpu.VMEM((n, rows // n, depth), jnp.bfloat16),
            pltpu.SemaphoreType.DMA((n,)),
            pltpu.VMEM((1, depth), jnp.float32),
            pltpu.SemaphoreType.DMA,
        ] + scratch
    else:
        args, in_specs = [x], [vmem]
    return pl.pallas_call(
        functools.partial(project_kernel, n, q_start, kv_start, first),
        out_shape=out_shape,
        in_specs=in_specs + [hbm] * 3,
        out_specs=[vmem] * len(out_shape),
        scratch_shapes=scratch,
        compiler_params=pltpu.CompilerParams(vmem_limit_bytes=16 * MIB),
        name="project",
    )(*args, in_hbm(w_query), in_hbm(w_key), in_hbm(w_value))


def attend_kernel(chunk, offsets, kv_offset, groups, heads, seqs, length_ref, *refs):
    sum_ref, square_ref = refs[:2]
    w_copies = []
    if chunk == 0:
        cos_ref, sin_ref, k_ref, v_ref, w_ref, out_ref, next_ref, q_scr, o_scr, w_sems = refs[2:]
        total = next_ref.shape[0]
        for p in range(4):
            at = slice(p * total // 4, (p + 1) * total // 4)
            w_copies.append(
                pltpu.make_async_copy(
                    w_ref.at[total + at.start : total + at.stop], next_ref.at[at], w_sems.at[p]
                )
            )
            w_copies[-1].start()
    else:
        cos_ref, sin_ref, k_ref, v_ref, out_ref, q_scr, o_scr = refs[2:]
    rows = seqs * NEW
    cols = groups * heads * HD
    kv = groups * HD
    seq_count = k_ref.shape[0]

    scale = HD**-0.5 * math.log2(math.e)
    slots = k_ref.shape[1]
    many = heads * NEW
    slot_ids = lax.broadcasted_iota(jnp.int32, (1, slots), 1)
    new_cols = lax.broadcasted_iota(jnp.int32, (many, rows), 1)
    new_rows = lax.broadcasted_iota(jnp.int32, (many, rows), 0) % NEW

    @pl.loop(0, seq_count // seqs)
    def _(step):
        mine = pl.ds(pl.multiple_of(step * rows, rows), rows)
        mean = jnp.sum(square_ref[mine, :], axis=1, keepdims=True) / D
        row_scale = lax.rsqrt(mean + EPS)
        cosine, sine = cos_ref[mine, :], sin_ref[mine, :]

        def raw(start):
            return sum_ref[mine, start : start + HD] * row_scale

        def rotary(value):
            return value * cosine + pltpu.roll(value, HD // 2, 1) * sine

        for h in range(heads * groups):
            turned = rotary(raw(offsets[h]))
            for s in range(seqs):
                q_scr[s, h * NEW : (h + 1) * NEW, :] = turned[s * NEW : (s + 1) * NEW]
        for g in range(groups):
            new_keys = rotary(raw(kv_offset + g * HD)).astype(jnp.bfloat16)
            new_values = raw(kv_offset + (groups + g) * HD).astype(jnp.bfloat16)
            lanes = slice(chunk * kv + g * HD, chunk * kv + (g + 1) * HD)
            olds, news, mixes = [], [], []
            for s in range(seqs):
                query = q_scr[s, g * many : (g + 1) * many, :].astype(jnp.bfloat16)
                keys = k_ref[step * seqs + s, :, lanes]
                olds.append(
                    lax.dot_general(
                        query, keys, (((1,), (1,)), ((), ())), preferred_element_type=jnp.float32
                    )
                )
                news.append(
                    lax.dot_general(
                        query, new_keys, (((1,), (1,)), ((), ())), preferred_element_type=jnp.float32
                    )
                )
            for s in range(seqs):
                live = slot_ids < length_ref[step * seqs + s]
                seen = (new_cols >= s * NEW) & (new_cols <= s * NEW + new_rows)
                old = jnp.where(live, olds[s] * scale, -1e30)
                new = jnp.where(seen, news[s] * scale, -1e30)
                top = jnp.maximum(
                    jnp.max(old, axis=1, keepdims=True), jnp.max(new, axis=1, keepdims=True)
                )
                old = jnp.exp2(old - top)
                new = jnp.exp2(new - top)
                total = jnp.sum(old, axis=1, keepdims=True) + jnp.sum(new, axis=1, keepdims=True)
                inverse = 1.0 / total
                olds[s] = (old * inverse).astype(jnp.bfloat16)
                news[s] = (new * inverse).astype(jnp.bfloat16)
            for s in range(seqs):
                values = v_ref[step * seqs + s, :, lanes]
                mixes.append(
                    jnp.dot(olds[s], values, preferred_element_type=jnp.float32)
                    + jnp.dot(news[s], new_values, preferred_element_type=jnp.float32)
                )
            for s in range(seqs):
                for h in range(heads):
                    at = (g * heads + h) * HD
                    o_scr[s * NEW : (s + 1) * NEW, at : at + HD] = mixes[s][
                        h * NEW : (h + 1) * NEW
                    ]
        out_ref[mine, :] = o_scr[...].astype(jnp.bfloat16)

    for copy in w_copies:
        copy.wait()


def attend(chunk, offsets, kv_offset, sums, squares, cosine, sine, cache_keys, cache_values, lengths, w_out):
    seq_count, slots, kv_all = cache_keys.shape
    kv = kv_all // CHUNKS
    groups = kv // HD
    heads = len(offsets) // groups
    cols = len(offsets) * HD
    seqs = min(4, seq_count)
    rows = seq_count * NEW
    source, copied = [], []
    if chunk == 0:
        source.append(in_hbm(w_out))
        copied.append(pltpu.VMEM((w_out.shape[0] // CHUNKS, w_out.shape[1]), w_out.dtype))
    vmem = pl.BlockSpec(memory_space=pltpu.VMEM)
    hbm = pl.BlockSpec(memory_space=pltpu.HBM)
    return pl.pallas_call(
        functools.partial(attend_kernel, chunk, offsets, kv_offset, groups, heads, seqs),
        out_shape=[pltpu.VMEM((rows, cols), jnp.bfloat16)] + copied,
        in_specs=[pl.BlockSpec(memory_space=pltpu.SMEM)] + [vmem] * 6 + [hbm] * len(source),
        out_specs=[vmem] * (1 + len(copied)),
        scratch_shapes=[
            pltpu.VMEM((seqs, groups * heads * NEW, HD), jnp.float32),
            pltpu.VMEM((seqs * NEW, cols), jnp.float32),
        ]
        + [pltpu.SemaphoreType.DMA((4,))] * len(copied),
        compiler_params=pltpu.CompilerParams(vmem_limit_bytes=16 * MIB),
        name="attend",
    )(lengths, sums, squares, cosine, sine, cache_keys, cache_values, *source)


def fetch_kernel(count, pieces, *refs):
    sources, targets, sems = refs[:count], refs[count : 2 * count], refs[2 * count]
    copies = []
    for i, (source, target) in enumerate(zip(sources, targets)):
        size = target.shape[0] // pieces
        for p in range(pieces):
            at = slice(p * size, (p + 1) * size)
            copies.append(
                pltpu.make_async_copy(source.at[at], target.at[at], sems.at[i * pieces + p])
            )
    for copy in copies:
        copy.start()
    for copy in copies:
        copy.wait()


def fetch(*arrays):
    pieces = 4
    return pl.pallas_call(
        functools.partial(fetch_kernel, len(arrays), pieces),
        out_shape=[pltpu.VMEM(array.shape, array.dtype) for array in arrays],
        in_specs=[pl.BlockSpec(memory_space=pltpu.HBM)] * len(arrays),
        out_specs=[pl.BlockSpec(memory_space=pltpu.VMEM)] * len(arrays),
        scratch_shapes=[pltpu.SemaphoreType.DMA((pieces * len(arrays),))],
        compiler_params=pltpu.CompilerParams(vmem_limit_bytes=4 * MIB),
        name="fetch",
    )(*[in_hbm(array) for array in arrays])


def fetch_rows_kernel(start, pieces, source, target, sems):
    size = target.shape[0] // pieces
    copies = [
        pltpu.make_async_copy(
            source.at[start + p * size : start + (p + 1) * size],
            target.at[p * size : (p + 1) * size],
            sems.at[p],
        )
        for p in range(pieces)
    ]
    for copy in copies:
        copy.start()
    for copy in copies:
        copy.wait()


def fetch_rows(array, start, rows):
    pieces = 4
    return pl.pallas_call(
        functools.partial(fetch_rows_kernel, start, pieces),
        out_shape=pltpu.VMEM((rows, array.shape[1]), array.dtype),
        in_specs=[pl.BlockSpec(memory_space=pltpu.HBM)],
        out_specs=pl.BlockSpec(memory_space=pltpu.VMEM),
        scratch_shapes=[pltpu.SemaphoreType.DMA((pieces,))],
        compiler_params=pltpu.CompilerParams(vmem_limit_bytes=4 * MIB),
        name="fetch_rows",
    )(in_hbm(array))


def combine_kernel(n, block, chunk, *refs):
    pieces, refs = refs[:n], refs[n:]
    gx, gy = lax.axis_index("gx"), lax.axis_index("gy")
    moved = jnp.where(gy == 0, n // 2, 0)
    if chunk:
        before_ref, refs = refs[0], refs[1:]
    w_ref, outs, x_buf = refs[0], refs[1:-1], refs[-1]
    depth, cols = x_buf.shape[1], w_ref.shape[1]
    half = x_buf.shape[0] // 2
    for slot, piece in enumerate(pieces):
        start = pl.multiple_of((slot_owner(n, slot, gx, gy, gather_orders(n, chunk)) ^ moved) * block, block)
        x_buf[pl.ds(start, block), :] = piece[...]

    tile = cols // TILES
    for start in range(0, cols, tile):
        at = slice(start, start + tile)
        product = jnp.dot(x_buf[...], w_ref[:, at], preferred_element_type=jnp.float32)
        if chunk:
            product = product + before_ref[:, at]
        if len(outs) == 1:
            outs[0][:, at] = product
        else:
            outs[0][:, at] = product[:half].astype(jnp.bfloat16)
            outs[1][:, at] = product[half:]


def combine(chunk, pieces, before, w_out):
    n, (block, depth) = len(pieces), pieces[0].shape
    rows = n * block
    cols = w_out.shape[1]
    last = chunk == CHUNKS - 1
    hbm = pl.BlockSpec(memory_space=pltpu.HBM)
    vmem = pl.BlockSpec(memory_space=pltpu.VMEM)
    if last:
        out_shape = [
            pltpu.VMEM((rows // 2, cols), jnp.bfloat16),
            pltpu.VMEM((rows // 2, cols), jnp.float32),
        ]
    else:
        out_shape = [pltpu.VMEM((rows, cols), jnp.float32)]
    earlier = [] if chunk == 0 else [before]
    return pl.pallas_call(
        functools.partial(combine_kernel, n, block, chunk),
        out_shape=out_shape,
        in_specs=[vmem] * (len(pieces) + len(earlier) + 1),
        out_specs=[vmem] * len(out_shape),
        scratch_shapes=[
            pltpu.VMEM((rows, depth), jnp.bfloat16),
        ],
        compiler_params=pltpu.CompilerParams(vmem_limit_bytes=16 * MIB),
        name="combine",
    )(*pieces, *earlier, w_out)


def shards(
    tokens, norm_gain, w_query, w_key, w_value, w_out, cache_keys, cache_values, cache_lengths
):
    n = lax.axis_size("gx")
    cores = lax.axis_size("gy")
    levels = n.bit_length() - 1
    position = (cache_lengths[:, None] + jnp.arange(NEW, dtype=jnp.int32)[None, :]).reshape(-1)
    inverse = THETA ** (-2.0 * jnp.arange(HD // 2, dtype=jnp.float32) / HD)
    angles = position.astype(jnp.float32)[:, None] * inverse[None, :]
    cosine, sine = jnp.cos(angles), jnp.sin(angles)
    cosine = jnp.concatenate([cosine, cosine], axis=1)
    sine = jnp.concatenate([-sine, sine], axis=1)

    x, gain = tokens, norm_gain[None, :]
    kv = w_key.shape[1] // CHUNKS
    q_cols = w_query.shape[1] // CHUNKS

    def column_part(start, size, kv_start):
        return project(
            n, start, size, kv_start, start == 0, x, gain, w_query, w_key, w_value
        )

    def after(value, *earlier):
        return lax.optimization_barrier((value, earlier))[0]

    share = q_cols // 2
    orders = bit_orders(n)
    send_a, keep_a, x = column_part(0, share, None)
    x = after(x, send_a)
    other_a = exchange(send_a, n, cores, 0, orders)
    send_b, keep_b = column_part(share, share, 0)
    x = after(x, send_b)
    other_b = exchange(send_b, n, cores, 0, orders)
    sum_a = keep_a + other_a.astype(jnp.float32)
    x = after(x, sum_a)
    later = []
    for chunk in range(1, CHUNKS):
        later.append(column_part(chunk * q_cols, q_cols, chunk * kv))
    other_b = after(other_b, *(send_c for send_c, _ in later))
    first = jnp.concatenate([sum_a, keep_b + other_b.astype(jnp.float32)], axis=1)
    half = first.shape[0] // 2
    send = first[half:].astype(jnp.bfloat16)
    flows = [[1, first[:half], send]]
    for send_c, keep_c in later:
        flows.append([0, keep_c, after(send_c, flows[-1][2])])

    def start(flow):
        return exchange(flow[2], n, cores, flow[0], orders)

    def finish(flow, other, *earlier):
        stage, keep, _ = flow
        if earlier:
            other = after(other, *earlier)
        value = keep + other.astype(jnp.float32)
        low = value.shape[0] // 2 if stage < levels - 1 else 0
        flow[:] = stage + 1, value[:low] if low else value, value[low:].astype(jnp.bfloat16)

    lead, follow = flows
    w_rows = w_out.shape[0] // CHUNKS
    weights = [fetch_rows(after(w_out, lead[2], follow[2]), 0, w_rows)]
    while follow[0] < levels:
        pending = [start(flow) for flow in flows if flow[0] < levels]
        if lead[0] == levels:
            finish(follow, pending[0])
        elif lead[0] == levels - 1:
            cache_keys, cache_values = fetch(*after((cache_keys, cache_values), follow[2]))
            finish(lead, pending[0], cache_keys, cache_values)
            finish(follow, pending[1], lead[1])
        else:
            finish(lead, pending[0], *weights)
            finish(follow, pending[1], lead[2])
    sums = [flow[1] for flow in flows]
    squares = sums[0][:, share : share + 128]
    plain = [h * HD for h in range(q_cols // HD)]
    offsets = [[at if at < share else at + 128 for at in plain], plain]
    kv_offsets = [q_cols + 128, q_cols]

    attentions = []
    for chunk in range(CHUNKS):
        out = attend(
            chunk,
            offsets[chunk],
            kv_offsets[chunk],
            sums[chunk],
            squares,
            cosine,
            sine,
            cache_keys,
            cache_values,
            cache_lengths,
            w_out,
        )
        attentions.append(out[0])
        weights += out[1:]
    gathered = []
    for chunk in range(CHUNKS):
        slots = [attentions[chunk]]
        for slot in range(1, n):
            top = slot.bit_length() - 1
            source = slots[slot - (1 << top)]
            if slot == 1 and chunk == 0:
                source = after(source, sums[1])
            if slot == 3 << (levels - 2):
                source = after(source, slots[1 << (levels - 1)])
            slots.append(
                exchange(source, n, cores, levels - 1 - top, gather_orders(n, chunk))
            )
        gathered.append(slots)
    result = None
    for chunk in range(CHUNKS):
        result = combine(chunk, gathered[chunk], result and result[0], weights[chunk])
    send, keep = result
    other = lax.ppermute(send, "gy", [(0, 1), (1, 0)])
    return (keep + other.astype(jnp.float32)).astype(jnp.bfloat16)


def solution(mesh):
    return jax.shard_map(
        shards,
        mesh=mesh,
        in_specs=(
            P("groups", "gx"),
            P("gx"),
            P("gx", "gy"),
            P("gx", "gy"),
            P("gx", "gy"),
            P("gy", "gx"),
            P(("groups", "gx"), None, "gy"),
            P(("groups", "gx"), None, "gy"),
            P(("groups", "gx")),
        ),
        out_specs=P(("groups", "gy"), "gx"),
        check_vma=False,
    )
```

```python
import functools
import math

import jax
import jax.numpy as jnp
from jax import lax
from jax.experimental import pallas as pl
from jax.experimental.pallas import tpu as pltpu
from jax.sharding import PartitionSpec as P

D = 16384
HD = 128
NEW = 4
EPS = 1e-05
THETA = 500000.0

CHUNKS = 2
TILES = 2
MIB = 1 << 20


def bit_orders(n):
    levels = n.bit_length() - 1
    first = list(range(levels))
    second = list(first)
    if levels > 1:
        second[0], second[1] = second[1], second[0]
    return first, second


def gather_orders(n, chunk):
    first, second = bit_orders(n)
    return (first, first) if chunk else (first, second)


def slot_shift(slot, order):
    levels = len(order)
    shift = 0
    for stage in range(levels):
        shift |= ((slot >> (levels - 1 - stage)) & 1) << order[stage]
    return shift


def slot_owner(n, slot, gx, gy, orders):
    first, second = (slot_shift(slot, order) for order in orders)
    return gx ^ jnp.where(gy == 0, first, second)


def exchange(value, n, cores, stage, orders):
    pairs = []
    for gx in range(n):
        for gy in range(cores):
            other = gx ^ (1 << orders[gy % 2][stage])
            pairs.append((gx * cores + gy, other * cores + gy))
    return lax.ppermute(value, ("gx", "gy"), pairs)


def project_kernel(n, q_start, kv_start, first, *refs):
    if first:
        tokens_ref, gain_ref, wq_ref, wk_ref, wv_ref, send_ref, keep_ref, x_ref = refs[:8]
        t_buf, t_sems, g_buf, g_sem = refs[8:12]
    else:
        x_ref, wq_ref, wk_ref, wv_ref, send_ref, keep_ref = refs[:6]
    w_buf, sems = refs[-2:]
    half = send_ref.shape[0]
    rows = 2 * half
    with_kv = kv_start is not None
    kv = wk_ref.shape[1] // CHUNKS if with_kv else 0
    width = w_buf.shape[1]
    cols = width - 2 * kv
    pieces = 1 if first else 4 if cols > 1024 else 2
    tile = cols // pieces

    def w_copy(ref, start, size, at, sem):
        return pltpu.make_async_copy(
            ref.at[:, start : start + size], w_buf.at[:, at : at + size], sems.at[sem]
        )

    copies = [[w_copy(wq_ref, q_start + p * tile, tile, p * tile, p)] for p in range(pieces)]
    if with_kv:
        copies[-1].append(w_copy(wk_ref, kv_start, kv, cols, pieces))
        copies[-1].append(w_copy(wv_ref, kv_start, kv, cols + kv, pieces + 1))

    if first:
        block = rows // n
        me, gy = lax.axis_index("gx"), lax.axis_index("gy")
        t_copies = []
        for slot in range(n):
            start = pl.multiple_of(slot_owner(n, slot, me, gy, bit_orders(n)) * block, block)
            t_copies.append(
                pltpu.make_async_copy(
                    tokens_ref.at[pl.ds(start, block), :], t_buf.at[slot], t_sems.at[slot]
                )
            )
            t_copies[-1].start()
        g_copy = pltpu.make_async_copy(gain_ref, g_buf, g_sem)
        g_copy.start()
    for group in copies:
        for copy in group:
            copy.start()
    if first:
        lanes = lax.broadcasted_iota(jnp.int32, (block, 128), 1)
        g_copy.wait()
        for slot in range(n):
            t_copies[slot].wait()
            wide = t_buf[slot].astype(jnp.float32)
            x_ref[slot * block : (slot + 1) * block, :] = (wide * g_buf[...]).astype(jnp.bfloat16)
            square = jnp.sum(wide * wide, axis=1, keepdims=True)
            high = square.astype(jnp.bfloat16).astype(jnp.float32)
            rest = square - high
            middle = rest.astype(jnp.bfloat16).astype(jnp.float32)
            low = rest - middle
            packed = jnp.where(
                lanes == 3 * me,
                high,
                jnp.where(lanes == 3 * me + 1, middle, jnp.where(lanes == 3 * me + 2, low, 0.0)),
            )
            if slot < n // 2:
                keep_ref[slot * block : (slot + 1) * block, width : width + 128] = packed
            else:
                at = (slot - n // 2) * block
                send_ref[at : at + block, width : width + 128] = packed.astype(jnp.bfloat16)

    for p in range(pieces):
        start, end = p * tile, (p + 1) * tile if p < pieces - 1 else width
        for copy in copies[p]:
            copy.wait()
        product = jnp.dot(x_ref[...], w_buf[:, start:end], preferred_element_type=jnp.float32)
        keep_ref[:, start:end] = product[:half]
        send_ref[:, start:end] = product[half:].astype(jnp.bfloat16)


def in_hbm(value):
    return pltpu.with_memory_space_constraint(value, pltpu.HBM)


def project(n, q_start, q_cols, kv_start, first, x, gain, w_query, w_key, w_value):
    rows, depth = x.shape
    kv = w_key.shape[1] // CHUNKS if kv_start is not None else 0
    width = q_cols + 2 * kv
    full = width + (128 if first else 0)
    hbm = pl.BlockSpec(memory_space=pltpu.HBM)
    vmem = pl.BlockSpec(memory_space=pltpu.VMEM)
    out_shape = [
        pltpu.VMEM((rows // 2, full), jnp.bfloat16),
        pltpu.VMEM((rows // 2, full), jnp.float32),
    ]
    scratch = [pltpu.VMEM((depth, width), jnp.bfloat16), pltpu.SemaphoreType.DMA((6,))]
    if first:
        out_shape.append(pltpu.VMEM((rows, depth), jnp.bfloat16))
        args = [in_hbm(x), in_hbm(gain)]
        in_specs = [hbm, hbm]
        scratch = [
            pltpu.VMEM((n, rows // n, depth), jnp.bfloat16),
            pltpu.SemaphoreType.DMA((n,)),
            pltpu.VMEM((1, depth), jnp.float32),
            pltpu.SemaphoreType.DMA,
        ] + scratch
    else:
        args, in_specs = [x], [vmem]
    return pl.pallas_call(
        functools.partial(project_kernel, n, q_start, kv_start, first),
        out_shape=out_shape,
        in_specs=in_specs + [hbm] * 3,
        out_specs=[vmem] * len(out_shape),
        scratch_shapes=scratch,
        compiler_params=pltpu.CompilerParams(vmem_limit_bytes=16 * MIB),
        name="project",
    )(*args, in_hbm(w_query), in_hbm(w_key), in_hbm(w_value))


def attend_kernel(chunk, offsets, kv_offset, groups, heads, seqs, length_ref, *refs):
    sum_ref, square_ref = refs[:2]
    w_copies = []
    if chunk == 0:
        cos_ref, sin_ref, k_ref, v_ref, w_ref, out_ref, next_ref, q_scr, o_scr, w_sems = refs[2:]
        total = next_ref.shape[0]
        for p in range(4):
            at = slice(p * total // 4, (p + 1) * total // 4)
            w_copies.append(
                pltpu.make_async_copy(
                    w_ref.at[total + at.start : total + at.stop], next_ref.at[at], w_sems.at[p]
                )
            )
            w_copies[-1].start()
    else:
        cos_ref, sin_ref, k_ref, v_ref, out_ref, q_scr, o_scr = refs[2:]
    rows = seqs * NEW
    cols = groups * heads * HD
    kv = groups * HD
    seq_count = k_ref.shape[0]

    scale = HD**-0.5 * math.log2(math.e)
    slots = k_ref.shape[1]
    many = heads * NEW
    slot_ids = lax.broadcasted_iota(jnp.int32, (1, slots), 1)
    new_cols = lax.broadcasted_iota(jnp.int32, (many, rows), 1)
    new_rows = lax.broadcasted_iota(jnp.int32, (many, rows), 0) % NEW

    @pl.loop(0, seq_count // seqs, unroll=True)
    def _(step):
        mine = pl.ds(pl.multiple_of(step * rows, rows), rows)
        mean = jnp.sum(square_ref[mine, :], axis=1, keepdims=True) / D
        row_scale = lax.rsqrt(mean + EPS)
        cosine, sine = cos_ref[mine, :], sin_ref[mine, :]

        def raw(start):
            return sum_ref[mine, start : start + HD] * row_scale

        def rotary(value):
            return value * cosine + pltpu.roll(value, HD // 2, 1) * sine

        for h in range(heads * groups):
            turned = rotary(raw(offsets[h]))
            for s in range(seqs):
                q_scr[s, h * NEW : (h + 1) * NEW, :] = turned[s * NEW : (s + 1) * NEW]
        for g in range(groups):
            new_keys = rotary(raw(kv_offset + g * HD)).astype(jnp.bfloat16)
            new_values = raw(kv_offset + (groups + g) * HD).astype(jnp.bfloat16)
            lanes = slice(chunk * kv + g * HD, chunk * kv + (g + 1) * HD)
            olds, news, mixes = [], [], []
            for s in range(seqs):
                query = q_scr[s, g * many : (g + 1) * many, :].astype(jnp.bfloat16)
                keys = k_ref[step * seqs + s, :, lanes]
                olds.append(
                    lax.dot_general(
                        query, keys, (((1,), (1,)), ((), ())), preferred_element_type=jnp.float32
                    )
                )
                news.append(
                    lax.dot_general(
                        query, new_keys, (((1,), (1,)), ((), ())), preferred_element_type=jnp.float32
                    )
                )
            for s in range(seqs):
                live = slot_ids < length_ref[step * seqs + s]
                seen = (new_cols >= s * NEW) & (new_cols <= s * NEW + new_rows)
                old = jnp.where(live, olds[s] * scale, -1e30)
                new = jnp.where(seen, news[s] * scale, -1e30)
                top = jnp.maximum(
                    jnp.max(old, axis=1, keepdims=True), jnp.max(new, axis=1, keepdims=True)
                )
                old = jnp.exp2(old - top)
                new = jnp.exp2(new - top)
                total = jnp.sum(old, axis=1, keepdims=True) + jnp.sum(new, axis=1, keepdims=True)
                inverse = 1.0 / total
                olds[s] = (old * inverse).astype(jnp.bfloat16)
                news[s] = (new * inverse).astype(jnp.bfloat16)
            for s in range(seqs):
                values = v_ref[step * seqs + s, :, lanes]
                mixes.append(
                    jnp.dot(olds[s], values, preferred_element_type=jnp.float32)
                    + jnp.dot(news[s], new_values, preferred_element_type=jnp.float32)
                )
            for s in range(seqs):
                for h in range(heads):
                    at = (g * heads + h) * HD
                    o_scr[s * NEW : (s + 1) * NEW, at : at + HD] = mixes[s][
                        h * NEW : (h + 1) * NEW
                    ]
        out_ref[mine, :] = o_scr[...].astype(jnp.bfloat16)

    for copy in w_copies:
        copy.wait()


def attend(chunk, offsets, kv_offset, sums, squares, cosine, sine, cache_keys, cache_values, lengths, w_out):
    seq_count, slots, kv_all = cache_keys.shape
    kv = kv_all // CHUNKS
    groups = kv // HD
    heads = len(offsets) // groups
    cols = len(offsets) * HD
    seqs = min(4, seq_count)
    rows = seq_count * NEW
    source, copied = [], []
    if chunk == 0:
        source.append(in_hbm(w_out))
        copied.append(pltpu.VMEM((w_out.shape[0] // CHUNKS, w_out.shape[1]), w_out.dtype))
    vmem = pl.BlockSpec(memory_space=pltpu.VMEM)
    hbm = pl.BlockSpec(memory_space=pltpu.HBM)
    return pl.pallas_call(
        functools.partial(attend_kernel, chunk, offsets, kv_offset, groups, heads, seqs),
        out_shape=[pltpu.VMEM((rows, cols), jnp.bfloat16)] + copied,
        in_specs=[pl.BlockSpec(memory_space=pltpu.SMEM)] + [vmem] * 6 + [hbm] * len(source),
        out_specs=[vmem] * (1 + len(copied)),
        scratch_shapes=[
            pltpu.VMEM((seqs, groups * heads * NEW, HD), jnp.float32),
            pltpu.VMEM((seqs * NEW, cols), jnp.float32),
        ]
        + [pltpu.SemaphoreType.DMA((4,))] * len(copied),
        compiler_params=pltpu.CompilerParams(vmem_limit_bytes=16 * MIB),
        name="attend",
    )(lengths, sums, squares, cosine, sine, cache_keys, cache_values, *source)


def fetch_kernel(count, pieces, *refs):
    sources, targets, sems = refs[:count], refs[count : 2 * count], refs[2 * count]
    copies = []
    for i, (source, target) in enumerate(zip(sources, targets)):
        size = target.shape[0] // pieces
        for p in range(pieces):
            at = slice(p * size, (p + 1) * size)
            copies.append(
                pltpu.make_async_copy(source.at[at], target.at[at], sems.at[i * pieces + p])
            )
    for copy in copies:
        copy.start()
    for copy in copies:
        copy.wait()


def fetch(*arrays):
    pieces = 4
    return pl.pallas_call(
        functools.partial(fetch_kernel, len(arrays), pieces),
        out_shape=[pltpu.VMEM(array.shape, array.dtype) for array in arrays],
        in_specs=[pl.BlockSpec(memory_space=pltpu.HBM)] * len(arrays),
        out_specs=[pl.BlockSpec(memory_space=pltpu.VMEM)] * len(arrays),
        scratch_shapes=[pltpu.SemaphoreType.DMA((pieces * len(arrays),))],
        compiler_params=pltpu.CompilerParams(vmem_limit_bytes=4 * MIB),
        name="fetch",
    )(*[in_hbm(array) for array in arrays])


def fetch_rows_kernel(start, pieces, source, target, sems):
    size = target.shape[0] // pieces
    copies = [
        pltpu.make_async_copy(
            source.at[start + p * size : start + (p + 1) * size],
            target.at[p * size : (p + 1) * size],
            sems.at[p],
        )
        for p in range(pieces)
    ]
    for copy in copies:
        copy.start()
    for copy in copies:
        copy.wait()


def fetch_rows(array, start, rows):
    pieces = 4
    return pl.pallas_call(
        functools.partial(fetch_rows_kernel, start, pieces),
        out_shape=pltpu.VMEM((rows, array.shape[1]), array.dtype),
        in_specs=[pl.BlockSpec(memory_space=pltpu.HBM)],
        out_specs=pl.BlockSpec(memory_space=pltpu.VMEM),
        scratch_shapes=[pltpu.SemaphoreType.DMA((pieces,))],
        compiler_params=pltpu.CompilerParams(vmem_limit_bytes=4 * MIB),
        name="fetch_rows",
    )(in_hbm(array))


def combine_kernel(n, block, chunk, *refs):
    pieces, refs = refs[:n], refs[n:]
    gx, gy = lax.axis_index("gx"), lax.axis_index("gy")
    moved = jnp.where(gy == 0, n // 2, 0)
    if chunk:
        before_ref, refs = refs[0], refs[1:]
    w_ref, outs, x_buf = refs[0], refs[1:-1], refs[-1]
    depth, cols = x_buf.shape[1], w_ref.shape[1]
    half = x_buf.shape[0] // 2
    for slot, piece in enumerate(pieces):
        start = pl.multiple_of((slot_owner(n, slot, gx, gy, gather_orders(n, chunk)) ^ moved) * block, block)
        x_buf[pl.ds(start, block), :] = piece[...]

    tile = cols // TILES
    for start in range(0, cols, tile):
        at = slice(start, start + tile)
        product = jnp.dot(x_buf[...], w_ref[:, at], preferred_element_type=jnp.float32)
        if chunk:
            product = product + before_ref[:, at]
        if len(outs) == 1:
            outs[0][:, at] = product
        else:
            outs[0][:, at] = product[:half].astype(jnp.bfloat16)
            outs[1][:, at] = product[half:]


def combine(chunk, pieces, before, w_out):
    n, (block, depth) = len(pieces), pieces[0].shape
    rows = n * block
    cols = w_out.shape[1]
    last = chunk == CHUNKS - 1
    hbm = pl.BlockSpec(memory_space=pltpu.HBM)
    vmem = pl.BlockSpec(memory_space=pltpu.VMEM)
    if last:
        out_shape = [
            pltpu.VMEM((rows // 2, cols), jnp.bfloat16),
            pltpu.VMEM((rows // 2, cols), jnp.float32),
        ]
    else:
        out_shape = [pltpu.VMEM((rows, cols), jnp.float32)]
    earlier = [] if chunk == 0 else [before]
    return pl.pallas_call(
        functools.partial(combine_kernel, n, block, chunk),
        out_shape=out_shape,
        in_specs=[vmem] * (len(pieces) + len(earlier) + 1),
        out_specs=[vmem] * len(out_shape),
        scratch_shapes=[
            pltpu.VMEM((rows, depth), jnp.bfloat16),
        ],
        compiler_params=pltpu.CompilerParams(vmem_limit_bytes=16 * MIB),
        name="combine",
    )(*pieces, *earlier, w_out)


def shards(
    tokens, norm_gain, w_query, w_key, w_value, w_out, cache_keys, cache_values, cache_lengths
):
    n = lax.axis_size("gx")
    cores = lax.axis_size("gy")
    levels = n.bit_length() - 1
    position = (cache_lengths[:, None] + jnp.arange(NEW, dtype=jnp.int32)[None, :]).reshape(-1)
    inverse = THETA ** (-2.0 * jnp.arange(HD // 2, dtype=jnp.float32) / HD)
    angles = position.astype(jnp.float32)[:, None] * inverse[None, :]
    cosine, sine = jnp.cos(angles), jnp.sin(angles)
    cosine = jnp.concatenate([cosine, cosine], axis=1)
    sine = jnp.concatenate([-sine, sine], axis=1)

    x, gain = tokens, norm_gain[None, :]
    kv = w_key.shape[1] // CHUNKS
    q_cols = w_query.shape[1] // CHUNKS

    def column_part(start, size, kv_start):
        return project(
            n, start, size, kv_start, start == 0, x, gain, w_query, w_key, w_value
        )

    def after(value, *earlier):
        return lax.optimization_barrier((value, earlier))[0]

    share = q_cols // 2
    orders = bit_orders(n)
    send_a, keep_a, x = column_part(0, share, None)
    x = after(x, send_a)
    other_a = exchange(send_a, n, cores, 0, orders)
    send_b, keep_b = column_part(share, share, 0)
    x = after(x, send_b)
    other_b = exchange(send_b, n, cores, 0, orders)
    sum_a = keep_a + other_a.astype(jnp.float32)
    x = after(x, sum_a)
    later = []
    for chunk in range(1, CHUNKS):
        later.append(column_part(chunk * q_cols, q_cols, chunk * kv))
    other_b = after(other_b, *(send_c for send_c, _ in later))
    first = jnp.concatenate([sum_a, keep_b + other_b.astype(jnp.float32)], axis=1)
    half = first.shape[0] // 2
    send = first[half:].astype(jnp.bfloat16)
    flows = [[1, first[:half], send]]
    for send_c, keep_c in later:
        flows.append([0, keep_c, after(send_c, flows[-1][2])])

    def start(flow):
        return exchange(flow[2], n, cores, flow[0], orders)

    def finish(flow, other, *earlier):
        stage, keep, _ = flow
        if earlier:
            other = after(other, *earlier)
        value = keep + other.astype(jnp.float32)
        low = value.shape[0] // 2 if stage < levels - 1 else 0
        flow[:] = stage + 1, value[:low] if low else value, value[low:].astype(jnp.bfloat16)

    lead, follow = flows
    w_rows = w_out.shape[0] // CHUNKS
    weights = [fetch_rows(after(w_out, lead[2], follow[2]), 0, w_rows)]
    while follow[0] < levels:
        pending = [start(flow) for flow in flows if flow[0] < levels]
        if lead[0] == levels:
            finish(follow, pending[0])
        elif lead[0] == levels - 1:
            cache_keys, cache_values = fetch(*after((cache_keys, cache_values), follow[2]))
            finish(lead, pending[0], cache_keys, cache_values)
            finish(follow, pending[1], lead[1])
        else:
            finish(lead, pending[0], *weights)
            finish(follow, pending[1], lead[2])
    sums = [flow[1] for flow in flows]
    squares = sums[0][:, share : share + 128]
    plain = [h * HD for h in range(q_cols // HD)]
    offsets = [[at if at < share else at + 128 for at in plain], plain]
    kv_offsets = [q_cols + 128, q_cols]

    attentions = []
    for chunk in range(CHUNKS):
        out = attend(
            chunk,
            offsets[chunk],
            kv_offsets[chunk],
            sums[chunk],
            squares,
            cosine,
            sine,
            cache_keys,
            cache_values,
            cache_lengths,
            w_out,
        )
        attentions.append(out[0])
        weights += out[1:]
    gathered = []
    for chunk in range(CHUNKS):
        slots = [attentions[chunk]]
        for slot in range(1, n):
            top = slot.bit_length() - 1
            source = slots[slot - (1 << top)]
            if slot == 1 and chunk == 0:
                source = after(source, sums[1])
            if slot == 3 << (levels - 2):
                source = after(source, slots[1 << (levels - 1)])
            slots.append(
                exchange(source, n, cores, levels - 1 - top, gather_orders(n, chunk))
            )
        gathered.append(slots)
    result = None
    for chunk in range(CHUNKS):
        result = combine(chunk, gathered[chunk], result and result[0], weights[chunk])
    send, keep = result
    other = lax.ppermute(send, "gy", [(0, 1), (1, 0)])
    return (keep + other.astype(jnp.float32)).astype(jnp.bfloat16)


def solution(mesh):
    return jax.shard_map(
        shards,
        mesh=mesh,
        in_specs=(
            P("groups", "gx"),
            P("gx"),
            P("gx", "gy"),
            P("gx", "gy"),
            P("gx", "gy"),
            P("gy", "gx"),
            P(("groups", "gx"), None, "gy"),
            P(("groups", "gx"), None, "gy"),
            P(("groups", "gx")),
        ),
        out_specs=P(("groups", "gy"), "gx"),
        check_vma=False,
    )
```

```python
import functools
import math

import jax
import jax.numpy as jnp
from jax import lax
from jax.experimental import pallas as pl
from jax.experimental.pallas import tpu as pltpu
from jax.sharding import PartitionSpec as P

D = 16384
HD = 128
NEW = 4
EPS = 1e-05
THETA = 500000.0

CHUNKS = 2
TILES = 2
MIB = 1 << 20


def bit_orders(n):
    levels = n.bit_length() - 1
    first = list(range(levels))
    second = list(first)
    if levels > 1:
        second[0], second[1] = second[1], second[0]
    return first, second


def gather_orders(n, chunk):
    first, second = bit_orders(n)
    return (first, second) if chunk else (first, first)


def slot_shift(slot, order):
    levels = len(order)
    shift = 0
    for stage in range(levels):
        shift |= ((slot >> (levels - 1 - stage)) & 1) << order[stage]
    return shift


def slot_owner(n, slot, gx, gy, orders):
    first, second = (slot_shift(slot, order) for order in orders)
    return gx ^ jnp.where(gy == 0, first, second)


def exchange(value, n, cores, stage, orders):
    pairs = []
    for gx in range(n):
        for gy in range(cores):
            other = gx ^ (1 << orders[gy % 2][stage])
            pairs.append((gx * cores + gy, other * cores + gy))
    return lax.ppermute(value, ("gx", "gy"), pairs)


def project_kernel(n, q_start, kv_start, first, *refs):
    if first:
        tokens_ref, gain_ref, wq_ref, wk_ref, wv_ref, send_ref, keep_ref, x_ref = refs[:8]
        t_buf, t_sems, g_buf, g_sem = refs[8:12]
    else:
        x_ref, wq_ref, wk_ref, wv_ref, send_ref, keep_ref = refs[:6]
    w_buf, sems = refs[-2:]
    half = send_ref.shape[0]
    rows = 2 * half
    with_kv = kv_start is not None
    kv = wk_ref.shape[1] // CHUNKS if with_kv else 0
    width = w_buf.shape[1]
    cols = width - 2 * kv
    pieces = 1 if first else 4 if cols > 1024 else 2
    tile = cols // pieces

    def w_copy(ref, start, size, at, sem):
        return pltpu.make_async_copy(
            ref.at[:, start : start + size], w_buf.at[:, at : at + size], sems.at[sem]
        )

    copies = [[w_copy(wq_ref, q_start + p * tile, tile, p * tile, p)] for p in range(pieces)]
    if with_kv:
        copies[-1].append(w_copy(wk_ref, kv_start, kv, cols, pieces))
        copies[-1].append(w_copy(wv_ref, kv_start, kv, cols + kv, pieces + 1))

    if first:
        block = rows // n
        me, gy = lax.axis_index("gx"), lax.axis_index("gy")
        t_copies = []
        for slot in range(n):
            start = pl.multiple_of(slot_owner(n, slot, me, gy, bit_orders(n)) * block, block)
            t_copies.append(
                pltpu.make_async_copy(
                    tokens_ref.at[pl.ds(start, block), :], t_buf.at[slot], t_sems.at[slot]
                )
            )
            t_copies[-1].start()
        g_copy = pltpu.make_async_copy(gain_ref, g_buf, g_sem)
        g_copy.start()
    for group in copies:
        for copy in group:
            copy.start()
    if first:
        lanes = lax.broadcasted_iota(jnp.int32, (block, 128), 1)
        g_copy.wait()
        for slot in range(n):
            t_copies[slot].wait()
            wide = t_buf[slot].astype(jnp.float32)
            x_ref[slot * block : (slot + 1) * block, :] = (wide * g_buf[...]).astype(jnp.bfloat16)
            square = jnp.sum(wide * wide, axis=1, keepdims=True)
            high = square.astype(jnp.bfloat16).astype(jnp.float32)
            rest = square - high
            middle = rest.astype(jnp.bfloat16).astype(jnp.float32)
            low = rest - middle
            packed = jnp.where(
                lanes == 3 * me,
                high,
                jnp.where(lanes == 3 * me + 1, middle, jnp.where(lanes == 3 * me + 2, low, 0.0)),
            )
            if slot < n // 2:
                keep_ref[slot * block : (slot + 1) * block, width : width + 128] = packed
            else:
                at = (slot - n // 2) * block
                send_ref[at : at + block, width : width + 128] = packed.astype(jnp.bfloat16)

    for p in range(pieces):
        start, end = p * tile, (p + 1) * tile if p < pieces - 1 else width
        for copy in copies[p]:
            copy.wait()
        product = jnp.dot(x_ref[...], w_buf[:, start:end], preferred_element_type=jnp.float32)
        keep_ref[:, start:end] = product[:half]
        send_ref[:, start:end] = product[half:].astype(jnp.bfloat16)


def in_hbm(value):
    return pltpu.with_memory_space_constraint(value, pltpu.HBM)


def project(n, q_start, q_cols, kv_start, first, x, gain, w_query, w_key, w_value):
    rows, depth = x.shape
    kv = w_key.shape[1] // CHUNKS if kv_start is not None else 0
    width = q_cols + 2 * kv
    full = width + (128 if first else 0)
    hbm = pl.BlockSpec(memory_space=pltpu.HBM)
    vmem = pl.BlockSpec(memory_space=pltpu.VMEM)
    out_shape = [
        pltpu.VMEM((rows // 2, full), jnp.bfloat16),
        pltpu.VMEM((rows // 2, full), jnp.float32),
    ]
    scratch = [pltpu.VMEM((depth, width), jnp.bfloat16), pltpu.SemaphoreType.DMA((6,))]
    if first:
        out_shape.append(pltpu.VMEM((rows, depth), jnp.bfloat16))
        args = [in_hbm(x), in_hbm(gain)]
        in_specs = [hbm, hbm]
        scratch = [
            pltpu.VMEM((n, rows // n, depth), jnp.bfloat16),
            pltpu.SemaphoreType.DMA((n,)),
            pltpu.VMEM((1, depth), jnp.float32),
            pltpu.SemaphoreType.DMA,
        ] + scratch
    else:
        args, in_specs = [x], [vmem]
    return pl.pallas_call(
        functools.partial(project_kernel, n, q_start, kv_start, first),
        out_shape=out_shape,
        in_specs=in_specs + [hbm] * 3,
        out_specs=[vmem] * len(out_shape),
        scratch_shapes=scratch,
        compiler_params=pltpu.CompilerParams(vmem_limit_bytes=16 * MIB),
        name="project",
    )(*args, in_hbm(w_query), in_hbm(w_key), in_hbm(w_value))


def attend_kernel(chunk, offsets, kv_offset, groups, heads, seqs, length_ref, *refs):
    sum_ref, square_ref = refs[:2]
    w_copies = []
    if chunk == 0:
        cos_ref, sin_ref, k_ref, v_ref, w_ref, out_ref, next_ref, q_scr, o_scr, w_sems = refs[2:]
        total = next_ref.shape[0]
        for p in range(4):
            at = slice(p * total // 4, (p + 1) * total // 4)
            w_copies.append(
                pltpu.make_async_copy(
                    w_ref.at[total + at.start : total + at.stop], next_ref.at[at], w_sems.at[p]
                )
            )
            w_copies[-1].start()
    else:
        cos_ref, sin_ref, k_ref, v_ref, out_ref, q_scr, o_scr = refs[2:]
    rows = seqs * NEW
    cols = groups * heads * HD
    kv = groups * HD
    seq_count = k_ref.shape[0]

    scale = HD**-0.5 * math.log2(math.e)
    slots = k_ref.shape[1]
    many = heads * NEW
    slot_ids = lax.broadcasted_iota(jnp.int32, (1, slots), 1)
    new_cols = lax.broadcasted_iota(jnp.int32, (many, rows), 1)
    new_rows = lax.broadcasted_iota(jnp.int32, (many, rows), 0) % NEW

    @pl.loop(0, seq_count // seqs, unroll=chunk > 0)
    def _(step):
        mine = pl.ds(pl.multiple_of(step * rows, rows), rows)
        mean = jnp.sum(square_ref[mine, :], axis=1, keepdims=True) / D
        row_scale = lax.rsqrt(mean + EPS)
        cosine, sine = cos_ref[mine, :], sin_ref[mine, :]

        def raw(start):
            return sum_ref[mine, start : start + HD] * row_scale

        def rotary(value):
            return value * cosine + pltpu.roll(value, HD // 2, 1) * sine

        for h in range(heads * groups):
            turned = rotary(raw(offsets[h]))
            for s in range(seqs):
                q_scr[s, h * NEW : (h + 1) * NEW, :] = turned[s * NEW : (s + 1) * NEW]
        for g in range(groups):
            new_keys = rotary(raw(kv_offset + g * HD)).astype(jnp.bfloat16)
            new_values = raw(kv_offset + (groups + g) * HD).astype(jnp.bfloat16)
            lanes = slice(chunk * kv + g * HD, chunk * kv + (g + 1) * HD)
            olds, news, mixes = [], [], []
            for s in range(seqs):
                query = q_scr[s, g * many : (g + 1) * many, :].astype(jnp.bfloat16)
                keys = k_ref[step * seqs + s, :, lanes]
                olds.append(
                    lax.dot_general(
                        query, keys, (((1,), (1,)), ((), ())), preferred_element_type=jnp.float32
                    )
                )
                news.append(
                    lax.dot_general(
                        query, new_keys, (((1,), (1,)), ((), ())), preferred_element_type=jnp.float32
                    )
                )
            for s in range(seqs):
                live = slot_ids < length_ref[step * seqs + s]
                seen = (new_cols >= s * NEW) & (new_cols <= s * NEW + new_rows)
                old = jnp.where(live, olds[s] * scale, -1e30)
                new = jnp.where(seen, news[s] * scale, -1e30)
                top = jnp.maximum(
                    jnp.max(old, axis=1, keepdims=True), jnp.max(new, axis=1, keepdims=True)
                )
                old = jnp.exp2(old - top)
                new = jnp.exp2(new - top)
                total = jnp.sum(old, axis=1, keepdims=True) + jnp.sum(new, axis=1, keepdims=True)
                inverse = 1.0 / total
                olds[s] = (old * inverse).astype(jnp.bfloat16)
                news[s] = (new * inverse).astype(jnp.bfloat16)
            for s in range(seqs):
                values = v_ref[step * seqs + s, :, lanes]
                mixes.append(
                    jnp.dot(olds[s], values, preferred_element_type=jnp.float32)
                    + jnp.dot(news[s], new_values, preferred_element_type=jnp.float32)
                )
            for s in range(seqs):
                for h in range(heads):
                    at = (g * heads + h) * HD
                    o_scr[s * NEW : (s + 1) * NEW, at : at + HD] = mixes[s][
                        h * NEW : (h + 1) * NEW
                    ]
        out_ref[mine, :] = o_scr[...].astype(jnp.bfloat16)

    for copy in w_copies:
        copy.wait()


def attend(chunk, offsets, kv_offset, sums, squares, cosine, sine, cache_keys, cache_values, lengths, w_out):
    seq_count, slots, kv_all = cache_keys.shape
    kv = kv_all // CHUNKS
    groups = kv // HD
    heads = len(offsets) // groups
    cols = len(offsets) * HD
    seqs = min(4, seq_count)
    rows = seq_count * NEW
    source, copied = [], []
    if chunk == 0:
        source.append(in_hbm(w_out))
        copied.append(pltpu.VMEM((w_out.shape[0] // CHUNKS, w_out.shape[1]), w_out.dtype))
    vmem = pl.BlockSpec(memory_space=pltpu.VMEM)
    hbm = pl.BlockSpec(memory_space=pltpu.HBM)
    return pl.pallas_call(
        functools.partial(attend_kernel, chunk, offsets, kv_offset, groups, heads, seqs),
        out_shape=[pltpu.VMEM((rows, cols), jnp.bfloat16)] + copied,
        in_specs=[pl.BlockSpec(memory_space=pltpu.SMEM)] + [vmem] * 6 + [hbm] * len(source),
        out_specs=[vmem] * (1 + len(copied)),
        scratch_shapes=[
            pltpu.VMEM((seqs, groups * heads * NEW, HD), jnp.float32),
            pltpu.VMEM((seqs * NEW, cols), jnp.float32),
        ]
        + [pltpu.SemaphoreType.DMA((4,))] * len(copied),
        compiler_params=pltpu.CompilerParams(vmem_limit_bytes=16 * MIB),
        name="attend",
    )(lengths, sums, squares, cosine, sine, cache_keys, cache_values, *source)


def fetch_kernel(count, pieces, *refs):
    sources, targets, sems = refs[:count], refs[count : 2 * count], refs[2 * count]
    copies = []
    for i, (source, target) in enumerate(zip(sources, targets)):
        size = target.shape[0] // pieces
        for p in range(pieces):
            at = slice(p * size, (p + 1) * size)
            copies.append(
                pltpu.make_async_copy(source.at[at], target.at[at], sems.at[i * pieces + p])
            )
    for copy in copies:
        copy.start()
    for copy in copies:
        copy.wait()


def fetch(*arrays):
    pieces = 4
    return pl.pallas_call(
        functools.partial(fetch_kernel, len(arrays), pieces),
        out_shape=[pltpu.VMEM(array.shape, array.dtype) for array in arrays],
        in_specs=[pl.BlockSpec(memory_space=pltpu.HBM)] * len(arrays),
        out_specs=[pl.BlockSpec(memory_space=pltpu.VMEM)] * len(arrays),
        scratch_shapes=[pltpu.SemaphoreType.DMA((pieces * len(arrays),))],
        compiler_params=pltpu.CompilerParams(vmem_limit_bytes=4 * MIB),
        name="fetch",
    )(*[in_hbm(array) for array in arrays])


def fetch_rows_kernel(start, pieces, source, target, sems):
    size = target.shape[0] // pieces
    copies = [
        pltpu.make_async_copy(
            source.at[start + p * size : start + (p + 1) * size],
            target.at[p * size : (p + 1) * size],
            sems.at[p],
        )
        for p in range(pieces)
    ]
    for copy in copies:
        copy.start()
    for copy in copies:
        copy.wait()


def fetch_rows(array, start, rows):
    pieces = 4
    return pl.pallas_call(
        functools.partial(fetch_rows_kernel, start, pieces),
        out_shape=pltpu.VMEM((rows, array.shape[1]), array.dtype),
        in_specs=[pl.BlockSpec(memory_space=pltpu.HBM)],
        out_specs=pl.BlockSpec(memory_space=pltpu.VMEM),
        scratch_shapes=[pltpu.SemaphoreType.DMA((pieces,))],
        compiler_params=pltpu.CompilerParams(vmem_limit_bytes=4 * MIB),
        name="fetch_rows",
    )(in_hbm(array))


def combine_kernel(n, block, chunk, *refs):
    pieces, refs = refs[:n], refs[n:]
    gx, gy = lax.axis_index("gx"), lax.axis_index("gy")
    moved = jnp.where(gy == 0, n // 2, 0)
    if chunk:
        before_ref, refs = refs[0], refs[1:]
    w_ref, outs, x_buf = refs[0], refs[1:-1], refs[-1]
    depth, cols = x_buf.shape[1], w_ref.shape[1]
    half = x_buf.shape[0] // 2
    for slot, piece in enumerate(pieces):
        owner = slot_owner(n, slot, gx, gy, gather_orders(n, chunk))
        start = pl.multiple_of((owner ^ moved) * block, block)
        x_buf[pl.ds(start, block), :] = piece[...]

    tile = cols // TILES
    for start in range(0, cols, tile):
        at = slice(start, start + tile)
        product = jnp.dot(x_buf[...], w_ref[:, at], preferred_element_type=jnp.float32)
        if chunk:
            product = product + before_ref[:, at]
        if len(outs) == 1:
            outs[0][:, at] = product
        else:
            outs[0][:, at] = product[:half].astype(jnp.bfloat16)
            outs[1][:, at] = product[half:]


def combine(chunk, pieces, before, w_out):
    n, (block, depth) = len(pieces), pieces[0].shape
    rows = n * block
    cols = w_out.shape[1]
    last = chunk == CHUNKS - 1
    hbm = pl.BlockSpec(memory_space=pltpu.HBM)
    vmem = pl.BlockSpec(memory_space=pltpu.VMEM)
    if last:
        out_shape = [
            pltpu.VMEM((rows // 2, cols), jnp.bfloat16),
            pltpu.VMEM((rows // 2, cols), jnp.float32),
        ]
    else:
        out_shape = [pltpu.VMEM((rows, cols), jnp.float32)]
    earlier = [] if chunk == 0 else [before]
    return pl.pallas_call(
        functools.partial(combine_kernel, n, block, chunk),
        out_shape=out_shape,
        in_specs=[vmem] * (len(pieces) + len(earlier) + 1),
        out_specs=[vmem] * len(out_shape),
        scratch_shapes=[
            pltpu.VMEM((rows, depth), jnp.bfloat16),
        ],
        compiler_params=pltpu.CompilerParams(vmem_limit_bytes=16 * MIB),
        name="combine",
    )(*pieces, *earlier, w_out)


def shards(
    tokens, norm_gain, w_query, w_key, w_value, w_out, cache_keys, cache_values, cache_lengths
):
    n = lax.axis_size("gx")
    cores = lax.axis_size("gy")
    levels = n.bit_length() - 1
    position = (cache_lengths[:, None] + jnp.arange(NEW, dtype=jnp.int32)[None, :]).reshape(-1)
    inverse = THETA ** (-2.0 * jnp.arange(HD // 2, dtype=jnp.float32) / HD)
    angles = position.astype(jnp.float32)[:, None] * inverse[None, :]
    cosine, sine = jnp.cos(angles), jnp.sin(angles)
    cosine = jnp.concatenate([cosine, cosine], axis=1)
    sine = jnp.concatenate([-sine, sine], axis=1)

    x, gain = tokens, norm_gain[None, :]
    kv = w_key.shape[1] // CHUNKS
    q_cols = w_query.shape[1] // CHUNKS

    def column_part(start, size, kv_start):
        return project(
            n, start, size, kv_start, start == 0, x, gain, w_query, w_key, w_value
        )

    def after(value, *earlier):
        return lax.optimization_barrier((value, earlier))[0]

    share = q_cols // 2
    orders = bit_orders(n)
    send_a, keep_a, x = column_part(0, share, None)
    x = after(x, send_a)
    other_a = exchange(send_a, n, cores, 0, orders)
    send_b, keep_b = column_part(share, share, 0)
    x = after(x, send_b)
    other_b = exchange(send_b, n, cores, 0, orders)
    sum_a = keep_a + other_a.astype(jnp.float32)
    x = after(x, sum_a)
    later = []
    for chunk in range(1, CHUNKS):
        later.append(column_part(chunk * q_cols, q_cols, chunk * kv))
    other_b = after(other_b, *(send_c for send_c, _ in later))
    first = jnp.concatenate([sum_a, keep_b + other_b.astype(jnp.float32)], axis=1)
    half = first.shape[0] // 2
    send = first[half:].astype(jnp.bfloat16)
    flows = [[1, first[:half], send]]
    for send_c, keep_c in later:
        flows.append([0, keep_c, after(send_c, flows[-1][2])])

    def start(flow):
        return exchange(flow[2], n, cores, flow[0], orders)

    def finish(flow, other, *earlier):
        stage, keep, _ = flow
        if earlier:
            other = after(other, *earlier)
        value = keep + other.astype(jnp.float32)
        low = value.shape[0] // 2 if stage < levels - 1 else 0
        flow[:] = stage + 1, value[:low] if low else value, value[low:].astype(jnp.bfloat16)

    lead, follow = flows
    w_rows = w_out.shape[0] // CHUNKS
    weights = [fetch_rows(after(w_out, lead[2], follow[2]), 0, w_rows)]
    while follow[0] < levels:
        pending = [start(flow) for flow in flows if flow[0] < levels]
        if lead[0] == levels:
            finish(follow, pending[0])
        elif lead[0] == levels - 1:
            cache_keys, cache_values = fetch(*after((cache_keys, cache_values), follow[2]))
            finish(lead, pending[0], cache_keys, cache_values)
            finish(follow, pending[1], lead[1])
        else:
            finish(lead, pending[0], *weights)
            finish(follow, pending[1], lead[2])
    sums = [flow[1] for flow in flows]
    squares = sums[0][:, share : share + 128]
    plain = [h * HD for h in range(q_cols // HD)]
    offsets = [[at if at < share else at + 128 for at in plain], plain]
    kv_offsets = [q_cols + 128, q_cols]

    attentions = []
    for chunk in range(CHUNKS):
        out = attend(
            chunk,
            offsets[chunk],
            kv_offsets[chunk],
            sums[chunk],
            squares,
            cosine,
            sine,
            cache_keys,
            cache_values,
            cache_lengths,
            w_out,
        )
        attentions.append(out[0])
        weights += out[1:]
    gathered = []
    for chunk in range(CHUNKS):
        slots = [attentions[chunk]]
        for slot in range(1, n):
            top = slot.bit_length() - 1
            source = slots[slot - (1 << top)]
            if slot == 1 and chunk == 0:
                source = after(source, sums[1])
            if slot == 3 << (levels - 2):
                source = after(source, slots[1 << (levels - 1)])
            slots.append(
                exchange(source, n, cores, levels - 1 - top, gather_orders(n, chunk))
            )
        gathered.append(slots)
    result = None
    for chunk in range(CHUNKS):
        result = combine(chunk, gathered[chunk], result and result[0], weights[chunk])
    send, keep = result
    other = lax.ppermute(send, "gy", [(0, 1), (1, 0)])
    return (keep + other.astype(jnp.float32)).astype(jnp.bfloat16)


def solution(mesh):
    return jax.shard_map(
        shards,
        mesh=mesh,
        in_specs=(
            P("groups", "gx"),
            P("gx"),
            P("gx", "gy"),
            P("gx", "gy"),
            P("gx", "gy"),
            P("gy", "gx"),
            P(("groups", "gx"), None, "gy"),
            P(("groups", "gx"), None, "gy"),
            P(("groups", "gx")),
        ),
        out_specs=P(("groups", "gy"), "gx"),
        check_vma=False,
    )
```

```python
import functools
import math

import jax
import jax.numpy as jnp
from jax import lax
from jax.experimental import pallas as pl
from jax.experimental.pallas import tpu as pltpu
from jax.sharding import PartitionSpec as P

D = 16384
HD = 128
NEW = 4
EPS = 1e-05
THETA = 500000.0

CHUNKS = 2
TILES = 2
MIB = 1 << 20


def bit_orders(n):
    levels = n.bit_length() - 1
    first = list(range(levels))
    second = list(first)
    if levels > 1:
        second[0], second[1] = second[1], second[0]
    return first, second


def gather_orders(n, chunk):
    first, second = bit_orders(n)
    return (first, second) if chunk else (first, first)


def slot_shift(slot, order):
    levels = len(order)
    shift = 0
    for stage in range(levels):
        shift |= ((slot >> (levels - 1 - stage)) & 1) << order[stage]
    return shift


def slot_owner(n, slot, gx, gy, orders):
    first, second = (slot_shift(slot, order) for order in orders)
    return gx ^ jnp.where(gy == 0, first, second)


def exchange(value, n, cores, stage, orders):
    pairs = []
    for gx in range(n):
        for gy in range(cores):
            other = gx ^ (1 << orders[gy % 2][stage])
            pairs.append((gx * cores + gy, other * cores + gy))
    return lax.ppermute(value, ("gx", "gy"), pairs)


def project_kernel(n, q_start, kv_start, first, *refs):
    if first:
        tokens_ref, gain_ref, wq_ref, wk_ref, wv_ref, send_ref, keep_ref, x_ref = refs[:8]
        t_buf, t_sems, g_buf, g_sem = refs[8:12]
    else:
        x_ref, wq_ref, wk_ref, wv_ref, send_ref, keep_ref = refs[:6]
    w_buf, sems = refs[-2:]
    half = send_ref.shape[0]
    rows = 2 * half
    with_kv = kv_start is not None
    kv = wk_ref.shape[1] // CHUNKS if with_kv else 0
    width = w_buf.shape[1]
    cols = width - 2 * kv
    pieces = 1 if first else 4 if cols > 1024 else 2
    tile = cols // pieces

    def w_copy(ref, start, size, at, sem):
        return pltpu.make_async_copy(
            ref.at[:, start : start + size], w_buf.at[:, at : at + size], sems.at[sem]
        )

    copies = [[w_copy(wq_ref, q_start + p * tile, tile, p * tile, p)] for p in range(pieces)]
    if with_kv:
        copies[-1].append(w_copy(wk_ref, kv_start, kv, cols, pieces))
        copies[-1].append(w_copy(wv_ref, kv_start, kv, cols + kv, pieces + 1))

    if first:
        block = rows // n
        me, gy = lax.axis_index("gx"), lax.axis_index("gy")
        t_copies = []
        for slot in range(n):
            start = pl.multiple_of(slot_owner(n, slot, me, gy, bit_orders(n)) * block, block)
            t_copies.append(
                pltpu.make_async_copy(
                    tokens_ref.at[pl.ds(start, block), :], t_buf.at[slot], t_sems.at[slot]
                )
            )
            t_copies[-1].start()
        g_copy = pltpu.make_async_copy(gain_ref, g_buf, g_sem)
        g_copy.start()
    for group in copies:
        for copy in group:
            copy.start()
    if first:
        lanes = lax.broadcasted_iota(jnp.int32, (block, 128), 1)
        g_copy.wait()
        for slot in range(n):
            t_copies[slot].wait()
            wide = t_buf[slot].astype(jnp.float32)
            x_ref[slot * block : (slot + 1) * block, :] = (wide * g_buf[...]).astype(jnp.bfloat16)
            square = jnp.sum(wide * wide, axis=1, keepdims=True)
            high = square.astype(jnp.bfloat16).astype(jnp.float32)
            rest = square - high
            middle = rest.astype(jnp.bfloat16).astype(jnp.float32)
            low = rest - middle
            packed = jnp.where(
                lanes == 3 * me,
                high,
                jnp.where(lanes == 3 * me + 1, middle, jnp.where(lanes == 3 * me + 2, low, 0.0)),
            )
            if slot < n // 2:
                keep_ref[slot * block : (slot + 1) * block, width : width + 128] = packed
            else:
                at = (slot - n // 2) * block
                send_ref[at : at + block, width : width + 128] = packed.astype(jnp.bfloat16)

    for p in range(pieces):
        start, end = p * tile, (p + 1) * tile if p < pieces - 1 else width
        for copy in copies[p]:
            copy.wait()
        product = jnp.dot(x_ref[...], w_buf[:, start:end], preferred_element_type=jnp.float32)
        keep_ref[:, start:end] = product[:half]
        send_ref[:, start:end] = product[half:].astype(jnp.bfloat16)


def in_hbm(value):
    return pltpu.with_memory_space_constraint(value, pltpu.HBM)


def project(n, q_start, q_cols, kv_start, first, x, gain, w_query, w_key, w_value):
    rows, depth = x.shape
    kv = w_key.shape[1] // CHUNKS if kv_start is not None else 0
    width = q_cols + 2 * kv
    full = width + (128 if first else 0)
    hbm = pl.BlockSpec(memory_space=pltpu.HBM)
    vmem = pl.BlockSpec(memory_space=pltpu.VMEM)
    out_shape = [
        pltpu.VMEM((rows // 2, full), jnp.bfloat16),
        pltpu.VMEM((rows // 2, full), jnp.float32),
    ]
    scratch = [pltpu.VMEM((depth, width), jnp.bfloat16), pltpu.SemaphoreType.DMA((6,))]
    if first:
        out_shape.append(pltpu.VMEM((rows, depth), jnp.bfloat16))
        args = [in_hbm(x), in_hbm(gain)]
        in_specs = [hbm, hbm]
        scratch = [
            pltpu.VMEM((n, rows // n, depth), jnp.bfloat16),
            pltpu.SemaphoreType.DMA((n,)),
            pltpu.VMEM((1, depth), jnp.float32),
            pltpu.SemaphoreType.DMA,
        ] + scratch
    else:
        args, in_specs = [x], [vmem]
    return pl.pallas_call(
        functools.partial(project_kernel, n, q_start, kv_start, first),
        out_shape=out_shape,
        in_specs=in_specs + [hbm] * 3,
        out_specs=[vmem] * len(out_shape),
        scratch_shapes=scratch,
        compiler_params=pltpu.CompilerParams(vmem_limit_bytes=16 * MIB),
        name="project",
    )(*args, in_hbm(w_query), in_hbm(w_key), in_hbm(w_value))


def attend_kernel(chunk, offsets, kv_offset, groups, heads, seqs, length_ref, *refs):
    sum_ref, square_ref = refs[:2]
    w_copies = []
    if chunk == 0:
        cos_ref, sin_ref, k_ref, v_ref, w_ref, out_ref, next_ref, q_scr, o_scr, w_sems = refs[2:]
        total = next_ref.shape[0]
        for p in range(4):
            at = slice(p * total // 4, (p + 1) * total // 4)
            w_copies.append(
                pltpu.make_async_copy(
                    w_ref.at[total + at.start : total + at.stop], next_ref.at[at], w_sems.at[p]
                )
            )
            w_copies[-1].start()
    else:
        cos_ref, sin_ref, k_ref, v_ref, out_ref, q_scr, o_scr = refs[2:]
    rows = seqs * NEW
    cols = groups * heads * HD
    kv = groups * HD
    seq_count = k_ref.shape[0]

    scale = HD**-0.5 * math.log2(math.e)
    slots = k_ref.shape[1]
    many = heads * NEW
    slot_ids = lax.broadcasted_iota(jnp.int32, (1, slots), 1)
    new_cols = lax.broadcasted_iota(jnp.int32, (many, rows), 1)
    new_rows = lax.broadcasted_iota(jnp.int32, (many, rows), 0) % NEW

    @pl.loop(0, seq_count // seqs, unroll=chunk > 0)
    def _(step):
        mine = pl.ds(pl.multiple_of(step * rows, rows), rows)
        mean = jnp.sum(square_ref[mine, :], axis=1, keepdims=True) / D
        row_scale = lax.rsqrt(mean + EPS)
        cosine, sine = cos_ref[mine, :], sin_ref[mine, :]

        def raw(start):
            return sum_ref[mine, start : start + HD] * row_scale

        def rotary(value):
            return value * cosine + pltpu.roll(value, HD // 2, 1) * sine

        for h in range(heads * groups):
            turned = rotary(raw(offsets[h]))
            for s in range(seqs):
                q_scr[s, h * NEW : (h + 1) * NEW, :] = turned[s * NEW : (s + 1) * NEW]
        for g in range(groups):
            new_keys = rotary(raw(kv_offset + g * HD)).astype(jnp.bfloat16)
            new_values = raw(kv_offset + (groups + g) * HD).astype(jnp.bfloat16)
            lanes = slice(chunk * kv + g * HD, chunk * kv + (g + 1) * HD)
            olds, news, mixes = [], [], []
            for s in range(seqs):
                query = q_scr[s, g * many : (g + 1) * many, :].astype(jnp.bfloat16)
                keys = k_ref[step * seqs + s, :, lanes]
                olds.append(
                    lax.dot_general(
                        query, keys, (((1,), (1,)), ((), ())), preferred_element_type=jnp.float32
                    )
                )
                news.append(
                    lax.dot_general(
                        query, new_keys, (((1,), (1,)), ((), ())), preferred_element_type=jnp.float32
                    )
                )
            for s in range(seqs):
                live = slot_ids < length_ref[step * seqs + s]
                seen = (new_cols >= s * NEW) & (new_cols <= s * NEW + new_rows)
                old = jnp.where(live, olds[s] * scale, -1e30)
                new = jnp.where(seen, news[s] * scale, -1e30)
                top = jnp.maximum(
                    jnp.max(old, axis=1, keepdims=True), jnp.max(new, axis=1, keepdims=True)
                )
                old = jnp.exp2(old - top)
                new = jnp.exp2(new - top)
                total = jnp.sum(old, axis=1, keepdims=True) + jnp.sum(new, axis=1, keepdims=True)
                inverse = 1.0 / total
                olds[s] = (old * inverse).astype(jnp.bfloat16)
                news[s] = (new * inverse).astype(jnp.bfloat16)
            for s in range(seqs):
                values = v_ref[step * seqs + s, :, lanes]
                mixes.append(
                    jnp.dot(olds[s], values, preferred_element_type=jnp.float32)
                    + jnp.dot(news[s], new_values, preferred_element_type=jnp.float32)
                )
            for s in range(seqs):
                for h in range(heads):
                    at = (g * heads + h) * HD
                    o_scr[s * NEW : (s + 1) * NEW, at : at + HD] = mixes[s][
                        h * NEW : (h + 1) * NEW
                    ]
        out_ref[mine, :] = o_scr[...].astype(jnp.bfloat16)

    for copy in w_copies:
        copy.wait()


def attend(chunk, offsets, kv_offset, sums, squares, cosine, sine, cache_keys, cache_values, lengths, w_out):
    seq_count, slots, kv_all = cache_keys.shape
    kv = kv_all // CHUNKS
    groups = kv // HD
    heads = len(offsets) // groups
    cols = len(offsets) * HD
    seqs = min(4, seq_count)
    rows = seq_count * NEW
    source, copied = [], []
    if chunk == 0:
        source.append(in_hbm(w_out))
        copied.append(pltpu.VMEM((w_out.shape[0] // CHUNKS, w_out.shape[1]), w_out.dtype))
    vmem = pl.BlockSpec(memory_space=pltpu.VMEM)
    hbm = pl.BlockSpec(memory_space=pltpu.HBM)
    return pl.pallas_call(
        functools.partial(attend_kernel, chunk, offsets, kv_offset, groups, heads, seqs),
        out_shape=[pltpu.VMEM((rows, cols), jnp.bfloat16)] + copied,
        in_specs=[pl.BlockSpec(memory_space=pltpu.SMEM)] + [vmem] * 6 + [hbm] * len(source),
        out_specs=[vmem] * (1 + len(copied)),
        scratch_shapes=[
            pltpu.VMEM((seqs, groups * heads * NEW, HD), jnp.float32),
            pltpu.VMEM((seqs * NEW, cols), jnp.float32),
        ]
        + [pltpu.SemaphoreType.DMA((4,))] * len(copied),
        compiler_params=pltpu.CompilerParams(vmem_limit_bytes=16 * MIB),
        name="attend",
    )(lengths, sums, squares, cosine, sine, cache_keys, cache_values, *source)


def fetch_kernel(count, pieces, *refs):
    sources, targets, sems = refs[:count], refs[count : 2 * count], refs[2 * count]
    copies = []
    for i, (source, target) in enumerate(zip(sources, targets)):
        size = target.shape[0] // pieces
        for p in range(pieces):
            at = slice(p * size, (p + 1) * size)
            copies.append(
                pltpu.make_async_copy(source.at[at], target.at[at], sems.at[i * pieces + p])
            )
    for copy in copies:
        copy.start()
    for copy in copies:
        copy.wait()


def fetch(*arrays):
    pieces = 4
    return pl.pallas_call(
        functools.partial(fetch_kernel, len(arrays), pieces),
        out_shape=[pltpu.VMEM(array.shape, array.dtype) for array in arrays],
        in_specs=[pl.BlockSpec(memory_space=pltpu.HBM)] * len(arrays),
        out_specs=[pl.BlockSpec(memory_space=pltpu.VMEM)] * len(arrays),
        scratch_shapes=[pltpu.SemaphoreType.DMA((pieces * len(arrays),))],
        compiler_params=pltpu.CompilerParams(vmem_limit_bytes=4 * MIB),
        name="fetch",
    )(*[in_hbm(array) for array in arrays])


def fetch_rows_kernel(start, pieces, source, target, sems):
    size = target.shape[0] // pieces
    copies = [
        pltpu.make_async_copy(
            source.at[start + p * size : start + (p + 1) * size],
            target.at[p * size : (p + 1) * size],
            sems.at[p],
        )
        for p in range(pieces)
    ]
    for copy in copies:
        copy.start()
    for copy in copies:
        copy.wait()


def fetch_rows(array, start, rows):
    pieces = 4
    return pl.pallas_call(
        functools.partial(fetch_rows_kernel, start, pieces),
        out_shape=pltpu.VMEM((rows, array.shape[1]), array.dtype),
        in_specs=[pl.BlockSpec(memory_space=pltpu.HBM)],
        out_specs=pl.BlockSpec(memory_space=pltpu.VMEM),
        scratch_shapes=[pltpu.SemaphoreType.DMA((pieces,))],
        compiler_params=pltpu.CompilerParams(vmem_limit_bytes=4 * MIB),
        name="fetch_rows",
    )(in_hbm(array))


def combine_kernel(n, block, chunk, *refs):
    pieces, refs = refs[:n], refs[n:]
    gx, gy = lax.axis_index("gx"), lax.axis_index("gy")
    moved = jnp.where(gy == 0, n // 2, 0)
    if chunk:
        before_ref, refs = refs[0], refs[1:]
    w_ref, outs, x_buf = refs[0], refs[1:-1], refs[-1]
    depth, cols = x_buf.shape[1], w_ref.shape[1]
    half = x_buf.shape[0] // 2
    for slot, piece in enumerate(pieces):
        owner = slot_owner(n, slot, gx, gy, gather_orders(n, chunk))
        start = pl.multiple_of((owner ^ moved) * block, block)
        x_buf[pl.ds(start, block), :] = piece[...]

    tile = cols // TILES
    for start in range(0, cols, tile):
        at = slice(start, start + tile)
        product = jnp.dot(x_buf[...], w_ref[:, at], preferred_element_type=jnp.float32)
        if chunk:
            product = product + before_ref[:, at]
        if len(outs) == 1:
            outs[0][:, at] = product
        else:
            outs[0][:, at] = product[:half].astype(jnp.bfloat16)
            outs[1][:, at] = product[half:]


def combine(chunk, pieces, before, w_out):
    n, (block, depth) = len(pieces), pieces[0].shape
    rows = n * block
    cols = w_out.shape[1]
    last = chunk == CHUNKS - 1
    hbm = pl.BlockSpec(memory_space=pltpu.HBM)
    vmem = pl.BlockSpec(memory_space=pltpu.VMEM)
    if last:
        out_shape = [
            pltpu.VMEM((rows // 2, cols), jnp.bfloat16),
            pltpu.VMEM((rows // 2, cols), jnp.float32),
        ]
    else:
        out_shape = [pltpu.VMEM((rows, cols), jnp.float32)]
    earlier = [] if chunk == 0 else [before]
    return pl.pallas_call(
        functools.partial(combine_kernel, n, block, chunk),
        out_shape=out_shape,
        in_specs=[vmem] * (len(pieces) + len(earlier) + 1),
        out_specs=[vmem] * len(out_shape),
        scratch_shapes=[
            pltpu.VMEM((rows, depth), jnp.bfloat16),
        ],
        compiler_params=pltpu.CompilerParams(vmem_limit_bytes=16 * MIB),
        name="combine",
    )(*pieces, *earlier, w_out)


def shards(
    tokens, norm_gain, w_query, w_key, w_value, w_out, cache_keys, cache_values, cache_lengths
):
    n = lax.axis_size("gx")
    cores = lax.axis_size("gy")
    levels = n.bit_length() - 1
    position = (cache_lengths[:, None] + jnp.arange(NEW, dtype=jnp.int32)[None, :]).reshape(-1)
    inverse = THETA ** (-2.0 * jnp.arange(HD // 2, dtype=jnp.float32) / HD)
    angles = position.astype(jnp.float32)[:, None] * inverse[None, :]
    cosine, sine = jnp.cos(angles), jnp.sin(angles)
    cosine = jnp.concatenate([cosine, cosine], axis=1)
    sine = jnp.concatenate([-sine, sine], axis=1)

    x, gain = tokens, norm_gain[None, :]
    kv = w_key.shape[1] // CHUNKS
    q_cols = w_query.shape[1] // CHUNKS

    def column_part(start, size, kv_start):
        return project(
            n, start, size, kv_start, start == 0, x, gain, w_query, w_key, w_value
        )

    def after(value, *earlier):
        return lax.optimization_barrier((value, earlier))[0]

    share = q_cols // 2
    orders = bit_orders(n)
    send_a, keep_a, x = column_part(0, share, None)
    x = after(x, send_a)
    other_a = exchange(send_a, n, cores, 0, orders)
    send_b, keep_b = column_part(share, share, 0)
    x = after(x, send_b)
    other_b = exchange(send_b, n, cores, 0, orders)
    sum_a = keep_a + other_a.astype(jnp.float32)
    x = after(x, sum_a)
    later = []
    for chunk in range(1, CHUNKS):
        later.append(column_part(chunk * q_cols, q_cols, chunk * kv))
    other_b = after(other_b, *(send_c for send_c, _ in later))
    first = jnp.concatenate([sum_a, keep_b + other_b.astype(jnp.float32)], axis=1)
    half = first.shape[0] // 2
    send = first[half:].astype(jnp.bfloat16)
    flows = [[1, first[:half], send]]
    for send_c, keep_c in later:
        flows.append([0, keep_c, after(send_c, flows[-1][2])])

    def start(flow):
        return exchange(flow[2], n, cores, flow[0], orders)

    def finish(flow, other, *earlier):
        stage, keep, _ = flow
        if earlier:
            other = after(other, *earlier)
        value = keep + other.astype(jnp.float32)
        low = value.shape[0] // 2 if stage < levels - 1 else 0
        flow[:] = stage + 1, value[:low] if low else value, value[low:].astype(jnp.bfloat16)

    lead, follow = flows
    w_rows = w_out.shape[0] // CHUNKS
    weights = [fetch_rows(after(w_out, lead[2], follow[2]), 0, w_rows)]
    while follow[0] < levels:
        pending = [start(flow) for flow in flows if flow[0] < levels]
        if lead[0] == levels:
            finish(follow, pending[0])
        elif lead[0] == levels - 1:
            cache_keys, cache_values = fetch(*after((cache_keys, cache_values), follow[2]))
            finish(lead, pending[0], cache_keys, cache_values)
            finish(follow, pending[1], lead[1])
        else:
            finish(lead, pending[0], *weights)
            finish(follow, pending[1], lead[2])
    sums = [flow[1] for flow in flows]
    squares = sums[0][:, share : share + 128]
    plain = [h * HD for h in range(q_cols // HD)]
    offsets = [[at if at < share else at + 128 for at in plain], plain]
    kv_offsets = [q_cols + 128, q_cols]

    attentions = []
    for chunk in range(CHUNKS):
        out = attend(
            chunk,
            offsets[chunk],
            kv_offsets[chunk],
            sums[chunk],
            squares,
            cosine,
            sine,
            cache_keys,
            cache_values,
            cache_lengths,
            w_out,
        )
        attentions.append(out[0])
        weights += out[1:]
    early = {
        1 << (levels - 1 - stage): exchange(
            attentions[1], n, cores, stage, gather_orders(n, 1)
        )
        for stage in range(min(2, levels - 1))
    }
    gathered = []
    for chunk in range(CHUNKS):
        slots = [attentions[chunk]]
        for slot in range(1, n):
            if chunk == 1 and slot in early:
                slots.append(early[slot])
                continue
            top = slot.bit_length() - 1
            source = slots[slot - (1 << top)]
            if slot == 3 << (levels - 2):
                source = after(source, slots[1 << (levels - 1)])
            if chunk == 0 and slot == 3:
                source = after(source, *early.values())
            slots.append(
                exchange(source, n, cores, levels - 1 - top, gather_orders(n, chunk))
            )
        gathered.append(slots)
    result = None
    for chunk in range(CHUNKS):
        result = combine(chunk, gathered[chunk], result and result[0], weights[chunk])
    send, keep = result
    other = lax.ppermute(send, "gy", [(0, 1), (1, 0)])
    return (keep + other.astype(jnp.float32)).astype(jnp.bfloat16)


def solution(mesh):
    return jax.shard_map(
        shards,
        mesh=mesh,
        in_specs=(
            P("groups", "gx"),
            P("gx"),
            P("gx", "gy"),
            P("gx", "gy"),
            P("gx", "gy"),
            P("gy", "gx"),
            P(("groups", "gx"), None, "gy"),
            P(("groups", "gx"), None, "gy"),
            P(("groups", "gx")),
        ),
        out_specs=P(("groups", "gy"), "gx"),
        check_vma=False,
    )
```

```python
import functools
import math

import jax
import jax.numpy as jnp
from jax import lax
from jax.experimental import pallas as pl
from jax.experimental.pallas import tpu as pltpu
from jax.sharding import PartitionSpec as P

D = 16384
HD = 128
NEW = 4
EPS = 1e-05
THETA = 500000.0

CHUNKS = 2
TILES = 1
MIB = 1 << 20


def bit_orders(n):
    levels = n.bit_length() - 1
    first = list(range(levels))
    second = list(first)
    if levels > 1:
        second[0], second[1] = second[1], second[0]
    return first, second


def gather_orders(n, chunk):
    first, second = bit_orders(n)
    return (first, second) if chunk else (first, first)


def slot_shift(slot, order):
    levels = len(order)
    shift = 0
    for stage in range(levels):
        shift |= ((slot >> (levels - 1 - stage)) & 1) << order[stage]
    return shift


def slot_owner(n, slot, gx, gy, orders):
    first, second = (slot_shift(slot, order) for order in orders)
    return gx ^ jnp.where(gy == 0, first, second)


def exchange(value, n, cores, stage, orders):
    pairs = []
    for gx in range(n):
        for gy in range(cores):
            other = gx ^ (1 << orders[gy % 2][stage])
            pairs.append((gx * cores + gy, other * cores + gy))
    return lax.ppermute(value, ("gx", "gy"), pairs)


def project_kernel(n, q_start, kv_start, first, *refs):
    if first:
        tokens_ref, gain_ref, wq_ref, wk_ref, wv_ref, send_ref, keep_ref, x_ref = refs[:8]
        t_buf, t_sems, g_buf, g_sem = refs[8:12]
    else:
        x_ref, wq_ref, wk_ref, wv_ref, send_ref, keep_ref = refs[:6]
    w_buf, sems = refs[-2:]
    half = send_ref.shape[0]
    rows = 2 * half
    with_kv = kv_start is not None
    kv = wk_ref.shape[1] // CHUNKS if with_kv else 0
    width = w_buf.shape[1]
    cols = width - 2 * kv
    pieces = 1 if first else 4 if cols > 1024 else 2
    tile = cols // pieces

    def w_copy(ref, start, size, at, sem):
        return pltpu.make_async_copy(
            ref.at[:, start : start + size], w_buf.at[:, at : at + size], sems.at[sem]
        )

    copies = [[w_copy(wq_ref, q_start + p * tile, tile, p * tile, p)] for p in range(pieces)]
    if with_kv:
        copies[-1].append(w_copy(wk_ref, kv_start, kv, cols, pieces))
        copies[-1].append(w_copy(wv_ref, kv_start, kv, cols + kv, pieces + 1))

    if first:
        block = rows // n
        me, gy = lax.axis_index("gx"), lax.axis_index("gy")
        t_copies = []
        for slot in range(n):
            start = pl.multiple_of(slot_owner(n, slot, me, gy, bit_orders(n)) * block, block)
            t_copies.append(
                pltpu.make_async_copy(
                    tokens_ref.at[pl.ds(start, block), :], t_buf.at[slot], t_sems.at[slot]
                )
            )
            t_copies[-1].start()
        g_copy = pltpu.make_async_copy(gain_ref, g_buf, g_sem)
        g_copy.start()
    for group in copies:
        for copy in group:
            copy.start()
    if first:
        lanes = lax.broadcasted_iota(jnp.int32, (block, 128), 1)
        g_copy.wait()
        for slot in range(n):
            t_copies[slot].wait()
            wide = t_buf[slot].astype(jnp.float32)
            x_ref[slot * block : (slot + 1) * block, :] = (wide * g_buf[...]).astype(jnp.bfloat16)
            square = jnp.sum(wide * wide, axis=1, keepdims=True)
            high = square.astype(jnp.bfloat16).astype(jnp.float32)
            rest = square - high
            middle = rest.astype(jnp.bfloat16).astype(jnp.float32)
            low = rest - middle
            packed = jnp.where(
                lanes == 3 * me,
                high,
                jnp.where(lanes == 3 * me + 1, middle, jnp.where(lanes == 3 * me + 2, low, 0.0)),
            )
            if slot < n // 2:
                keep_ref[slot * block : (slot + 1) * block, width : width + 128] = packed
            else:
                at = (slot - n // 2) * block
                send_ref[at : at + block, width : width + 128] = packed.astype(jnp.bfloat16)

    for p in range(pieces):
        start, end = p * tile, (p + 1) * tile if p < pieces - 1 else width
        for copy in copies[p]:
            copy.wait()
        product = jnp.dot(x_ref[...], w_buf[:, start:end], preferred_element_type=jnp.float32)
        keep_ref[:, start:end] = product[:half]
        send_ref[:, start:end] = product[half:].astype(jnp.bfloat16)


def in_hbm(value):
    return pltpu.with_memory_space_constraint(value, pltpu.HBM)


def project(n, q_start, q_cols, kv_start, first, x, gain, w_query, w_key, w_value):
    rows, depth = x.shape
    kv = w_key.shape[1] // CHUNKS if kv_start is not None else 0
    width = q_cols + 2 * kv
    full = width + (128 if first else 0)
    hbm = pl.BlockSpec(memory_space=pltpu.HBM)
    vmem = pl.BlockSpec(memory_space=pltpu.VMEM)
    out_shape = [
        pltpu.VMEM((rows // 2, full), jnp.bfloat16),
        pltpu.VMEM((rows // 2, full), jnp.float32),
    ]
    scratch = [pltpu.VMEM((depth, width), jnp.bfloat16), pltpu.SemaphoreType.DMA((6,))]
    if first:
        out_shape.append(pltpu.VMEM((rows, depth), jnp.bfloat16))
        args = [in_hbm(x), in_hbm(gain)]
        in_specs = [hbm, hbm]
        scratch = [
            pltpu.VMEM((n, rows // n, depth), jnp.bfloat16),
            pltpu.SemaphoreType.DMA((n,)),
            pltpu.VMEM((1, depth), jnp.float32),
            pltpu.SemaphoreType.DMA,
        ] + scratch
    else:
        args, in_specs = [x], [vmem]
    return pl.pallas_call(
        functools.partial(project_kernel, n, q_start, kv_start, first),
        out_shape=out_shape,
        in_specs=in_specs + [hbm] * 3,
        out_specs=[vmem] * len(out_shape),
        scratch_shapes=scratch,
        compiler_params=pltpu.CompilerParams(vmem_limit_bytes=16 * MIB),
        name="project",
    )(*args, in_hbm(w_query), in_hbm(w_key), in_hbm(w_value))


def attend_kernel(chunk, offsets, kv_offset, groups, heads, seqs, length_ref, *refs):
    sum_ref, square_ref = refs[:2]
    w_copies = []
    if chunk == 0:
        cos_ref, sin_ref, k_ref, v_ref, w_ref, out_ref, next_ref, q_scr, o_scr, w_sems = refs[2:]
        total = next_ref.shape[0]
        for p in range(4):
            at = slice(p * total // 4, (p + 1) * total // 4)
            w_copies.append(
                pltpu.make_async_copy(
                    w_ref.at[total + at.start : total + at.stop], next_ref.at[at], w_sems.at[p]
                )
            )
            w_copies[-1].start()
    else:
        cos_ref, sin_ref, k_ref, v_ref, out_ref, q_scr, o_scr = refs[2:]
    rows = seqs * NEW
    cols = groups * heads * HD
    kv = groups * HD
    seq_count = k_ref.shape[0]

    scale = HD**-0.5 * math.log2(math.e)
    slots = k_ref.shape[1]
    many = heads * NEW
    slot_ids = lax.broadcasted_iota(jnp.int32, (1, slots), 1)
    new_cols = lax.broadcasted_iota(jnp.int32, (many, rows), 1)
    new_rows = lax.broadcasted_iota(jnp.int32, (many, rows), 0) % NEW

    @pl.loop(0, seq_count // seqs, unroll=chunk > 0)
    def _(step):
        mine = pl.ds(pl.multiple_of(step * rows, rows), rows)
        mean = jnp.sum(square_ref[mine, :], axis=1, keepdims=True) / D
        row_scale = lax.rsqrt(mean + EPS)
        cosine, sine = cos_ref[mine, :], sin_ref[mine, :]

        def raw(start):
            return sum_ref[mine, start : start + HD] * row_scale

        def rotary(value):
            return value * cosine + pltpu.roll(value, HD // 2, 1) * sine

        for h in range(heads * groups):
            turned = rotary(raw(offsets[h]))
            for s in range(seqs):
                q_scr[s, h * NEW : (h + 1) * NEW, :] = turned[s * NEW : (s + 1) * NEW]
        for g in range(groups):
            new_keys = rotary(raw(kv_offset + g * HD)).astype(jnp.bfloat16)
            new_values = raw(kv_offset + (groups + g) * HD).astype(jnp.bfloat16)
            lanes = slice(chunk * kv + g * HD, chunk * kv + (g + 1) * HD)
            olds, news, mixes = [], [], []
            for s in range(seqs):
                query = q_scr[s, g * many : (g + 1) * many, :].astype(jnp.bfloat16)
                keys = k_ref[step * seqs + s, :, lanes]
                olds.append(
                    lax.dot_general(
                        query, keys, (((1,), (1,)), ((), ())), preferred_element_type=jnp.float32
                    )
                )
                news.append(
                    lax.dot_general(
                        query, new_keys, (((1,), (1,)), ((), ())), preferred_element_type=jnp.float32
                    )
                )
            for s in range(seqs):
                live = slot_ids < length_ref[step * seqs + s]
                seen = (new_cols >= s * NEW) & (new_cols <= s * NEW + new_rows)
                old = jnp.where(live, olds[s] * scale, -1e30)
                new = jnp.where(seen, news[s] * scale, -1e30)
                top = jnp.maximum(
                    jnp.max(old, axis=1, keepdims=True), jnp.max(new, axis=1, keepdims=True)
                )
                old = jnp.exp2(old - top)
                new = jnp.exp2(new - top)
                total = jnp.sum(old, axis=1, keepdims=True) + jnp.sum(new, axis=1, keepdims=True)
                inverse = 1.0 / total
                olds[s] = (old * inverse).astype(jnp.bfloat16)
                news[s] = (new * inverse).astype(jnp.bfloat16)
            for s in range(seqs):
                values = v_ref[step * seqs + s, :, lanes]
                mixes.append(
                    jnp.dot(olds[s], values, preferred_element_type=jnp.float32)
                    + jnp.dot(news[s], new_values, preferred_element_type=jnp.float32)
                )
            for s in range(seqs):
                for h in range(heads):
                    at = (g * heads + h) * HD
                    o_scr[s * NEW : (s + 1) * NEW, at : at + HD] = mixes[s][
                        h * NEW : (h + 1) * NEW
                    ]
        out_ref[mine, :] = o_scr[...].astype(jnp.bfloat16)

    for copy in w_copies:
        copy.wait()


def attend(chunk, offsets, kv_offset, sums, squares, cosine, sine, cache_keys, cache_values, lengths, w_out):
    seq_count, slots, kv_all = cache_keys.shape
    kv = kv_all // CHUNKS
    groups = kv // HD
    heads = len(offsets) // groups
    cols = len(offsets) * HD
    seqs = min(4, seq_count)
    rows = seq_count * NEW
    source, copied = [], []
    if chunk == 0:
        source.append(in_hbm(w_out))
        copied.append(pltpu.VMEM((w_out.shape[0] // CHUNKS, w_out.shape[1]), w_out.dtype))
    vmem = pl.BlockSpec(memory_space=pltpu.VMEM)
    hbm = pl.BlockSpec(memory_space=pltpu.HBM)
    return pl.pallas_call(
        functools.partial(attend_kernel, chunk, offsets, kv_offset, groups, heads, seqs),
        out_shape=[pltpu.VMEM((rows, cols), jnp.bfloat16)] + copied,
        in_specs=[pl.BlockSpec(memory_space=pltpu.SMEM)] + [vmem] * 6 + [hbm] * len(source),
        out_specs=[vmem] * (1 + len(copied)),
        scratch_shapes=[
            pltpu.VMEM((seqs, groups * heads * NEW, HD), jnp.float32),
            pltpu.VMEM((seqs * NEW, cols), jnp.float32),
        ]
        + [pltpu.SemaphoreType.DMA((4,))] * len(copied),
        compiler_params=pltpu.CompilerParams(vmem_limit_bytes=16 * MIB),
        name="attend",
    )(lengths, sums, squares, cosine, sine, cache_keys, cache_values, *source)


def fetch_kernel(count, pieces, *refs):
    sources, targets, sems = refs[:count], refs[count : 2 * count], refs[2 * count]
    copies = []
    for i, (source, target) in enumerate(zip(sources, targets)):
        size = target.shape[0] // pieces
        for p in range(pieces):
            at = slice(p * size, (p + 1) * size)
            copies.append(
                pltpu.make_async_copy(source.at[at], target.at[at], sems.at[i * pieces + p])
            )
    for copy in copies:
        copy.start()
    for copy in copies:
        copy.wait()


def fetch(*arrays):
    pieces = 4
    return pl.pallas_call(
        functools.partial(fetch_kernel, len(arrays), pieces),
        out_shape=[pltpu.VMEM(array.shape, array.dtype) for array in arrays],
        in_specs=[pl.BlockSpec(memory_space=pltpu.HBM)] * len(arrays),
        out_specs=[pl.BlockSpec(memory_space=pltpu.VMEM)] * len(arrays),
        scratch_shapes=[pltpu.SemaphoreType.DMA((pieces * len(arrays),))],
        compiler_params=pltpu.CompilerParams(vmem_limit_bytes=4 * MIB),
        name="fetch",
    )(*[in_hbm(array) for array in arrays])


def fetch_rows_kernel(start, pieces, source, target, sems):
    size = target.shape[0] // pieces
    copies = [
        pltpu.make_async_copy(
            source.at[start + p * size : start + (p + 1) * size],
            target.at[p * size : (p + 1) * size],
            sems.at[p],
        )
        for p in range(pieces)
    ]
    for copy in copies:
        copy.start()
    for copy in copies:
        copy.wait()


def fetch_rows(array, start, rows):
    pieces = 4
    return pl.pallas_call(
        functools.partial(fetch_rows_kernel, start, pieces),
        out_shape=pltpu.VMEM((rows, array.shape[1]), array.dtype),
        in_specs=[pl.BlockSpec(memory_space=pltpu.HBM)],
        out_specs=pl.BlockSpec(memory_space=pltpu.VMEM),
        scratch_shapes=[pltpu.SemaphoreType.DMA((pieces,))],
        compiler_params=pltpu.CompilerParams(vmem_limit_bytes=4 * MIB),
        name="fetch_rows",
    )(in_hbm(array))


def combine_kernel(n, block, chunk, *refs):
    pieces, refs = refs[:n], refs[n:]
    gx, gy = lax.axis_index("gx"), lax.axis_index("gy")
    moved = jnp.where(gy == 0, n // 2, 0)
    if chunk:
        before_ref, refs = refs[0], refs[1:]
    w_ref, outs, x_buf = refs[0], refs[1:-1], refs[-1]
    depth, cols = x_buf.shape[1], w_ref.shape[1]
    half = x_buf.shape[0] // 2
    for slot, piece in enumerate(pieces):
        owner = slot_owner(n, slot, gx, gy, gather_orders(n, chunk))
        start = pl.multiple_of((owner ^ moved) * block, block)
        x_buf[pl.ds(start, block), :] = piece[...]

    tile = cols // TILES
    for start in range(0, cols, tile):
        at = slice(start, start + tile)
        product = jnp.dot(x_buf[...], w_ref[:, at], preferred_element_type=jnp.float32)
        if chunk:
            product = product + before_ref[:, at]
        if len(outs) == 1:
            outs[0][:, at] = product
        else:
            outs[0][:, at] = product[:half].astype(jnp.bfloat16)
            outs[1][:, at] = product[half:]


def combine(chunk, pieces, before, w_out):
    n, (block, depth) = len(pieces), pieces[0].shape
    rows = n * block
    cols = w_out.shape[1]
    last = chunk == CHUNKS - 1
    hbm = pl.BlockSpec(memory_space=pltpu.HBM)
    vmem = pl.BlockSpec(memory_space=pltpu.VMEM)
    if last:
        out_shape = [
            pltpu.VMEM((rows // 2, cols), jnp.bfloat16),
            pltpu.VMEM((rows // 2, cols), jnp.float32),
        ]
    else:
        out_shape = [pltpu.VMEM((rows, cols), jnp.float32)]
    earlier = [] if chunk == 0 else [before]
    return pl.pallas_call(
        functools.partial(combine_kernel, n, block, chunk),
        out_shape=out_shape,
        in_specs=[vmem] * (len(pieces) + len(earlier) + 1),
        out_specs=[vmem] * len(out_shape),
        scratch_shapes=[
            pltpu.VMEM((rows, depth), jnp.bfloat16),
        ],
        compiler_params=pltpu.CompilerParams(vmem_limit_bytes=16 * MIB),
        name="combine",
    )(*pieces, *earlier, w_out)


def shards(
    tokens, norm_gain, w_query, w_key, w_value, w_out, cache_keys, cache_values, cache_lengths
):
    n = lax.axis_size("gx")
    cores = lax.axis_size("gy")
    levels = n.bit_length() - 1
    position = (cache_lengths[:, None] + jnp.arange(NEW, dtype=jnp.int32)[None, :]).reshape(-1)
    inverse = THETA ** (-2.0 * jnp.arange(HD // 2, dtype=jnp.float32) / HD)
    angles = position.astype(jnp.float32)[:, None] * inverse[None, :]
    cosine, sine = jnp.cos(angles), jnp.sin(angles)
    cosine = jnp.concatenate([cosine, cosine], axis=1)
    sine = jnp.concatenate([-sine, sine], axis=1)

    x, gain = tokens, norm_gain[None, :]
    kv = w_key.shape[1] // CHUNKS
    q_cols = w_query.shape[1] // CHUNKS

    def column_part(start, size, kv_start):
        return project(
            n, start, size, kv_start, start == 0, x, gain, w_query, w_key, w_value
        )

    def after(value, *earlier):
        return lax.optimization_barrier((value, earlier))[0]

    share = q_cols // 2
    orders = bit_orders(n)
    send_a, keep_a, x = column_part(0, share, None)
    x = after(x, send_a)
    other_a = exchange(send_a, n, cores, 0, orders)
    send_b, keep_b = column_part(share, share, 0)
    x = after(x, send_b)
    other_b = exchange(send_b, n, cores, 0, orders)
    sum_a = keep_a + other_a.astype(jnp.float32)
    x = after(x, sum_a)
    later = []
    for chunk in range(1, CHUNKS):
        later.append(column_part(chunk * q_cols, q_cols, chunk * kv))
    other_b = after(other_b, *(send_c for send_c, _ in later))
    first = jnp.concatenate([sum_a, keep_b + other_b.astype(jnp.float32)], axis=1)
    half = first.shape[0] // 2
    send = first[half:].astype(jnp.bfloat16)
    flows = [[1, first[:half], send]]
    for send_c, keep_c in later:
        flows.append([0, keep_c, after(send_c, flows[-1][2])])

    def start(flow):
        return exchange(flow[2], n, cores, flow[0], orders)

    def finish(flow, other, *earlier):
        stage, keep, _ = flow
        if earlier:
            other = after(other, *earlier)
        value = keep + other.astype(jnp.float32)
        low = value.shape[0] // 2 if stage < levels - 1 else 0
        flow[:] = stage + 1, value[:low] if low else value, value[low:].astype(jnp.bfloat16)

    lead, follow = flows
    w_rows = w_out.shape[0] // CHUNKS
    weights = [fetch_rows(after(w_out, lead[2], follow[2]), 0, w_rows)]
    while follow[0] < levels:
        pending = [start(flow) for flow in flows if flow[0] < levels]
        if lead[0] == levels:
            finish(follow, pending[0])
        elif lead[0] == levels - 1:
            cache_keys, cache_values = fetch(*after((cache_keys, cache_values), follow[2]))
            finish(lead, pending[0], cache_keys, cache_values)
            finish(follow, pending[1], lead[1])
        else:
            finish(lead, pending[0], *weights)
            finish(follow, pending[1], lead[2])
    sums = [flow[1] for flow in flows]
    squares = sums[0][:, share : share + 128]
    plain = [h * HD for h in range(q_cols // HD)]
    offsets = [[at if at < share else at + 128 for at in plain], plain]
    kv_offsets = [q_cols + 128, q_cols]

    attentions = []
    for chunk in range(CHUNKS):
        out = attend(
            chunk,
            offsets[chunk],
            kv_offsets[chunk],
            sums[chunk],
            squares,
            cosine,
            sine,
            cache_keys,
            cache_values,
            cache_lengths,
            w_out,
        )
        attentions.append(out[0])
        weights += out[1:]
    gathered = []
    for chunk in range(CHUNKS):
        slots = [attentions[chunk]]
        for slot in range(1, n):
            top = slot.bit_length() - 1
            source = slots[slot - (1 << top)]
            if slot == 1 and chunk == 0:
                source = after(source, sums[1])
            if slot == 3 << (levels - 2):
                source = after(source, slots[1 << (levels - 1)])
            slots.append(
                exchange(source, n, cores, levels - 1 - top, gather_orders(n, chunk))
            )
        gathered.append(slots)
    result = None
    for chunk in range(CHUNKS):
        result = combine(chunk, gathered[chunk], result and result[0], weights[chunk])
    send, keep = result
    other = lax.ppermute(send, "gy", [(0, 1), (1, 0)])
    return (keep + other.astype(jnp.float32)).astype(jnp.bfloat16)


def solution(mesh):
    return jax.shard_map(
        shards,
        mesh=mesh,
        in_specs=(
            P("groups", "gx"),
            P("gx"),
            P("gx", "gy"),
            P("gx", "gy"),
            P("gx", "gy"),
            P("gy", "gx"),
            P(("groups", "gx"), None, "gy"),
            P(("groups", "gx"), None, "gy"),
            P(("groups", "gx")),
        ),
        out_specs=P(("groups", "gy"), "gx"),
        check_vma=False,
    )
```

```python
import functools
import math

import jax
import jax.numpy as jnp
from jax import lax
from jax.experimental import pallas as pl
from jax.experimental.pallas import tpu as pltpu
from jax.sharding import PartitionSpec as P

D = 16384
HD = 128
NEW = 4
EPS = 1e-05
THETA = 500000.0

CHUNKS = 2
TILES = 2
MIB = 1 << 20


def bit_orders(n):
    levels = n.bit_length() - 1
    first = list(range(levels))
    second = list(first)
    if levels > 1:
        second[0], second[1] = second[1], second[0]
    return first, second


def gather_orders(n, chunk):
    first, second = bit_orders(n)
    return (first, second) if chunk else (first, first)


def slot_shift(slot, order):
    levels = len(order)
    shift = 0
    for stage in range(levels):
        shift |= ((slot >> (levels - 1 - stage)) & 1) << order[stage]
    return shift


def slot_owner(n, slot, gx, gy, orders):
    first, second = (slot_shift(slot, order) for order in orders)
    return gx ^ jnp.where(gy == 0, first, second)


def exchange(value, n, cores, stage, orders):
    pairs = []
    for gx in range(n):
        for gy in range(cores):
            other = gx ^ (1 << orders[gy % 2][stage])
            pairs.append((gx * cores + gy, other * cores + gy))
    return lax.ppermute(value, ("gx", "gy"), pairs)


def project_kernel(n, q_start, kv_start, first, *refs):
    if first:
        tokens_ref, gain_ref, wq_ref, wk_ref, wv_ref, send_ref, keep_ref, x_ref = refs[:8]
        t_buf, t_sems, g_buf, g_sem = refs[8:12]
    else:
        x_ref, wq_ref, wk_ref, wv_ref, send_ref, keep_ref = refs[:6]
    w_buf, sems = refs[-2:]
    half = send_ref.shape[0]
    rows = 2 * half
    with_kv = kv_start is not None
    kv = wk_ref.shape[1] // CHUNKS if with_kv else 0
    width = w_buf.shape[1]
    cols = width - 2 * kv
    pieces = 4 if cols > 1024 else 1
    tile = cols // pieces

    def w_copy(ref, start, size, at, sem):
        return pltpu.make_async_copy(
            ref.at[:, start : start + size], w_buf.at[:, at : at + size], sems.at[sem]
        )

    copies = [[w_copy(wq_ref, q_start + p * tile, tile, p * tile, p)] for p in range(pieces)]
    if with_kv:
        copies[-1].append(w_copy(wk_ref, kv_start, kv, cols, pieces))
        copies[-1].append(w_copy(wv_ref, kv_start, kv, cols + kv, pieces + 1))

    if first:
        block = rows // n
        me, gy = lax.axis_index("gx"), lax.axis_index("gy")
        t_copies = []
        for slot in range(n):
            start = pl.multiple_of(slot_owner(n, slot, me, gy, bit_orders(n)) * block, block)
            t_copies.append(
                pltpu.make_async_copy(
                    tokens_ref.at[pl.ds(start, block), :], t_buf.at[slot], t_sems.at[slot]
                )
            )
            t_copies[-1].start()
        g_copy = pltpu.make_async_copy(gain_ref, g_buf, g_sem)
        g_copy.start()
    for group in copies:
        for copy in group:
            copy.start()
    if first:
        lanes = lax.broadcasted_iota(jnp.int32, (block, 128), 1)
        g_copy.wait()
        for slot in range(n):
            t_copies[slot].wait()
            wide = t_buf[slot].astype(jnp.float32)
            x_ref[slot * block : (slot + 1) * block, :] = (wide * g_buf[...]).astype(jnp.bfloat16)
            square = jnp.sum(wide * wide, axis=1, keepdims=True)
            high = square.astype(jnp.bfloat16).astype(jnp.float32)
            rest = square - high
            middle = rest.astype(jnp.bfloat16).astype(jnp.float32)
            low = rest - middle
            packed = jnp.where(
                lanes == 3 * me,
                high,
                jnp.where(lanes == 3 * me + 1, middle, jnp.where(lanes == 3 * me + 2, low, 0.0)),
            )
            if slot < n // 2:
                keep_ref[slot * block : (slot + 1) * block, width : width + 128] = packed
            else:
                at = (slot - n // 2) * block
                send_ref[at : at + block, width : width + 128] = packed.astype(jnp.bfloat16)

    for p in range(pieces):
        start, end = p * tile, (p + 1) * tile if p < pieces - 1 else width
        for copy in copies[p]:
            copy.wait()
        product = jnp.dot(x_ref[...], w_buf[:, start:end], preferred_element_type=jnp.float32)
        keep_ref[:, start:end] = product[:half]
        send_ref[:, start:end] = product[half:].astype(jnp.bfloat16)


def in_hbm(value):
    return pltpu.with_memory_space_constraint(value, pltpu.HBM)


def project(n, q_start, q_cols, kv_start, first, x, gain, w_query, w_key, w_value):
    rows, depth = x.shape
    kv = w_key.shape[1] // CHUNKS if kv_start is not None else 0
    width = q_cols + 2 * kv
    full = width + (128 if first else 0)
    hbm = pl.BlockSpec(memory_space=pltpu.HBM)
    vmem = pl.BlockSpec(memory_space=pltpu.VMEM)
    out_shape = [
        pltpu.VMEM((rows // 2, full), jnp.bfloat16),
        pltpu.VMEM((rows // 2, full), jnp.float32),
    ]
    scratch = [pltpu.VMEM((depth, width), jnp.bfloat16), pltpu.SemaphoreType.DMA((6,))]
    if first:
        out_shape.append(pltpu.VMEM((rows, depth), jnp.bfloat16))
        args = [in_hbm(x), in_hbm(gain)]
        in_specs = [hbm, hbm]
        scratch = [
            pltpu.VMEM((n, rows // n, depth), jnp.bfloat16),
            pltpu.SemaphoreType.DMA((n,)),
            pltpu.VMEM((1, depth), jnp.float32),
            pltpu.SemaphoreType.DMA,
        ] + scratch
    else:
        args, in_specs = [x], [vmem]
    return pl.pallas_call(
        functools.partial(project_kernel, n, q_start, kv_start, first),
        out_shape=out_shape,
        in_specs=in_specs + [hbm] * 3,
        out_specs=[vmem] * len(out_shape),
        scratch_shapes=scratch,
        compiler_params=pltpu.CompilerParams(vmem_limit_bytes=16 * MIB),
        name="project",
    )(*args, in_hbm(w_query), in_hbm(w_key), in_hbm(w_value))


def attend_kernel(chunk, offsets, kv_offset, groups, heads, seqs, length_ref, *refs):
    sum_ref, square_ref = refs[:2]
    w_copies = []
    if chunk == 0:
        cos_ref, sin_ref, k_ref, v_ref, w_ref, out_ref, next_ref, q_scr, o_scr, w_sems = refs[2:]
        total = next_ref.shape[0]
        for p in range(4):
            at = slice(p * total // 4, (p + 1) * total // 4)
            w_copies.append(
                pltpu.make_async_copy(
                    w_ref.at[total + at.start : total + at.stop], next_ref.at[at], w_sems.at[p]
                )
            )
            w_copies[-1].start()
    else:
        cos_ref, sin_ref, k_ref, v_ref, out_ref, q_scr, o_scr = refs[2:]
    rows = seqs * NEW
    cols = groups * heads * HD
    kv = groups * HD
    seq_count = k_ref.shape[0]

    scale = HD**-0.5 * math.log2(math.e)
    slots = k_ref.shape[1]
    many = heads * NEW
    slot_ids = lax.broadcasted_iota(jnp.int32, (1, slots), 1)
    new_cols = lax.broadcasted_iota(jnp.int32, (many, rows), 1)
    new_rows = lax.broadcasted_iota(jnp.int32, (many, rows), 0) % NEW

    @pl.loop(0, seq_count // seqs, unroll=chunk > 0)
    def _(step):
        mine = pl.ds(pl.multiple_of(step * rows, rows), rows)
        mean = jnp.sum(square_ref[mine, :], axis=1, keepdims=True) / D
        row_scale = lax.rsqrt(mean + EPS)
        cosine, sine = cos_ref[mine, :], sin_ref[mine, :]

        def raw(start):
            return sum_ref[mine, start : start + HD] * row_scale

        def rotary(value):
            return value * cosine + pltpu.roll(value, HD // 2, 1) * sine

        for h in range(heads * groups):
            turned = rotary(raw(offsets[h]))
            for s in range(seqs):
                q_scr[s, h * NEW : (h + 1) * NEW, :] = turned[s * NEW : (s + 1) * NEW]
        for g in range(groups):
            new_keys = rotary(raw(kv_offset + g * HD)).astype(jnp.bfloat16)
            new_values = raw(kv_offset + (groups + g) * HD).astype(jnp.bfloat16)
            lanes = slice(chunk * kv + g * HD, chunk * kv + (g + 1) * HD)
            olds, news, mixes = [], [], []
            for s in range(seqs):
                query = q_scr[s, g * many : (g + 1) * many, :].astype(jnp.bfloat16)
                keys = k_ref[step * seqs + s, :, lanes]
                olds.append(
                    lax.dot_general(
                        query, keys, (((1,), (1,)), ((), ())), preferred_element_type=jnp.float32
                    )
                )
                news.append(
                    lax.dot_general(
                        query, new_keys, (((1,), (1,)), ((), ())), preferred_element_type=jnp.float32
                    )
                )
            for s in range(seqs):
                live = slot_ids < length_ref[step * seqs + s]
                seen = (new_cols >= s * NEW) & (new_cols <= s * NEW + new_rows)
                old = jnp.where(live, olds[s] * scale, -1e30)
                new = jnp.where(seen, news[s] * scale, -1e30)
                top = jnp.maximum(
                    jnp.max(old, axis=1, keepdims=True), jnp.max(new, axis=1, keepdims=True)
                )
                old = jnp.exp2(old - top)
                new = jnp.exp2(new - top)
                total = jnp.sum(old, axis=1, keepdims=True) + jnp.sum(new, axis=1, keepdims=True)
                inverse = 1.0 / total
                olds[s] = (old * inverse).astype(jnp.bfloat16)
                news[s] = (new * inverse).astype(jnp.bfloat16)
            for s in range(seqs):
                values = v_ref[step * seqs + s, :, lanes]
                mixes.append(
                    jnp.dot(olds[s], values, preferred_element_type=jnp.float32)
                    + jnp.dot(news[s], new_values, preferred_element_type=jnp.float32)
                )
            for s in range(seqs):
                for h in range(heads):
                    at = (g * heads + h) * HD
                    o_scr[s * NEW : (s + 1) * NEW, at : at + HD] = mixes[s][
                        h * NEW : (h + 1) * NEW
                    ]
        out_ref[mine, :] = o_scr[...].astype(jnp.bfloat16)

    for copy in w_copies:
        copy.wait()


def attend(chunk, offsets, kv_offset, sums, squares, cosine, sine, cache_keys, cache_values, lengths, w_out):
    seq_count, slots, kv_all = cache_keys.shape
    kv = kv_all // CHUNKS
    groups = kv // HD
    heads = len(offsets) // groups
    cols = len(offsets) * HD
    seqs = min(4, seq_count)
    rows = seq_count * NEW
    source, copied = [], []
    if chunk == 0:
        source.append(in_hbm(w_out))
        copied.append(pltpu.VMEM((w_out.shape[0] // CHUNKS, w_out.shape[1]), w_out.dtype))
    vmem = pl.BlockSpec(memory_space=pltpu.VMEM)
    hbm = pl.BlockSpec(memory_space=pltpu.HBM)
    return pl.pallas_call(
        functools.partial(attend_kernel, chunk, offsets, kv_offset, groups, heads, seqs),
        out_shape=[pltpu.VMEM((rows, cols), jnp.bfloat16)] + copied,
        in_specs=[pl.BlockSpec(memory_space=pltpu.SMEM)] + [vmem] * 6 + [hbm] * len(source),
        out_specs=[vmem] * (1 + len(copied)),
        scratch_shapes=[
            pltpu.VMEM((seqs, groups * heads * NEW, HD), jnp.float32),
            pltpu.VMEM((seqs * NEW, cols), jnp.float32),
        ]
        + [pltpu.SemaphoreType.DMA((4,))] * len(copied),
        compiler_params=pltpu.CompilerParams(vmem_limit_bytes=16 * MIB),
        name="attend",
    )(lengths, sums, squares, cosine, sine, cache_keys, cache_values, *source)


def fetch_kernel(count, pieces, *refs):
    sources, targets, sems = refs[:count], refs[count : 2 * count], refs[2 * count]
    copies = []
    for i, (source, target) in enumerate(zip(sources, targets)):
        size = target.shape[0] // pieces
        for p in range(pieces):
            at = slice(p * size, (p + 1) * size)
            copies.append(
                pltpu.make_async_copy(source.at[at], target.at[at], sems.at[i * pieces + p])
            )
    for copy in copies:
        copy.start()
    for copy in copies:
        copy.wait()


def fetch(*arrays):
    pieces = 4
    return pl.pallas_call(
        functools.partial(fetch_kernel, len(arrays), pieces),
        out_shape=[pltpu.VMEM(array.shape, array.dtype) for array in arrays],
        in_specs=[pl.BlockSpec(memory_space=pltpu.HBM)] * len(arrays),
        out_specs=[pl.BlockSpec(memory_space=pltpu.VMEM)] * len(arrays),
        scratch_shapes=[pltpu.SemaphoreType.DMA((pieces * len(arrays),))],
        compiler_params=pltpu.CompilerParams(vmem_limit_bytes=4 * MIB),
        name="fetch",
    )(*[in_hbm(array) for array in arrays])


def fetch_rows_kernel(start, pieces, source, target, sems):
    size = target.shape[0] // pieces
    copies = [
        pltpu.make_async_copy(
            source.at[start + p * size : start + (p + 1) * size],
            target.at[p * size : (p + 1) * size],
            sems.at[p],
        )
        for p in range(pieces)
    ]
    for copy in copies:
        copy.start()
    for copy in copies:
        copy.wait()


def fetch_rows(array, start, rows):
    pieces = 4
    return pl.pallas_call(
        functools.partial(fetch_rows_kernel, start, pieces),
        out_shape=pltpu.VMEM((rows, array.shape[1]), array.dtype),
        in_specs=[pl.BlockSpec(memory_space=pltpu.HBM)],
        out_specs=pl.BlockSpec(memory_space=pltpu.VMEM),
        scratch_shapes=[pltpu.SemaphoreType.DMA((pieces,))],
        compiler_params=pltpu.CompilerParams(vmem_limit_bytes=4 * MIB),
        name="fetch_rows",
    )(in_hbm(array))


def combine_kernel(n, block, chunk, *refs):
    pieces, refs = refs[:n], refs[n:]
    gx, gy = lax.axis_index("gx"), lax.axis_index("gy")
    moved = jnp.where(gy == 0, n // 2, 0)
    if chunk:
        before_ref, refs = refs[0], refs[1:]
    w_ref, outs, x_buf = refs[0], refs[1:-1], refs[-1]
    depth, cols = x_buf.shape[1], w_ref.shape[1]
    half = x_buf.shape[0] // 2
    for slot, piece in enumerate(pieces):
        owner = slot_owner(n, slot, gx, gy, gather_orders(n, chunk))
        start = pl.multiple_of((owner ^ moved) * block, block)
        x_buf[pl.ds(start, block), :] = piece[...]

    tile = cols // TILES
    for start in range(0, cols, tile):
        at = slice(start, start + tile)
        product = jnp.dot(x_buf[...], w_ref[:, at], preferred_element_type=jnp.float32)
        if chunk:
            product = product + before_ref[:, at]
        if len(outs) == 1:
            outs[0][:, at] = product
        else:
            outs[0][:, at] = product[:half].astype(jnp.bfloat16)
            outs[1][:, at] = product[half:]


def combine(chunk, pieces, before, w_out):
    n, (block, depth) = len(pieces), pieces[0].shape
    rows = n * block
    cols = w_out.shape[1]
    last = chunk == CHUNKS - 1
    hbm = pl.BlockSpec(memory_space=pltpu.HBM)
    vmem = pl.BlockSpec(memory_space=pltpu.VMEM)
    if last:
        out_shape = [
            pltpu.VMEM((rows // 2, cols), jnp.bfloat16),
            pltpu.VMEM((rows // 2, cols), jnp.float32),
        ]
    else:
        out_shape = [pltpu.VMEM((rows, cols), jnp.float32)]
    earlier = [] if chunk == 0 else [before]
    return pl.pallas_call(
        functools.partial(combine_kernel, n, block, chunk),
        out_shape=out_shape,
        in_specs=[vmem] * (len(pieces) + len(earlier) + 1),
        out_specs=[vmem] * len(out_shape),
        scratch_shapes=[
            pltpu.VMEM((rows, depth), jnp.bfloat16),
        ],
        compiler_params=pltpu.CompilerParams(vmem_limit_bytes=16 * MIB),
        name="combine",
    )(*pieces, *earlier, w_out)


def shards(
    tokens, norm_gain, w_query, w_key, w_value, w_out, cache_keys, cache_values, cache_lengths
):
    n = lax.axis_size("gx")
    cores = lax.axis_size("gy")
    levels = n.bit_length() - 1
    position = (cache_lengths[:, None] + jnp.arange(NEW, dtype=jnp.int32)[None, :]).reshape(-1)
    inverse = THETA ** (-2.0 * jnp.arange(HD // 2, dtype=jnp.float32) / HD)
    angles = position.astype(jnp.float32)[:, None] * inverse[None, :]
    cosine, sine = jnp.cos(angles), jnp.sin(angles)
    cosine = jnp.concatenate([cosine, cosine], axis=1)
    sine = jnp.concatenate([-sine, sine], axis=1)

    x, gain = tokens, norm_gain[None, :]
    kv = w_key.shape[1] // CHUNKS
    q_cols = w_query.shape[1] // CHUNKS

    def column_part(start, size, kv_start):
        return project(
            n, start, size, kv_start, start == 0, x, gain, w_query, w_key, w_value
        )

    def after(value, *earlier):
        return lax.optimization_barrier((value, earlier))[0]

    share = q_cols // 2
    orders = bit_orders(n)
    send_a, keep_a, x = column_part(0, share, None)
    x = after(x, send_a)
    other_a = exchange(send_a, n, cores, 0, orders)
    send_b, keep_b = column_part(share, share, 0)
    x = after(x, send_b)
    other_b = exchange(send_b, n, cores, 0, orders)
    sum_a = keep_a + other_a.astype(jnp.float32)
    x = after(x, sum_a)
    later = []
    for chunk in range(1, CHUNKS):
        later.append(column_part(chunk * q_cols, q_cols, chunk * kv))
    other_b = after(other_b, *(send_c for send_c, _ in later))
    first = jnp.concatenate([sum_a, keep_b + other_b.astype(jnp.float32)], axis=1)
    half = first.shape[0] // 2
    send = first[half:].astype(jnp.bfloat16)
    flows = [[1, first[:half], send]]
    for send_c, keep_c in later:
        flows.append([0, keep_c, after(send_c, flows[-1][2])])

    def start(flow):
        return exchange(flow[2], n, cores, flow[0], orders)

    def finish(flow, other, *earlier):
        stage, keep, _ = flow
        if earlier:
            other = after(other, *earlier)
        value = keep + other.astype(jnp.float32)
        low = value.shape[0] // 2 if stage < levels - 1 else 0
        flow[:] = stage + 1, value[:low] if low else value, value[low:].astype(jnp.bfloat16)

    lead, follow = flows
    w_rows = w_out.shape[0] // CHUNKS
    weights = [fetch_rows(after(w_out, lead[2], follow[2]), 0, w_rows)]
    while follow[0] < levels:
        pending = [start(flow) for flow in flows if flow[0] < levels]
        if lead[0] == levels:
            finish(follow, pending[0])
        elif lead[0] == levels - 1:
            cache_keys, cache_values = fetch(*after((cache_keys, cache_values), follow[2]))
            finish(lead, pending[0], cache_keys, cache_values)
            finish(follow, pending[1], lead[1])
        else:
            finish(lead, pending[0], *weights)
            finish(follow, pending[1], lead[2])
    sums = [flow[1] for flow in flows]
    squares = sums[0][:, share : share + 128]
    plain = [h * HD for h in range(q_cols // HD)]
    offsets = [[at if at < share else at + 128 for at in plain], plain]
    kv_offsets = [q_cols + 128, q_cols]

    attentions = []
    for chunk in range(CHUNKS):
        out = attend(
            chunk,
            offsets[chunk],
            kv_offsets[chunk],
            sums[chunk],
            squares,
            cosine,
            sine,
            cache_keys,
            cache_values,
            cache_lengths,
            w_out,
        )
        attentions.append(out[0])
        weights += out[1:]
    gathered = []
    for chunk in range(CHUNKS):
        slots = [attentions[chunk]]
        for slot in range(1, n):
            top = slot.bit_length() - 1
            source = slots[slot - (1 << top)]
            if slot == 1 and chunk == 0:
                source = after(source, sums[1])
            if slot == 3 << (levels - 2):
                source = after(source, slots[1 << (levels - 1)])
            slots.append(
                exchange(source, n, cores, levels - 1 - top, gather_orders(n, chunk))
            )
        gathered.append(slots)
    result = None
    for chunk in range(CHUNKS):
        result = combine(chunk, gathered[chunk], result and result[0], weights[chunk])
    send, keep = result
    other = lax.ppermute(send, "gy", [(0, 1), (1, 0)])
    return (keep + other.astype(jnp.float32)).astype(jnp.bfloat16)


def solution(mesh):
    return jax.shard_map(
        shards,
        mesh=mesh,
        in_specs=(
            P("groups", "gx"),
            P("gx"),
            P("gx", "gy"),
            P("gx", "gy"),
            P("gx", "gy"),
            P("gy", "gx"),
            P(("groups", "gx"), None, "gy"),
            P(("groups", "gx"), None, "gy"),
            P(("groups", "gx")),
        ),
        out_specs=P(("groups", "gy"), "gx"),
        check_vma=False,
    )
```
